128 devices in a mesh: batch: 128 (over z, x, y, core).
Axes of the slice: x: 4, y: 4, z: 4, core: 2. Of those that a mesh axis runs over, the one named last changes fastest.
Arguments:
- inputs: bfloat16 [384, 70, 1150], P('batch')
- d_out: bfloat16 [384, 70, 1150], P('batch'), may hold values from -6 to 6
- h_start: float32 [384, 1150], P('batch'), may hold values from -0.9 to 0.9
- c_start: float32 [384, 1150], P('batch'), may hold values from -4 to 4
- pieces: int32 [384, 3], P('batch'), may hold values from 1 to 40, 70 in all within a row
- in_mask: int32 [384, 1150], P('batch'), may hold values 0 or 1
- out_mask: int32 [384, 1150], P('batch'), may hold values 0 or 1
- w_mask: int32 [10584704], P('batch'), may hold values 0 or 1
- master: float32 [10584704], P('batch'), may hold values from -2 to 6
- moment_one: float32 [10584704], P('batch'), may hold values from -0.00048828125 to 0.00048828125
- moment_two: float32 [10584704], P('batch'), may hold values from 9.4476885e-11 to 3.7790754e-10
Outputs:
- output: bfloat16 [384, 70, 1150], P('batch')
- d_inputs: bfloat16 [384, 70, 1150], P('batch')
- moment_new: float32 [10584704], P('batch')
- second_new: float32 [10584704], P('batch')
- master_new: float32 [10584704], P('batch')
- grad_norm: float32 [], replicated
The draws below stay inside these ranges and needn't reach their ends.
Inputs may be any that keep to these rules, and one draw needn't show every extreme that they name: `pieces`: each row's three lengths sum to 70; the padding comes last.
All inputs are finite; a program needn't handle non-finite values. No bound on the sum of `in_mask` or of `out_mask` or of `w_mask` on one device may be relied on, other than what follows from the above.
Results may differ from the reference program's by a relative error of at most 0.012.
The reference program's roundings to bfloat16 on the way count: a program that leaves them out, or rounds other values in their place, can miss the bound.
Values may be sent and summed in bfloat16 or wider, within the bound.
No kernel may reach another device: no remote copies, remote signals or barrier semaphores. Data moves between devices by JAX's collectives and lax.ppermute only.
A program may use at most 256 MiB of HBM per device.

```python
import math
import jax
import jax.numpy as jnp
import numpy as np
from jax import lax

D = 1150
G = 4600
BLOCK = 70
STEP = 10
STREAMS = 384
FLAT = 10584704


def draw_inputs(key, part):
    key = jax.random.fold_in(key, 1)
    ramp = jnp.arange(D, dtype=jnp.float32) / D
    base = jax.random.normal(key, (STREAMS, BLOCK, D), jnp.float32)
    scale = 0.5 * 3.0 ** ramp
    return (base * scale).astype(jnp.bfloat16)


def draw_master(key, part):
    key = jax.random.fold_in(key, 2)
    key_base, key_slow, key_bias = jax.random.split(key, 3)
    count_w = 2 * D * G
    base = jnp.clip(jax.random.normal(key_base, (FLAT,), jnp.float32), -4.0, 4.0)
    share = 0.5
    slow = (jax.random.uniform(key_slow, (D,), jnp.float32) < share).astype(jnp.float32)
    column_scale = 1.0 - 0.5 * slow
    ones = jnp.ones((D,), jnp.float32)
    gate_scale = jnp.concatenate([ones, column_scale, ones, ones])
    row_scale = jnp.concatenate([gate_scale, gate_scale])
    weights = base[:count_w].reshape(D, 2 * G) * D ** (-0.5) * row_scale[None, :]
    uniform_bias = jax.random.uniform(key_bias, (4, D), jnp.float32)
    in_bias = -2.0 + uniform_bias[0]
    forget_bias = slow * (4.5 + 1.5 * uniform_bias[1]) + (1.0 - slow) * (2.5 + uniform_bias[1])
    cand_bias = -0.5 + uniform_bias[2]
    out_bias = -0.5 + uniform_bias[3]
    bias = jnp.concatenate([in_bias, forget_bias, cand_bias, out_bias])
    tail = base[count_w + G:] * D ** (-0.5)
    return jnp.concatenate([weights.reshape(-1), bias, tail])


def set_ends(values, own_key, smallest, top_value):
    longest = values.shape.index(max(values.shape))
    spots = []
    for shift in (0, 1):
        where = [jax.random.randint(jax.random.fold_in(own_key, axis), (), 0, length) for axis, length in enumerate(values.shape)]
        where[longest] = (where[longest] + shift) % values.shape[longest]
        spots.append(tuple(where))
    return values.at[spots[0]].set(smallest).at[spots[1]].set(top_value)


def level_of(rng, shape, shards, low, top_value):
    def one(dim, shards_of):
        steps = jax.random.uniform(jax.random.fold_in(jax.random.fold_in(rng, 6), dim), (shards_of,), jnp.float32, low / len(shards), top_value / len(shards))
        return jnp.repeat(jnp.exp(steps), shape[dim] // shards_of).reshape((-1,) + (1,) * (len(shape) - dim - 1))

    loudness = one(*shards[0])
    for cut in shards[1:]:
        loudness = loudness * one(*cut)
    return loudness


def length_profile(count, total, bound, lean):
    weights = [(1 << 20) // math.isqrt(rank ** lean) + 1 for rank in range(2, count + 1)]
    spare, given = total - bound - (count - 1), [1] * (count - 1)
    while spare > 0:
        candidates = [i for i in range(count - 1) if given[i] < bound]
        whole, left = sum([weights[i] for i in candidates]), spare
        for i in candidates:
            extra = min(bound - given[i], max(1, left * weights[i] // whole), spare)
            given[i] = given[i] + extra
            spare = spare - extra
    return np.array([bound] + given)


def uneven_parts(key, count, total, bound, lean):
    if count == 2:
        one = jax.random.randint(key, (), max(1, total - bound), min(bound, total - 1) + 1)
        return jnp.stack([one, total - one])
    tallies = jnp.asarray(length_profile(count, total, bound, lean), jnp.int32)
    twos = (count - 1) // 2
    giver, taker = tallies[1:1 + 2 * twos:2], tallies[2:2 + 2 * twos:2]
    room = jnp.minimum(giver - 1, bound - taker)
    shifted = jax.random.randint(jax.random.fold_in(key, 1), (twos,), 0, 1 << 20) % (room + 1)
    tallies = tallies.at[1:1 + 2 * twos:2].set(giver - shifted).at[2:2 + 2 * twos:2].set(taker + shifted)
    return tallies[jax.random.permutation(jax.random.fold_in(key, 2), count)]


def gaussian(rng, extent, scale, limit, cuts=(), kind=jnp.bfloat16):
    drawn = jax.random.normal(rng, extent, jnp.float32) * scale
    if len(cuts) > 0:
        drawn = level_of(rng, extent, cuts, -0.22, 0.18) * drawn
    return jnp.clip(drawn, min=-limit, max=limit).astype(kind)


def setup_inputs(seed: int = 0) -> dict:
    seeds = jax.random.split(jax.random.key(seed), 12)
    return {
        "inputs": draw_inputs(jax.random.fold_in(seeds[11], 71), 0),
        "d_out": gaussian(seeds[1], (STREAMS, BLOCK, D), 1.0, 6.0, ((0, 128),)),
        "h_start": jnp.clip(jax.random.uniform(seeds[2], (STREAMS, D), jnp.float32, -0.9, 0.9) * level_of(seeds[2], (STREAMS, D), ((0, 128),), -0.4, 0.0), -0.9, 0.9),
        "c_start": gaussian(seeds[3], (STREAMS, D), 1.0, 4.0, ((0, 128),), jnp.float32),
        "pieces": jax.vmap(lambda own: uneven_parts(own, 3, BLOCK, BLOCK * 4 // 7, 0))(jax.random.split(seeds[4], STREAMS)).reshape((STREAMS, 3)).astype(jnp.int32),
        "in_mask": set_ends((jax.random.randint(seeds[5], (STREAMS, D), 0, 4) < 3).astype(jnp.int32), jax.random.fold_in(seeds[5], 1), 0, 1),
        "out_mask": set_ends((jax.random.randint(seeds[6], (STREAMS, D), 0, 4) < 3).astype(jnp.int32), jax.random.fold_in(seeds[6], 1), 0, 1),
        "w_mask": set_ends((jax.random.randint(seeds[7], (FLAT,), 0, 2) < 1).astype(jnp.int32), jax.random.fold_in(seeds[7], 1), 0, 1),
        "master": draw_master(jax.random.fold_in(seeds[11], 71), 0),
        "moment_one": gaussian(seeds[9], (FLAT,), (0.11 * (2 * D * G + G) ** -0.5), 0.00048828125, ((0, 128),), jnp.float32),
        "moment_two": jnp.clip(jnp.exp(math.log(3.779075385956787e-10) - 1.3862944 * jax.random.uniform(seeds[10], (FLAT,), jnp.float32) ** level_of(seeds[10], (FLAT,), ((0, 128),), -0.2, 0.2)), 9.447688464891968e-11, 3.779075385956787e-10),
    }


@jax.custom_vjp
def low(v):
    return lax.optimization_barrier(v.astype(jnp.bfloat16)).astype(jnp.float32)

@jax.custom_vjp
def low_back(v):
    return v

def low_keep(v):
    return (low(v), None)

def low_pass(kept, grad):
    return (grad,)

def back_keep(v):
    return (v, None)

def back_low(kept, grad):
    return (low(grad),)
low.defvjp(low_keep, low_pass)
low_back.defvjp(back_keep, back_low)
LEARN_RATE = 0.03
BETA_ONE = 0.9
BETA_TWO = 0.999
WEIGHT_DECAY = 0.01
EPSILON = 1e-08
CLIP_NORM = 1.0
KEEP_INPUT = 4.0 / 3.0
KEEP_OUTPUT = 4.0 / 3.0
KEEP_RECURRENT = 2.0

def reference(inputs, d_out, h_start, c_start, pieces, in_mask, out_mask, w_mask, master, moment_one, moment_two):
    precise = lax.Precision.HIGHEST
    count_w = 2 * D * G
    total = count_w + G
    position = jnp.arange(BLOCK, dtype=jnp.int32)
    resets = (position[None, :] == pieces[:, 0:1]).astype(jnp.float32)
    valid = (position[None, :] < pieces[:, 0:1] + pieces[:, 1:2]).astype(jnp.float32)
    in_scale = in_mask.astype(jnp.float32) * KEEP_INPUT
    out_scale = out_mask.astype(jnp.float32) * KEEP_OUTPUT
    rec_scale = w_mask[:count_w].reshape(D, 2 * G)[:, G:].astype(jnp.float32) * KEEP_RECURRENT

    def forward(source, params):
        weights = low(params[:count_w]).reshape(D, 2 * G)
        bias = low(params[count_w:])
        w_in = weights[:, :G]
        w_rec = weights[:, G:] * rec_scale
        mixed = low(source * in_scale[:, None, :])
        pre = jnp.einsum('btd,dg->tbg', mixed, w_in, precision=precise) + bias

        def step(carry, slab):
            hidden, cell = carry
            pre_t, reset_t = slab
            keep = 1.0 - reset_t[:, None]
            hidden = hidden * keep
            cell = cell * keep
            gates = low_back(pre_t + jnp.dot(low(hidden), w_rec, precision=precise))
            in_gate = jax.nn.sigmoid(gates[:, :D])
            forget = jax.nn.sigmoid(gates[:, D:2 * D])
            candid = jnp.tanh(gates[:, 2 * D:3 * D])
            out_gate = jax.nn.sigmoid(gates[:, 3 * D:])
            cell = forget * cell + in_gate * candid
            hidden = out_gate * jnp.tanh(cell)
            return ((hidden, cell), hidden)
        _, states = lax.scan(jax.checkpoint(step), (h_start, c_start), (pre, resets.T))
        states = jnp.transpose(states, (1, 0, 2))
        return states * valid[:, :, None] * out_scale[:, None, :]
    source = inputs.astype(jnp.float32)
    params = master[:total]
    output, pullback = jax.vjp(forward, source, params)
    d_source, d_params = pullback(d_out.astype(jnp.float32))
    grad = jnp.concatenate([d_params, jnp.zeros((FLAT - total,), jnp.float32)])
    grad_norm = jnp.sqrt(jnp.sum(grad * grad))
    factor = jnp.minimum(1.0, CLIP_NORM / (grad_norm + 1e-06))
    clipped = grad * factor
    moment_new = BETA_ONE * moment_one + (1.0 - BETA_ONE) * clipped
    second_new = BETA_TWO * moment_two + (1.0 - BETA_TWO) * clipped * clipped
    first_hat = moment_new / (1.0 - BETA_ONE ** STEP)
    second_hat = second_new / (1.0 - BETA_TWO ** STEP)
    master_new = master - LEARN_RATE * (first_hat / (jnp.sqrt(second_hat) + EPSILON) + WEIGHT_DECAY * master)
    return (output.astype(jnp.bfloat16), d_source.astype(jnp.bfloat16), moment_new, second_new, master_new, grad_norm)
```

```python
import functools

import jax
import jax.numpy as jnp
from jax import lax
from jax.experimental import pallas as pl
from jax.experimental.pallas import tpu as pltpu
from jax.sharding import PartitionSpec as P

STEP = 10


LEARN_RATE = 0.03
BETA_ONE = 0.9
BETA_TWO = 0.999
WEIGHT_DECAY = 0.01
EPSILON = 1e-08
CLIP_NORM = 1.0
KEEP_INPUT = 4.0 / 3.0
KEEP_OUTPUT = 4.0 / 3.0
KEEP_RECURRENT = 2.0

LONGEST = 40
LANES = 8
TILE = 8
OWN = TILE + 1
VMEM_LIMIT = 60 * 2**20

f32 = jnp.float32
bf16 = jnp.bfloat16


def dot(left, right):
    return lax.dot_general(left, right, (((1,), (0,)), ((), ())), preferred_element_type=f32)


def one_hot(rows, columns, wanted):
    row = lax.broadcasted_iota(jnp.int32, (rows, columns), 0)
    column = lax.broadcasted_iota(jnp.int32, (rows, columns), 1)
    return wanted(row, column).astype(bf16)


def place_of(natural, devices):
    owner, rest = natural // OWN, natural % OWN
    return jnp.where(rest < TILE, owner * TILE + rest, devices * TILE + owner)


def load_weights(wall, extra, half, into, sems, width, devices):
    main = devices * TILE
    gates_n = 4 * width
    copies = [
        pltpu.make_async_copy(
            wall.at[:, pl.ds(half * gates_n, gates_n)], into.at[pl.ds(0, main), :], sems.at[0]
        )
    ]
    for gate in range(4):
        copies.append(
            pltpu.make_async_copy(
                extra.at[pl.ds((4 * half + gate) * devices, devices), :],
                into.at[pl.ds(main, devices), pl.ds(gate * width, width)],
                sems.at[1 + gate],
            )
        )
    return copies


def step_rows(step):
    return pl.ds(pl.multiple_of(step * LANES, LANES), LANES)


def forward_kernel(
    devices,
    wall,
    extra,
    mixed,
    spread,
    collect,
    h_first,
    c_first,
    out_scale,
    hidden_rows,
    output_rows,
    kept,
    w_in,
    w_rec,
    pre,
    hiddens,
    outs,
    sems_in,
    sems_rec,
):
    width = mixed.shape[1]
    gates_n = 4 * width
    copies_in = load_weights(wall, extra, 0, w_in, sems_in, width, devices)
    copies_rec = load_weights(wall, extra, 1, w_rec, sems_rec, width, devices)
    for copy in copies_in + copies_rec:
        copy.start()
    rows = dot(spread[...], mixed[...]).astype(bf16)
    for copy in copies_in:
        copy.wait()
    chunk = 512

    def pre_chunk(index, carry):
        columns = pl.ds(pl.multiple_of(index * chunk, chunk), chunk)
        pre[:, columns] = dot(rows, w_in[:, columns])
        return carry

    lax.fori_loop(0, gates_n // chunk, pre_chunk, 0)
    for copy in copies_rec:
        copy.wait()
    scale = out_scale[...]

    def step(index, carry):
        hidden, cell = carry
        at = step_rows(index)
        gates = pre[at, :] + dot(hidden.astype(bf16), w_rec[...])
        in_gate = jax.nn.sigmoid(gates[:, :width])
        forget = jax.nn.sigmoid(gates[:, width : 2 * width])
        candid = jnp.tanh(gates[:, 2 * width : 3 * width])
        out_gate = jax.nn.sigmoid(gates[:, 3 * width :])
        cell_new = forget * cell + in_gate * candid
        squash = jnp.tanh(cell_new)
        hidden_new = out_gate * squash
        hiddens[at, :] = hidden
        outs[at, :] = hidden_new * scale
        kept[0, at, :] = out_gate * (1.0 - squash * squash)
        kept[1, at, :] = candid * in_gate * (1.0 - in_gate)
        kept[2, at, :] = cell * forget * (1.0 - forget)
        kept[3, at, :] = in_gate * (1.0 - candid * candid)
        kept[4, at, :] = squash * out_gate * (1.0 - out_gate)
        kept[5, at, :] = forget
        return (hidden_new, cell_new)

    lax.fori_loop(0, LONGEST, step, (h_first[...], c_first[...]))
    hidden_rows[...] = dot(collect[...], hiddens[...].astype(bf16)).astype(bf16)
    output_rows[...] = dot(collect[...], outs[...].astype(bf16)).astype(bf16)


def backward_kernel(
    devices,
    wall,
    extra,
    coming,
    spread,
    collect,
    out_scale,
    kept,
    gate_rows,
    w_rec,
    w_turned,
    come,
    dgates,
    sems,
):
    width = coming.shape[1]
    copies = load_weights(wall, extra, 1, w_rec, sems, width, devices)
    for copy in copies:
        copy.start()
    come[...] = dot(spread[...], coming[...])
    for copy in copies:
        copy.wait()

    def turn(index, carry):
        columns = pl.ds(pl.multiple_of(index * 128, 128), 128)
        w_turned[columns, :] = w_rec[:, columns].T
        return carry

    lax.fori_loop(0, 4 * width // 128, turn, 0)
    scale = out_scale[...]

    def step(count, carry):
        dh_next, dc_next = carry
        at = step_rows(LONGEST - 1 - count)
        grad_h = come[at, :] * scale + dh_next
        grad_c = dc_next + grad_h * kept[0, at, :]
        grads = jnp.concatenate(
            [
                grad_c * kept[1, at, :],
                grad_c * kept[2, at, :],
                grad_c * kept[3, at, :],
                grad_h * kept[4, at, :],
            ],
            axis=1,
        )
        dgates[at, :] = grads
        return (dot(grads.astype(bf16), w_turned[...]), grad_c * kept[5, at, :])

    zero = jnp.zeros((LANES, width), f32)
    lax.fori_loop(0, LONGEST, step, (zero, zero))
    for gate in range(4):
        columns = pl.ds(gate * width, width)
        gate_rows[gate] = dot(collect[...], dgates[:, columns].astype(bf16)).astype(bf16)


def in_vmem():
    return pl.BlockSpec(memory_space=pltpu.VMEM)


def in_place():
    return pl.BlockSpec(memory_space=pl.ANY)


def run_forward(devices, wall, extra, mixed, spread, collect, h_first, c_first, out_scale):
    steps_rows, rows = spread.shape
    width = mixed.shape[1]
    return pl.pallas_call(
        functools.partial(forward_kernel, devices),
        out_shape=(
            jax.ShapeDtypeStruct((rows, width), bf16),
            jax.ShapeDtypeStruct((rows, width), bf16),
            jax.ShapeDtypeStruct((6, steps_rows, width), f32),
        ),
        in_specs=[in_place()] * 2 + [in_vmem()] * 6,
        out_specs=(in_vmem(),) * 3,
        scratch_shapes=[
            pltpu.VMEM((width, 4 * width), bf16),
            pltpu.VMEM((width, 4 * width), bf16),
            pltpu.VMEM((steps_rows, 4 * width), f32),
            pltpu.VMEM((steps_rows, width), f32),
            pltpu.VMEM((steps_rows, width), f32),
            pltpu.SemaphoreType.DMA((5,)),
            pltpu.SemaphoreType.DMA((5,)),
        ],
        compiler_params=pltpu.CompilerParams(vmem_limit_bytes=VMEM_LIMIT),
        cost_estimate=pl.CostEstimate(
            flops=60_000_000_000, bytes_accessed=30_000_000, transcendentals=2_000_000
        ),
        name="forward",
    )(wall, extra, mixed, spread, collect, h_first, c_first, out_scale)


def run_backward(devices, wall, extra, coming, spread, collect, out_scale, kept):
    steps_rows, rows = spread.shape
    width = coming.shape[1]
    return pl.pallas_call(
        functools.partial(backward_kernel, devices),
        out_shape=jax.ShapeDtypeStruct((4, rows, width), bf16),
        in_specs=[in_place()] * 2 + [in_vmem()] * 5,
        out_specs=in_vmem(),
        scratch_shapes=[
            pltpu.VMEM((width, 4 * width), bf16),
            pltpu.VMEM((4 * width, width), bf16),
            pltpu.VMEM((steps_rows, width), f32),
            pltpu.VMEM((steps_rows, 4 * width), f32),
            pltpu.SemaphoreType.DMA((5,)),
        ],
        compiler_params=pltpu.CompilerParams(vmem_limit_bytes=VMEM_LIMIT),
        cost_estimate=pl.CostEstimate(
            flops=60_000_000_000, bytes_accessed=30_000_000, transcendentals=0
        ),
        name="backward",
    )(wall, extra, coming, spread, collect, out_scale, kept)


def split_exact(values):
    parts = []
    rest = values
    for _ in range(3):
        part = lax.reduce_precision(rest, 8, 7)
        parts.append(part.astype(bf16))
        rest = rest - part
    return parts


def body(
    inputs,
    d_out,
    h_start,
    c_start,
    pieces,
    in_mask,
    out_mask,
    w_mask,
    master,
    moment_one,
    moment_two,
):
    streams, steps, width = inputs.shape
    gates_n = 4 * width
    count_w = 2 * width * gates_n
    total = count_w + gates_n
    shard = master.shape[0]
    devices = lax.axis_size("batch")
    me = lax.axis_index("batch")
    wide = OWN * devices
    block = OWN * 2 * gates_n
    gap = block - shard
    most = gap * devices
    tokens = streams * steps
    rows_n = -(-tokens // 32) * 32
    line = 8
    lines = devices // line

    line_groups = [[line * q + m for m in range(line)] for q in range(lines)]
    across_groups = [[line * q + m for q in range(lines)] for m in range(line)]
    column_groups = [
        [line * q + 2 * y + c for y in range(line // 2)] for q in range(lines) for c in range(2)
    ]
    twins = [(i, i ^ 1) for i in range(devices)]

    to_kept = one_hot(width, wide, lambda k, p: place_of(k, devices) == p)
    to_natural = one_hot(wide, width, lambda p, k: place_of(k, devices) == p)

    places = me * shard + lax.iota(jnp.int32, shard)
    recurrent = (places < count_w) & (places % (2 * gates_n) >= gates_n)
    rec_scale = jnp.where(recurrent, w_mask.astype(f32) * KEEP_RECURRENT, 1.0)
    local_low = master.astype(bf16) * rec_scale.astype(bf16)
    local_low = jnp.where(places < total, local_low, jnp.zeros((), bf16))
    head = lax.ppermute(local_low[:most], "batch", [(i + 1, i) for i in range(devices - 1)])
    own = lax.dynamic_slice(jnp.concatenate([local_low, head]), (gap * me,), (block,))
    own = own.reshape(OWN * 8, width)
    order = one_hot(
        OWN * 8,
        OWN * 8,
        lambda a, b: jnp.where(a < 64, (a % 8) * 8 + a // 8, 64 + a % 8) == b,
    )
    own = dot(order, dot(own, to_kept).astype(bf16)).astype(bf16)
    own = jnp.concatenate([own[TILE * j : TILE * (j + 1)] for j in range(OWN)], axis=1)
    wall = lax.all_gather(own, "batch", axis=0, tiled=True)
    gather_ninth = one_hot(
        8 * devices, 8 * devices, lambda a, b: (a % devices) * 8 + a // devices == b
    )
    extra = dot(gather_ninth, wall[:, 8 * wide :]).astype(bf16)

    in_scale = in_mask.astype(f32) * KEEP_INPUT
    mixed = (inputs.astype(f32) * in_scale[:, None, :]).astype(bf16).reshape(tokens, width)
    spare = ((0, rows_n - tokens), (0, 0))
    mixed = dot(jnp.pad(mixed, spare), to_kept).astype(bf16)
    bias_place = place_of(jnp.int32(width), devices)
    column = lax.broadcasted_iota(jnp.int32, mixed.shape, 1)
    mixed = jnp.where(column == bias_place, jnp.ones((), bf16), mixed)
    coming = dot(jnp.pad(d_out.reshape(tokens, width), spare), to_kept).astype(bf16)
    small = jnp.concatenate(
        [h_start.astype(bf16)]
        + split_exact(c_start)
        + [in_mask.astype(bf16), out_mask.astype(bf16)],
        axis=0,
    )
    small = dot(small, to_kept)
    part = [small[streams * j : streams * (j + 1)] for j in range(6)]
    empty = jnp.zeros((LANES - streams, wide), f32)
    h_first = jnp.concatenate([part[0], empty], axis=0)
    c_first = jnp.concatenate([part[1] + part[2] + part[3], empty], axis=0)
    in_scale_kept = part[4] * KEEP_INPUT
    out_scale_kept = part[5] * KEEP_OUTPUT
    out_scale = jnp.concatenate(
        [out_scale_kept, out_scale_kept, jnp.zeros((LANES - 2 * streams, wide), f32)], axis=0
    )
    base = jnp.arange(streams, dtype=jnp.int32) * steps
    none = jnp.zeros((LANES - 2 * streams,), jnp.int32)
    begins = jnp.concatenate([base, base + pieces[:, 0], none])
    lengths = jnp.concatenate([pieces[:, 0], pieces[:, 1], none])
    ticks = lax.broadcasted_iota(jnp.int32, (LONGEST, LANES), 0)
    where = jnp.where(ticks < lengths[None, :], begins[None, :] + ticks, -1).reshape(-1)
    spread = (where[:, None] == lax.iota(jnp.int32, rows_n)[None, :]).astype(bf16)
    collect = (lax.iota(jnp.int32, rows_n)[:, None] == where[None, :]).astype(bf16)

    hidden_rows, output_rows, kept = run_forward(
        devices, wall, extra, mixed, spread, collect, h_first, c_first, out_scale
    )

    core = me % 2
    mine = jnp.where(core == 0, mixed, hidden_rows)
    other = lax.ppermute(jnp.where(core == 0, hidden_rows, mixed), "batch", twins)
    left_mine = lax.all_gather(
        mine, "batch", axis=0, tiled=True, axis_index_groups=column_groups
    )
    left_other = lax.all_gather(
        other, "batch", axis=0, tiled=True, axis_index_groups=column_groups
    )

    gate_rows = run_backward(devices, wall, extra, coming, spread, collect, out_scale, kept)

    right_mine = lax.all_to_all(
        gate_rows, "batch", 0, 0, tiled=True, axis_index_groups=column_groups
    ).reshape(4 * rows_n, wide)
    right_other = lax.ppermute(right_mine, "batch", twins)

    def turned_dot(left, right):
        return lax.dot_general(left, right, (((0,), (0,)), ((), ())), preferred_element_type=f32)

    grad = turned_dot(left_mine, right_mine) + turned_dot(left_other, right_other)
    grad = grad.astype(bf16)
    main = devices * TILE
    grad = jnp.concatenate(
        [
            grad[:main].reshape(lines, line * TILE, wide),
            grad[main:].reshape(lines, line, wide),
        ],
        axis=1,
    )
    grad = lax.psum_scatter(
        grad, "batch", scatter_dimension=0, tiled=True, axis_index_groups=across_groups
    ).reshape(line * OWN, wide)

    slot = 16
    send = one_hot(
        line * slot,
        line * OWN,
        lambda a, b: ((a % slot < TILE) & (a // slot * TILE + a % slot == b))
        | ((a % slot == TILE) & (line * TILE + a // slot == b)),
    )
    home = lax.all_to_all(
        dot(send, grad).astype(bf16), "batch", 0, 0, tiled=True, axis_index_groups=line_groups
    )
    settle = one_hot(
        OWN * 8,
        line * slot,
        lambda a, b: (a % 4 * 2 + a // 4 % 2) * slot + a // 8 == b,
    )
    home = dot(dot(settle, home).astype(bf16), to_natural).astype(bf16).reshape(block)
    tail = lax.ppermute(home[block - most :], "batch", [(i, i + 1) for i in range(devices - 1)])
    grad_shard = lax.dynamic_slice(
        jnp.concatenate([tail, home]), (most - gap * me,), (shard,)
    ).astype(f32)
    grad_shard = grad_shard * rec_scale
    squares = jnp.broadcast_to(jnp.sum(grad_shard * grad_shard), (devices, 128))
    squares = jnp.sum(lax.all_to_all(squares, "batch", 0, 0, tiled=True)[:, 0])
    grad_norm = jnp.sqrt(squares)

    output = dot(output_rows, to_natural)[:tokens].astype(bf16).reshape(streams, steps, width)
    gates_flat = [gate_rows[gate] for gate in range(4)]
    d_main = sum(
        lax.dot_general(
            gates_flat[gate],
            wall[:, gate * wide : (gate + 1) * wide],
            (((1,), (1,)), ((), ())),
            preferred_element_type=f32,
        )
        for gate in range(4)
    )
    d_extra = sum(
        lax.dot_general(
            gates_flat[gate],
            extra[gate * devices : (gate + 1) * devices],
            (((1,), (1,)), ((), ())),
            preferred_element_type=f32,
        )
        for gate in range(4)
    )
    row_stream = lax.iota(jnp.int32, rows_n) // steps
    d_rows = jnp.concatenate([d_main, d_extra], axis=1)
    stream_scale = sum(
        jnp.where((row_stream == s)[:, None], in_scale_kept[s][None, :], 0.0)
        for s in range(streams)
    )
    d_rows = (d_rows * stream_scale).astype(bf16)
    d_inputs = dot(d_rows, to_natural)[:tokens].astype(bf16).reshape(streams, steps, width)

    factor = jnp.minimum(1.0, CLIP_NORM / (grad_norm + 1e-06))
    clipped = grad_shard * factor
    moment_new = BETA_ONE * moment_one + (1.0 - BETA_ONE) * clipped
    second_new = BETA_TWO * moment_two + (1.0 - BETA_TWO) * clipped * clipped
    first_hat = moment_new / (1.0 - BETA_ONE**STEP)
    second_hat = second_new / (1.0 - BETA_TWO**STEP)
    master_new = master - LEARN_RATE * (
        first_hat / (jnp.sqrt(second_hat) + EPSILON) + WEIGHT_DECAY * master
    )
    return (output, d_inputs, moment_new, second_new, master_new, grad_norm)


def solution(mesh):
    placed = (
        P("batch", None, None),
        P("batch", None, None),
        P("batch", None),
        P("batch", None),
        P("batch", None),
        P("batch", None),
        P("batch", None),
        P("batch"),
        P("batch"),
        P("batch"),
        P("batch"),
    )
    return jax.shard_map(
        body,
        mesh=mesh,
        in_specs=placed,
        out_specs=(
            P("batch", None, None),
            P("batch", None, None),
            P("batch"),
            P("batch"),
            P("batch"),
            P(),
        ),
        check_vma=False,
    )
```

```python
import jax
import jax.numpy as jnp
from jax import lax
from jax.experimental import pallas as pl
from jax.experimental.pallas import tpu as pltpu
from jax.sharding import PartitionSpec as P

STEP = 10


LEARN_RATE = 0.03
BETA_ONE = 0.9
BETA_TWO = 0.999
WEIGHT_DECAY = 0.01
EPSILON = 1e-08
CLIP_NORM = 1.0
KEEP_INPUT = 4.0 / 3.0
KEEP_OUTPUT = 4.0 / 3.0
KEEP_RECURRENT = 2.0

LONGEST = 40
LANES = 8
TILE = 8
OWN = TILE + 1
KINDS = 6
PART = 8
UNROLL_FORWARD = 3
UNROLL_BACKWARD = 4
MESSAGE = 88
VMEM_LIMIT = 60 * 2**20

f32 = jnp.float32
bf16 = jnp.bfloat16


def dot(left, right):
    return lax.dot_general(left, right, (((1,), (0,)), ((), ())), preferred_element_type=f32)


def one_hot(rows, columns, wanted):
    row = lax.broadcasted_iota(jnp.int32, (rows, columns), 0)
    column = lax.broadcasted_iota(jnp.int32, (rows, columns), 1)
    return wanted(row, column).astype(bf16)


def place_of(natural, devices):
    owner, rest = natural // OWN, natural % OWN
    return jnp.where(rest < TILE, owner * TILE + rest, devices * TILE + owner)


def step_rows(step):
    return pl.ds(pl.multiple_of(step * LANES, LANES), LANES)


def kept_rows(step, kind):
    return pl.ds(pl.multiple_of((step * KINDS + kind) * LANES, LANES), LANES)


def forward_kernel(
    wall,
    mixed,
    spread,
    collect,
    h_first,
    c_first,
    out_scale,
    hidden_turned,
    output_rows,
    ninth_in,
    kept,
    turned,
    square,
    w_rec,
    ninth,
    apart,
    pre,
    kept_here,
    hiddens,
    outs,
    sems_in,
    sem_ninth,
    sem_rec,
    sems_kept,
    sems_turned,
):
    width = mixed.shape[1]
    main = wall.shape[0]
    devices = main // TILE
    gates_n = 4 * width

    copy_ninth = pltpu.make_async_copy(wall.at[:, pl.ds(2 * gates_n, width)], ninth, sem_ninth)
    copies_in = [
        pltpu.make_async_copy(
            wall.at[:, pl.ds(gate * width, width)],
            square.at[gate, pl.ds(0, main), :],
            sems_in.at[gate],
        )
        for gate in range(4)
    ]
    copy_rec = pltpu.make_async_copy(
        wall.at[:, pl.ds(gates_n, gates_n)], w_rec.at[pl.ds(0, main), :], sem_rec
    )
    copy_ninth.start()
    for copy in copies_in:
        copy.start()
    rows = dot(spread[...], mixed[...]).astype(bf16)
    copy_ninth.wait()
    for tile in range(width // 128):
        columns = pl.ds(tile * 128, 128)
        apart[tile] = ninth[:, columns].astype(f32)
        for gate in range(8):
            rest = apart[tile, pl.ds(gate, devices, stride=8), :].astype(bf16)
            if gate < 4:
                square[gate, pl.ds(main, devices), columns] = rest
                ninth_in[gate, :, columns] = rest
            else:
                there = pl.ds((gate - 4) * width + tile * 128, 128)
                w_rec[pl.ds(main, devices), there] = rest
    copy_rec.start()
    for gate in range(4):
        copies_in[gate].wait()
        pre[:, pl.ds(gate * width, width)] = dot(rows, square[gate])
    copy_rec.wait()
    scale = out_scale[...]

    def step(index, carry):
        hidden, cell = carry
        at = step_rows(index)
        gates = pre[at, :] + dot(hidden.astype(bf16), w_rec[...])
        in_gate = jax.nn.sigmoid(gates[:, :width])
        forget = jax.nn.sigmoid(gates[:, width : 2 * width])
        candid = jnp.tanh(gates[:, 2 * width : 3 * width])
        out_gate = jax.nn.sigmoid(gates[:, 3 * width :])
        cell_new = forget * cell + in_gate * candid
        squash = jnp.tanh(cell_new)
        hidden_new = out_gate * squash
        hiddens[at, :] = hidden
        outs[at, :] = hidden_new * scale
        kept_here[kept_rows(index, 0), :] = out_gate * (1.0 - squash * squash)
        kept_here[kept_rows(index, 1), :] = candid * in_gate * (1.0 - in_gate)
        kept_here[kept_rows(index, 2), :] = cell * forget * (1.0 - forget)
        kept_here[kept_rows(index, 3), :] = in_gate * (1.0 - candid * candid)
        kept_here[kept_rows(index, 4), :] = squash * out_gate * (1.0 - out_gate)
        kept_here[kept_rows(index, 5), :] = forget
        return (hidden_new, cell_new)

    turns = width // 128

    def copy_kept(part):
        size = turns * KINDS * LANES
        at = pl.ds(pl.multiple_of(part * size, LANES), size)
        return pltpu.make_async_copy(kept_here.at[at, :], kept.at[at, :], sems_kept.at[part])

    def copy_turned(gate):
        return pltpu.make_async_copy(square.at[gate], turned.at[gate], sems_turned.at[gate])

    def part(gate, carry):
        def turning(count, carry):
            columns = pl.ds(pl.multiple_of(gate * width + count * 128, 128), 128)
            into = pl.ds(pl.multiple_of(count * 128, 128), 128)
            square[gate, into, :] = w_rec[:, columns].T
            return step(gate * turns + count, carry)

        carry = lax.fori_loop(0, turns, turning, carry, unroll=UNROLL_FORWARD)
        copy_kept(gate).start()
        copy_turned(gate).start()
        return carry

    carry = lax.fori_loop(0, 4, part, (h_first[...], c_first[...]))
    lax.fori_loop(4 * turns, LONGEST, step, carry, unroll=UNROLL_FORWARD)
    begin = 4 * turns * KINDS * LANES
    rest = pl.ds(begin, kept_here.shape[0] - begin)
    last = pltpu.make_async_copy(kept_here.at[rest, :], kept.at[rest, :], sems_kept.at[4])
    last.start()
    hidden_turned[...] = lax.dot_general(
        hiddens[...].astype(bf16),
        collect[...],
        (((0,), (1,)), ((), ())),
        preferred_element_type=f32,
    ).astype(bf16)
    output_rows[...] = dot(collect[...], outs[...].astype(bf16)).astype(bf16)
    for gate in range(4):
        copy_kept(gate).wait()
        copy_turned(gate).wait()
    last.wait()


def backward_kernel(
    turned,
    kept,
    coming,
    spread,
    collect,
    out_scale,
    gate_rows,
    w_turned,
    kept_here,
    come,
    dgates,
    sems_turned,
    sems_kept,
):
    width = coming.shape[1]
    rows = gate_rows.shape[1]
    size = PART * KINDS * LANES
    parts = LONGEST // PART

    def copy_kept(part):
        at = pl.ds(pl.multiple_of(part * size, LANES), size)
        return pltpu.make_async_copy(kept.at[at, :], kept_here.at[at, :], sems_kept.at[part])

    copies = [
        pltpu.make_async_copy(
            turned.at[gate], w_turned.at[pl.ds(gate * width, width), :], sems_turned.at[gate]
        )
        for gate in range(4)
    ]
    copy_kept(parts - 1).start()
    for copy in copies:
        copy.start()
    for part in range(parts - 1):
        copy_kept(parts - 2 - part).start()
    come[...] = dot(spread[...], coming[...])
    scale = out_scale[...]

    def gradients(index, carry):
        dh_next, dc_next = carry
        at = step_rows(index)
        grad_h = come[at, :] * scale + dh_next
        grad_c = dc_next + grad_h * kept_here[kept_rows(index, 0), :]
        grads = jnp.concatenate(
            [
                grad_c * kept_here[kept_rows(index, 1), :],
                grad_c * kept_here[kept_rows(index, 2), :],
                grad_c * kept_here[kept_rows(index, 3), :],
                grad_h * kept_here[kept_rows(index, 4), :],
            ],
            axis=1,
        )
        dgates[at, :] = grads
        return (grads, grad_c * kept_here[kept_rows(index, 5), :])

    def step(index, carry):
        grads, dc_next = gradients(index, carry)
        return (dot(grads.astype(bf16), w_turned[...]), dc_next)

    def run(part, count, carry):
        first = (part + 1) * PART - 1
        return lax.fori_loop(
            0, count, lambda back, c: step(first - back, c), carry, unroll=UNROLL_BACKWARD
        )

    copy_kept(parts - 1).wait()
    for copy in copies:
        copy.wait()
    zero = jnp.zeros((LANES, width), f32)

    def whole_part(back, carry):
        part = parts - 1 - back

        @pl.when(back > 0)
        def _():
            copy_kept(part).wait()

        return run(part, PART, carry)

    carry = lax.fori_loop(0, parts - 1, whole_part, (zero, zero))
    copy_kept(0).wait()
    carry = run(0, PART - 1, carry)
    gradients(0, carry)
    for gate in range(4):
        columns = pl.ds(gate * width, width)
        gate_rows[gate] = dot(
            collect[pl.ds(0, rows), :], dgates[:, columns].astype(bf16)
        ).astype(bf16)


def gradient_kernel(
    core, mixed_all, hidden_all, mine, other, message, left, right, packed, sems_left, sems_right
):
    width = mine.shape[2]
    rows = mine.shape[1]
    half = mine.shape[0]
    line = 2 * half
    slot = mixed_all.shape[1]
    devices = message.shape[0]
    main = devices * TILE
    which = core[0]

    def copies_left(source):
        found = []
        for place in range(line):
            chip, twin = place % half, place // half
            block = 2 * chip + (which if twin == 0 else 1 - which)
            found.append(
                pltpu.make_async_copy(
                    source.at[pl.ds(block * width, width), :],
                    left.at[:, pl.ds(place * slot, slot)],
                    sems_left.at[place],
                )
            )
        return found

    @pl.when(which == 0)
    def _():
        for copy in copies_left(mixed_all):
            copy.start()

    @pl.when(which != 0)
    def _():
        for copy in copies_left(hidden_all):
            copy.start()

    copies_right = [
        pltpu.make_async_copy(
            (mine if place < half else other).at[place % half],
            right.at[pl.ds(place * slot, rows), :],
            sems_right.at[place],
        )
        for place in range(line)
    ]
    for copy in copies_right:
        copy.start()
    for place in range(line):
        right[pl.ds(place * slot + rows, slot - rows), :] = jnp.zeros((slot - rows, width), bf16)
    packed[:, pl.ds(OWN * TILE, TILE * 2), :] = jnp.zeros((devices, TILE * 2, 128), f32)
    for copy in copies_left(mixed_all) + copies_right:
        copy.wait()
    tiles = 3
    for begin in range(0, width // 128, tiles):
        grad = dot(left[...], right[:, pl.ds(begin * 128, tiles * 128)])
        for tile in range(tiles):
            here = grad[:, tile * 128 : (tile + 1) * 128]
            place = begin + tile
            packed[:, pl.ds(place * TILE, TILE), :] = here[:main].reshape(devices, TILE, 128)
            packed[:, OWN * TILE + place, :] = here[main:]
    message[...] = packed[...].astype(bf16)


def settle_kernel(got, to_natural, home, total, placed):
    line = total.shape[0]
    tiles = placed.shape[0]
    half = line // 2
    lines = got.shape[0] // line
    found = got[pl.ds(0, line)].astype(f32)
    for index in range(1, lines):
        found = found + got[pl.ds(index * line, line)].astype(f32)
    total[...] = found
    for source in range(line):
        gate = (source % 2) * half + source // 2
        for tile in range(tiles):
            placed[tile, pl.ds(gate, TILE, stride=8), :] = total[
                source, pl.ds(tile * TILE, TILE), :
            ]
            placed[tile, pl.ds(TILE * 8 + gate, 1), :] = total[
                source, pl.ds(OWN * TILE + tile, 1), :
            ]
    values = jnp.concatenate([placed[tile] for tile in range(tiles)], axis=1)
    high = values.astype(bf16)
    rest = (values - high.astype(f32)).astype(bf16)
    home[...] = dot(high, to_natural[...]) + dot(rest, to_natural[...])


def in_vmem():
    return pl.BlockSpec(memory_space=pltpu.VMEM)


def in_place():
    return pl.BlockSpec(memory_space=pl.ANY)


def run_forward(wall, mixed, spread, collect, h_first, c_first, out_scale):
    steps_rows = spread.shape[0]
    rows, width = mixed.shape
    devices = wall.shape[0] // TILE
    all_kept = LONGEST * KINDS * LANES
    return pl.pallas_call(
        forward_kernel,
        out_shape=(
            jax.ShapeDtypeStruct((width, collect.shape[0]), bf16),
            jax.ShapeDtypeStruct((collect.shape[0], width), bf16),
            jax.ShapeDtypeStruct((4, devices, width), bf16),
            jax.ShapeDtypeStruct((all_kept, width), f32),
            jax.ShapeDtypeStruct((4, width, width), bf16),
        ),
        in_specs=[in_place()] + [in_vmem()] * 6,
        out_specs=(in_vmem(),) * 3 + (in_place(),) * 2,
        scratch_shapes=[
            pltpu.VMEM((4, width, width), bf16),
            pltpu.VMEM((width, 4 * width), bf16),
            pltpu.VMEM((devices * TILE, width), bf16),
            pltpu.VMEM((width // 128, devices * TILE, 128), f32),
            pltpu.VMEM((steps_rows, 4 * width), f32),
            pltpu.VMEM((all_kept, width), f32),
            pltpu.VMEM((steps_rows, width), f32),
            pltpu.VMEM((steps_rows, width), f32),
            pltpu.SemaphoreType.DMA((4,)),
            pltpu.SemaphoreType.DMA,
            pltpu.SemaphoreType.DMA,
            pltpu.SemaphoreType.DMA((5,)),
            pltpu.SemaphoreType.DMA((4,)),
        ],
        compiler_params=pltpu.CompilerParams(vmem_limit_bytes=VMEM_LIMIT),
        cost_estimate=pl.CostEstimate(
            flops=60_000_000_000, bytes_accessed=30_000_000, transcendentals=2_000_000
        ),
        name="forward",
    )(wall, mixed, spread, collect, h_first, c_first, out_scale)


def run_backward(turned, kept, coming, spread, collect, out_scale):
    steps_rows = spread.shape[0]
    rows, width = coming.shape
    return pl.pallas_call(
        backward_kernel,
        out_shape=jax.ShapeDtypeStruct((4, rows, width), bf16),
        in_specs=[in_place()] * 2 + [in_vmem()] * 4,
        out_specs=in_vmem(),
        scratch_shapes=[
            pltpu.VMEM((4 * width, width), bf16),
            pltpu.VMEM(kept.shape, f32),
            pltpu.VMEM((steps_rows, width), f32),
            pltpu.VMEM((steps_rows, 4 * width), f32),
            pltpu.SemaphoreType.DMA((4,)),
            pltpu.SemaphoreType.DMA((LONGEST // PART,)),
        ],
        compiler_params=pltpu.CompilerParams(vmem_limit_bytes=VMEM_LIMIT),
        cost_estimate=pl.CostEstimate(
            flops=60_000_000_000, bytes_accessed=30_000_000, transcendentals=0
        ),
        name="backward",
    )(turned, kept, coming, spread, collect, out_scale)


def run_gradient(core, mixed_all, hidden_all, mine, other, devices):
    half, rows, width = mine.shape
    line, slot = 2 * half, mixed_all.shape[1]
    return pl.pallas_call(
        gradient_kernel,
        out_shape=jax.ShapeDtypeStruct((devices, MESSAGE, 128), bf16),
        in_specs=[pl.BlockSpec(memory_space=pltpu.SMEM)] + [in_place()] * 4,
        out_specs=in_vmem(),
        scratch_shapes=[
            pltpu.VMEM((width, line * slot), bf16),
            pltpu.VMEM((line * slot, width), bf16),
            pltpu.VMEM((devices, MESSAGE, 128), f32),
            pltpu.SemaphoreType.DMA((line,)),
            pltpu.SemaphoreType.DMA((line,)),
        ],
        compiler_params=pltpu.CompilerParams(vmem_limit_bytes=VMEM_LIMIT),
        cost_estimate=pl.CostEstimate(
            flops=6_000_000_000, bytes_accessed=12_000_000, transcendentals=0
        ),
        name="gradient",
    )(core, mixed_all, hidden_all, mine, other)


def run_settle(got, to_natural, line):
    wide, width = to_natural.shape
    return pl.pallas_call(
        settle_kernel,
        out_shape=jax.ShapeDtypeStruct((OWN * 8, width), f32),
        in_specs=[in_vmem()] * 2,
        out_specs=in_vmem(),
        scratch_shapes=[
            pltpu.VMEM((line, MESSAGE, 128), f32),
            pltpu.VMEM((wide // 128, OWN * 8, 128), f32),
        ],
        compiler_params=pltpu.CompilerParams(vmem_limit_bytes=VMEM_LIMIT),
        name="settle",
    )(got, to_natural)


def split_exact(values):
    parts = []
    rest = values
    for _ in range(3):
        part = lax.reduce_precision(rest, 8, 7)
        parts.append(part.astype(bf16))
        rest = rest - part
    return parts


def body(
    inputs,
    d_out,
    h_start,
    c_start,
    pieces,
    in_mask,
    out_mask,
    w_mask,
    master,
    moment_one,
    moment_two,
):
    streams, steps, width = inputs.shape
    gates_n = 4 * width
    count_w = 2 * width * gates_n
    total = count_w + gates_n
    shard = master.shape[0]
    devices = lax.axis_size("batch")
    me = lax.axis_index("batch")
    wide = OWN * devices
    block = OWN * 2 * gates_n
    gap = block - shard
    most = gap * devices
    tokens = streams * steps
    rows_n = -(-tokens // 32) * 32
    slot = -(-tokens // 128) * 128
    line = 8
    lines = devices // line

    line_groups = [[line * q + m for m in range(line)] for q in range(lines)]
    column_groups = [
        [line * q + 2 * y + c for y in range(line // 2)] for q in range(lines) for c in range(2)
    ]
    twins = [(i, i ^ 1) for i in range(devices)]

    to_kept = one_hot(width, wide, lambda k, p: place_of(k, devices) == p)
    to_natural = one_hot(wide, width, lambda p, k: place_of(k, devices) == p)

    places = me * shard + lax.iota(jnp.int32, shard)
    recurrent = (places < count_w) & (places % (2 * gates_n) >= gates_n)
    rec_scale = jnp.where(recurrent, w_mask.astype(f32) * KEEP_RECURRENT, 1.0)
    local_low = master.astype(bf16) * rec_scale.astype(bf16)
    local_low = jnp.where(places < total, local_low, jnp.zeros((), bf16))
    head = lax.ppermute(local_low[:most], "batch", [(i + 1, i) for i in range(devices - 1)])
    own = lax.dynamic_slice(jnp.concatenate([local_low, head]), (gap * me,), (block,))
    own = own.reshape(OWN * 8, width)
    order = one_hot(
        OWN * 8,
        OWN * 8,
        lambda a, b: jnp.where(a < 64, (a % 8) * 8 + a // 8, 64 + a % 8) == b,
    )
    own = dot(order, dot(own, to_kept).astype(bf16)).astype(bf16)
    own = jnp.concatenate([own[TILE * j : TILE * (j + 1)] for j in range(OWN)], axis=1)
    wall = lax.all_gather(own, "batch", axis=0, tiled=True)
    in_scale = in_mask.astype(f32) * KEEP_INPUT
    mixed = (inputs.astype(f32) * in_scale[:, None, :]).astype(bf16).reshape(tokens, width)
    spare = ((0, rows_n - tokens), (0, 0))
    mixed = dot(jnp.pad(mixed, spare), to_kept).astype(bf16)
    bias_place = place_of(jnp.int32(width), devices)
    column = lax.broadcasted_iota(jnp.int32, mixed.shape, 1)
    mixed = jnp.where(column == bias_place, jnp.ones((), bf16), mixed)
    mixed_turned = jnp.pad(mixed, ((0, slot - rows_n), (0, 0))).T
    coming = dot(jnp.pad(d_out.reshape(tokens, width), spare), to_kept).astype(bf16)
    small = jnp.concatenate(
        [h_start.astype(bf16)]
        + split_exact(c_start)
        + [in_mask.astype(bf16), out_mask.astype(bf16)],
        axis=0,
    )
    small = dot(small, to_kept)
    part = [small[streams * j : streams * (j + 1)] for j in range(6)]
    empty = jnp.zeros((LANES - streams, wide), f32)
    h_first = jnp.concatenate([part[0], empty], axis=0)
    c_first = jnp.concatenate([part[1] + part[2] + part[3], empty], axis=0)
    in_scale_kept = part[4] * KEEP_INPUT
    out_scale_kept = part[5] * KEEP_OUTPUT
    out_scale = jnp.concatenate(
        [out_scale_kept, out_scale_kept, jnp.zeros((LANES - 2 * streams, wide), f32)], axis=0
    )
    base = jnp.arange(streams, dtype=jnp.int32) * steps
    none = jnp.zeros((LANES - 2 * streams,), jnp.int32)
    begins = jnp.concatenate([base, base + pieces[:, 0], none])
    lengths = jnp.concatenate([pieces[:, 0], pieces[:, 1], none])
    ticks = lax.broadcasted_iota(jnp.int32, (LONGEST, LANES), 0)
    where = jnp.where(ticks < lengths[None, :], begins[None, :] + ticks, -1).reshape(-1)
    spread = (where[:, None] == lax.iota(jnp.int32, rows_n)[None, :]).astype(bf16)
    collect = (lax.iota(jnp.int32, slot)[:, None] == where[None, :]).astype(bf16)

    mixed_turned, wall = lax.optimization_barrier((mixed_turned, wall))
    mixed_all = lax.all_gather(
        mixed_turned, "batch", axis=0, tiled=True, axis_index_groups=line_groups
    )
    hidden_turned, output_rows, ninth_in, kept, turned = run_forward(
        wall, mixed, spread, collect, h_first, c_first, out_scale
    )
    hidden_all = lax.all_gather(
        hidden_turned, "batch", axis=0, tiled=True, axis_index_groups=line_groups
    )
    gate_rows = run_backward(turned, kept, coming, spread, collect, out_scale)

    mine = lax.all_to_all(
        gate_rows, "batch", 0, 0, tiled=True, axis_index_groups=column_groups
    )
    other = lax.ppermute(mine, "batch", twins)
    core = (me % 2).reshape(1)
    message = run_gradient(core, mixed_all, hidden_all, mine, other, devices)
    got = lax.all_to_all(message, "batch", 0, 0, tiled=True)
    home = run_settle(got, to_natural, line).reshape(block)
    tail = lax.ppermute(home[block - most :], "batch", [(i, i + 1) for i in range(devices - 1)])
    grad_shard = lax.dynamic_slice(
        jnp.concatenate([tail, home]), (most - gap * me,), (shard,)
    )
    grad_shard = grad_shard * rec_scale
    squares = jnp.broadcast_to(jnp.sum(grad_shard * grad_shard), (devices, 128))
    squares = jnp.sum(lax.all_to_all(squares, "batch", 0, 0, tiled=True)[:, 0])
    grad_norm = jnp.sqrt(squares)

    output = dot(output_rows, to_natural)[:tokens].astype(bf16).reshape(streams, steps, width)
    gates_flat = [gate_rows[gate] for gate in range(4)]
    d_main = sum(
        lax.dot_general(
            gates_flat[gate],
            wall[:, gate * wide : (gate + 1) * wide],
            (((1,), (1,)), ((), ())),
            preferred_element_type=f32,
        )
        for gate in range(4)
    )
    d_extra = sum(
        lax.dot_general(
            gates_flat[gate],
            ninth_in[gate],
            (((1,), (1,)), ((), ())),
            preferred_element_type=f32,
        )
        for gate in range(4)
    )
    row_stream = lax.iota(jnp.int32, rows_n) // steps
    d_rows = jnp.concatenate([d_main, d_extra], axis=1)
    stream_scale = sum(
        jnp.where((row_stream == s)[:, None], in_scale_kept[s][None, :], 0.0)
        for s in range(streams)
    )
    d_rows = (d_rows * stream_scale).astype(bf16)
    d_inputs = dot(d_rows, to_natural)[:tokens].astype(bf16).reshape(streams, steps, width)

    factor = jnp.minimum(1.0, CLIP_NORM / (grad_norm + 1e-06))
    clipped = grad_shard * factor
    moment_new = BETA_ONE * moment_one + (1.0 - BETA_ONE) * clipped
    second_new = BETA_TWO * moment_two + (1.0 - BETA_TWO) * clipped * clipped
    first_hat = moment_new / (1.0 - BETA_ONE**STEP)
    second_hat = second_new / (1.0 - BETA_TWO**STEP)
    master_new = master - LEARN_RATE * (
        first_hat / (jnp.sqrt(second_hat) + EPSILON) + WEIGHT_DECAY * master
    )
    return (output, d_inputs, moment_new, second_new, master_new, grad_norm)


def solution(mesh):
    placed = (
        P("batch", None, None),
        P("batch", None, None),
        P("batch", None),
        P("batch", None),
        P("batch", None),
        P("batch", None),
        P("batch", None),
        P("batch"),
        P("batch"),
        P("batch"),
        P("batch"),
    )
    return jax.shard_map(
        body,
        mesh=mesh,
        in_specs=placed,
        out_specs=(
            P("batch", None, None),
            P("batch", None, None),
            P("batch"),
            P("batch"),
            P("batch"),
            P(),
        ),
        check_vma=False,
    )
```

```python
import jax
import jax.numpy as jnp
from jax import lax
from jax.experimental import pallas as pl
from jax.experimental.pallas import tpu as pltpu
from jax.sharding import PartitionSpec as P

STEP = 10


LEARN_RATE = 0.03
BETA_ONE = 0.9
BETA_TWO = 0.999
WEIGHT_DECAY = 0.01
EPSILON = 1e-08
CLIP_NORM = 1.0
KEEP_INPUT = 4.0 / 3.0
KEEP_OUTPUT = 4.0 / 3.0
KEEP_RECURRENT = 2.0

LONGEST = 40
LANES = 8
TILE = 8
OWN = TILE + 1
KINDS = 6
PART = 8
UNROLL_FORWARD = 3
UNROLL_BACKWARD = 4
CUT = 640
MESSAGE = 88
VMEM_LIMIT = 60 * 2**20

f32 = jnp.float32
bf16 = jnp.bfloat16


def dot(left, right):
    return lax.dot_general(left, right, (((1,), (0,)), ((), ())), preferred_element_type=f32)


def one_hot(rows, columns, wanted):
    row = lax.broadcasted_iota(jnp.int32, (rows, columns), 0)
    column = lax.broadcasted_iota(jnp.int32, (rows, columns), 1)
    return wanted(row, column).astype(bf16)


def place_of(natural, devices):
    owner, rest = natural // OWN, natural % OWN
    return jnp.where(rest < TILE, owner * TILE + rest, devices * TILE + owner)


def step_rows(step):
    return pl.ds(pl.multiple_of(step * LANES, LANES), LANES)


def kept_rows(step, kind):
    return pl.ds(pl.multiple_of((step * KINDS + kind) * LANES, LANES), LANES)


def forward_kernel(
    wall,
    mixed,
    spread,
    collect,
    h_first,
    c_first,
    out_scale,
    hidden_turned,
    output_rows,
    ninth_in,
    kept,
    turned,
    square,
    w_rec,
    ninth,
    apart,
    pre,
    kept_here,
    hiddens,
    outs,
    sems_in,
    sem_ninth,
    sem_rec,
    sems_kept,
    sems_turned,
):
    width = mixed.shape[1]
    main = wall.shape[0]
    devices = main // TILE
    gates_n = 4 * width

    copy_ninth = pltpu.make_async_copy(wall.at[:, pl.ds(2 * gates_n, width)], ninth, sem_ninth)
    copies_in = [
        pltpu.make_async_copy(
            wall.at[:, pl.ds(gate * width, width)],
            square.at[gate, pl.ds(0, main), :],
            sems_in.at[gate],
        )
        for gate in range(4)
    ]
    copy_rec = pltpu.make_async_copy(
        wall.at[:, pl.ds(gates_n, gates_n)], w_rec.at[pl.ds(0, main), :], sem_rec
    )
    copy_ninth.start()
    for copy in copies_in:
        copy.start()
    rows = dot(spread[...], mixed[...]).astype(bf16)
    copy_ninth.wait()
    for tile in range(width // 128):
        columns = pl.ds(tile * 128, 128)
        apart[tile] = ninth[:, columns].astype(f32)
        for gate in range(8):
            rest = apart[tile, pl.ds(gate, devices, stride=8), :].astype(bf16)
            if gate < 4:
                square[gate, pl.ds(main, devices), columns] = rest
                ninth_in[gate, :, columns] = rest
            else:
                there = pl.ds((gate - 4) * width + tile * 128, 128)
                w_rec[pl.ds(main, devices), there] = rest
    copy_rec.start()
    for gate in range(4):
        copies_in[gate].wait()
        pre[:, pl.ds(gate * width, width)] = dot(rows, square[gate])
    copy_rec.wait()
    scale = out_scale[...]

    def step(index, carry):
        hidden, cell = carry
        at = step_rows(index)
        gates = pre[at, :] + dot(hidden.astype(bf16), w_rec[...])
        in_gate = jax.nn.sigmoid(gates[:, :width])
        forget = jax.nn.sigmoid(gates[:, width : 2 * width])
        candid = jnp.tanh(gates[:, 2 * width : 3 * width])
        out_gate = jax.nn.sigmoid(gates[:, 3 * width :])
        cell_new = forget * cell + in_gate * candid
        squash = jnp.tanh(cell_new)
        hidden_new = out_gate * squash
        hiddens[at, :] = hidden
        outs[at, :] = hidden_new * scale
        kept_here[kept_rows(index, 0), :] = out_gate * (1.0 - squash * squash)
        kept_here[kept_rows(index, 1), :] = candid * in_gate * (1.0 - in_gate)
        kept_here[kept_rows(index, 2), :] = cell * forget * (1.0 - forget)
        kept_here[kept_rows(index, 3), :] = in_gate * (1.0 - candid * candid)
        kept_here[kept_rows(index, 4), :] = squash * out_gate * (1.0 - out_gate)
        kept_here[kept_rows(index, 5), :] = forget
        return (hidden_new, cell_new)

    turns = width // 128

    def copy_kept(part):
        size = turns * KINDS * LANES
        at = pl.ds(pl.multiple_of(part * size, LANES), size)
        return pltpu.make_async_copy(kept_here.at[at, :], kept.at[at, :], sems_kept.at[part])

    def copy_turned(gate):
        return pltpu.make_async_copy(square.at[gate], turned.at[gate], sems_turned.at[gate])

    def part(gate, carry):
        def turning(count, carry):
            columns = pl.ds(pl.multiple_of(gate * width + count * 128, 128), 128)
            into = pl.ds(pl.multiple_of(count * 128, 128), 128)
            square[gate, into, :] = w_rec[:, columns].T
            return step(gate * turns + count, carry)

        carry = lax.fori_loop(0, turns, turning, carry, unroll=UNROLL_FORWARD)
        copy_kept(gate).start()
        copy_turned(gate).start()
        return carry

    carry = lax.fori_loop(0, 4, part, (h_first[...], c_first[...]))
    lax.fori_loop(4 * turns, LONGEST, step, carry, unroll=UNROLL_FORWARD)
    begin = 4 * turns * KINDS * LANES
    rest = pl.ds(begin, kept_here.shape[0] - begin)
    last = pltpu.make_async_copy(kept_here.at[rest, :], kept.at[rest, :], sems_kept.at[4])
    last.start()
    hidden_turned[...] = lax.dot_general(
        hiddens[...].astype(bf16),
        collect[...],
        (((0,), (1,)), ((), ())),
        preferred_element_type=f32,
    ).astype(bf16)
    output_rows[...] = dot(collect[...], outs[...].astype(bf16)).astype(bf16)
    for gate in range(4):
        copy_kept(gate).wait()
        copy_turned(gate).wait()
    last.wait()


def backward_kernel(
    turned,
    kept,
    coming,
    spread,
    collect,
    out_scale,
    first_part,
    second_part,
    w_turned,
    kept_here,
    come,
    dgates,
    sems_turned,
    sems_kept,
):
    width = coming.shape[1]
    rows, cut = first_part.shape[1:]
    size = PART * KINDS * LANES
    parts = LONGEST // PART

    def copy_kept(part):
        at = pl.ds(pl.multiple_of(part * size, LANES), size)
        return pltpu.make_async_copy(kept.at[at, :], kept_here.at[at, :], sems_kept.at[part])

    copies = [
        pltpu.make_async_copy(
            turned.at[gate], w_turned.at[pl.ds(gate * width, width), :], sems_turned.at[gate]
        )
        for gate in range(4)
    ]
    copy_kept(parts - 1).start()
    for copy in copies:
        copy.start()
    for part in range(parts - 1):
        copy_kept(parts - 2 - part).start()
    come[...] = dot(spread[...], coming[...])
    scale = out_scale[...]

    def gradients(index, carry):
        dh_next, dc_next = carry
        at = step_rows(index)
        grad_h = come[at, :] * scale + dh_next
        grad_c = dc_next + grad_h * kept_here[kept_rows(index, 0), :]
        grads = jnp.concatenate(
            [
                grad_c * kept_here[kept_rows(index, 1), :],
                grad_c * kept_here[kept_rows(index, 2), :],
                grad_c * kept_here[kept_rows(index, 3), :],
                grad_h * kept_here[kept_rows(index, 4), :],
            ],
            axis=1,
        )
        dgates[at, :] = grads
        return (grads, grad_c * kept_here[kept_rows(index, 5), :])

    def step(index, carry):
        grads, dc_next = gradients(index, carry)
        return (dot(grads.astype(bf16), w_turned[...]), dc_next)

    def run(part, count, carry):
        first = (part + 1) * PART - 1
        return lax.fori_loop(
            0, count, lambda back, c: step(first - back, c), carry, unroll=UNROLL_BACKWARD
        )

    copy_kept(parts - 1).wait()
    for copy in copies:
        copy.wait()
    zero = jnp.zeros((LANES, width), f32)

    def whole_part(back, carry):
        part = parts - 1 - back

        @pl.when(back > 0)
        def _():
            copy_kept(part).wait()

        return run(part, PART, carry)

    carry = lax.fori_loop(0, parts - 1, whole_part, (zero, zero))
    copy_kept(0).wait()
    carry = run(0, PART - 1, carry)
    gradients(0, carry)
    for gate in range(4):
        columns = pl.ds(gate * width, width)
        natural = dot(collect[pl.ds(0, rows), :], dgates[:, columns].astype(bf16)).astype(bf16)
        first_part[gate] = natural[:, :cut]
        second_part[gate] = natural[:, cut:]


def gradient_kernel(
    core, mixed_all, hidden_all, mine, other, message, left, right, sems_left, sems_right
):
    half, rows, columns = mine.shape
    line = 2 * half
    lines = message.shape[0]
    width, slot = left.shape[0], mixed_all.shape[1]
    main = lines * line * TILE
    which = core[0]

    def copies_left(source):
        found = []
        for place in range(line):
            chip, twin = place % half, place // half
            block = 2 * chip + (which if twin == 0 else 1 - which)
            found.append(
                pltpu.make_async_copy(
                    source.at[pl.ds(block * width, width), :],
                    left.at[:, pl.ds(place * slot, slot)],
                    sems_left.at[place],
                )
            )
        return found

    @pl.when(which == 0)
    def _():
        for copy in copies_left(mixed_all):
            copy.start()

    @pl.when(which != 0)
    def _():
        for copy in copies_left(hidden_all):
            copy.start()

    copies_right = [
        pltpu.make_async_copy(
            (mine if place < half else other).at[place % half],
            right.at[pl.ds(place * slot, rows), :],
            sems_right.at[place],
        )
        for place in range(line)
    ]
    for copy in copies_right:
        copy.start()
    for place in range(line):
        right[pl.ds(place * slot + rows, slot - rows), :] = jnp.zeros((slot - rows, columns), bf16)
    for copy in copies_left(mixed_all) + copies_right:
        copy.wait()
    size = 128
    for begin in range(0, columns, size):
        grad = dot(left[...], right[:, pl.ds(begin, size)])
        packed = jnp.concatenate(
            [
                grad[:main].reshape(lines, line * TILE, size),
                grad[main:].reshape(lines, line, size),
            ],
            axis=1,
        )
        message[:, :, pl.ds(begin, size)] = packed.astype(bf16)


def reduce_kernel(first, second, scale, homeward, squares, packed):
    line = homeward.shape[0]
    lines = first.shape[0]
    total = jnp.zeros((1, 128), f32)
    packed[:, pl.ds(OWN * TILE, TILE * 2), :] = jnp.zeros((line, TILE * 2, 128), f32)
    place = 0
    for source in (first, second):
        for tile in range(source.shape[2] // 128):
            columns = pl.ds(tile * 128, 128)
            found = source[0, :, columns].astype(f32)
            for index in range(1, lines):
                found = found + source[index, :, columns].astype(f32)
            found = found * scale[:, pl.ds(place * 128, 128)].astype(f32)
            total = total + jnp.sum(found * found, axis=0, keepdims=True)
            tiles = found[: line * TILE].reshape(line, TILE, 128)
            packed[:, pl.ds(place * TILE, TILE), :] = tiles
            packed[:, OWN * TILE + place, :] = found[line * TILE :]
            place += 1
    homeward[...] = packed[...].astype(bf16)
    squares[...] = jnp.broadcast_to(jnp.sum(total, axis=1, keepdims=True), squares.shape)


def settle_kernel(got, to_natural, home, placed, wide):
    line = got.shape[0]
    tiles = placed.shape[0]
    half = line // 2
    wide[...] = got[...].astype(f32)
    for source in range(line):
        gate = (source % 2) * half + source // 2
        for tile in range(tiles):
            placed[tile, pl.ds(gate, TILE, stride=8), :] = wide[
                source, pl.ds(tile * TILE, TILE), :
            ]
            placed[tile, pl.ds(TILE * 8 + gate, 1), :] = wide[
                source, pl.ds(OWN * TILE + tile, 1), :
            ]
    values = jnp.concatenate([placed[tile] for tile in range(tiles)], axis=1)
    home[...] = dot(values.astype(bf16), to_natural[...]).astype(bf16)


def own_kernel(
    wall, ninth_in, first, second, in_rows, output_rows, to_natural, d_out, out, square, sems
):
    width = in_rows.shape[1]
    rows = in_rows.shape[0]
    main = wall.shape[0]
    rest = width - main
    cut = first.shape[2]
    copies = []
    for gate in range(4):
        copies.append(
            pltpu.make_async_copy(
                wall.at[:, pl.ds(gate * width, width)],
                square.at[gate, pl.ds(0, main), :],
                sems.at[2 * gate],
            )
        )
        copies.append(
            pltpu.make_async_copy(
                ninth_in.at[gate], square.at[gate, pl.ds(main, rest), :], sems.at[2 * gate + 1]
            )
        )
    for copy in copies:
        copy.start()
    out[...] = dot(output_rows[pl.ds(0, rows), :], to_natural[...]).astype(bf16)

    def right_product(left, matrix):
        return lax.dot_general(
            left, matrix, (((1,), (1,)), ((), ())), preferred_element_type=f32
        )

    found = jnp.zeros((rows, width), f32)
    for gate in range(4):
        copies[2 * gate].wait()
        copies[2 * gate + 1].wait()
        found = found + right_product(first[gate], square[gate, :, pl.ds(0, cut)])
        found = found + right_product(second[gate], square[gate, :, pl.ds(cut, width - cut)])
    found = found * (in_rows[...].astype(f32) * KEEP_INPUT)
    d_out[...] = dot(found.astype(bf16), to_natural[...]).astype(bf16)


def in_vmem():
    return pl.BlockSpec(memory_space=pltpu.VMEM)


def in_place():
    return pl.BlockSpec(memory_space=pl.ANY)


def run_forward(wall, mixed, spread, collect, h_first, c_first, out_scale):
    steps_rows = spread.shape[0]
    rows, width = mixed.shape
    devices = wall.shape[0] // TILE
    all_kept = LONGEST * KINDS * LANES
    return pl.pallas_call(
        forward_kernel,
        out_shape=(
            jax.ShapeDtypeStruct((width, collect.shape[0]), bf16),
            jax.ShapeDtypeStruct((collect.shape[0], width), bf16),
            jax.ShapeDtypeStruct((4, devices, width), bf16),
            jax.ShapeDtypeStruct((all_kept, width), f32),
            jax.ShapeDtypeStruct((4, width, width), bf16),
        ),
        in_specs=[in_place()] + [in_vmem()] * 6,
        out_specs=(in_vmem(),) * 3 + (in_place(),) * 2,
        scratch_shapes=[
            pltpu.VMEM((4, width, width), bf16),
            pltpu.VMEM((width, 4 * width), bf16),
            pltpu.VMEM((devices * TILE, width), bf16),
            pltpu.VMEM((width // 128, devices * TILE, 128), f32),
            pltpu.VMEM((steps_rows, 4 * width), f32),
            pltpu.VMEM((all_kept, width), f32),
            pltpu.VMEM((steps_rows, width), f32),
            pltpu.VMEM((steps_rows, width), f32),
            pltpu.SemaphoreType.DMA((4,)),
            pltpu.SemaphoreType.DMA,
            pltpu.SemaphoreType.DMA,
            pltpu.SemaphoreType.DMA((5,)),
            pltpu.SemaphoreType.DMA((4,)),
        ],
        compiler_params=pltpu.CompilerParams(vmem_limit_bytes=VMEM_LIMIT),
        cost_estimate=pl.CostEstimate(
            flops=60_000_000_000, bytes_accessed=30_000_000, transcendentals=2_000_000
        ),
        name="forward",
    )(wall, mixed, spread, collect, h_first, c_first, out_scale)


def run_backward(turned, kept, coming, spread, collect, out_scale):
    steps_rows = spread.shape[0]
    rows, width = coming.shape
    return pl.pallas_call(
        backward_kernel,
        out_shape=(
            jax.ShapeDtypeStruct((4, rows, CUT), bf16),
            jax.ShapeDtypeStruct((4, rows, width - CUT), bf16),
        ),
        in_specs=[in_place()] * 2 + [in_vmem()] * 4,
        out_specs=(in_vmem(),) * 2,
        scratch_shapes=[
            pltpu.VMEM((4 * width, width), bf16),
            pltpu.VMEM(kept.shape, f32),
            pltpu.VMEM((steps_rows, width), f32),
            pltpu.VMEM((steps_rows, 4 * width), f32),
            pltpu.SemaphoreType.DMA((4,)),
            pltpu.SemaphoreType.DMA((LONGEST // PART,)),
        ],
        compiler_params=pltpu.CompilerParams(vmem_limit_bytes=VMEM_LIMIT),
        cost_estimate=pl.CostEstimate(
            flops=60_000_000_000, bytes_accessed=30_000_000, transcendentals=0
        ),
        name="backward",
    )(turned, kept, coming, spread, collect, out_scale)


def run_gradient(core, mixed_all, hidden_all, mine, other, lines):
    half, rows, columns = mine.shape
    line, slot = 2 * half, mixed_all.shape[1]
    width = mixed_all.shape[0] // line
    return pl.pallas_call(
        gradient_kernel,
        out_shape=jax.ShapeDtypeStruct((lines, line * OWN, columns), bf16),
        in_specs=[pl.BlockSpec(memory_space=pltpu.SMEM)] + [in_place()] * 4,
        out_specs=in_vmem(),
        scratch_shapes=[
            pltpu.VMEM((width, line * slot), bf16),
            pltpu.VMEM((line * slot, columns), bf16),
            pltpu.SemaphoreType.DMA((line,)),
            pltpu.SemaphoreType.DMA((line,)),
        ],
        compiler_params=pltpu.CompilerParams(vmem_limit_bytes=VMEM_LIMIT),
        cost_estimate=pl.CostEstimate(
            flops=6_000_000_000, bytes_accessed=12_000_000, transcendentals=0
        ),
        name="gradient",
    )(core, mixed_all, hidden_all, mine, other)


def run_reduce(first, second, scale, line, devices):
    return pl.pallas_call(
        reduce_kernel,
        out_shape=(
            jax.ShapeDtypeStruct((line, MESSAGE, 128), bf16),
            jax.ShapeDtypeStruct((devices, 128), f32),
        ),
        in_specs=[in_vmem()] * 3,
        out_specs=(in_vmem(),) * 2,
        scratch_shapes=[pltpu.VMEM((line, MESSAGE, 128), f32)],
        compiler_params=pltpu.CompilerParams(vmem_limit_bytes=VMEM_LIMIT),
        name="reduce",
    )(first, second, scale)


def run_settle(got, to_natural):
    wide, width = to_natural.shape
    return pl.pallas_call(
        settle_kernel,
        out_shape=jax.ShapeDtypeStruct((OWN * 8, width), bf16),
        in_specs=[in_vmem()] * 2,
        out_specs=in_vmem(),
        scratch_shapes=[
            pltpu.VMEM((wide // 128, OWN * 8, 128), f32),
            pltpu.VMEM(got.shape, f32),
        ],
        compiler_params=pltpu.CompilerParams(vmem_limit_bytes=VMEM_LIMIT),
        name="settle",
    )(got, to_natural)


def run_own(wall, ninth_in, first, second, in_rows, output_rows, to_natural):
    rows, width = in_rows.shape
    natural = to_natural.shape[1]
    return pl.pallas_call(
        own_kernel,
        out_shape=(jax.ShapeDtypeStruct((rows, natural), bf16),) * 2,
        in_specs=[in_place()] * 2 + [in_vmem()] * 5,
        out_specs=(in_vmem(),) * 2,
        scratch_shapes=[
            pltpu.VMEM((4, width, width), bf16),
            pltpu.SemaphoreType.DMA((8,)),
        ],
        compiler_params=pltpu.CompilerParams(vmem_limit_bytes=VMEM_LIMIT),
        cost_estimate=pl.CostEstimate(
            flops=8_000_000_000, bytes_accessed=15_000_000, transcendentals=0
        ),
        name="own",
    )(wall, ninth_in, first, second, in_rows, output_rows, to_natural)


def split_exact(values):
    parts = []
    rest = values
    for _ in range(3):
        part = lax.reduce_precision(rest, 8, 7)
        parts.append(part.astype(bf16))
        rest = rest - part
    return parts


def body(
    inputs,
    d_out,
    h_start,
    c_start,
    pieces,
    in_mask,
    out_mask,
    w_mask,
    master,
    moment_one,
    moment_two,
):
    streams, steps, width = inputs.shape
    gates_n = 4 * width
    count_w = 2 * width * gates_n
    total = count_w + gates_n
    shard = master.shape[0]
    devices = lax.axis_size("batch")
    me = lax.axis_index("batch")
    wide = OWN * devices
    block = OWN * 2 * gates_n
    gap = block - shard
    most = gap * devices
    tokens = streams * steps
    rows_n = -(-tokens // 32) * 32
    slot = -(-tokens // 128) * 128
    line = 8
    lines = devices // line

    line_groups = [[line * q + m for m in range(line)] for q in range(lines)]
    across_groups = [[line * q + m for q in range(lines)] for m in range(line)]
    column_groups = [
        [line * q + 2 * y + c for y in range(line // 2)] for q in range(lines) for c in range(2)
    ]
    twins = [(i, i ^ 1) for i in range(devices)]

    to_kept = one_hot(width, wide, lambda k, p: place_of(k, devices) == p)
    to_natural = one_hot(wide, width, lambda p, k: place_of(k, devices) == p)

    places = me * shard + lax.iota(jnp.int32, shard)
    recurrent = (places < count_w) & (places % (2 * gates_n) >= gates_n)
    rec_scale = jnp.where(recurrent, w_mask.astype(f32) * KEEP_RECURRENT, 1.0)
    local_low = master.astype(bf16) * rec_scale.astype(bf16)
    local_low = jnp.where(places < total, local_low, jnp.zeros((), bf16))

    def realigned(flat, following):
        joined = jnp.concatenate([flat, following])
        rows = lax.dynamic_slice(joined, (gap * me,), (block,)).reshape(OWN * 8, width)
        return dot(rows, to_kept).astype(bf16)

    before = [(i + 1, i) for i in range(devices - 1)]
    order = one_hot(
        OWN * 8,
        OWN * 8,
        lambda a, b: jnp.where(a < 64, (a % 8) * 8 + a // 8, 64 + a % 8) == b,
    )
    own = realigned(local_low, lax.ppermute(local_low[:most], "batch", before))
    own = dot(order, own).astype(bf16)
    own = jnp.concatenate([own[TILE * j : TILE * (j + 1)] for j in range(OWN)], axis=1)
    wall = lax.all_gather(own, "batch", axis=0, tiled=True)
    room = 16
    scale_low = rec_scale.astype(bf16)
    scales = realigned(scale_low, lax.ppermute(scale_low[:most], "batch", before))
    send = one_hot(
        line * room,
        OWN * 8,
        lambda a, b: (a % room < OWN) & (a % room * 8 + a // room % 2 * 4 + a // room // 2 == b),
    )
    scales = lax.all_to_all(
        dot(send, scales).astype(bf16), "batch", 0, 0, tiled=True, axis_index_groups=line_groups
    )
    into = one_hot(
        line * OWN,
        line * room,
        lambda a, b: jnp.where(
            a < line * TILE, a // TILE * room + a % TILE, a % TILE * room + TILE
        )
        == b,
    )
    scales = dot(into, scales).astype(bf16)

    in_scale = in_mask.astype(f32) * KEEP_INPUT
    mixed = (inputs.astype(f32) * in_scale[:, None, :]).astype(bf16).reshape(tokens, width)
    spare = ((0, rows_n - tokens), (0, 0))
    mixed = dot(jnp.pad(mixed, spare), to_kept).astype(bf16)
    bias_place = place_of(jnp.int32(width), devices)
    column = lax.broadcasted_iota(jnp.int32, mixed.shape, 1)
    mixed = jnp.where(column == bias_place, jnp.ones((), bf16), mixed)
    mixed_turned = jnp.pad(mixed, ((0, slot - rows_n), (0, 0))).T
    coming = dot(jnp.pad(d_out.reshape(tokens, width), spare), to_kept).astype(bf16)
    small = jnp.concatenate(
        [h_start.astype(bf16)]
        + split_exact(c_start)
        + [in_mask.astype(bf16), out_mask.astype(bf16)],
        axis=0,
    )
    small = dot(small, to_kept)
    part = [small[streams * j : streams * (j + 1)] for j in range(6)]
    empty = jnp.zeros((LANES - streams, wide), f32)
    h_first = jnp.concatenate([part[0], empty], axis=0)
    c_first = jnp.concatenate([part[1] + part[2] + part[3], empty], axis=0)
    row_stream = lax.broadcasted_iota(jnp.int32, (rows_n, 1), 0) // steps
    in_rows = sum(
        jnp.where(row_stream == s, part[4][s : s + 1], 0.0) for s in range(streams)
    ).astype(bf16)
    out_scale_kept = part[5] * KEEP_OUTPUT
    out_scale = jnp.concatenate(
        [out_scale_kept, out_scale_kept, jnp.zeros((LANES - 2 * streams, wide), f32)], axis=0
    )
    base = jnp.arange(streams, dtype=jnp.int32) * steps
    none = jnp.zeros((LANES - 2 * streams,), jnp.int32)
    begins = jnp.concatenate([base, base + pieces[:, 0], none])
    lengths = jnp.concatenate([pieces[:, 0], pieces[:, 1], none])
    ticks = lax.broadcasted_iota(jnp.int32, (LONGEST, LANES), 0)
    where = jnp.where(ticks < lengths[None, :], begins[None, :] + ticks, -1).reshape(-1)
    spread = (where[:, None] == lax.iota(jnp.int32, rows_n)[None, :]).astype(bf16)
    collect = (lax.iota(jnp.int32, slot)[:, None] == where[None, :]).astype(bf16)

    ready = (wall, mixed, mixed_turned, coming, spread, collect, h_first, c_first, out_scale)
    ready = lax.optimization_barrier(ready + (in_rows, to_natural, scales))
    wall, mixed, mixed_turned, coming, spread, collect, h_first, c_first, out_scale = ready[:9]
    in_rows, to_natural, scales = ready[9:]
    mixed_all = lax.all_gather(
        mixed_turned, "batch", axis=0, tiled=True, axis_index_groups=line_groups
    )
    hidden_turned, output_rows, ninth_in, kept, turned = run_forward(
        wall, mixed, spread, collect, h_first, c_first, out_scale
    )
    hidden_all = lax.all_gather(
        hidden_turned, "batch", axis=0, tiled=True, axis_index_groups=line_groups
    )
    gate_rows = run_backward(turned, kept, coming, spread, collect, out_scale)

    core = (me % 2).reshape(1)
    mine = [
        lax.all_to_all(part, "batch", 0, 0, tiled=True, axis_index_groups=column_groups)
        for part in gate_rows
    ]
    other = [lax.ppermute(part, "batch", twins) for part in mine]
    sums = []
    for index in range(2):
        message = run_gradient(core, mixed_all, hidden_all, mine[index], other[index], lines)
        sums.append(
            lax.all_to_all(
                message, "batch", 0, 0, tiled=True, axis_index_groups=across_groups
            )
        )
    homeward, squares = run_reduce(sums[0], sums[1], scales, line, devices)
    homeward = lax.all_to_all(
        homeward, "batch", 0, 0, tiled=True, axis_index_groups=line_groups
    )
    squares = lax.all_to_all(squares, "batch", 0, 0, tiled=True)
    home = run_settle(homeward, to_natural).reshape(block)
    tail = lax.ppermute(home[block - most :], "batch", [(i, i + 1) for i in range(devices - 1)])
    grad_shard = lax.dynamic_slice(
        jnp.concatenate([tail, home]), (most - gap * me,), (shard,)
    ).astype(f32)
    grad_norm = jnp.sqrt(jnp.sum(squares[:, 0]))

    d_rows, out_rows = run_own(
        wall, ninth_in, gate_rows[0], gate_rows[1], in_rows, output_rows, to_natural
    )
    output = out_rows[:tokens].reshape(streams, steps, width)
    d_inputs = d_rows[:tokens].reshape(streams, steps, width)

    factor = jnp.minimum(1.0, CLIP_NORM / (grad_norm + 1e-06))
    clipped = grad_shard * factor
    moment_new = BETA_ONE * moment_one + (1.0 - BETA_ONE) * clipped
    second_new = BETA_TWO * moment_two + (1.0 - BETA_TWO) * clipped * clipped
    first_hat = moment_new / (1.0 - BETA_ONE**STEP)
    second_hat = second_new / (1.0 - BETA_TWO**STEP)
    master_new = master - LEARN_RATE * (
        first_hat / (jnp.sqrt(second_hat) + EPSILON) + WEIGHT_DECAY * master
    )
    return (output, d_inputs, moment_new, second_new, master_new, grad_norm)


def solution(mesh):
    placed = (
        P("batch", None, None),
        P("batch", None, None),
        P("batch", None),
        P("batch", None),
        P("batch", None),
        P("batch", None),
        P("batch", None),
        P("batch"),
        P("batch"),
        P("batch"),
        P("batch"),
    )
    return jax.shard_map(
        body,
        mesh=mesh,
        in_specs=placed,
        out_specs=(
            P("batch", None, None),
            P("batch", None, None),
            P("batch"),
            P("batch"),
            P("batch"),
            P(),
        ),
        check_vma=False,
    )
```

```python
import jax
import jax.numpy as jnp
from jax import lax
from jax.experimental import pallas as pl
from jax.experimental.pallas import tpu as pltpu
from jax.sharding import PartitionSpec as P

STEP = 10


LEARN_RATE = 0.03
BETA_ONE = 0.9
BETA_TWO = 0.999
WEIGHT_DECAY = 0.01
EPSILON = 1e-08
CLIP_NORM = 1.0
KEEP_INPUT = 4.0 / 3.0
KEEP_OUTPUT = 4.0 / 3.0
KEEP_RECURRENT = 2.0

LONGEST = 40
LANES = 8
TILE = 8
OWN = TILE + 1
KINDS = 6
PART = 8
UNROLL_FORWARD = 3
UNROLL_BACKWARD = 4
MESSAGE = 88
SQUARES = 81
VMEM_LIMIT = 60 * 2**20

f32 = jnp.float32
bf16 = jnp.bfloat16


def dot(left, right):
    return lax.dot_general(left, right, (((1,), (0,)), ((), ())), preferred_element_type=f32)


def one_hot(rows, columns, wanted):
    row = lax.broadcasted_iota(jnp.int32, (rows, columns), 0)
    column = lax.broadcasted_iota(jnp.int32, (rows, columns), 1)
    return wanted(row, column).astype(bf16)


def place_of(natural, devices):
    owner, rest = natural // OWN, natural % OWN
    return jnp.where(rest < TILE, owner * TILE + rest, devices * TILE + owner)


def step_rows(step):
    return pl.ds(pl.multiple_of(step * LANES, LANES), LANES)


def kept_rows(step, kind):
    return pl.ds(pl.multiple_of((step * KINDS + kind) * LANES, LANES), LANES)


def forward_kernel(
    wall,
    mixed,
    spread,
    collect,
    h_first,
    c_first,
    out_scale,
    hidden_turned,
    output_rows,
    ninth_in,
    kept,
    turned,
    square,
    w_rec,
    ninth,
    apart,
    pre,
    kept_here,
    hiddens,
    outs,
    sems_in,
    sem_ninth,
    sem_rec,
    sems_kept,
    sems_turned,
):
    width = mixed.shape[1]
    main = wall.shape[0]
    devices = main // TILE
    gates_n = 4 * width

    copy_ninth = pltpu.make_async_copy(wall.at[:, pl.ds(2 * gates_n, width)], ninth, sem_ninth)
    copies_in = [
        pltpu.make_async_copy(
            wall.at[:, pl.ds(gate * width, width)],
            square.at[gate, pl.ds(0, main), :],
            sems_in.at[gate],
        )
        for gate in range(4)
    ]
    copy_rec = pltpu.make_async_copy(
        wall.at[:, pl.ds(gates_n, gates_n)], w_rec.at[pl.ds(0, main), :], sem_rec
    )
    copy_ninth.start()
    for copy in copies_in:
        copy.start()
    rows = dot(spread[...], mixed[...]).astype(bf16)
    copy_ninth.wait()
    for tile in range(width // 128):
        columns = pl.ds(tile * 128, 128)
        apart[tile] = ninth[:, columns].astype(f32)
        for gate in range(8):
            rest = apart[tile, pl.ds(gate, devices, stride=8), :].astype(bf16)
            if gate < 4:
                square[gate, pl.ds(main, devices), columns] = rest
                ninth_in[gate, :, columns] = rest
            else:
                there = pl.ds((gate - 4) * width + tile * 128, 128)
                w_rec[pl.ds(main, devices), there] = rest
    copy_rec.start()
    for gate in range(4):
        copies_in[gate].wait()
        pre[:, pl.ds(gate * width, width)] = dot(rows, square[gate])
    copy_rec.wait()
    scale = out_scale[...]

    def step(index, carry):
        hidden, cell = carry
        at = step_rows(index)
        gates = pre[at, :] + dot(hidden.astype(bf16), w_rec[...])
        in_gate = jax.nn.sigmoid(gates[:, :width])
        forget = jax.nn.sigmoid(gates[:, width : 2 * width])
        candid = jnp.tanh(gates[:, 2 * width : 3 * width])
        out_gate = jax.nn.sigmoid(gates[:, 3 * width :])
        cell_new = forget * cell + in_gate * candid
        squash = jnp.tanh(cell_new)
        hidden_new = out_gate * squash
        hiddens[at, :] = hidden
        outs[at, :] = hidden_new * scale
        kept_here[kept_rows(index, 0), :] = out_gate * (1.0 - squash * squash)
        kept_here[kept_rows(index, 1), :] = candid * in_gate * (1.0 - in_gate)
        kept_here[kept_rows(index, 2), :] = cell * forget * (1.0 - forget)
        kept_here[kept_rows(index, 3), :] = in_gate * (1.0 - candid * candid)
        kept_here[kept_rows(index, 4), :] = squash * out_gate * (1.0 - out_gate)
        kept_here[kept_rows(index, 5), :] = forget
        return (hidden_new, cell_new)

    turns = width // 128

    def copy_kept(part):
        size = turns * KINDS * LANES
        at = pl.ds(pl.multiple_of(part * size, LANES), size)
        return pltpu.make_async_copy(kept_here.at[at, :], kept.at[at, :], sems_kept.at[part])

    def copy_turned(gate):
        return pltpu.make_async_copy(square.at[gate], turned.at[gate], sems_turned.at[gate])

    def part(gate, carry):
        def turning(count, carry):
            columns = pl.ds(pl.multiple_of(gate * width + count * 128, 128), 128)
            into = pl.ds(pl.multiple_of(count * 128, 128), 128)
            square[gate, into, :] = w_rec[:, columns].T
            return step(gate * turns + count, carry)

        carry = lax.fori_loop(0, turns, turning, carry, unroll=UNROLL_FORWARD)
        copy_kept(gate).start()
        copy_turned(gate).start()
        return carry

    carry = lax.fori_loop(0, 4, part, (h_first[...], c_first[...]))
    lax.fori_loop(4 * turns, LONGEST, step, carry, unroll=UNROLL_FORWARD)
    begin = 4 * turns * KINDS * LANES
    rest = pl.ds(begin, kept_here.shape[0] - begin)
    last = pltpu.make_async_copy(kept_here.at[rest, :], kept.at[rest, :], sems_kept.at[4])
    last.start()
    hidden_turned[...] = lax.dot_general(
        hiddens[...].astype(bf16),
        collect[...],
        (((0,), (1,)), ((), ())),
        preferred_element_type=f32,
    ).astype(bf16)
    output_rows[...] = dot(collect[...], outs[...].astype(bf16)).astype(bf16)
    for gate in range(4):
        copy_kept(gate).wait()
        copy_turned(gate).wait()
    last.wait()


def backward_kernel(
    turned,
    kept,
    coming,
    spread,
    collect,
    out_scale,
    gate_rows,
    w_turned,
    kept_here,
    come,
    dgates,
    sems_turned,
    sems_kept,
):
    width = coming.shape[1]
    rows = gate_rows.shape[1]
    size = PART * KINDS * LANES
    parts = LONGEST // PART

    def copy_kept(part):
        at = pl.ds(pl.multiple_of(part * size, LANES), size)
        return pltpu.make_async_copy(kept.at[at, :], kept_here.at[at, :], sems_kept.at[part])

    copies = [
        pltpu.make_async_copy(
            turned.at[gate], w_turned.at[pl.ds(gate * width, width), :], sems_turned.at[gate]
        )
        for gate in range(4)
    ]
    copy_kept(parts - 1).start()
    for copy in copies:
        copy.start()
    for part in range(parts - 1):
        copy_kept(parts - 2 - part).start()
    come[...] = dot(spread[...], coming[...])
    scale = out_scale[...]

    def gradients(index, carry):
        dh_next, dc_next = carry
        at = step_rows(index)
        grad_h = come[at, :] * scale + dh_next
        grad_c = dc_next + grad_h * kept_here[kept_rows(index, 0), :]
        grads = jnp.concatenate(
            [
                grad_c * kept_here[kept_rows(index, 1), :],
                grad_c * kept_here[kept_rows(index, 2), :],
                grad_c * kept_here[kept_rows(index, 3), :],
                grad_h * kept_here[kept_rows(index, 4), :],
            ],
            axis=1,
        )
        dgates[at, :] = grads
        return (grads, grad_c * kept_here[kept_rows(index, 5), :])

    def step(index, carry):
        grads, dc_next = gradients(index, carry)
        return (dot(grads.astype(bf16), w_turned[...]), dc_next)

    def run(part, count, carry):
        first = (part + 1) * PART - 1
        return lax.fori_loop(
            0, count, lambda back, c: step(first - back, c), carry, unroll=UNROLL_BACKWARD
        )

    copy_kept(parts - 1).wait()
    for copy in copies:
        copy.wait()
    zero = jnp.zeros((LANES, width), f32)

    def whole_part(back, carry):
        part = parts - 1 - back

        @pl.when(back > 0)
        def _():
            copy_kept(part).wait()

        return run(part, PART, carry)

    carry = lax.fori_loop(0, parts - 1, whole_part, (zero, zero))
    copy_kept(0).wait()
    carry = run(0, PART - 1, carry)
    gradients(0, carry)
    for gate in range(4):
        columns = pl.ds(gate * width, width)
        gate_rows[gate] = dot(
            collect[pl.ds(0, rows), :], dgates[:, columns].astype(bf16)
        ).astype(bf16)


def gradient_kernel(
    core, mixed_all, hidden_all, mine, other, message, left, right, sems_left, sems_right
):
    half, rows, columns = mine.shape
    line = 2 * half
    lines = message.shape[0]
    width, slot = left.shape[0], mixed_all.shape[1]
    main = lines * line * TILE
    which = core[0]

    def copies_left(source):
        found = []
        for place in range(line):
            chip, twin = place % half, place // half
            block = 2 * chip + (which if twin == 0 else 1 - which)
            found.append(
                pltpu.make_async_copy(
                    source.at[pl.ds(block * width, width), :],
                    left.at[:, pl.ds(place * slot, slot)],
                    sems_left.at[place],
                )
            )
        return found

    @pl.when(which == 0)
    def _():
        for copy in copies_left(mixed_all):
            copy.start()

    @pl.when(which != 0)
    def _():
        for copy in copies_left(hidden_all):
            copy.start()

    copies_right = [
        pltpu.make_async_copy(
            (mine if place < half else other).at[place % half],
            right.at[pl.ds(place * slot, rows), :],
            sems_right.at[place],
        )
        for place in range(line)
    ]
    for copy in copies_right:
        copy.start()
    for place in range(line):
        right[pl.ds(place * slot + rows, slot - rows), :] = jnp.zeros((slot - rows, columns), bf16)
    for copy in copies_left(mixed_all) + copies_right:
        copy.wait()
    grad = dot(left[...], right[...])
    packed = jnp.concatenate(
        [
            grad[:main].reshape(lines, line * TILE, columns),
            grad[main:].reshape(lines, line, columns),
        ],
        axis=1,
    )
    message[...] = packed.astype(bf16)


def reduce_kernel(got, scale, homeward, packed):
    line = homeward.shape[0]
    lines = got.shape[0]
    tiles = got.shape[2] // 128
    total = jnp.zeros((1, 128), f32)
    packed[:, pl.ds(OWN * TILE, TILE * 2), :] = jnp.zeros((line, TILE * 2, 128), f32)
    for tile in range(tiles):
        columns = pl.ds(tile * 128, 128)
        found = got[0, :, columns].astype(f32)
        for index in range(1, lines):
            found = found + got[index, :, columns].astype(f32)
        found = found * scale[:, columns].astype(f32)
        total = total + jnp.sum(found * found, axis=0, keepdims=True)
        packed[:, pl.ds(tile * TILE, TILE), :] = found[: line * TILE].reshape(line, TILE, 128)
        packed[:, OWN * TILE + tile, :] = found[line * TILE :]
    rest = jnp.broadcast_to(jnp.sum(total, axis=1, keepdims=True), (line, 128))
    for index in range(3):
        part = rest.astype(bf16).astype(f32)
        packed[:, SQUARES + index, :] = part
        rest = rest - part
    homeward[...] = packed[...].astype(bf16)


def settle_kernel(got, to_natural, home, squares, placed, wide):
    line = got.shape[0]
    tiles = placed.shape[0]
    half = line // 2
    wide[...] = got[...].astype(f32)
    total = jnp.zeros((1, 128), f32)
    for source in range(line):
        gate = (source % 2) * half + source // 2
        for tile in range(tiles):
            placed[tile, pl.ds(gate, TILE, stride=8), :] = wide[
                source, pl.ds(tile * TILE, TILE), :
            ]
            placed[tile, pl.ds(TILE * 8 + gate, 1), :] = wide[
                source, pl.ds(OWN * TILE + tile, 1), :
            ]
        for index in range(3):
            total = total + wide[source, pl.ds(SQUARES + index, 1), :]
    squares[...] = jnp.broadcast_to(total, squares.shape)
    values = jnp.concatenate([placed[tile] for tile in range(tiles)], axis=1)
    home[...] = dot(values.astype(bf16), to_natural[...]).astype(bf16)


def own_kernel(
    wall, ninth_in, gate_rows, in_rows, output_rows, to_natural, d_out, out, square, sems
):
    width = in_rows.shape[1]
    rows = in_rows.shape[0]
    main = wall.shape[0]
    rest = width - main
    copies = []
    for gate in range(4):
        copies.append(
            pltpu.make_async_copy(
                wall.at[:, pl.ds(gate * width, width)],
                square.at[gate, pl.ds(0, main), :],
                sems.at[2 * gate],
            )
        )
        copies.append(
            pltpu.make_async_copy(
                ninth_in.at[gate], square.at[gate, pl.ds(main, rest), :], sems.at[2 * gate + 1]
            )
        )
    for copy in copies:
        copy.start()
    out[...] = dot(output_rows[pl.ds(0, rows), :], to_natural[...]).astype(bf16)

    def right_product(left, matrix):
        return lax.dot_general(
            left, matrix, (((1,), (1,)), ((), ())), preferred_element_type=f32
        )

    found = jnp.zeros((rows, width), f32)
    for gate in range(4):
        copies[2 * gate].wait()
        copies[2 * gate + 1].wait()
        found = found + right_product(gate_rows[gate], square[gate])
    found = found * (in_rows[...].astype(f32) * KEEP_INPUT)
    d_out[...] = dot(found.astype(bf16), to_natural[...]).astype(bf16)


def in_vmem():
    return pl.BlockSpec(memory_space=pltpu.VMEM)


def in_place():
    return pl.BlockSpec(memory_space=pl.ANY)


def run_forward(wall, mixed, spread, collect, h_first, c_first, out_scale):
    steps_rows = spread.shape[0]
    rows, width = mixed.shape
    devices = wall.shape[0] // TILE
    all_kept = LONGEST * KINDS * LANES
    return pl.pallas_call(
        forward_kernel,
        out_shape=(
            jax.ShapeDtypeStruct((width, collect.shape[0]), bf16),
            jax.ShapeDtypeStruct((collect.shape[0], width), bf16),
            jax.ShapeDtypeStruct((4, devices, width), bf16),
            jax.ShapeDtypeStruct((all_kept, width), f32),
            jax.ShapeDtypeStruct((4, width, width), bf16),
        ),
        in_specs=[in_place()] + [in_vmem()] * 6,
        out_specs=(in_vmem(),) * 3 + (in_place(),) * 2,
        scratch_shapes=[
            pltpu.VMEM((4, width, width), bf16),
            pltpu.VMEM((width, 4 * width), bf16),
            pltpu.VMEM((devices * TILE, width), bf16),
            pltpu.VMEM((width // 128, devices * TILE, 128), f32),
            pltpu.VMEM((steps_rows, 4 * width), f32),
            pltpu.VMEM((all_kept, width), f32),
            pltpu.VMEM((steps_rows, width), f32),
            pltpu.VMEM((steps_rows, width), f32),
            pltpu.SemaphoreType.DMA((4,)),
            pltpu.SemaphoreType.DMA,
            pltpu.SemaphoreType.DMA,
            pltpu.SemaphoreType.DMA((5,)),
            pltpu.SemaphoreType.DMA((4,)),
        ],
        compiler_params=pltpu.CompilerParams(vmem_limit_bytes=VMEM_LIMIT),
        cost_estimate=pl.CostEstimate(
            flops=60_000_000_000, bytes_accessed=30_000_000, transcendentals=2_000_000
        ),
        name="forward",
    )(wall, mixed, spread, collect, h_first, c_first, out_scale)


def run_backward(turned, kept, coming, spread, collect, out_scale):
    steps_rows = spread.shape[0]
    rows, width = coming.shape
    return pl.pallas_call(
        backward_kernel,
        out_shape=jax.ShapeDtypeStruct((4, rows, width), bf16),
        in_specs=[in_place()] * 2 + [in_vmem()] * 4,
        out_specs=in_vmem(),
        scratch_shapes=[
            pltpu.VMEM((4 * width, width), bf16),
            pltpu.VMEM(kept.shape, f32),
            pltpu.VMEM((steps_rows, width), f32),
            pltpu.VMEM((steps_rows, 4 * width), f32),
            pltpu.SemaphoreType.DMA((4,)),
            pltpu.SemaphoreType.DMA((LONGEST // PART,)),
        ],
        compiler_params=pltpu.CompilerParams(vmem_limit_bytes=VMEM_LIMIT),
        cost_estimate=pl.CostEstimate(
            flops=60_000_000_000, bytes_accessed=30_000_000, transcendentals=0
        ),
        name="backward",
    )(turned, kept, coming, spread, collect, out_scale)


def run_gradient(core, mixed_all, hidden_all, mine, other, lines):
    half, rows, columns = mine.shape
    line, slot = 2 * half, mixed_all.shape[1]
    width = mixed_all.shape[0] // line
    return pl.pallas_call(
        gradient_kernel,
        out_shape=jax.ShapeDtypeStruct((lines, line * OWN, columns), bf16),
        in_specs=[pl.BlockSpec(memory_space=pltpu.SMEM)] + [in_place()] * 4,
        out_specs=in_vmem(),
        scratch_shapes=[
            pltpu.VMEM((width, line * slot), bf16),
            pltpu.VMEM((line * slot, columns), bf16),
            pltpu.SemaphoreType.DMA((line,)),
            pltpu.SemaphoreType.DMA((line,)),
        ],
        compiler_params=pltpu.CompilerParams(vmem_limit_bytes=VMEM_LIMIT),
        cost_estimate=pl.CostEstimate(
            flops=6_000_000_000, bytes_accessed=12_000_000, transcendentals=0
        ),
        name="gradient",
    )(core, mixed_all, hidden_all, mine, other)


def run_reduce(got, scale, line):
    return pl.pallas_call(
        reduce_kernel,
        out_shape=jax.ShapeDtypeStruct((line, MESSAGE, 128), bf16),
        in_specs=[in_vmem()] * 2,
        out_specs=in_vmem(),
        scratch_shapes=[pltpu.VMEM((line, MESSAGE, 128), f32)],
        compiler_params=pltpu.CompilerParams(vmem_limit_bytes=VMEM_LIMIT),
        name="reduce",
    )(got, scale)


def run_settle(got, to_natural, lines):
    wide, width = to_natural.shape
    return pl.pallas_call(
        settle_kernel,
        out_shape=(
            jax.ShapeDtypeStruct((OWN * 8, width), bf16),
            jax.ShapeDtypeStruct((lines, 128), f32),
        ),
        in_specs=[in_vmem()] * 2,
        out_specs=(in_vmem(),) * 2,
        scratch_shapes=[
            pltpu.VMEM((wide // 128, OWN * 8, 128), f32),
            pltpu.VMEM(got.shape, f32),
        ],
        compiler_params=pltpu.CompilerParams(vmem_limit_bytes=VMEM_LIMIT),
        name="settle",
    )(got, to_natural)


def run_own(wall, ninth_in, gate_rows, in_rows, output_rows, to_natural):
    rows, width = in_rows.shape
    natural = to_natural.shape[1]
    return pl.pallas_call(
        own_kernel,
        out_shape=(jax.ShapeDtypeStruct((rows, natural), bf16),) * 2,
        in_specs=[in_place()] * 2 + [in_vmem()] * 4,
        out_specs=(in_vmem(),) * 2,
        scratch_shapes=[
            pltpu.VMEM((4, width, width), bf16),
            pltpu.SemaphoreType.DMA((8,)),
        ],
        compiler_params=pltpu.CompilerParams(vmem_limit_bytes=VMEM_LIMIT),
        cost_estimate=pl.CostEstimate(
            flops=8_000_000_000, bytes_accessed=15_000_000, transcendentals=0
        ),
        name="own",
    )(wall, ninth_in, gate_rows, in_rows, output_rows, to_natural)


def split_exact(values):
    parts = []
    rest = values
    for _ in range(3):
        part = lax.reduce_precision(rest, 8, 7)
        parts.append(part.astype(bf16))
        rest = rest - part
    return parts


def body(
    inputs,
    d_out,
    h_start,
    c_start,
    pieces,
    in_mask,
    out_mask,
    w_mask,
    master,
    moment_one,
    moment_two,
):
    streams, steps, width = inputs.shape
    gates_n = 4 * width
    count_w = 2 * width * gates_n
    total = count_w + gates_n
    shard = master.shape[0]
    devices = lax.axis_size("batch")
    me = lax.axis_index("batch")
    wide = OWN * devices
    block = OWN * 2 * gates_n
    gap = block - shard
    most = gap * devices
    tokens = streams * steps
    rows_n = -(-tokens // 32) * 32
    slot = -(-tokens // 128) * 128
    line = 8
    lines = devices // line

    line_groups = [[line * q + m for m in range(line)] for q in range(lines)]
    across_groups = [[line * q + m for q in range(lines)] for m in range(line)]
    column_groups = [
        [line * q + 2 * y + c for y in range(line // 2)] for q in range(lines) for c in range(2)
    ]
    twins = [(i, i ^ 1) for i in range(devices)]

    to_kept = one_hot(width, wide, lambda k, p: place_of(k, devices) == p)
    to_natural = one_hot(wide, width, lambda p, k: place_of(k, devices) == p)

    places = me * shard + lax.iota(jnp.int32, shard)
    recurrent = (places < count_w) & (places % (2 * gates_n) >= gates_n)
    rec_scale = jnp.where(recurrent, w_mask.astype(f32) * KEEP_RECURRENT, 1.0)
    local_low = master.astype(bf16) * rec_scale.astype(bf16)
    local_low = jnp.where(places < total, local_low, jnp.zeros((), bf16))

    def realigned(flat, following):
        joined = jnp.concatenate([flat, following])
        rows = lax.dynamic_slice(joined, (gap * me,), (block,)).reshape(OWN * 8, width)
        return dot(rows, to_kept).astype(bf16)

    before = [(i + 1, i) for i in range(devices - 1)]
    order = one_hot(
        OWN * 8,
        OWN * 8,
        lambda a, b: jnp.where(a < 64, (a % 8) * 8 + a // 8, 64 + a % 8) == b,
    )
    own = realigned(local_low, lax.ppermute(local_low[:most], "batch", before))
    own = dot(order, own).astype(bf16)
    own = jnp.concatenate([own[TILE * j : TILE * (j + 1)] for j in range(OWN)], axis=1)
    wall = lax.all_gather(own, "batch", axis=0, tiled=True)
    room = 16
    scale_low = rec_scale.astype(bf16)
    scales = realigned(scale_low, lax.ppermute(scale_low[:most], "batch", before))
    send = one_hot(
        line * room,
        OWN * 8,
        lambda a, b: (a % room < OWN) & (a % room * 8 + a // room % 2 * 4 + a // room // 2 == b),
    )
    scales = lax.all_to_all(
        dot(send, scales).astype(bf16), "batch", 0, 0, tiled=True, axis_index_groups=line_groups
    )
    into = one_hot(
        line * OWN,
        line * room,
        lambda a, b: jnp.where(
            a < line * TILE, a // TILE * room + a % TILE, a % TILE * room + TILE
        )
        == b,
    )
    scales = dot(into, scales).astype(bf16)

    in_scale = in_mask.astype(f32) * KEEP_INPUT
    mixed = (inputs.astype(f32) * in_scale[:, None, :]).astype(bf16).reshape(tokens, width)
    spare = ((0, rows_n - tokens), (0, 0))
    mixed = dot(jnp.pad(mixed, spare), to_kept).astype(bf16)
    bias_place = place_of(jnp.int32(width), devices)
    column = lax.broadcasted_iota(jnp.int32, mixed.shape, 1)
    mixed = jnp.where(column == bias_place, jnp.ones((), bf16), mixed)
    mixed_turned = jnp.pad(mixed, ((0, slot - rows_n), (0, 0))).T
    coming = dot(jnp.pad(d_out.reshape(tokens, width), spare), to_kept).astype(bf16)
    small = jnp.concatenate(
        [h_start.astype(bf16)]
        + split_exact(c_start)
        + [in_mask.astype(bf16), out_mask.astype(bf16)],
        axis=0,
    )
    small = dot(small, to_kept)
    part = [small[streams * j : streams * (j + 1)] for j in range(6)]
    empty = jnp.zeros((LANES - streams, wide), f32)
    h_first = jnp.concatenate([part[0], empty], axis=0)
    c_first = jnp.concatenate([part[1] + part[2] + part[3], empty], axis=0)
    row_stream = lax.broadcasted_iota(jnp.int32, (rows_n, 1), 0) // steps
    in_rows = sum(
        jnp.where(row_stream == s, part[4][s : s + 1], 0.0) for s in range(streams)
    ).astype(bf16)
    out_scale_kept = part[5] * KEEP_OUTPUT
    out_scale = jnp.concatenate(
        [out_scale_kept, out_scale_kept, jnp.zeros((LANES - 2 * streams, wide), f32)], axis=0
    )
    base = jnp.arange(streams, dtype=jnp.int32) * steps
    none = jnp.zeros((LANES - 2 * streams,), jnp.int32)
    begins = jnp.concatenate([base, base + pieces[:, 0], none])
    lengths = jnp.concatenate([pieces[:, 0], pieces[:, 1], none])
    ticks = lax.broadcasted_iota(jnp.int32, (LONGEST, LANES), 0)
    where = jnp.where(ticks < lengths[None, :], begins[None, :] + ticks, -1).reshape(-1)
    spread = (where[:, None] == lax.iota(jnp.int32, rows_n)[None, :]).astype(bf16)
    collect = (lax.iota(jnp.int32, slot)[:, None] == where[None, :]).astype(bf16)

    ready = (wall, mixed, mixed_turned, coming, spread, collect, h_first, c_first, out_scale)
    ready = lax.optimization_barrier(ready + (in_rows, to_natural, scales))
    wall, mixed, mixed_turned, coming, spread, collect, h_first, c_first, out_scale = ready[:9]
    in_rows, to_natural, scales = ready[9:]
    mixed_all = lax.all_gather(
        mixed_turned, "batch", axis=0, tiled=True, axis_index_groups=line_groups
    )
    hidden_turned, output_rows, ninth_in, kept, turned = run_forward(
        wall, mixed, spread, collect, h_first, c_first, out_scale
    )
    hidden_turned, mixed_all = lax.optimization_barrier((hidden_turned, mixed_all))
    hidden_all = lax.all_gather(
        hidden_turned, "batch", axis=0, tiled=True, axis_index_groups=line_groups
    )
    gate_rows = run_backward(turned, kept, coming, spread, collect, out_scale)

    core = (me % 2).reshape(1)
    mine = lax.all_to_all(
        gate_rows, "batch", 0, 0, tiled=True, axis_index_groups=column_groups
    )
    other = lax.ppermute(mine, "batch", twins)
    message = run_gradient(core, mixed_all, hidden_all, mine, other, lines)
    got = lax.all_to_all(
        message, "batch", 0, 0, tiled=True, axis_index_groups=across_groups
    )
    homeward = lax.all_to_all(
        run_reduce(got, scales, line), "batch", 0, 0, tiled=True, axis_index_groups=line_groups
    )
    home, squares = run_settle(homeward, to_natural, lines)
    squares = lax.all_to_all(
        squares, "batch", 0, 0, tiled=True, axis_index_groups=across_groups
    )
    home = home.reshape(block)
    tail = lax.ppermute(home[block - most :], "batch", [(i, i + 1) for i in range(devices - 1)])
    grad_shard = lax.dynamic_slice(
        jnp.concatenate([tail, home]), (most - gap * me,), (shard,)
    ).astype(f32)
    grad_norm = jnp.sqrt(jnp.sum(squares[:, 0]))

    d_rows, out_rows = run_own(
        wall, ninth_in, gate_rows, in_rows, output_rows, to_natural
    )
    output = out_rows[:tokens].reshape(streams, steps, width)
    d_inputs = d_rows[:tokens].reshape(streams, steps, width)

    factor = jnp.minimum(1.0, CLIP_NORM / (grad_norm + 1e-06))
    clipped = grad_shard * factor
    moment_new = BETA_ONE * moment_one + (1.0 - BETA_ONE) * clipped
    second_new = BETA_TWO * moment_two + (1.0 - BETA_TWO) * clipped * clipped
    first_hat = moment_new / (1.0 - BETA_ONE**STEP)
    second_hat = second_new / (1.0 - BETA_TWO**STEP)
    master_new = master - LEARN_RATE * (
        first_hat / (jnp.sqrt(second_hat) + EPSILON) + WEIGHT_DECAY * master
    )
    return (output, d_inputs, moment_new, second_new, master_new, grad_norm)


def solution(mesh):
    placed = (
        P("batch", None, None),
        P("batch", None, None),
        P("batch", None),
        P("batch", None),
        P("batch", None),
        P("batch", None),
        P("batch", None),
        P("batch"),
        P("batch"),
        P("batch"),
        P("batch"),
    )
    return jax.shard_map(
        body,
        mesh=mesh,
        in_specs=placed,
        out_specs=(
            P("batch", None, None),
            P("batch", None, None),
            P("batch"),
            P("batch"),
            P("batch"),
            P(),
        ),
        check_vma=False,
    )
```

```python
import functools

import jax
import jax.numpy as jnp
from jax import lax
from jax.experimental import pallas as pl
from jax.experimental.pallas import tpu as pltpu
from jax.sharding import PartitionSpec as P

STEP = 10


LEARN_RATE = 0.03
BETA_ONE = 0.9
BETA_TWO = 0.999
WEIGHT_DECAY = 0.01
EPSILON = 1e-08
CLIP_NORM = 1.0
KEEP_INPUT = 4.0 / 3.0
KEEP_OUTPUT = 4.0 / 3.0
KEEP_RECURRENT = 2.0

LONGEST = 40
LANES = 8
TILE = 8
OWN = TILE + 1
KINDS = 6
SOON = 4
SPLIT = 14
LATE = 128
LATE_BLOCK = LATE // 3
EARLY = 96
UNROLL_FORWARD = 3
UNROLL_BACKWARD = 4
MESSAGE = 88
SQUARES = 81
VMEM_LIMIT = 60 * 2**20

f32 = jnp.float32
bf16 = jnp.bfloat16


def dot(left, right):
    return lax.dot_general(left, right, (((1,), (0,)), ((), ())), preferred_element_type=f32)


def one_hot(rows, columns, wanted):
    row = lax.broadcasted_iota(jnp.int32, (rows, columns), 0)
    column = lax.broadcasted_iota(jnp.int32, (rows, columns), 1)
    return wanted(row, column).astype(bf16)


def place_of(natural, devices):
    owner, rest = natural // OWN, natural % OWN
    return jnp.where(rest < TILE, owner * TILE + rest, devices * TILE + owner)


def step_rows(step):
    return pl.ds(pl.multiple_of(step * LANES, LANES), LANES)


def kept_rows(step, kind):
    return pl.ds(pl.multiple_of((step * KINDS + kind) * LANES, LANES), LANES)


def forward_kernel(
    wall,
    mixed,
    spread,
    collect,
    h_first,
    c_first,
    out_scale,
    hidden_turned,
    output_rows,
    ninth_in,
    kept,
    turned,
    square,
    w_rec,
    ninth,
    apart,
    pre,
    kept_here,
    hiddens,
    outs,
    sems_in,
    sem_ninth,
    sem_rec,
    sems_kept,
    sems_turned,
):
    width = mixed.shape[1]
    main = wall.shape[0]
    devices = main // TILE
    gates_n = 4 * width

    copy_ninth = pltpu.make_async_copy(wall.at[:, pl.ds(2 * gates_n, width)], ninth, sem_ninth)
    copies_in = [
        pltpu.make_async_copy(
            wall.at[:, pl.ds(gate * width, width)],
            square.at[gate, pl.ds(0, main), :],
            sems_in.at[gate],
        )
        for gate in range(4)
    ]
    copy_rec = pltpu.make_async_copy(
        wall.at[:, pl.ds(gates_n, gates_n)], w_rec.at[pl.ds(0, main), :], sem_rec
    )
    copy_ninth.start()
    for copy in copies_in:
        copy.start()
    rows = dot(spread[...], mixed[...]).astype(bf16)
    copy_ninth.wait()
    for tile in range(width // 128):
        columns = pl.ds(tile * 128, 128)
        apart[tile] = ninth[:, columns].astype(f32)
        for gate in range(8):
            rest = apart[tile, pl.ds(gate, devices, stride=8), :].astype(bf16)
            if gate < 4:
                square[gate, pl.ds(main, devices), columns] = rest
                ninth_in[gate, :, columns] = rest
            else:
                there = pl.ds((gate - 4) * width + tile * 128, 128)
                w_rec[pl.ds(main, devices), there] = rest
    copy_rec.start()
    for gate in range(4):
        copies_in[gate].wait()
        pre[:, pl.ds(gate * width, width)] = dot(rows, square[gate])
    copy_rec.wait()
    scale = out_scale[...]

    def step(index, carry):
        hidden, cell = carry
        at = step_rows(index)
        gates = pre[at, :] + dot(hidden.astype(bf16), w_rec[...])
        in_gate = jax.nn.sigmoid(gates[:, :width])
        forget = jax.nn.sigmoid(gates[:, width : 2 * width])
        candid = jnp.tanh(gates[:, 2 * width : 3 * width])
        out_gate = jax.nn.sigmoid(gates[:, 3 * width :])
        cell_new = forget * cell + in_gate * candid
        squash = jnp.tanh(cell_new)
        hidden_new = out_gate * squash
        hiddens[at, :] = hidden
        outs[at, :] = hidden_new * scale
        kept_here[kept_rows(index, 0), :] = out_gate * (1.0 - squash * squash)
        kept_here[kept_rows(index, 1), :] = candid * in_gate * (1.0 - in_gate)
        kept_here[kept_rows(index, 2), :] = cell * forget * (1.0 - forget)
        kept_here[kept_rows(index, 3), :] = in_gate * (1.0 - candid * candid)
        kept_here[kept_rows(index, 4), :] = squash * out_gate * (1.0 - out_gate)
        kept_here[kept_rows(index, 5), :] = forget
        return (hidden_new, cell_new)

    turns = width // 128

    def copy_kept(part):
        size = turns * KINDS * LANES
        at = pl.ds(pl.multiple_of(part * size, LANES), size)
        return pltpu.make_async_copy(kept_here.at[at, :], kept.at[at, :], sems_kept.at[part])

    def copy_turned(gate):
        return pltpu.make_async_copy(square.at[gate], turned.at[gate], sems_turned.at[gate])

    def part(gate, carry):
        def turning(count, carry):
            columns = pl.ds(pl.multiple_of(gate * width + count * 128, 128), 128)
            into = pl.ds(pl.multiple_of(count * 128, 128), 128)
            square[gate, into, :] = w_rec[:, columns].T
            return step(gate * turns + count, carry)

        carry = lax.fori_loop(0, turns, turning, carry, unroll=UNROLL_FORWARD)
        copy_kept(gate).start()
        copy_turned(gate).start()
        return carry

    carry = lax.fori_loop(0, 4, part, (h_first[...], c_first[...]))
    lax.fori_loop(4 * turns, LONGEST, step, carry, unroll=UNROLL_FORWARD)
    begin = 4 * turns * KINDS * LANES
    rest = pl.ds(begin, kept_here.shape[0] - begin)
    last = pltpu.make_async_copy(kept_here.at[rest, :], kept.at[rest, :], sems_kept.at[4])
    last.start()
    hidden_turned[...] = lax.dot_general(
        hiddens[...].astype(bf16),
        collect[...],
        (((0,), (1,)), ((), ())),
        preferred_element_type=f32,
    ).astype(bf16)
    output_rows[...] = dot(collect[...], outs[...].astype(bf16)).astype(bf16)
    for gate in range(4):
        copy_kept(gate).wait()
        copy_turned(gate).wait()
    last.wait()


def backward_kernel(
    turned,
    kept,
    coming,
    spread,
    collect,
    out_scale,
    carry_in,
    gate_rows,
    carry_out,
    w_turned,
    kept_here,
    come,
    dgates,
    sems_turned,
    sems_kept,
    *,
    first_step,
):
    width = coming.shape[1]
    steps = spread.shape[0] // LANES
    size = KINDS * LANES

    def copy_kept(part):
        begin, count = ((steps - SOON) * size, SOON * size) if part == 0 else (
            0,
            (steps - SOON) * size,
        )
        return pltpu.make_async_copy(
            kept.at[pl.ds(first_step * size + begin, count), :],
            kept_here.at[pl.ds(begin, count), :],
            sems_kept.at[part],
        )

    copies = [
        pltpu.make_async_copy(
            turned.at[gate], w_turned.at[pl.ds(gate * width, width), :], sems_turned.at[gate]
        )
        for gate in range(4)
    ]
    copy_kept(0).start()
    for copy in copies:
        copy.start()
    copy_kept(1).start()
    come[...] = dot(spread[...], coming[...])
    scale = out_scale[...]

    def gradients(index, carry):
        dh_next, dc_next = carry
        at = step_rows(index)
        grad_h = come[at, :] * scale + dh_next
        grad_c = dc_next + grad_h * kept_here[kept_rows(index, 0), :]
        grads = jnp.concatenate(
            [
                grad_c * kept_here[kept_rows(index, 1), :],
                grad_c * kept_here[kept_rows(index, 2), :],
                grad_c * kept_here[kept_rows(index, 3), :],
                grad_h * kept_here[kept_rows(index, 4), :],
            ],
            axis=1,
        )
        dgates[at, :] = grads
        return (grads, grad_c * kept_here[kept_rows(index, 5), :])

    def step(index, carry):
        grads, dc_next = gradients(index, carry)
        return (dot(grads.astype(bf16), w_turned[...]), dc_next)

    def run(last, count, carry):
        return lax.fori_loop(
            0, count, lambda back, c: step(last - back, c), carry, unroll=UNROLL_BACKWARD
        )

    copy_kept(0).wait()
    for copy in copies:
        copy.wait()
    carry = (carry_in[pl.ds(0, LANES), :], carry_in[pl.ds(LANES, LANES), :])
    carry = run(steps - 1, SOON, carry)
    copy_kept(1).wait()
    if first_step > 0:
        carry = run(steps - SOON - 1, steps - SOON, carry)
        carry_out[pl.ds(0, LANES), :] = carry[0]
        carry_out[pl.ds(LANES, LANES), :] = carry[1]
    else:
        carry = run(steps - SOON - 1, steps - SOON - 1, carry)
        gradients(0, carry)
        carry_out[...] = jnp.zeros(carry_out.shape, f32)
    for gate in range(4):
        columns = pl.ds(gate * width, width)
        gate_rows[gate] = dot(collect[...], dgates[:, columns].astype(bf16)).astype(bf16)


def gradient_kernel(
    core,
    mixed_all,
    hidden_all,
    mine,
    other,
    *refs,
    begin,
):
    so_far, (result, left, right, sems_left, sems_right) = refs[:-5], refs[-5:]
    half, rows, columns = mine.shape
    line = 2 * half
    width, size = left.shape[0], left.shape[1] // line
    which = core[0]

    def copies_left(source):
        found = []
        for place in range(line):
            chip, twin = place % half, place // half
            block = 2 * chip + (which if twin == 0 else 1 - which)
            found.append(
                pltpu.make_async_copy(
                    source.at[pl.ds(block * width, width), pl.ds(begin, size)],
                    left.at[:, pl.ds(place * size, size)],
                    sems_left.at[place],
                )
            )
        return found

    @pl.when(which == 0)
    def _():
        for copy in copies_left(mixed_all):
            copy.start()

    @pl.when(which != 0)
    def _():
        for copy in copies_left(hidden_all):
            copy.start()

    copies_right = [
        pltpu.make_async_copy(
            (mine if place < half else other).at[place % half],
            right.at[pl.ds(place * size, rows), :],
            sems_right.at[place],
        )
        for place in range(line)
    ]
    for copy in copies_right:
        copy.start()
    if rows < size:
        for place in range(line):
            right[pl.ds(place * size + rows, size - rows), :] = jnp.zeros(
                (size - rows, columns), bf16
            )
    for copy in copies_left(mixed_all) + copies_right:
        copy.wait()
    grad = dot(left[...], right[...])
    if not so_far:
        result[...] = grad
        return
    grad = grad + so_far[0][...]
    lines = result.shape[0]
    main = lines * line * TILE
    packed = jnp.concatenate(
        [
            grad[:main].reshape(lines, line * TILE, columns),
            grad[main:].reshape(lines, line, columns),
        ],
        axis=1,
    )
    result[...] = packed.astype(bf16)


def reduce_kernel(got, scale, homeward, packed):
    line = homeward.shape[0]
    lines = got.shape[0]
    tiles = got.shape[2] // 128
    total = jnp.zeros((1, 128), f32)
    packed[:, pl.ds(OWN * TILE, TILE * 2), :] = jnp.zeros((line, TILE * 2, 128), f32)
    for tile in range(tiles):
        columns = pl.ds(tile * 128, 128)
        found = got[0, :, columns].astype(f32)
        for index in range(1, lines):
            found = found + got[index, :, columns].astype(f32)
        found = found * scale[:, columns].astype(f32)
        total = total + jnp.sum(found * found, axis=0, keepdims=True)
        packed[:, pl.ds(tile * TILE, TILE), :] = found[: line * TILE].reshape(line, TILE, 128)
        packed[:, OWN * TILE + tile, :] = found[line * TILE :]
    rest = jnp.broadcast_to(jnp.sum(total, axis=1, keepdims=True), (line, 128))
    for index in range(3):
        part = rest.astype(bf16).astype(f32)
        packed[:, SQUARES + index, :] = part
        rest = rest - part
    homeward[...] = packed[...].astype(bf16)


def settle_kernel(got, to_natural, home, squares, placed, wide):
    line = got.shape[0]
    tiles = placed.shape[0]
    half = line // 2
    wide[...] = got[...].astype(f32)
    total = jnp.zeros((1, 128), f32)
    for source in range(line):
        gate = (source % 2) * half + source // 2
        for tile in range(tiles):
            placed[tile, pl.ds(gate, TILE, stride=8), :] = wide[
                source, pl.ds(tile * TILE, TILE), :
            ]
            placed[tile, pl.ds(TILE * 8 + gate, 1), :] = wide[
                source, pl.ds(OWN * TILE + tile, 1), :
            ]
        for index in range(3):
            total = total + wide[source, pl.ds(SQUARES + index, 1), :]
    squares[...] = jnp.broadcast_to(total, squares.shape)
    values = jnp.concatenate([placed[tile] for tile in range(tiles)], axis=1)
    home[...] = dot(values.astype(bf16), to_natural[...]).astype(bf16)


def own_kernel(
    wall,
    ninth_in,
    late,
    early,
    in_rows,
    output_rows,
    unpack,
    to_natural,
    d_out,
    out,
    square,
    sems,
):
    width = in_rows.shape[1]
    rows = in_rows.shape[0]
    main = wall.shape[0]
    rest = width - main
    copies = []
    for gate in range(4):
        copies.append(
            pltpu.make_async_copy(
                wall.at[:, pl.ds(gate * width, width)],
                square.at[gate, pl.ds(0, main), :],
                sems.at[2 * gate],
            )
        )
        copies.append(
            pltpu.make_async_copy(
                ninth_in.at[gate], square.at[gate, pl.ds(main, rest), :], sems.at[2 * gate + 1]
            )
        )
    for copy in copies:
        copy.start()

    def natural(values):
        values = dot(unpack[...], values).astype(bf16)
        return dot(values, to_natural[...]).astype(bf16)

    out[...] = natural(output_rows[pl.ds(0, unpack.shape[1]), :])

    def right_product(left, matrix):
        return lax.dot_general(
            left, matrix, (((1,), (1,)), ((), ())), preferred_element_type=f32
        )

    found = jnp.zeros((rows, width), f32)
    for gate in range(4):
        copies[2 * gate].wait()
        copies[2 * gate + 1].wait()
        both = jnp.concatenate([late[gate], early[gate]], axis=0)
        found = found + right_product(both, square[gate])
    found = found * (in_rows[...].astype(f32) * KEEP_INPUT)
    d_out[...] = natural(found.astype(bf16))


def in_vmem():
    return pl.BlockSpec(memory_space=pltpu.VMEM)


def in_place():
    return pl.BlockSpec(memory_space=pl.ANY)


def run_forward(wall, mixed, spread, collect, h_first, c_first, out_scale):
    steps_rows = spread.shape[0]
    rows, width = mixed.shape
    devices = wall.shape[0] // TILE
    all_kept = LONGEST * KINDS * LANES
    return pl.pallas_call(
        forward_kernel,
        out_shape=(
            jax.ShapeDtypeStruct((width, collect.shape[0]), bf16),
            jax.ShapeDtypeStruct((collect.shape[0], width), bf16),
            jax.ShapeDtypeStruct((4, devices, width), bf16),
            jax.ShapeDtypeStruct((all_kept, width), f32),
            jax.ShapeDtypeStruct((4, width, width), bf16),
        ),
        in_specs=[in_place()] + [in_vmem()] * 6,
        out_specs=(in_vmem(),) * 3 + (in_place(),) * 2,
        scratch_shapes=[
            pltpu.VMEM((4, width, width), bf16),
            pltpu.VMEM((width, 4 * width), bf16),
            pltpu.VMEM((devices * TILE, width), bf16),
            pltpu.VMEM((width // 128, devices * TILE, 128), f32),
            pltpu.VMEM((steps_rows, 4 * width), f32),
            pltpu.VMEM((all_kept, width), f32),
            pltpu.VMEM((steps_rows, width), f32),
            pltpu.VMEM((steps_rows, width), f32),
            pltpu.SemaphoreType.DMA((4,)),
            pltpu.SemaphoreType.DMA,
            pltpu.SemaphoreType.DMA,
            pltpu.SemaphoreType.DMA((5,)),
            pltpu.SemaphoreType.DMA((4,)),
        ],
        compiler_params=pltpu.CompilerParams(vmem_limit_bytes=VMEM_LIMIT),
        cost_estimate=pl.CostEstimate(
            flops=60_000_000_000, bytes_accessed=30_000_000, transcendentals=2_000_000
        ),
        name="forward",
    )(wall, mixed, spread, collect, h_first, c_first, out_scale)


def run_backward(turned, kept, coming, spread, collect, out_scale, carry, first_step):
    steps_rows = spread.shape[0]
    rows, width = collect.shape[0], coming.shape[1]
    return pl.pallas_call(
        functools.partial(backward_kernel, first_step=first_step),
        out_shape=(
            jax.ShapeDtypeStruct((4, rows, width), bf16),
            jax.ShapeDtypeStruct((2 * LANES, width), f32),
        ),
        in_specs=[in_place()] * 2 + [in_vmem()] * 5,
        out_specs=(in_vmem(),) * 2,
        scratch_shapes=[
            pltpu.VMEM((4 * width, width), bf16),
            pltpu.VMEM((steps_rows * KINDS, width), f32),
            pltpu.VMEM((steps_rows, width), f32),
            pltpu.VMEM((steps_rows, 4 * width), f32),
            pltpu.SemaphoreType.DMA((4,)),
            pltpu.SemaphoreType.DMA((2,)),
        ],
        compiler_params=pltpu.CompilerParams(vmem_limit_bytes=VMEM_LIMIT),
        cost_estimate=pl.CostEstimate(
            flops=steps_rows // LANES * 1_500_000_000, bytes_accessed=20_000_000, transcendentals=0
        ),
        name="backward_late" if first_step else "backward_early",
    )(turned, kept, coming, spread, collect, out_scale, carry)


def run_gradient(core, mixed_all, hidden_all, mine, other, begin, lines, so_far=()):
    half, rows, columns = mine.shape
    line = 2 * half
    width = mixed_all.shape[0] // line
    size = -(-rows // 128) * 128
    if so_far:
        result = jax.ShapeDtypeStruct((lines, line * OWN, columns), bf16)
    else:
        result = jax.ShapeDtypeStruct((width, columns), f32)
    return pl.pallas_call(
        functools.partial(gradient_kernel, begin=begin),
        out_shape=result,
        in_specs=[pl.BlockSpec(memory_space=pltpu.SMEM)]
        + [in_place()] * 4
        + [in_vmem()] * len(so_far),
        out_specs=in_vmem(),
        scratch_shapes=[
            pltpu.VMEM((width, line * size), bf16),
            pltpu.VMEM((line * size, columns), bf16),
            pltpu.SemaphoreType.DMA((line,)),
            pltpu.SemaphoreType.DMA((line,)),
        ],
        compiler_params=pltpu.CompilerParams(vmem_limit_bytes=VMEM_LIMIT),
        cost_estimate=pl.CostEstimate(
            flops=5_000_000_000, bytes_accessed=12_000_000, transcendentals=0
        ),
        name="gradient_early" if so_far else "gradient_late",
    )(core, mixed_all, hidden_all, mine, other, *so_far)


def run_reduce(got, scale, line):
    return pl.pallas_call(
        reduce_kernel,
        out_shape=jax.ShapeDtypeStruct((line, MESSAGE, 128), bf16),
        in_specs=[in_vmem()] * 2,
        out_specs=in_vmem(),
        scratch_shapes=[pltpu.VMEM((line, MESSAGE, 128), f32)],
        compiler_params=pltpu.CompilerParams(vmem_limit_bytes=VMEM_LIMIT),
        name="reduce",
    )(got, scale)


def run_settle(got, to_natural, lines):
    wide, width = to_natural.shape
    return pl.pallas_call(
        settle_kernel,
        out_shape=(
            jax.ShapeDtypeStruct((OWN * 8, width), bf16),
            jax.ShapeDtypeStruct((lines, 128), f32),
        ),
        in_specs=[in_vmem()] * 2,
        out_specs=(in_vmem(),) * 2,
        scratch_shapes=[
            pltpu.VMEM((wide // 128, OWN * 8, 128), f32),
            pltpu.VMEM(got.shape, f32),
        ],
        compiler_params=pltpu.CompilerParams(vmem_limit_bytes=VMEM_LIMIT),
        name="settle",
    )(got, to_natural)


def run_own(wall, ninth_in, late, early, in_rows, output_rows, unpack, to_natural):
    width, natural = to_natural.shape
    rows = unpack.shape[0]
    return pl.pallas_call(
        own_kernel,
        out_shape=(jax.ShapeDtypeStruct((rows, natural), bf16),) * 2,
        in_specs=[in_place()] * 2 + [in_vmem()] * 6,
        out_specs=(in_vmem(),) * 2,
        scratch_shapes=[
            pltpu.VMEM((4, width, width), bf16),
            pltpu.SemaphoreType.DMA((8,)),
        ],
        compiler_params=pltpu.CompilerParams(vmem_limit_bytes=VMEM_LIMIT),
        cost_estimate=pl.CostEstimate(
            flops=8_000_000_000, bytes_accessed=15_000_000, transcendentals=0
        ),
        name="own",
    )(wall, ninth_in, late, early, in_rows, output_rows, unpack, to_natural)


def split_exact(values):
    parts = []
    rest = values
    for _ in range(3):
        part = lax.reduce_precision(rest, 8, 7)
        parts.append(part.astype(bf16))
        rest = rest - part
    return parts


def body(
    inputs,
    d_out,
    h_start,
    c_start,
    pieces,
    in_mask,
    out_mask,
    w_mask,
    master,
    moment_one,
    moment_two,
):
    streams, steps, width = inputs.shape
    gates_n = 4 * width
    count_w = 2 * width * gates_n
    total = count_w + gates_n
    shard = master.shape[0]
    devices = lax.axis_size("batch")
    me = lax.axis_index("batch")
    wide = OWN * devices
    block = OWN * 2 * gates_n
    gap = block - shard
    most = gap * devices
    tokens = streams * steps
    rows_n = LATE + EARLY
    slot = -(-rows_n // 128) * 128
    line = 8
    lines = devices // line

    line_groups = [[line * q + m for m in range(line)] for q in range(lines)]
    across_groups = [[line * q + m for q in range(lines)] for m in range(line)]
    column_groups = [
        [line * q + 2 * y + c for y in range(line // 2)] for q in range(lines) for c in range(2)
    ]
    twins = [(i, i ^ 1) for i in range(devices)]

    to_kept = one_hot(width, wide, lambda k, p: place_of(k, devices) == p)
    to_natural = one_hot(wide, width, lambda p, k: place_of(k, devices) == p)

    places = me * shard + lax.iota(jnp.int32, shard)
    recurrent = (places < count_w) & (places % (2 * gates_n) >= gates_n)
    rec_scale = jnp.where(recurrent, w_mask.astype(f32) * KEEP_RECURRENT, 1.0)
    local_low = master.astype(bf16) * rec_scale.astype(bf16)
    local_low = jnp.where(places < total, local_low, jnp.zeros((), bf16))

    def realigned(flat, following):
        joined = jnp.concatenate([flat, following])
        rows = lax.dynamic_slice(joined, (gap * me,), (block,)).reshape(OWN * 8, width)
        return dot(rows, to_kept).astype(bf16)

    before = [(i + 1, i) for i in range(devices - 1)]
    order = one_hot(
        OWN * 8,
        OWN * 8,
        lambda a, b: jnp.where(a < 64, (a % 8) * 8 + a // 8, 64 + a % 8) == b,
    )
    own = realigned(local_low, lax.ppermute(local_low[:most], "batch", before))
    own = dot(order, own).astype(bf16)
    own = jnp.concatenate([own[TILE * j : TILE * (j + 1)] for j in range(OWN)], axis=1)
    wall = lax.all_gather(own, "batch", axis=0, tiled=True)
    room = 16
    scale_low = rec_scale.astype(bf16)
    scales = realigned(scale_low, lax.ppermute(scale_low[:most], "batch", before))
    send = one_hot(
        line * room,
        OWN * 8,
        lambda a, b: (a % room < OWN) & (a % room * 8 + a // room % 2 * 4 + a // room // 2 == b),
    )
    scales = lax.all_to_all(
        dot(send, scales).astype(bf16), "batch", 0, 0, tiled=True, axis_index_groups=line_groups
    )
    into = one_hot(
        line * OWN,
        line * room,
        lambda a, b: jnp.where(
            a < line * TILE, a // TILE * room + a % TILE, a % TILE * room + TILE
        )
        == b,
    )
    scales = dot(into, scales).astype(bf16)

    in_scale = in_mask.astype(f32) * KEEP_INPUT
    mixed = (inputs.astype(f32) * in_scale[:, None, :]).astype(bf16).reshape(tokens, width)
    spare = ((0, rows_n - tokens), (0, 0))
    mixed = dot(jnp.pad(mixed, spare), to_kept).astype(bf16)
    bias_place = place_of(jnp.int32(width), devices)
    column = lax.broadcasted_iota(jnp.int32, mixed.shape, 1)
    mixed = jnp.where(column == bias_place, jnp.ones((), bf16), mixed)
    coming = dot(jnp.pad(d_out.reshape(tokens, width), spare), to_kept).astype(bf16)
    small = jnp.concatenate(
        [h_start.astype(bf16)]
        + split_exact(c_start)
        + [in_mask.astype(bf16), out_mask.astype(bf16)],
        axis=0,
    )
    small = dot(small, to_kept)
    part = [small[streams * j : streams * (j + 1)] for j in range(6)]
    empty = jnp.zeros((LANES - streams, wide), f32)
    h_first = jnp.concatenate([part[0], empty], axis=0)
    c_first = jnp.concatenate([part[1] + part[2] + part[3], empty], axis=0)
    out_scale_kept = part[5] * KEEP_OUTPUT
    out_scale = jnp.concatenate(
        [out_scale_kept, out_scale_kept, jnp.zeros((LANES - 2 * streams, wide), f32)], axis=0
    )
    base = jnp.arange(streams, dtype=jnp.int32) * steps
    none = jnp.zeros((LANES - 2 * streams,), jnp.int32)
    begins = jnp.concatenate([base, base + pieces[:, 0], none])
    lengths = jnp.concatenate([pieces[:, 0], pieces[:, 1], none])
    ticks = lax.broadcasted_iota(jnp.int32, (LONGEST, LANES), 0)
    active = ticks < lengths[None, :]
    where = jnp.where(active, begins[None, :] + ticks, -1).reshape(-1)
    spread = (where[:, None] == lax.iota(jnp.int32, rows_n)[None, :]).astype(bf16)
    late_first = jnp.maximum(pieces[:, 0] - SPLIT, 0)
    late_base = jnp.arange(streams, dtype=jnp.int32) * LATE_BLOCK
    late_base = jnp.concatenate([late_base, late_base + late_first, none])
    early_base = LATE + SPLIT * jnp.arange(LANES, dtype=jnp.int32)
    packed = jnp.where(ticks < SPLIT, early_base[None] + ticks, late_base[None] + ticks - SPLIT)
    packed = jnp.where(active, packed, -1).reshape(-1)
    collect = (lax.iota(jnp.int32, slot)[:, None] == packed[None, :]).astype(bf16)
    pack = dot(collect, spread).astype(bf16)
    unpack = (
        lax.dot_general(spread, collect[:rows_n], (((0,), (1,)), ((), ())), preferred_element_type=f32)
    ).astype(bf16)
    mixed_turned = lax.dot_general(
        mixed, pack, (((0,), (1,)), ((), ())), preferred_element_type=f32
    ).astype(bf16)
    row_stream = lax.iota(jnp.int32, rows_n) // steps
    row_stream = (row_stream[:, None] == lax.iota(jnp.int32, streams)[None]).astype(bf16)
    in_rows = dot(pack[:rows_n], dot(row_stream, part[4].astype(bf16)).astype(bf16)).astype(bf16)

    ready = (wall, mixed, mixed_turned, coming, spread, collect, h_first, c_first, out_scale)
    ready = lax.optimization_barrier(ready + (in_rows, unpack, to_natural, scales))
    wall, mixed, mixed_turned, coming, spread, collect, h_first, c_first, out_scale = ready[:9]
    in_rows, unpack, to_natural, scales = ready[9:]
    mixed_all = lax.all_gather(
        mixed_turned, "batch", axis=0, tiled=True, axis_index_groups=line_groups
    )
    hidden_turned, output_rows, ninth_in, kept, turned = run_forward(
        wall, mixed, spread, collect, h_first, c_first, out_scale
    )
    hidden_turned, mixed_all = lax.optimization_barrier((hidden_turned, mixed_all))
    hidden_all = lax.all_gather(
        hidden_turned, "batch", axis=0, tiled=True, axis_index_groups=line_groups
    )
    begin = SPLIT * LANES
    carry = jnp.zeros((2 * LANES, wide), f32)
    late, carry = run_backward(
        turned, kept, coming, spread[begin:], collect[:LATE, begin:], out_scale, carry, SPLIT
    )

    def exchange(rows):
        return lax.all_to_all(
            rows, "batch", 0, 0, tiled=True, axis_index_groups=column_groups
        )

    late_mine = exchange(late)
    early, _ = run_backward(
        turned, kept, coming, spread[:begin], collect[LATE:rows_n, :begin], out_scale, carry, 0
    )
    late_mine, early = lax.optimization_barrier((late_mine, early))
    early_mine = exchange(early)
    core = (me % 2).reshape(1)
    so_far = run_gradient(
        core, mixed_all, hidden_all, late_mine, lax.ppermute(late_mine, "batch", twins), 0, lines
    )
    early_mine, so_far = lax.optimization_barrier((early_mine, so_far))
    message = run_gradient(
        core,
        mixed_all,
        hidden_all,
        early_mine,
        lax.ppermute(early_mine, "batch", twins),
        LATE,
        lines,
        (so_far,),
    )
    got = lax.all_to_all(
        message, "batch", 0, 0, tiled=True, axis_index_groups=across_groups
    )

    d_rows, out_rows = run_own(
        wall, ninth_in, late, early, in_rows, output_rows, unpack, to_natural
    )
    output = out_rows[:tokens].reshape(streams, steps, width)
    d_inputs = d_rows[:tokens].reshape(streams, steps, width)
    got, output, d_inputs = lax.optimization_barrier((got, output, d_inputs))

    homeward = lax.all_to_all(
        run_reduce(got, scales, line), "batch", 0, 0, tiled=True, axis_index_groups=line_groups
    )
    home, squares = run_settle(homeward, to_natural, lines)
    squares = lax.all_to_all(
        squares, "batch", 0, 0, tiled=True, axis_index_groups=across_groups
    )
    home = home.reshape(block)
    tail = lax.ppermute(home[block - most :], "batch", [(i, i + 1) for i in range(devices - 1)])
    grad_shard = lax.dynamic_slice(
        jnp.concatenate([tail, home]), (most - gap * me,), (shard,)
    ).astype(f32)
    grad_norm = jnp.sqrt(jnp.sum(squares[:, 0]))

    factor = jnp.minimum(1.0, CLIP_NORM / (grad_norm + 1e-06))
    clipped = grad_shard * factor
    moment_new = BETA_ONE * moment_one + (1.0 - BETA_ONE) * clipped
    second_new = BETA_TWO * moment_two + (1.0 - BETA_TWO) * clipped * clipped
    first_hat = moment_new / (1.0 - BETA_ONE**STEP)
    second_hat = second_new / (1.0 - BETA_TWO**STEP)
    master_new = master - LEARN_RATE * (
        first_hat / (jnp.sqrt(second_hat) + EPSILON) + WEIGHT_DECAY * master
    )
    return (output, d_inputs, moment_new, second_new, master_new, grad_norm)


def solution(mesh):
    placed = (
        P("batch", None, None),
        P("batch", None, None),
        P("batch", None),
        P("batch", None),
        P("batch", None),
        P("batch", None),
        P("batch", None),
        P("batch"),
        P("batch"),
        P("batch"),
        P("batch"),
    )
    return jax.shard_map(
        body,
        mesh=mesh,
        in_specs=placed,
        out_specs=(
            P("batch", None, None),
            P("batch", None, None),
            P("batch"),
            P("batch"),
            P("batch"),
            P(),
        ),
        check_vma=False,
    )
```

```python
import functools

import jax
import jax.numpy as jnp
from jax import lax
from jax.experimental import pallas as pl
from jax.experimental.pallas import tpu as pltpu
from jax.sharding import PartitionSpec as P

STEP = 10


LEARN_RATE = 0.03
BETA_ONE = 0.9
BETA_TWO = 0.999
WEIGHT_DECAY = 0.01
EPSILON = 1e-08
CLIP_NORM = 1.0
KEEP_INPUT = 4.0 / 3.0
KEEP_OUTPUT = 4.0 / 3.0
KEEP_RECURRENT = 2.0

LONGEST = 40
LANES = 8
TILE = 8
OWN = TILE + 1
KINDS = 6
SOON = 4
SPLIT = 14
LATE = 128
LATE_BLOCK = LATE // 3
EARLY = 96
UNROLL_FORWARD = 3
UNROLL_BACKWARD = 4
MESSAGE = 88
VMEM_LIMIT = 60 * 2**20
VMEM_MEDIUM = 40 * 2**20
VMEM_SMALL = 16 * 2**20

f32 = jnp.float32
bf16 = jnp.bfloat16


def dot(left, right):
    return lax.dot_general(left, right, (((1,), (0,)), ((), ())), preferred_element_type=f32)


def one_hot(rows, columns, wanted):
    row = lax.broadcasted_iota(jnp.int32, (rows, columns), 0)
    column = lax.broadcasted_iota(jnp.int32, (rows, columns), 1)
    return wanted(row, column).astype(bf16)


def place_of(natural, devices):
    owner, rest = natural // OWN, natural % OWN
    return jnp.where(rest < TILE, owner * TILE + rest, devices * TILE + owner)


def step_rows(step):
    return pl.ds(pl.multiple_of(step * LANES, LANES), LANES)


def kept_rows(step, kind):
    return pl.ds(pl.multiple_of((step * KINDS + kind) * LANES, LANES), LANES)


def forward_kernel(
    wall,
    mixed,
    spread,
    collect,
    h_first,
    c_first,
    out_scale,
    hidden_turned,
    output_rows,
    ninth_in,
    kept,
    turned,
    square,
    w_rec,
    ninth,
    apart,
    pre,
    kept_here,
    hiddens,
    outs,
    sems_in,
    sem_ninth,
    sem_rec,
    sems_kept,
    sems_turned,
):
    width = mixed.shape[1]
    main = wall.shape[0]
    devices = main // TILE
    gates_n = 4 * width

    copy_ninth = pltpu.make_async_copy(wall.at[:, pl.ds(2 * gates_n, width)], ninth, sem_ninth)
    copies_in = [
        pltpu.make_async_copy(
            wall.at[:, pl.ds(gate * width, width)],
            square.at[gate, pl.ds(0, main), :],
            sems_in.at[gate],
        )
        for gate in range(4)
    ]
    copy_rec = pltpu.make_async_copy(
        wall.at[:, pl.ds(gates_n, gates_n)], w_rec.at[pl.ds(0, main), :], sem_rec
    )
    copy_ninth.start()
    for copy in copies_in:
        copy.start()
    rows = dot(spread[...], mixed[...]).astype(bf16)
    copy_ninth.wait()
    for tile in range(width // 128):
        columns = pl.ds(tile * 128, 128)
        apart[tile] = ninth[:, columns].astype(f32)
        for gate in range(8):
            rest = apart[tile, pl.ds(gate, devices, stride=8), :].astype(bf16)
            if gate < 4:
                square[gate, pl.ds(main, devices), columns] = rest
                ninth_in[gate, :, columns] = rest
            else:
                there = pl.ds((gate - 4) * width + tile * 128, 128)
                w_rec[pl.ds(main, devices), there] = rest
    copy_rec.start()
    for gate in range(4):
        copies_in[gate].wait()
        pre[:, pl.ds(gate * width, width)] = dot(rows, square[gate])
    copy_rec.wait()
    scale = out_scale[...]

    def step(index, carry):
        hidden, cell = carry
        at = step_rows(index)
        gates = pre[at, :] + dot(hidden.astype(bf16), w_rec[...])
        in_gate = jax.nn.sigmoid(gates[:, :width])
        forget = jax.nn.sigmoid(gates[:, width : 2 * width])
        candid = jnp.tanh(gates[:, 2 * width : 3 * width])
        out_gate = jax.nn.sigmoid(gates[:, 3 * width :])
        cell_new = forget * cell + in_gate * candid
        squash = jnp.tanh(cell_new)
        hidden_new = out_gate * squash
        hiddens[at, :] = hidden
        outs[at, :] = hidden_new * scale
        kept_here[kept_rows(index, 0), :] = out_gate * (1.0 - squash * squash)
        kept_here[kept_rows(index, 1), :] = candid * in_gate * (1.0 - in_gate)
        kept_here[kept_rows(index, 2), :] = cell * forget * (1.0 - forget)
        kept_here[kept_rows(index, 3), :] = in_gate * (1.0 - candid * candid)
        kept_here[kept_rows(index, 4), :] = squash * out_gate * (1.0 - out_gate)
        kept_here[kept_rows(index, 5), :] = forget
        return (hidden_new, cell_new)

    turns = width // 128

    def copy_kept(part):
        size = turns * KINDS * LANES
        at = pl.ds(pl.multiple_of(part * size, LANES), size)
        return pltpu.make_async_copy(kept_here.at[at, :], kept.at[at, :], sems_kept.at[part])

    def copy_turned(gate):
        return pltpu.make_async_copy(square.at[gate], turned.at[gate], sems_turned.at[gate])

    def part(gate, carry):
        def turning(count, carry):
            columns = pl.ds(pl.multiple_of(gate * width + count * 128, 128), 128)
            into = pl.ds(pl.multiple_of(count * 128, 128), 128)
            square[gate, into, :] = w_rec[:, columns].T
            return step(gate * turns + count, carry)

        carry = lax.fori_loop(0, turns, turning, carry, unroll=UNROLL_FORWARD)
        copy_kept(gate).start()
        copy_turned(gate).start()
        return carry

    carry = lax.fori_loop(0, 4, part, (h_first[...], c_first[...]))
    lax.fori_loop(4 * turns, LONGEST, step, carry, unroll=UNROLL_FORWARD)
    begin = 4 * turns * KINDS * LANES
    rest = pl.ds(begin, kept_here.shape[0] - begin)
    last = pltpu.make_async_copy(kept_here.at[rest, :], kept.at[rest, :], sems_kept.at[4])
    last.start()
    hidden_turned[...] = lax.dot_general(
        hiddens[...].astype(bf16),
        collect[...],
        (((0,), (1,)), ((), ())),
        preferred_element_type=f32,
    ).astype(bf16)
    output_rows[...] = dot(collect[...], outs[...].astype(bf16)).astype(bf16)
    for gate in range(4):
        copy_kept(gate).wait()
        copy_turned(gate).wait()
    last.wait()


def backward_kernel(
    turned,
    kept,
    coming,
    spread,
    collect,
    out_scale,
    carry_in,
    gate_rows,
    *refs,
    first_step,
):
    carry_out = refs[0]
    w_turned, kept_here, come, dgates, sems_turned, sems_kept = refs[-6:]
    width = coming.shape[1]
    steps = spread.shape[0] // LANES
    size = KINDS * LANES

    def copy_kept(part):
        begin, count = ((steps - SOON) * size, SOON * size) if part == 0 else (
            0,
            (steps - SOON) * size,
        )
        return pltpu.make_async_copy(
            kept.at[pl.ds(first_step * size + begin, count), :],
            kept_here.at[pl.ds(begin, count), :],
            sems_kept.at[part],
        )

    copies = [
        pltpu.make_async_copy(
            turned.at[gate], w_turned.at[pl.ds(gate * width, width), :], sems_turned.at[gate]
        )
        for gate in range(4)
    ]
    copy_kept(0).start()
    for copy in copies:
        copy.start()
    come[...] = dot(spread[...], coming[...])
    scale = out_scale[...]

    def gradients(index, carry):
        dh_next, dc_next = carry
        at = step_rows(index)
        grad_h = come[at, :] * scale + dh_next
        grad_c = dc_next + grad_h * kept_here[kept_rows(index, 0), :]
        grads = jnp.concatenate(
            [
                grad_c * kept_here[kept_rows(index, 1), :],
                grad_c * kept_here[kept_rows(index, 2), :],
                grad_c * kept_here[kept_rows(index, 3), :],
                grad_h * kept_here[kept_rows(index, 4), :],
            ],
            axis=1,
        )
        dgates[at, :] = grads
        return (grads, grad_c * kept_here[kept_rows(index, 5), :])

    def step(index, carry):
        grads, dc_next = gradients(index, carry)
        return (dot(grads.astype(bf16), w_turned[...]), dc_next)

    def run(last, count, carry):
        return lax.fori_loop(
            0, count, lambda back, c: step(last - back, c), carry, unroll=UNROLL_BACKWARD
        )

    copy_kept(0).wait()
    for copy in copies:
        copy.wait()
    copy_kept(1).start()
    if first_step > 0:
        carry = (jnp.zeros((LANES, width), f32),) * 2
    else:
        carry = (carry_in[pl.ds(0, LANES), :], carry_in[pl.ds(LANES, LANES), :])
    carry = run(steps - 1, SOON, carry)
    copy_kept(1).wait()
    if first_step > 0:
        carry = run(steps - SOON - 1, steps - SOON, carry)
        carry_out[pl.ds(0, LANES), :] = carry[0]
        carry_out[pl.ds(LANES, LANES), :] = carry[1]
    else:
        carry = run(steps - SOON - 1, steps - SOON - 1, carry)
        gradients(0, carry)
    for gate in range(4):
        columns = pl.ds(gate * width, width)
        gate_rows[gate] = dot(collect[...], dgates[:, columns].astype(bf16)).astype(bf16)


def gradient_kernel(
    core,
    mixed_all,
    hidden_all,
    mine,
    other,
    *refs,
    begin,
):
    result, left, right, ninth, sems_left, sems_right = refs[-6:]
    so_far = refs[:-6]
    half, rows, columns = mine.shape
    line = 2 * half
    width, size = left.shape[0], left.shape[1] // line
    which = core[0]

    def copies_left(source):
        found = []
        for place in range(line):
            chip, twin = place % half, place // half
            block = 2 * chip + (which if twin == 0 else 1 - which)
            found.append(
                pltpu.make_async_copy(
                    source.at[pl.ds(block * width, width), pl.ds(begin, size)],
                    left.at[:, pl.ds(place * size, size)],
                    sems_left.at[place],
                )
            )
        return found

    @pl.when(which == 0)
    def _():
        for copy in copies_left(mixed_all):
            copy.start()

    @pl.when(which != 0)
    def _():
        for copy in copies_left(hidden_all):
            copy.start()

    copies_right = [
        pltpu.make_async_copy(
            (mine if place < half else other).at[place % half],
            right.at[pl.ds(place * size, rows), :],
            sems_right.at[place],
        )
        for place in range(line)
    ]
    for copy in copies_right:
        copy.start()
    if rows < size:
        for place in range(line):
            right[pl.ds(place * size + rows, size - rows), :] = jnp.zeros(
                (size - rows, columns), bf16
            )
    for copy in copies_left(mixed_all) + copies_right:
        copy.wait()
    grad = dot(left[...], right[...])
    if not so_far:
        result[...] = grad
        return
    grad = grad + so_far[0][...]
    devices = result.shape[0]
    main = devices * TILE
    tiles = columns // 128

    def tile_of(tile):
        here = grad[:main, tile * 128 : (tile + 1) * 128]
        return here.reshape(devices, TILE, 128)

    ninth[...] = jnp.zeros(ninth.shape, f32)
    for tile in range(tiles):
        ninth[:, tile, :] = grad[main:, tile * 128 : (tile + 1) * 128]
    for tile in range(0, tiles - 1, 2):
        pair = jnp.concatenate([tile_of(tile), tile_of(tile + 1)], axis=1)
        result[:, pl.ds(tile * TILE, 2 * TILE), :] = pair.astype(bf16)
    rest = jnp.concatenate([tile_of(tiles - 1), ninth[...]], axis=1)
    result[:, pl.ds((tiles - 1) * TILE, 3 * TILE), :] = rest.astype(bf16)


def settle_kernel(got, scale, to_natural, home, squares, placed):
    devices = got.shape[0]
    tiles = placed.shape[0]
    line = 8
    half = line // 2
    for source in range(line):
        gate = (source % 2) * half + source // 2
        found = got[source].astype(f32)
        for index in range(source + line, devices, line):
            found = found + got[index].astype(f32)
        for tile in range(tiles):
            placed[tile, pl.ds(gate, TILE, stride=8), :] = found[tile * TILE : (tile + 1) * TILE]
            ninth = OWN * TILE + tile
            placed[tile, pl.ds(TILE * 8 + gate, 1), :] = found[ninth : ninth + 1]
    values = jnp.concatenate([placed[tile] for tile in range(tiles)], axis=1)
    values = values * scale[...].astype(f32)
    total = jnp.sum(jnp.sum(values * values, axis=0, keepdims=True), axis=1, keepdims=True)
    squares[...] = jnp.broadcast_to(total, squares.shape)
    home[...] = dot(values.astype(bf16), to_natural[...]).astype(bf16)


def own_kernel(
    wall,
    ninth_in,
    late,
    early,
    in_rows,
    output_rows,
    unpack,
    to_natural,
    d_out,
    out,
    square,
    sems,
):
    width = in_rows.shape[1]
    rows = in_rows.shape[0]
    main = wall.shape[0]
    rest = width - main
    copies = []
    for gate in range(4):
        copies.append(
            pltpu.make_async_copy(
                wall.at[:, pl.ds(gate * width, width)],
                square.at[gate, pl.ds(0, main), :],
                sems.at[2 * gate],
            )
        )
        copies.append(
            pltpu.make_async_copy(
                ninth_in.at[gate], square.at[gate, pl.ds(main, rest), :], sems.at[2 * gate + 1]
            )
        )
    for copy in copies:
        copy.start()

    def natural(values):
        values = dot(unpack[...], values).astype(bf16)
        return dot(values, to_natural[...]).astype(bf16)

    out[...] = natural(output_rows[pl.ds(0, unpack.shape[1]), :])

    def right_product(left, matrix):
        return lax.dot_general(
            left, matrix, (((1,), (1,)), ((), ())), preferred_element_type=f32
        )

    found = jnp.zeros((rows, width), f32)
    for gate in range(4):
        copies[2 * gate].wait()
        copies[2 * gate + 1].wait()
        both = jnp.concatenate([late[gate], early[gate]], axis=0)
        found = found + right_product(both, square[gate])
    found = found * (in_rows[...].astype(f32) * KEEP_INPUT)
    d_out[...] = natural(found.astype(bf16))


def in_vmem():
    return pl.BlockSpec(memory_space=pltpu.VMEM)


def in_place():
    return pl.BlockSpec(memory_space=pl.ANY)


def run_forward(wall, mixed, spread, collect, h_first, c_first, out_scale):
    steps_rows = spread.shape[0]
    rows, width = mixed.shape
    devices = wall.shape[0] // TILE
    all_kept = LONGEST * KINDS * LANES
    return pl.pallas_call(
        forward_kernel,
        out_shape=(
            jax.ShapeDtypeStruct((width, collect.shape[0]), bf16),
            jax.ShapeDtypeStruct((collect.shape[0], width), bf16),
            jax.ShapeDtypeStruct((4, devices, width), bf16),
            jax.ShapeDtypeStruct((all_kept, width), f32),
            jax.ShapeDtypeStruct((4, width, width), bf16),
        ),
        in_specs=[in_place()] + [in_vmem()] * 6,
        out_specs=(in_vmem(),) * 3 + (in_place(),) * 2,
        scratch_shapes=[
            pltpu.VMEM((4, width, width), bf16),
            pltpu.VMEM((width, 4 * width), bf16),
            pltpu.VMEM((devices * TILE, width), bf16),
            pltpu.VMEM((width // 128, devices * TILE, 128), f32),
            pltpu.VMEM((steps_rows, 4 * width), f32),
            pltpu.VMEM((all_kept, width), f32),
            pltpu.VMEM((steps_rows, width), f32),
            pltpu.VMEM((steps_rows, width), f32),
            pltpu.SemaphoreType.DMA((4,)),
            pltpu.SemaphoreType.DMA,
            pltpu.SemaphoreType.DMA,
            pltpu.SemaphoreType.DMA((5,)),
            pltpu.SemaphoreType.DMA((4,)),
        ],
        compiler_params=pltpu.CompilerParams(vmem_limit_bytes=VMEM_LIMIT),
        cost_estimate=pl.CostEstimate(
            flops=60_000_000_000, bytes_accessed=30_000_000, transcendentals=2_000_000
        ),
        name="forward",
    )(wall, mixed, spread, collect, h_first, c_first, out_scale)


def run_backward(turned, kept, coming, spread, collect, out_scale, carry, first_step):
    steps_rows = spread.shape[0]
    rows, width = collect.shape[0], coming.shape[1]
    results = [jax.ShapeDtypeStruct((4, rows, width), bf16)]
    if first_step > 0:
        results.append(jax.ShapeDtypeStruct((2 * LANES, width), f32))
    return pl.pallas_call(
        functools.partial(backward_kernel, first_step=first_step),
        out_shape=results,
        in_specs=[in_place()] * 2 + [in_vmem()] * 5,
        out_specs=[in_vmem()] * len(results),
        scratch_shapes=[
            pltpu.VMEM((4 * width, width), bf16),
            pltpu.VMEM((steps_rows * KINDS, width), f32),
            pltpu.VMEM((steps_rows, width), f32),
            pltpu.VMEM((steps_rows, 4 * width), f32),
            pltpu.SemaphoreType.DMA((4,)),
            pltpu.SemaphoreType.DMA((2,)),
        ],
        compiler_params=pltpu.CompilerParams(vmem_limit_bytes=VMEM_MEDIUM),
        cost_estimate=pl.CostEstimate(
            flops=steps_rows // LANES * 1_500_000_000, bytes_accessed=20_000_000, transcendentals=0
        ),
        name="backward_late" if first_step else "backward_early",
    )(turned, kept, coming, spread, collect, out_scale, carry)


def run_gradient(core, mixed_all, hidden_all, mine, other, begin, devices, so_far=()):
    half, rows, columns = mine.shape
    line = 2 * half
    width = mixed_all.shape[0] // line
    size = -(-rows // 128) * 128
    if so_far:
        result = jax.ShapeDtypeStruct((devices, MESSAGE, 128), bf16)
    else:
        result = jax.ShapeDtypeStruct((width, columns), f32)
    return pl.pallas_call(
        functools.partial(gradient_kernel, begin=begin),
        out_shape=result,
        in_specs=[pl.BlockSpec(memory_space=pltpu.SMEM)]
        + [in_place()] * 4
        + [in_vmem()] * len(so_far),
        out_specs=in_vmem(),
        scratch_shapes=[
            pltpu.VMEM((width, line * size), bf16),
            pltpu.VMEM((line * size, columns), bf16),
            pltpu.VMEM((devices, 2 * TILE, 128), f32),
            pltpu.SemaphoreType.DMA((line,)),
            pltpu.SemaphoreType.DMA((line,)),
        ],
        compiler_params=pltpu.CompilerParams(vmem_limit_bytes=VMEM_MEDIUM),
        cost_estimate=pl.CostEstimate(
            flops=5_000_000_000, bytes_accessed=12_000_000, transcendentals=0
        ),
        name="gradient_early" if so_far else "gradient_late",
    )(core, mixed_all, hidden_all, mine, other, *so_far)


def run_settle(got, scale, to_natural):
    wide, width = to_natural.shape
    devices = got.shape[0]
    return pl.pallas_call(
        settle_kernel,
        out_shape=(
            jax.ShapeDtypeStruct((OWN * 8, width), bf16),
            jax.ShapeDtypeStruct((devices, 128), f32),
        ),
        in_specs=[in_vmem()] * 3,
        out_specs=(in_vmem(),) * 2,
        scratch_shapes=[pltpu.VMEM((wide // 128, OWN * 8, 128), f32)],
        compiler_params=pltpu.CompilerParams(vmem_limit_bytes=VMEM_SMALL),
        name="settle",
    )(got, scale, to_natural)


def run_own(wall, ninth_in, late, early, in_rows, output_rows, unpack, to_natural):
    width, natural = to_natural.shape
    rows = unpack.shape[0]
    return pl.pallas_call(
        own_kernel,
        out_shape=(jax.ShapeDtypeStruct((rows, natural), bf16),) * 2,
        in_specs=[in_place()] * 2 + [in_vmem()] * 6,
        out_specs=(in_vmem(),) * 2,
        scratch_shapes=[
            pltpu.VMEM((4, width, width), bf16),
            pltpu.SemaphoreType.DMA((8,)),
        ],
        compiler_params=pltpu.CompilerParams(vmem_limit_bytes=VMEM_MEDIUM),
        cost_estimate=pl.CostEstimate(
            flops=8_000_000_000, bytes_accessed=15_000_000, transcendentals=0
        ),
        name="own",
    )(wall, ninth_in, late, early, in_rows, output_rows, unpack, to_natural)


def split_exact(values):
    parts = []
    rest = values
    for _ in range(3):
        part = lax.reduce_precision(rest, 8, 7)
        parts.append(part.astype(bf16))
        rest = rest - part
    return parts


def body(
    inputs,
    d_out,
    h_start,
    c_start,
    pieces,
    in_mask,
    out_mask,
    w_mask,
    master,
    moment_one,
    moment_two,
):
    streams, steps, width = inputs.shape
    gates_n = 4 * width
    count_w = 2 * width * gates_n
    total = count_w + gates_n
    shard = master.shape[0]
    devices = lax.axis_size("batch")
    me = lax.axis_index("batch")
    wide = OWN * devices
    block = OWN * 2 * gates_n
    gap = block - shard
    most = gap * devices
    tokens = streams * steps
    rows_n = LATE + EARLY
    slot = -(-rows_n // 128) * 128
    line = 8
    lines = devices // line

    line_groups = [[line * q + m for m in range(line)] for q in range(lines)]
    column_groups = [
        [line * q + 2 * y + c for y in range(line // 2)] for q in range(lines) for c in range(2)
    ]
    twins = [(i, i ^ 1) for i in range(devices)]

    to_kept = one_hot(width, wide, lambda k, p: place_of(k, devices) == p)
    to_natural = one_hot(wide, width, lambda p, k: place_of(k, devices) == p)

    places = me * shard + lax.iota(jnp.int32, shard)
    recurrent = (places < count_w) & (places % (2 * gates_n) >= gates_n)
    rec_scale = jnp.where(recurrent, w_mask.astype(f32) * KEEP_RECURRENT, 1.0)
    local_low = master.astype(bf16) * rec_scale.astype(bf16)
    local_low = jnp.where(places < total, local_low, jnp.zeros((), bf16))

    def realigned(flat, following):
        joined = jnp.concatenate([flat, following])
        rows = lax.dynamic_slice(joined, (gap * me,), (block,)).reshape(OWN * 8, width)
        return dot(rows, to_kept).astype(bf16)

    before = [(i + 1, i) for i in range(devices - 1)]
    order = one_hot(
        OWN * 8,
        OWN * 8,
        lambda a, b: jnp.where(a < 64, (a % 8) * 8 + a // 8, 64 + a % 8) == b,
    )
    own = realigned(local_low, lax.ppermute(local_low[:most], "batch", before))
    own = dot(order, own).astype(bf16)
    own = jnp.concatenate([own[TILE * j : TILE * (j + 1)] for j in range(OWN)], axis=1)
    wall = lax.all_gather(own, "batch", axis=0, tiled=True)
    scale_low = rec_scale.astype(bf16)
    scales = realigned(scale_low, lax.ppermute(scale_low[:most], "batch", before))

    in_scale = in_mask.astype(f32) * KEEP_INPUT
    mixed = (inputs.astype(f32) * in_scale[:, None, :]).astype(bf16).reshape(tokens, width)
    spare = ((0, rows_n - tokens), (0, 0))
    mixed = dot(jnp.pad(mixed, spare), to_kept).astype(bf16)
    bias_place = place_of(jnp.int32(width), devices)
    column = lax.broadcasted_iota(jnp.int32, mixed.shape, 1)
    mixed = jnp.where(column == bias_place, jnp.ones((), bf16), mixed)
    coming = dot(jnp.pad(d_out.reshape(tokens, width), spare), to_kept).astype(bf16)
    small = jnp.concatenate(
        [h_start.astype(bf16)]
        + split_exact(c_start)
        + [in_mask.astype(bf16), out_mask.astype(bf16)],
        axis=0,
    )
    small = dot(small, to_kept)
    part = [small[streams * j : streams * (j + 1)] for j in range(6)]
    empty = jnp.zeros((LANES - streams, wide), f32)
    h_first = jnp.concatenate([part[0], empty], axis=0)
    c_first = jnp.concatenate([part[1] + part[2] + part[3], empty], axis=0)
    out_scale_kept = part[5] * KEEP_OUTPUT
    out_scale = jnp.concatenate(
        [out_scale_kept, out_scale_kept, jnp.zeros((LANES - 2 * streams, wide), f32)], axis=0
    )
    base = jnp.arange(streams, dtype=jnp.int32) * steps
    none = jnp.zeros((LANES - 2 * streams,), jnp.int32)
    begins = jnp.concatenate([base, base + pieces[:, 0], none])
    lengths = jnp.concatenate([pieces[:, 0], pieces[:, 1], none])
    ticks = lax.broadcasted_iota(jnp.int32, (LONGEST, LANES), 0)
    active = ticks < lengths[None, :]
    where = jnp.where(active, begins[None, :] + ticks, -1).reshape(-1)
    spread = (where[:, None] == lax.iota(jnp.int32, rows_n)[None, :]).astype(bf16)
    late_first = jnp.maximum(pieces[:, 0] - SPLIT, 0)
    late_base = jnp.arange(streams, dtype=jnp.int32) * LATE_BLOCK
    late_base = jnp.concatenate([late_base, late_base + late_first, none])
    early_base = LATE + SPLIT * jnp.arange(LANES, dtype=jnp.int32)
    packed = jnp.where(ticks < SPLIT, early_base[None] + ticks, late_base[None] + ticks - SPLIT)
    packed = jnp.where(active, packed, -1).reshape(-1)
    collect = (lax.iota(jnp.int32, slot)[:, None] == packed[None, :]).astype(bf16)
    pack = dot(collect, spread).astype(bf16)
    unpack = (
        lax.dot_general(spread, collect[:rows_n], (((0,), (1,)), ((), ())), preferred_element_type=f32)
    ).astype(bf16)
    mixed_turned = lax.dot_general(
        mixed, pack, (((0,), (1,)), ((), ())), preferred_element_type=f32
    ).astype(bf16)
    row_stream = lax.iota(jnp.int32, rows_n) // steps
    row_stream = (row_stream[:, None] == lax.iota(jnp.int32, streams)[None]).astype(bf16)
    in_rows = dot(pack[:rows_n], dot(row_stream, part[4].astype(bf16)).astype(bf16)).astype(bf16)

    begin = SPLIT * LANES
    ready = (wall, mixed, mixed_turned, coming, spread, collect, h_first, c_first, out_scale)
    ready += (in_rows, unpack, to_natural, scales, spread[:begin], spread[begin:])
    ready += (collect[LATE:rows_n, :begin], collect[:LATE, begin:])
    ready = lax.optimization_barrier(ready)
    wall, mixed, mixed_turned, coming, spread, collect, h_first, c_first, out_scale = ready[:9]
    in_rows, unpack, to_natural, scales, spread_early, spread_late = ready[9:15]
    collect_early, collect_late = ready[15:]
    mixed_all = lax.all_gather(
        mixed_turned, "batch", axis=0, tiled=True, axis_index_groups=line_groups
    )
    hidden_turned, output_rows, ninth_in, kept, turned = run_forward(
        wall, mixed, spread, collect, h_first, c_first, out_scale
    )
    hidden_turned, mixed_all = lax.optimization_barrier((hidden_turned, mixed_all))
    hidden_all = lax.all_gather(
        hidden_turned, "batch", axis=0, tiled=True, axis_index_groups=line_groups
    )
    late, carry = run_backward(
        turned, kept, coming, spread_late, collect_late, out_scale, out_scale, SPLIT
    )

    def exchange(rows):
        return lax.all_to_all(
            rows, "batch", 0, 0, tiled=True, axis_index_groups=column_groups
        )

    late_mine = exchange(late)
    (early,) = run_backward(
        turned, kept, coming, spread_early, collect_early, out_scale, carry, 0
    )
    late_mine, early = lax.optimization_barrier((late_mine, early))
    early_mine = exchange(early)
    core = (me % 2).reshape(1)
    so_far = run_gradient(
        core, mixed_all, hidden_all, late_mine, lax.ppermute(late_mine, "batch", twins), 0, devices
    )
    early_mine, so_far = lax.optimization_barrier((early_mine, so_far))
    message = run_gradient(
        core,
        mixed_all,
        hidden_all,
        early_mine,
        lax.ppermute(early_mine, "batch", twins),
        LATE,
        devices,
        (so_far,),
    )
    got = lax.all_to_all(message, "batch", 0, 0, tiled=True)

    d_rows, out_rows = run_own(
        wall, ninth_in, late, early, in_rows, output_rows, unpack, to_natural
    )
    output = out_rows[:tokens].reshape(streams, steps, width)
    d_inputs = d_rows[:tokens].reshape(streams, steps, width)
    got, output, d_inputs = lax.optimization_barrier((got, output, d_inputs))

    home, squares = run_settle(got, scales, to_natural)
    squares = lax.all_to_all(squares, "batch", 0, 0, tiled=True)
    home = home.reshape(block)
    tail = lax.ppermute(home[block - most :], "batch", [(i, i + 1) for i in range(devices - 1)])
    grad_shard = lax.dynamic_slice(
        jnp.concatenate([tail, home]), (most - gap * me,), (shard,)
    ).astype(f32)
    grad_norm = jnp.sqrt(jnp.sum(squares[:, 0]))

    factor = jnp.minimum(1.0, CLIP_NORM / (grad_norm + 1e-06))
    clipped = grad_shard * factor
    moment_new = BETA_ONE * moment_one + (1.0 - BETA_ONE) * clipped
    second_new = BETA_TWO * moment_two + (1.0 - BETA_TWO) * clipped * clipped
    first_hat = moment_new / (1.0 - BETA_ONE**STEP)
    second_hat = second_new / (1.0 - BETA_TWO**STEP)
    master_new = master - LEARN_RATE * (
        first_hat / (jnp.sqrt(second_hat) + EPSILON) + WEIGHT_DECAY * master
    )
    return (output, d_inputs, moment_new, second_new, master_new, grad_norm)


def solution(mesh):
    placed = (
        P("batch", None, None),
        P("batch", None, None),
        P("batch", None),
        P("batch", None),
        P("batch", None),
        P("batch", None),
        P("batch", None),
        P("batch"),
        P("batch"),
        P("batch"),
        P("batch"),
    )
    return jax.shard_map(
        body,
        mesh=mesh,
        in_specs=placed,
        out_specs=(
            P("batch", None, None),
            P("batch", None, None),
            P("batch"),
            P("batch"),
            P("batch"),
            P(),
        ),
        check_vma=False,
    )
```

```python
import functools

import jax
import jax.numpy as jnp
import ml_dtypes
import numpy as np
from jax import lax
from jax.experimental import pallas as pl
from jax.experimental.pallas import tpu as pltpu
from jax.sharding import PartitionSpec as P

STEP = 10


LEARN_RATE = 0.03
BETA_ONE = 0.9
BETA_TWO = 0.999
WEIGHT_DECAY = 0.01
EPSILON = 1e-08
CLIP_NORM = 1.0
KEEP_INPUT = 4.0 / 3.0
KEEP_OUTPUT = 4.0 / 3.0
KEEP_RECURRENT = 2.0

LONGEST = 40
LANES = 8
TILE = 8
OWN = TILE + 1
KINDS = 6
SOON = 5
SPLIT = 14
LATE = 128
LATE_BLOCK = LATE // 3
EARLY = 96
UNROLL_FORWARD = 3
UNROLL_BACKWARD = 4
MESSAGE = 88
VMEM_LIMIT = 60 * 2**20
VMEM_SMALL = 16 * 2**20

f32 = jnp.float32
bf16 = jnp.bfloat16


def dot(left, right):
    return lax.dot_general(left, right, (((1,), (0,)), ((), ())), preferred_element_type=f32)


def one_hot(rows, columns, wanted):
    row = lax.broadcasted_iota(jnp.int32, (rows, columns), 0)
    column = lax.broadcasted_iota(jnp.int32, (rows, columns), 1)
    return wanted(row, column).astype(bf16)


def place_of(natural, devices):
    owner, rest = natural // OWN, natural % OWN
    return jnp.where(rest < TILE, owner * TILE + rest, devices * TILE + owner)


def step_rows(step):
    return pl.ds(pl.multiple_of(step * LANES, LANES), LANES)


def kept_rows(step, kind):
    return pl.ds(pl.multiple_of((step * KINDS + kind) * LANES, LANES), LANES)


def forward_kernel(
    wall,
    mixed,
    spread,
    collect,
    h_first,
    c_first,
    out_scale,
    hidden_turned,
    output_rows,
    ninth_in,
    kept,
    turned,
    square,
    w_rec,
    ninth,
    apart,
    pre,
    kept_here,
    hiddens,
    outs,
    sems_in,
    sem_ninth,
    sem_rec,
    sems_kept,
    sems_turned,
):
    width = mixed.shape[1]
    main = wall.shape[0]
    devices = main // TILE
    gates_n = 4 * width

    copy_ninth = pltpu.make_async_copy(wall.at[:, pl.ds(2 * gates_n, width)], ninth, sem_ninth)
    copies_in = [
        pltpu.make_async_copy(
            wall.at[:, pl.ds(gate * width, width)],
            square.at[gate, pl.ds(0, main), :],
            sems_in.at[gate],
        )
        for gate in range(4)
    ]
    copy_rec = pltpu.make_async_copy(
        wall.at[:, pl.ds(gates_n, gates_n)], w_rec.at[pl.ds(0, main), :], sem_rec
    )
    copy_ninth.start()
    for copy in copies_in:
        copy.start()
    rows = dot(spread[...], mixed[...]).astype(bf16)
    copy_ninth.wait()
    for tile in range(width // 128):
        columns = pl.ds(tile * 128, 128)
        apart[tile] = ninth[:, columns].astype(f32)
        for gate in range(8):
            rest = apart[tile, pl.ds(gate, devices, stride=8), :].astype(bf16)
            if gate < 4:
                square[gate, pl.ds(main, devices), columns] = rest
                ninth_in[gate, :, columns] = rest
            else:
                there = pl.ds((gate - 4) * width + tile * 128, 128)
                w_rec[pl.ds(main, devices), there] = rest
    copy_rec.start()
    for gate in range(4):
        copies_in[gate].wait()
        pre[:, pl.ds(gate * width, width)] = dot(rows, square[gate])
    copy_rec.wait()
    scale = out_scale[...]

    def step(index, carry):
        hidden, cell = carry
        at = step_rows(index)
        gates = pre[at, :] + dot(hidden.astype(bf16), w_rec[...])
        in_gate = jax.nn.sigmoid(gates[:, :width])
        forget = jax.nn.sigmoid(gates[:, width : 2 * width])
        candid = jnp.tanh(gates[:, 2 * width : 3 * width])
        out_gate = jax.nn.sigmoid(gates[:, 3 * width :])
        cell_new = forget * cell + in_gate * candid
        squash = jnp.tanh(cell_new)
        hidden_new = out_gate * squash
        hiddens[at, :] = hidden
        outs[at, :] = hidden_new * scale
        kept_here[kept_rows(index, 0), :] = out_gate * (1.0 - squash * squash)
        kept_here[kept_rows(index, 1), :] = candid * in_gate * (1.0 - in_gate)
        kept_here[kept_rows(index, 2), :] = cell * forget * (1.0 - forget)
        kept_here[kept_rows(index, 3), :] = in_gate * (1.0 - candid * candid)
        kept_here[kept_rows(index, 4), :] = squash * out_gate * (1.0 - out_gate)
        kept_here[kept_rows(index, 5), :] = forget
        return (hidden_new, cell_new)

    turns = width // 128

    def copy_kept(part):
        size = turns * KINDS * LANES
        at = pl.ds(pl.multiple_of(part * size, LANES), size)
        return pltpu.make_async_copy(kept_here.at[at, :], kept.at[at, :], sems_kept.at[part])

    def copy_turned(gate):
        return pltpu.make_async_copy(square.at[gate], turned.at[gate], sems_turned.at[gate])

    def part(gate, carry):
        def turning(count, carry):
            columns = pl.ds(pl.multiple_of(gate * width + count * 128, 128), 128)
            into = pl.ds(pl.multiple_of(count * 128, 128), 128)
            square[gate, into, :] = w_rec[:, columns].T
            return step(gate * turns + count, carry)

        carry = lax.fori_loop(0, turns, turning, carry, unroll=UNROLL_FORWARD)
        copy_kept(gate).start()
        copy_turned(gate).start()
        return carry

    carry = lax.fori_loop(0, 4, part, (h_first[...], c_first[...]))
    lax.fori_loop(4 * turns, LONGEST, step, carry, unroll=UNROLL_FORWARD)
    begin = 4 * turns * KINDS * LANES
    rest = pl.ds(begin, kept_here.shape[0] - begin)
    last = pltpu.make_async_copy(kept_here.at[rest, :], kept.at[rest, :], sems_kept.at[4])
    last.start()
    hidden_turned[...] = lax.dot_general(
        hiddens[...].astype(bf16),
        collect[...],
        (((0,), (1,)), ((), ())),
        preferred_element_type=f32,
    ).astype(bf16)
    output_rows[...] = outs[...].astype(bf16)
    for gate in range(4):
        copy_kept(gate).wait()
        copy_turned(gate).wait()
    last.wait()


def backward_kernel(
    turned,
    kept,
    coming,
    spread,
    collect,
    out_scale,
    carry_in,
    gate_rows,
    *refs,
    first_step,
):
    carry_out = refs[0]
    w_turned, kept_here, come, dgates, sems_turned, sems_kept = refs[-6:]
    width = coming.shape[1]
    steps = spread.shape[0] // LANES
    size = KINDS * LANES

    def copy_kept(part):
        begin, count = ((steps - SOON) * size, SOON * size) if part == 0 else (
            0,
            (steps - SOON) * size,
        )
        return pltpu.make_async_copy(
            kept.at[pl.ds(first_step * size + begin, count), :],
            kept_here.at[pl.ds(begin, count), :],
            sems_kept.at[part],
        )

    copies = [
        pltpu.make_async_copy(
            turned.at[gate], w_turned.at[pl.ds(gate * width, width), :], sems_turned.at[gate]
        )
        for gate in range(4)
    ]
    copy_kept(0).start()
    for copy in copies:
        copy.start()
    come[...] = dot(spread[...], coming[...])
    scale = out_scale[...]

    def gradients(index, carry):
        dh_next, dc_next = carry
        at = step_rows(index)
        grad_h = come[at, :] * scale + dh_next
        grad_c = dc_next + grad_h * kept_here[kept_rows(index, 0), :]
        grads = jnp.concatenate(
            [
                grad_c * kept_here[kept_rows(index, 1), :],
                grad_c * kept_here[kept_rows(index, 2), :],
                grad_c * kept_here[kept_rows(index, 3), :],
                grad_h * kept_here[kept_rows(index, 4), :],
            ],
            axis=1,
        )
        dgates[at, :] = grads
        return (grads, grad_c * kept_here[kept_rows(index, 5), :])

    def step(index, carry):
        grads, dc_next = gradients(index, carry)
        return (dot(grads.astype(bf16), w_turned[...]), dc_next)

    def run(last, count, carry):
        return lax.fori_loop(
            0, count, lambda back, c: step(last - back, c), carry, unroll=UNROLL_BACKWARD
        )

    copy_kept(0).wait()
    if first_step > 0:
        carry = (jnp.zeros((LANES, width), f32),) * 2
    else:
        carry = (carry_in[pl.ds(0, LANES), :], carry_in[pl.ds(LANES, LANES), :])
    grads, dc_next = gradients(steps - 1, carry)
    grads = grads.astype(bf16)
    dh_next = jnp.zeros((LANES, width), f32)
    for gate in range(4):
        copies[gate].wait()
        here = slice(gate * width, (gate + 1) * width)
        dh_next = dh_next + dot(grads[:, here], w_turned[here, :])
    copy_kept(1).start()
    carry = run(steps - 2, SOON - 1, (dh_next, dc_next))
    copy_kept(1).wait()
    if first_step > 0:
        carry = run(steps - SOON - 1, steps - SOON, carry)
        carry_out[pl.ds(0, LANES), :] = carry[0]
        carry_out[pl.ds(LANES, LANES), :] = carry[1]
    else:
        carry = run(steps - SOON - 1, steps - SOON - 1, carry)
        gradients(0, carry)
    for gate in range(4):
        columns = pl.ds(gate * width, width)
        gate_rows[gate] = dot(collect[...], dgates[:, columns].astype(bf16)).astype(bf16)


def gradient_kernel(
    core,
    mixed_all,
    hidden_all,
    mine,
    other,
    *refs,
    begin,
):
    result, left, right, ninth, before, sems_left, sems_right, sem_before = refs[-8:]
    so_far = refs[:-8]
    half, rows, columns = mine.shape
    line = 2 * half
    width, size = left.shape[0], left.shape[1] // line
    which = core[0]

    def copies_left(source):
        found = []
        for place in range(line):
            chip, twin = place % half, place // half
            block = 2 * chip + (which if twin == 0 else 1 - which)
            found.append(
                pltpu.make_async_copy(
                    source.at[pl.ds(block * width, width), pl.ds(begin, size)],
                    left.at[:, pl.ds(place * size, size)],
                    sems_left.at[place],
                )
            )
        return found

    @pl.when(which == 0)
    def _():
        for copy in copies_left(mixed_all):
            copy.start()

    @pl.when(which != 0)
    def _():
        for copy in copies_left(hidden_all):
            copy.start()

    copies_right = [
        pltpu.make_async_copy(
            (mine if place < half else other).at[place % half],
            right.at[pl.ds(place * size, rows), :],
            sems_right.at[place],
        )
        for place in range(line)
    ]
    for copy in copies_right:
        copy.start()
    if so_far:
        copy_before = pltpu.make_async_copy(so_far[0], before, sem_before)
        copy_before.start()
    if rows < size:
        for place in range(line):
            right[pl.ds(place * size + rows, size - rows), :] = jnp.zeros(
                (size - rows, columns), bf16
            )
    for copy in copies_left(mixed_all) + copies_right:
        copy.wait()
    grad = dot(left[...], right[...])
    if not so_far:
        result[...] = grad
        return
    copy_before.wait()
    grad = grad + before[...]
    devices = result.shape[0]
    main = devices * TILE
    tiles = columns // 128

    def tile_of(tile):
        here = grad[:main, tile * 128 : (tile + 1) * 128]
        return here.reshape(devices, TILE, 128)

    ninth[...] = jnp.zeros(ninth.shape, f32)
    for tile in range(tiles):
        ninth[:, tile, :] = grad[main:, tile * 128 : (tile + 1) * 128]
    for tile in range(0, tiles - 1, 2):
        pair = jnp.concatenate([tile_of(tile), tile_of(tile + 1)], axis=1)
        result[:, pl.ds(tile * TILE, 2 * TILE), :] = pair.astype(bf16)
    rest = jnp.concatenate([tile_of(tiles - 1), ninth[...]], axis=1)
    result[:, pl.ds((tiles - 1) * TILE, 3 * TILE), :] = rest.astype(bf16)


def settle_kernel(got, scale, to_natural, home, squares, placed):
    devices = got.shape[0]
    tiles = placed.shape[0]
    line = 8
    half = line // 2
    for source in range(line):
        gate = (source % 2) * half + source // 2
        found = got[source].astype(f32)
        for index in range(source + line, devices, line):
            found = found + got[index].astype(f32)
        for tile in range(tiles):
            placed[tile, pl.ds(gate, TILE, stride=8), :] = found[tile * TILE : (tile + 1) * TILE]
            ninth = OWN * TILE + tile
            placed[tile, pl.ds(TILE * 8 + gate, 1), :] = found[ninth : ninth + 1]
    values = jnp.concatenate([placed[tile] for tile in range(tiles)], axis=1)
    values = values * scale[...].astype(f32)
    total = jnp.sum(jnp.sum(values * values, axis=0, keepdims=True), axis=1, keepdims=True)
    squares[...] = jnp.broadcast_to(total, squares.shape)
    home[...] = dot(values.astype(bf16), to_natural[...]).astype(bf16)


def own_kernel(
    wall,
    ninth_in,
    late,
    early,
    in_rows,
    output_rows,
    gather,
    unpack,
    to_natural,
    d_out,
    out,
    square,
    sems,
):
    width = in_rows.shape[1]
    rows = in_rows.shape[0]
    main = wall.shape[0]
    rest = width - main
    copies = []
    for gate in range(4):
        copies.append(
            pltpu.make_async_copy(
                wall.at[:, pl.ds(gate * width, width)],
                square.at[gate, pl.ds(0, main), :],
                sems.at[2 * gate],
            )
        )
        copies.append(
            pltpu.make_async_copy(
                ninth_in.at[gate], square.at[gate, pl.ds(main, rest), :], sems.at[2 * gate + 1]
            )
        )
    for copy in copies:
        copy.start()

    def natural(places, values):
        return dot(dot(places[...], values).astype(bf16), to_natural[...]).astype(bf16)

    out[...] = natural(gather, output_rows[...])

    def right_product(left, matrix):
        return lax.dot_general(
            left, matrix, (((1,), (1,)), ((), ())), preferred_element_type=f32
        )

    found = jnp.zeros((rows, width), f32)
    for gate in range(4):
        copies[2 * gate].wait()
        copies[2 * gate + 1].wait()
        both = jnp.concatenate([late[gate], early[gate]], axis=0)
        found = found + right_product(both, square[gate])
    found = found * (in_rows[...].astype(f32) * KEEP_INPUT)
    d_out[...] = natural(unpack, found.astype(bf16))


def in_vmem():
    return pl.BlockSpec(memory_space=pltpu.VMEM)


def in_place():
    return pl.BlockSpec(memory_space=pl.ANY)


def run_forward(wall, mixed, spread, collect, h_first, c_first, out_scale):
    steps_rows = spread.shape[0]
    rows, width = mixed.shape
    devices = wall.shape[0] // TILE
    all_kept = LONGEST * KINDS * LANES
    return pl.pallas_call(
        forward_kernel,
        out_shape=(
            jax.ShapeDtypeStruct((width, collect.shape[0]), bf16),
            jax.ShapeDtypeStruct((steps_rows, width), bf16),
            jax.ShapeDtypeStruct((4, devices, width), bf16),
            jax.ShapeDtypeStruct((all_kept, width), f32),
            jax.ShapeDtypeStruct((4, width, width), bf16),
        ),
        in_specs=[in_place()] + [in_vmem()] * 6,
        out_specs=(in_vmem(),) * 3 + (in_place(),) * 2,
        scratch_shapes=[
            pltpu.VMEM((4, width, width), bf16),
            pltpu.VMEM((width, 4 * width), bf16),
            pltpu.VMEM((devices * TILE, width), bf16),
            pltpu.VMEM((width // 128, devices * TILE, 128), f32),
            pltpu.VMEM((steps_rows, 4 * width), f32),
            pltpu.VMEM((all_kept, width), f32),
            pltpu.VMEM((steps_rows, width), f32),
            pltpu.VMEM((steps_rows, width), f32),
            pltpu.SemaphoreType.DMA((4,)),
            pltpu.SemaphoreType.DMA,
            pltpu.SemaphoreType.DMA,
            pltpu.SemaphoreType.DMA((5,)),
            pltpu.SemaphoreType.DMA((4,)),
        ],
        compiler_params=pltpu.CompilerParams(vmem_limit_bytes=VMEM_LIMIT),
        cost_estimate=pl.CostEstimate(
            flops=60_000_000_000, bytes_accessed=30_000_000, transcendentals=2_000_000
        ),
        name="forward",
    )(wall, mixed, spread, collect, h_first, c_first, out_scale)


def run_backward(turned, kept, coming, spread, collect, out_scale, carry, first_step):
    steps_rows = spread.shape[0]
    rows, width = collect.shape[0], coming.shape[1]
    results = [jax.ShapeDtypeStruct((4, rows, width), bf16)]
    if first_step > 0:
        results.append(jax.ShapeDtypeStruct((2 * LANES, width), f32))
    return pl.pallas_call(
        functools.partial(backward_kernel, first_step=first_step),
        out_shape=results,
        in_specs=[in_place()] * 2 + [in_vmem()] * 5,
        out_specs=[in_vmem()] * len(results),
        scratch_shapes=[
            pltpu.VMEM((4 * width, width), bf16),
            pltpu.VMEM((steps_rows * KINDS, width), f32),
            pltpu.VMEM((steps_rows, width), f32),
            pltpu.VMEM((steps_rows, 4 * width), f32),
            pltpu.SemaphoreType.DMA((4,)),
            pltpu.SemaphoreType.DMA((2,)),
        ],
        compiler_params=pltpu.CompilerParams(vmem_limit_bytes=VMEM_LIMIT),
        cost_estimate=pl.CostEstimate(
            flops=steps_rows // LANES * 1_500_000_000, bytes_accessed=20_000_000, transcendentals=0
        ),
        name="backward_late" if first_step else "backward_early",
    )(turned, kept, coming, spread, collect, out_scale, carry)


def run_gradient(core, mixed_all, hidden_all, mine, other, begin, devices, so_far=()):
    half, rows, columns = mine.shape
    line = 2 * half
    width = mixed_all.shape[0] // line
    size = -(-rows // 128) * 128
    if so_far:
        result = jax.ShapeDtypeStruct((devices, MESSAGE, 128), bf16)
    else:
        result = jax.ShapeDtypeStruct((width, columns), f32)
    return pl.pallas_call(
        functools.partial(gradient_kernel, begin=begin),
        out_shape=result,
        in_specs=[pl.BlockSpec(memory_space=pltpu.SMEM)]
        + [in_place()] * (4 + len(so_far)),
        out_specs=in_vmem(),
        scratch_shapes=[
            pltpu.VMEM((width, line * size), bf16),
            pltpu.VMEM((line * size, columns), bf16),
            pltpu.VMEM((devices, 2 * TILE, 128), f32),
            pltpu.VMEM((width, columns), f32),
            pltpu.SemaphoreType.DMA((line,)),
            pltpu.SemaphoreType.DMA((line,)),
            pltpu.SemaphoreType.DMA,
        ],
        compiler_params=pltpu.CompilerParams(vmem_limit_bytes=VMEM_LIMIT),
        cost_estimate=pl.CostEstimate(
            flops=5_000_000_000, bytes_accessed=12_000_000, transcendentals=0
        ),
        name="gradient_early" if so_far else "gradient_late",
    )(core, mixed_all, hidden_all, mine, other, *so_far)


def run_settle(got, scale, to_natural):
    wide, width = to_natural.shape
    devices = got.shape[0]
    return pl.pallas_call(
        settle_kernel,
        out_shape=(
            jax.ShapeDtypeStruct((OWN * 8, width), bf16),
            jax.ShapeDtypeStruct((devices, 128), f32),
        ),
        in_specs=[in_vmem()] * 3,
        out_specs=(in_vmem(),) * 2,
        scratch_shapes=[pltpu.VMEM((wide // 128, OWN * 8, 128), f32)],
        compiler_params=pltpu.CompilerParams(vmem_limit_bytes=VMEM_SMALL),
        name="settle",
    )(got, scale, to_natural)


def run_own(wall, ninth_in, late, early, in_rows, output_rows, gather, unpack, to_natural):
    width, natural = to_natural.shape
    rows = unpack.shape[0]
    return pl.pallas_call(
        own_kernel,
        out_shape=(jax.ShapeDtypeStruct((rows, natural), bf16),) * 2,
        in_specs=[in_place()] * 2 + [in_vmem()] * 7,
        out_specs=(in_vmem(),) * 2,
        scratch_shapes=[
            pltpu.VMEM((4, width, width), bf16),
            pltpu.SemaphoreType.DMA((8,)),
        ],
        compiler_params=pltpu.CompilerParams(vmem_limit_bytes=VMEM_LIMIT),
        cost_estimate=pl.CostEstimate(
            flops=8_000_000_000, bytes_accessed=15_000_000, transcendentals=0
        ),
        name="own",
    )(wall, ninth_in, late, early, in_rows, output_rows, gather, unpack, to_natural)


def split_exact(values):
    parts = []
    rest = values
    for _ in range(3):
        part = lax.reduce_precision(rest, 8, 7)
        parts.append(part.astype(bf16))
        rest = rest - part
    return parts


def body(
    inputs,
    d_out,
    h_start,
    c_start,
    pieces,
    in_mask,
    out_mask,
    w_mask,
    master,
    moment_one,
    moment_two,
):
    streams, steps, width = inputs.shape
    gates_n = 4 * width
    count_w = 2 * width * gates_n
    total = count_w + gates_n
    shard = master.shape[0]
    devices = lax.axis_size("batch")
    me = lax.axis_index("batch")
    wide = OWN * devices
    block = OWN * 2 * gates_n
    gap = block - shard
    most = gap * devices
    tokens = streams * steps
    rows_n = LATE + EARLY
    slot = -(-rows_n // 128) * 128
    line = 8
    lines = devices // line

    line_groups = [[line * q + m for m in range(line)] for q in range(lines)]
    column_groups = [
        [line * q + 2 * y + c for y in range(line // 2)] for q in range(lines) for c in range(2)
    ]
    twins = [(i, i ^ 1) for i in range(devices)]

    order = np.arange(width)
    order = np.where(
        order % OWN < TILE, order // OWN * TILE + order % OWN, devices * TILE + order // OWN
    )
    to_kept = np.zeros((width, wide), ml_dtypes.bfloat16)
    to_kept[np.arange(width), order] = 1
    to_natural = jnp.asarray(to_kept.T.copy())
    to_kept = jnp.asarray(to_kept)

    def rounded(values, mask):
        places = me * shard + lax.iota(jnp.int32, values.shape[0])
        recurrent = (places < count_w) & (places % (2 * gates_n) >= gates_n)
        factor = jnp.where(recurrent, mask.astype(bf16) * KEEP_RECURRENT, jnp.ones((), bf16))
        low = values.astype(bf16) * factor
        return jnp.where(places < total, low, jnp.zeros((), bf16)), factor

    local_low, scale_low = rounded(master, w_mask)
    head_low, head_scale = rounded(master[:most], w_mask[:most])

    def realigned(flat, following):
        joined = jnp.concatenate([flat, following])
        rows = lax.dynamic_slice(joined, (gap * me,), (block,)).reshape(OWN * 8, width)
        return dot(rows, to_kept).astype(bf16)

    before = [(i + 1, i) for i in range(devices - 1)]
    order = one_hot(
        OWN * 8,
        OWN * 8,
        lambda a, b: jnp.where(a < 64, (a % 8) * 8 + a // 8, 64 + a % 8) == b,
    )
    own = realigned(local_low, lax.ppermute(head_low, "batch", before))
    own = dot(order, own).astype(bf16)
    own = jnp.concatenate([own[TILE * j : TILE * (j + 1)] for j in range(OWN)], axis=1)
    wall = lax.all_gather(own, "batch", axis=0, tiled=True)
    scales = realigned(scale_low, lax.ppermute(head_scale, "batch", before))

    in_scale = in_mask.astype(f32) * KEEP_INPUT
    mixed = (inputs.astype(f32) * in_scale[:, None, :]).astype(bf16).reshape(tokens, width)
    spare = ((0, rows_n - tokens), (0, 0))
    mixed = dot(jnp.pad(mixed, spare), to_kept).astype(bf16)
    bias_place = place_of(jnp.int32(width), devices)
    column = lax.broadcasted_iota(jnp.int32, mixed.shape, 1)
    mixed = jnp.where(column == bias_place, jnp.ones((), bf16), mixed)
    coming = dot(jnp.pad(d_out.reshape(tokens, width), spare), to_kept).astype(bf16)
    small = jnp.concatenate(
        [h_start.astype(bf16)]
        + split_exact(c_start)
        + [in_mask.astype(bf16), out_mask.astype(bf16)],
        axis=0,
    )
    small = dot(small, to_kept)
    part = [small[streams * j : streams * (j + 1)] for j in range(6)]
    empty = jnp.zeros((LANES - streams, wide), f32)
    h_first = jnp.concatenate([part[0], empty], axis=0)
    c_first = jnp.concatenate([part[1] + part[2] + part[3], empty], axis=0)
    out_scale_kept = part[5] * KEEP_OUTPUT
    out_scale = jnp.concatenate(
        [out_scale_kept, out_scale_kept, jnp.zeros((LANES - 2 * streams, wide), f32)], axis=0
    )
    base = jnp.arange(streams, dtype=jnp.int32) * steps
    none = jnp.zeros((LANES - 2 * streams,), jnp.int32)
    begins = jnp.concatenate([base, base + pieces[:, 0], none])
    lengths = jnp.concatenate([pieces[:, 0], pieces[:, 1], none])
    ticks = lax.broadcasted_iota(jnp.int32, (LONGEST, LANES), 0)
    active = ticks < lengths[None, :]
    where = jnp.where(active, begins[None, :] + ticks, -1).reshape(-1)
    spread = (where[:, None] == lax.iota(jnp.int32, rows_n)[None, :]).astype(bf16)
    late_first = jnp.maximum(pieces[:, 0] - SPLIT, 0)
    late_base = jnp.arange(streams, dtype=jnp.int32) * LATE_BLOCK
    late_base = jnp.concatenate([late_base, late_base + late_first, none])
    early_base = LATE + SPLIT * jnp.arange(LANES, dtype=jnp.int32)
    packed = jnp.where(ticks < SPLIT, early_base[None] + ticks, late_base[None] + ticks - SPLIT)
    packed = jnp.where(active, packed, -1).reshape(-1)
    collect = (lax.iota(jnp.int32, slot)[:, None] == packed[None, :]).astype(bf16)
    pack = dot(collect, spread).astype(bf16)
    unpack = (
        lax.dot_general(spread, collect[:rows_n], (((0,), (1,)), ((), ())), preferred_element_type=f32)
    ).astype(bf16)
    mixed_turned = lax.dot_general(
        mixed, pack, (((0,), (1,)), ((), ())), preferred_element_type=f32
    ).astype(bf16)
    row_stream = lax.iota(jnp.int32, rows_n) // steps
    row_stream = (row_stream[:, None] == lax.iota(jnp.int32, streams)[None]).astype(bf16)
    in_rows = dot(pack[:rows_n], dot(row_stream, part[4].astype(bf16)).astype(bf16)).astype(bf16)

    begin = SPLIT * LANES
    ready = (wall, mixed, mixed_turned, coming, spread, collect, h_first, c_first, out_scale)
    ready += (in_rows, unpack, to_natural, scales, spread[:begin], spread[begin:])
    ready += (collect[LATE:rows_n, :begin], collect[:LATE, begin:], spread.T)
    ready = lax.optimization_barrier(ready)
    wall, mixed, mixed_turned, coming, spread, collect, h_first, c_first, out_scale = ready[:9]
    in_rows, unpack, to_natural, scales, spread_early, spread_late = ready[9:15]
    collect_early, collect_late, gather = ready[15:]
    mixed_all = lax.all_gather(
        mixed_turned, "batch", axis=0, tiled=True, axis_index_groups=line_groups
    )
    hidden_turned, output_rows, ninth_in, kept, turned = run_forward(
        wall, mixed, spread, collect, h_first, c_first, out_scale
    )
    hidden_turned, mixed_all = lax.optimization_barrier((hidden_turned, mixed_all))
    hidden_all = lax.all_gather(
        hidden_turned, "batch", axis=0, tiled=True, axis_index_groups=line_groups
    )
    late, carry = run_backward(
        turned, kept, coming, spread_late, collect_late, out_scale, out_scale, SPLIT
    )

    def exchange(rows):
        return lax.all_to_all(
            rows, "batch", 0, 0, tiled=True, axis_index_groups=column_groups
        )

    late_mine = exchange(late)
    (early,) = run_backward(
        turned, kept, coming, spread_early, collect_early, out_scale, carry, 0
    )
    late_mine, early = lax.optimization_barrier((late_mine, early))
    early_mine = exchange(early)
    core = (me % 2).reshape(1)
    so_far = run_gradient(
        core, mixed_all, hidden_all, late_mine, lax.ppermute(late_mine, "batch", twins), 0, devices
    )
    early_mine, so_far = lax.optimization_barrier((early_mine, so_far))
    message = run_gradient(
        core,
        mixed_all,
        hidden_all,
        early_mine,
        lax.ppermute(early_mine, "batch", twins),
        LATE,
        devices,
        (so_far,),
    )
    got = lax.all_to_all(message, "batch", 0, 0, tiled=True)

    d_rows, out_rows = run_own(
        wall, ninth_in, late, early, in_rows, output_rows, gather, unpack, to_natural
    )
    output = out_rows[:tokens].reshape(streams, steps, width)
    d_inputs = d_rows[:tokens].reshape(streams, steps, width)
    got, output, d_inputs = lax.optimization_barrier((got, output, d_inputs))

    home, squares = run_settle(got, scales, to_natural)
    squares = lax.all_to_all(squares, "batch", 0, 0, tiled=True)
    home = home.reshape(block)
    tail = lax.ppermute(home[block - most :], "batch", [(i, i + 1) for i in range(devices - 1)])
    grad_shard = lax.dynamic_slice(
        jnp.concatenate([tail, home]), (most - gap * me,), (shard,)
    ).astype(f32)
    grad_norm = jnp.sqrt(jnp.sum(squares[:, 0]))

    factor = jnp.minimum(1.0, CLIP_NORM / (grad_norm + 1e-06))
    clipped = grad_shard * factor
    moment_new = BETA_ONE * moment_one + (1.0 - BETA_ONE) * clipped
    second_new = BETA_TWO * moment_two + (1.0 - BETA_TWO) * clipped * clipped
    first_hat = moment_new / (1.0 - BETA_ONE**STEP)
    second_hat = second_new / (1.0 - BETA_TWO**STEP)
    master_new = master - LEARN_RATE * (
        first_hat / (jnp.sqrt(second_hat) + EPSILON) + WEIGHT_DECAY * master
    )
    return (output, d_inputs, moment_new, second_new, master_new, grad_norm)


def solution(mesh):
    placed = (
        P("batch", None, None),
        P("batch", None, None),
        P("batch", None),
        P("batch", None),
        P("batch", None),
        P("batch", None),
        P("batch", None),
        P("batch"),
        P("batch"),
        P("batch"),
        P("batch"),
    )
    return jax.shard_map(
        body,
        mesh=mesh,
        in_specs=placed,
        out_specs=(
            P("batch", None, None),
            P("batch", None, None),
            P("batch"),
            P("batch"),
            P("batch"),
            P(),
        ),
        check_vma=False,
    )
```

```python
import functools

import jax
import jax.numpy as jnp
from jax import lax
from jax.experimental import pallas as pl
from jax.experimental.pallas import tpu as pltpu
from jax.sharding import PartitionSpec as P

STEP = 10


LEARN_RATE = 0.03
BETA_ONE = 0.9
BETA_TWO = 0.999
WEIGHT_DECAY = 0.01
EPSILON = 1e-08
CLIP_NORM = 1.0
KEEP_INPUT = 4.0 / 3.0
KEEP_OUTPUT = 4.0 / 3.0
KEEP_RECURRENT = 2.0

LONGEST = 40
LANES = 8
TILE = 8
OWN = TILE + 1
KINDS = 6
SOON = 5
SPLIT = 14
LATE = 128
LATE_BLOCK = LATE // 3
EARLY = 96
UNROLL_FORWARD = 3
UNROLL_BACKWARD = 4
MESSAGE = 88
VMEM_LIMIT = 60 * 2**20
VMEM_SMALL = 16 * 2**20

f32 = jnp.float32
bf16 = jnp.bfloat16


def dot(left, right):
    return lax.dot_general(left, right, (((1,), (0,)), ((), ())), preferred_element_type=f32)


def one_hot(rows, columns, wanted):
    row = lax.broadcasted_iota(jnp.int32, (rows, columns), 0)
    column = lax.broadcasted_iota(jnp.int32, (rows, columns), 1)
    return wanted(row, column).astype(bf16)


def place_of(natural, devices):
    owner, rest = natural // OWN, natural % OWN
    return jnp.where(rest < TILE, owner * TILE + rest, devices * TILE + owner)


def step_rows(step):
    return pl.ds(pl.multiple_of(step * LANES, LANES), LANES)


def kept_rows(step, kind):
    return pl.ds(pl.multiple_of((step * KINDS + kind) * LANES, LANES), LANES)


def fetch(sources, into, sems):
    copies = [
        pltpu.make_async_copy(source, place, sems.at[index])
        for index, (source, place) in enumerate(zip(sources, into))
    ]
    for copy in copies:
        copy.start()
    return copies


def forward_kernel(
    wall,
    mixed,
    spread,
    collect,
    h_first,
    c_first,
    out_scale,
    hidden_turned,
    output_rows,
    ninth_in,
    kept,
    turned,
    *refs,
):
    fetched, (square, w_rec, ninth, apart, pre, kept_here, hiddens, outs) = refs[:6], refs[6:14]
    sems_small, sems_in, sem_ninth, sem_rec, sems_kept, sems_turned = refs[14:]
    fetches = fetch((mixed, spread, collect, h_first, c_first, out_scale), fetched, sems_small)
    mixed, spread, collect, h_first, c_first, out_scale = fetched
    width = mixed.shape[1]
    main = wall.shape[0]
    devices = main // TILE
    gates_n = 4 * width

    copy_ninth = pltpu.make_async_copy(wall.at[:, pl.ds(2 * gates_n, width)], ninth, sem_ninth)
    copies_in = [
        pltpu.make_async_copy(
            wall.at[:, pl.ds(gate * width, width)],
            square.at[gate, pl.ds(0, main), :],
            sems_in.at[gate],
        )
        for gate in range(4)
    ]
    copy_rec = pltpu.make_async_copy(
        wall.at[:, pl.ds(gates_n, gates_n)], w_rec.at[pl.ds(0, main), :], sem_rec
    )
    copy_ninth.start()
    for copy in copies_in:
        copy.start()
    for copy in fetches:
        copy.wait()
    rows = dot(spread[...], mixed[...]).astype(bf16)
    copy_ninth.wait()
    for tile in range(width // 128):
        columns = pl.ds(tile * 128, 128)
        apart[tile] = ninth[:, columns].astype(f32)
        for gate in range(8):
            rest = apart[tile, pl.ds(gate, devices, stride=8), :].astype(bf16)
            if gate < 4:
                square[gate, pl.ds(main, devices), columns] = rest
                ninth_in[gate, :, columns] = rest
            else:
                there = pl.ds((gate - 4) * width + tile * 128, 128)
                w_rec[pl.ds(main, devices), there] = rest
    copy_rec.start()
    for gate in range(4):
        copies_in[gate].wait()
        pre[:, pl.ds(gate * width, width)] = dot(rows, square[gate])
    copy_rec.wait()
    scale = out_scale[...]
    soon = width - 128
    sizes = (256,) * (width // 256) + ((128,) if width % 256 else ())

    def step(index, carry):
        hidden, cell = carry
        at = step_rows(index)
        hiddens[at, :] = hidden
        low = hidden.astype(bf16)
        early = pre[at, :] + dot(low[:, :soon], w_rec[pl.ds(0, soon), :])
        states = ([], [])
        begin = 0
        for size in sizes:
            lanes = pl.ds(begin, size)
            gates = []
            for gate in range(4):
                first = gate * width + begin
                late = dot(low[:, soon:], w_rec[pl.ds(soon, width - soon), pl.ds(first, size)])
                gates.append(early[:, first : first + size] + late)
            in_gate = jax.nn.sigmoid(gates[0])
            forget = jax.nn.sigmoid(gates[1])
            candid = jnp.tanh(gates[2])
            out_gate = jax.nn.sigmoid(gates[3])
            before = cell[:, begin : begin + size]
            cell_new = forget * before + in_gate * candid
            squash = jnp.tanh(cell_new)
            hidden_new = out_gate * squash
            outs[at, lanes] = hidden_new * scale[:, begin : begin + size]
            kept_here[kept_rows(index, 0), lanes] = out_gate * (1.0 - squash * squash)
            kept_here[kept_rows(index, 1), lanes] = candid * in_gate * (1.0 - in_gate)
            kept_here[kept_rows(index, 2), lanes] = before * forget * (1.0 - forget)
            kept_here[kept_rows(index, 3), lanes] = in_gate * (1.0 - candid * candid)
            kept_here[kept_rows(index, 4), lanes] = squash * out_gate * (1.0 - out_gate)
            kept_here[kept_rows(index, 5), lanes] = forget
            states[0].append(hidden_new)
            states[1].append(cell_new)
            begin += size
        return tuple(jnp.concatenate(state, axis=1) for state in states)

    turns = width // 128

    def copy_kept(part):
        size = turns * KINDS * LANES
        at = pl.ds(pl.multiple_of(part * size, LANES), size)
        return pltpu.make_async_copy(kept_here.at[at, :], kept.at[at, :], sems_kept.at[part])

    def copy_turned(gate):
        return pltpu.make_async_copy(square.at[gate], turned.at[gate], sems_turned.at[gate])

    def part(gate, carry):
        def turning(count, carry):
            columns = pl.ds(pl.multiple_of(gate * width + count * 128, 128), 128)
            into = pl.ds(pl.multiple_of(count * 128, 128), 128)
            square[gate, into, :] = w_rec[:, columns].T
            return step(gate * turns + count, carry)

        carry = lax.fori_loop(0, turns, turning, carry, unroll=UNROLL_FORWARD)
        copy_kept(gate).start()
        copy_turned(gate).start()
        return carry

    carry = lax.fori_loop(0, 4, part, (h_first[...], c_first[...]))
    lax.fori_loop(4 * turns, LONGEST, step, carry, unroll=UNROLL_FORWARD)
    begin = 4 * turns * KINDS * LANES
    rest = pl.ds(begin, kept_here.shape[0] - begin)
    last = pltpu.make_async_copy(kept_here.at[rest, :], kept.at[rest, :], sems_kept.at[4])
    last.start()
    hidden_turned[...] = lax.dot_general(
        hiddens[...].astype(bf16),
        collect[...],
        (((0,), (1,)), ((), ())),
        preferred_element_type=f32,
    ).astype(bf16)
    output_rows[...] = outs[...].astype(bf16)
    for gate in range(4):
        copy_kept(gate).wait()
        copy_turned(gate).wait()
    last.wait()


def backward_kernel(
    turned,
    kept,
    coming,
    spread,
    collect,
    out_scale,
    carry_in,
    gate_rows,
    *refs,
    first_step,
):
    carry_out = refs[0]
    *fetched, w_turned, kept_here, come, dgates, sems_small, sems_turned, sems_kept = refs[-12:]
    fetches = fetch((coming, spread, collect, out_scale, carry_in), fetched, sems_small)
    coming, spread, collect, out_scale, carry_in = fetched
    width = coming.shape[1]
    steps = spread.shape[0] // LANES
    size = KINDS * LANES

    def copy_kept(part):
        begin, count = ((steps - SOON) * size, SOON * size) if part == 0 else (
            0,
            (steps - SOON) * size,
        )
        return pltpu.make_async_copy(
            kept.at[pl.ds(first_step * size + begin, count), :],
            kept_here.at[pl.ds(begin, count), :],
            sems_kept.at[part],
        )

    copies = [
        pltpu.make_async_copy(
            turned.at[gate], w_turned.at[pl.ds(gate * width, width), :], sems_turned.at[gate]
        )
        for gate in range(4)
    ]
    copy_kept(0).start()
    for copy in copies:
        copy.start()
    for copy in fetches:
        copy.wait()
    come[...] = dot(spread[...], coming[...])
    scale = out_scale[...]

    def gradients(index, carry):
        dh_next, dc_next = carry
        at = step_rows(index)
        grad_h = come[at, :] * scale + dh_next
        grad_c = dc_next + grad_h * kept_here[kept_rows(index, 0), :]
        grads = jnp.concatenate(
            [
                grad_c * kept_here[kept_rows(index, 1), :],
                grad_c * kept_here[kept_rows(index, 2), :],
                grad_c * kept_here[kept_rows(index, 3), :],
                grad_h * kept_here[kept_rows(index, 4), :],
            ],
            axis=1,
        )
        dgates[at, :] = grads
        return (grads, grad_c * kept_here[kept_rows(index, 5), :])

    def step(index, carry):
        grads, dc_next = gradients(index, carry)
        return (dot(grads.astype(bf16), w_turned[...]), dc_next)

    def run(last, count, carry):
        return lax.fori_loop(
            0, count, lambda back, c: step(last - back, c), carry, unroll=UNROLL_BACKWARD
        )

    copy_kept(0).wait()
    if first_step > 0:
        carry = (jnp.zeros((LANES, width), f32),) * 2
    else:
        carry = (carry_in[pl.ds(0, LANES), :], carry_in[pl.ds(LANES, LANES), :])
    grads, dc_next = gradients(steps - 1, carry)
    grads = grads.astype(bf16)
    dh_next = jnp.zeros((LANES, width), f32)
    for gate in range(4):
        copies[gate].wait()
        here = slice(gate * width, (gate + 1) * width)
        dh_next = dh_next + dot(grads[:, here], w_turned[here, :])
    copy_kept(1).start()
    carry = run(steps - 2, SOON - 1, (dh_next, dc_next))
    copy_kept(1).wait()
    if first_step > 0:
        carry = run(steps - SOON - 1, steps - SOON, carry)
        carry_out[pl.ds(0, LANES), :] = carry[0]
        carry_out[pl.ds(LANES, LANES), :] = carry[1]
    else:
        carry = run(steps - SOON - 1, steps - SOON - 1, carry)
        gradients(0, carry)
    for gate in range(4):
        columns = pl.ds(gate * width, width)
        gate_rows[gate] = dot(collect[...], dgates[:, columns].astype(bf16)).astype(bf16)


def gradient_kernel(
    core,
    mixed_all,
    hidden_all,
    mine,
    other,
    *refs,
    begin,
):
    result, left, right, ninth, before, sems_left, sems_right, sem_before = refs[-8:]
    so_far = refs[:-8]
    half, rows, columns = mine.shape
    line = 2 * half
    width, size = left.shape[0], left.shape[1] // line
    which = core[0]

    def copies_left(source):
        found = []
        for place in range(line):
            chip, twin = place % half, place // half
            block = 2 * chip + (which if twin == 0 else 1 - which)
            found.append(
                pltpu.make_async_copy(
                    source.at[pl.ds(block * width, width), pl.ds(begin, size)],
                    left.at[:, pl.ds(place * size, size)],
                    sems_left.at[place],
                )
            )
        return found

    @pl.when(which == 0)
    def _():
        for copy in copies_left(mixed_all):
            copy.start()

    @pl.when(which != 0)
    def _():
        for copy in copies_left(hidden_all):
            copy.start()

    copies_right = [
        pltpu.make_async_copy(
            (mine if place < half else other).at[place % half],
            right.at[pl.ds(place * size, rows), :],
            sems_right.at[place],
        )
        for place in range(line)
    ]
    for copy in copies_right:
        copy.start()
    if so_far:
        copy_before = pltpu.make_async_copy(so_far[0], before, sem_before)
        copy_before.start()
    if rows < size:
        for place in range(line):
            right[pl.ds(place * size + rows, size - rows), :] = jnp.zeros(
                (size - rows, columns), bf16
            )
    for copy in copies_left(mixed_all) + copies_right:
        copy.wait()
    grad = dot(left[...], right[...])
    if not so_far:
        result[...] = grad
        return
    copy_before.wait()
    devices = result.shape[0]
    main = devices * TILE
    tiles = columns // 128
    ninth[...] = jnp.zeros(ninth.shape, f32)
    for tile in range(0, tiles, 2):
        parts = []
        for place in range(tile, min(tile + 2, tiles)):
            here = grad[:, place * 128 : (place + 1) * 128] + before[:, pl.ds(place * 128, 128)]
            parts.append(here[:main].reshape(devices, TILE, 128))
            ninth[:, place, :] = here[main:]
        if tile + 2 > tiles:
            parts.append(ninth[...])
        rows = jnp.concatenate(parts, axis=1)
        result[:, pl.ds(tile * TILE, rows.shape[1]), :] = rows.astype(bf16)


def settle_kernel(got, scale, to_natural, home, squares, placed):
    devices = got.shape[0]
    tiles = placed.shape[0]
    line = 8
    half = line // 2
    for source in range(line):
        gate = (source % 2) * half + source // 2
        found = got[source].astype(f32)
        for index in range(source + line, devices, line):
            found = found + got[index].astype(f32)
        for tile in range(tiles):
            placed[tile, pl.ds(gate, TILE, stride=8), :] = found[tile * TILE : (tile + 1) * TILE]
            ninth = OWN * TILE + tile
            placed[tile, pl.ds(TILE * 8 + gate, 1), :] = found[ninth : ninth + 1]
    values = jnp.concatenate([placed[tile] for tile in range(tiles)], axis=1)
    values = values * scale[...].astype(f32)
    total = jnp.sum(jnp.sum(values * values, axis=0, keepdims=True), axis=1, keepdims=True)
    squares[...] = jnp.broadcast_to(total, squares.shape)
    home[...] = dot(values.astype(bf16), to_natural[...]).astype(bf16)


def own_kernel(
    wall,
    ninth_in,
    late,
    early,
    in_rows,
    output_rows,
    gather,
    unpack,
    to_natural,
    d_out,
    out,
    square,
    sems,
):
    width = in_rows.shape[1]
    rows = in_rows.shape[0]
    main = wall.shape[0]
    rest = width - main
    copies = []
    for gate in range(4):
        copies.append(
            pltpu.make_async_copy(
                wall.at[:, pl.ds(gate * width, width)],
                square.at[gate, pl.ds(0, main), :],
                sems.at[2 * gate],
            )
        )
        copies.append(
            pltpu.make_async_copy(
                ninth_in.at[gate], square.at[gate, pl.ds(main, rest), :], sems.at[2 * gate + 1]
            )
        )
    for copy in copies:
        copy.start()

    def natural(places, values):
        return dot(dot(places[...], values).astype(bf16), to_natural[...]).astype(bf16)

    out[...] = natural(gather, output_rows[...])

    def right_product(left, matrix):
        return lax.dot_general(
            left, matrix, (((1,), (1,)), ((), ())), preferred_element_type=f32
        )

    found = jnp.zeros((rows, width), f32)
    for gate in range(4):
        copies[2 * gate].wait()
        copies[2 * gate + 1].wait()
        both = jnp.concatenate([late[gate], early[gate]], axis=0)
        found = found + right_product(both, square[gate])
    found = found * (in_rows[...].astype(f32) * KEEP_INPUT)
    d_out[...] = natural(unpack, found.astype(bf16))


def in_vmem():
    return pl.BlockSpec(memory_space=pltpu.VMEM)


def in_place():
    return pl.BlockSpec(memory_space=pl.ANY)


def places_for(*arrays):
    return [pltpu.VMEM(array.shape, array.dtype) for array in arrays]


def run_forward(wall, mixed, spread, collect, h_first, c_first, out_scale):
    steps_rows = spread.shape[0]
    rows, width = mixed.shape
    devices = wall.shape[0] // TILE
    all_kept = LONGEST * KINDS * LANES
    return pl.pallas_call(
        forward_kernel,
        out_shape=(
            jax.ShapeDtypeStruct((width, collect.shape[0]), bf16),
            jax.ShapeDtypeStruct((steps_rows, width), bf16),
            jax.ShapeDtypeStruct((4, devices, width), bf16),
            jax.ShapeDtypeStruct((all_kept, width), f32),
            jax.ShapeDtypeStruct((4, width, width), bf16),
        ),
        in_specs=[in_place()] * 7,
        out_specs=(in_vmem(),) * 3 + (in_place(),) * 2,
        scratch_shapes=places_for(mixed, spread, collect, h_first, c_first, out_scale)
        + [
            pltpu.VMEM((4, width, width), bf16),
            pltpu.VMEM((width, 4 * width), bf16),
            pltpu.VMEM((devices * TILE, width), bf16),
            pltpu.VMEM((width // 128, devices * TILE, 128), f32),
            pltpu.VMEM((steps_rows, 4 * width), f32),
            pltpu.VMEM((all_kept, width), f32),
            pltpu.VMEM((steps_rows, width), f32),
            pltpu.VMEM((steps_rows, width), f32),
            pltpu.SemaphoreType.DMA((6,)),
            pltpu.SemaphoreType.DMA((4,)),
            pltpu.SemaphoreType.DMA,
            pltpu.SemaphoreType.DMA,
            pltpu.SemaphoreType.DMA((5,)),
            pltpu.SemaphoreType.DMA((4,)),
        ],
        compiler_params=pltpu.CompilerParams(vmem_limit_bytes=VMEM_LIMIT),
        cost_estimate=pl.CostEstimate(
            flops=60_000_000_000, bytes_accessed=30_000_000, transcendentals=2_000_000
        ),
        name="forward",
    )(wall, mixed, spread, collect, h_first, c_first, out_scale)


def run_backward(turned, kept, coming, spread, collect, out_scale, carry, first_step):
    steps_rows = spread.shape[0]
    rows, width = collect.shape[0], coming.shape[1]
    results = [jax.ShapeDtypeStruct((4, rows, width), bf16)]
    if first_step > 0:
        results.append(jax.ShapeDtypeStruct((2 * LANES, width), f32))
    return pl.pallas_call(
        functools.partial(backward_kernel, first_step=first_step),
        out_shape=results,
        in_specs=[in_place()] * 7,
        out_specs=[in_vmem()] * len(results),
        scratch_shapes=places_for(coming, spread, collect, out_scale, carry)
        + [
            pltpu.VMEM((4 * width, width), bf16),
            pltpu.VMEM((steps_rows * KINDS, width), f32),
            pltpu.VMEM((steps_rows, width), f32),
            pltpu.VMEM((steps_rows, 4 * width), f32),
            pltpu.SemaphoreType.DMA((5,)),
            pltpu.SemaphoreType.DMA((4,)),
            pltpu.SemaphoreType.DMA((2,)),
        ],
        compiler_params=pltpu.CompilerParams(vmem_limit_bytes=VMEM_LIMIT),
        cost_estimate=pl.CostEstimate(
            flops=steps_rows // LANES * 1_500_000_000, bytes_accessed=20_000_000, transcendentals=0
        ),
        name="backward_late" if first_step else "backward_early",
    )(turned, kept, coming, spread, collect, out_scale, carry)


def run_gradient(core, mixed_all, hidden_all, mine, other, begin, devices, so_far=()):
    half, rows, columns = mine.shape
    line = 2 * half
    width = mixed_all.shape[0] // line
    size = -(-rows // 128) * 128
    if so_far:
        result = jax.ShapeDtypeStruct((devices, MESSAGE, 128), bf16)
    else:
        result = jax.ShapeDtypeStruct((width, columns), f32)
    return pl.pallas_call(
        functools.partial(gradient_kernel, begin=begin),
        out_shape=result,
        in_specs=[pl.BlockSpec(memory_space=pltpu.SMEM)]
        + [in_place()] * (4 + len(so_far)),
        out_specs=in_vmem(),
        scratch_shapes=[
            pltpu.VMEM((width, line * size), bf16),
            pltpu.VMEM((line * size, columns), bf16),
            pltpu.VMEM((devices, 2 * TILE, 128), f32),
            pltpu.VMEM((width, columns), f32),
            pltpu.SemaphoreType.DMA((line,)),
            pltpu.SemaphoreType.DMA((line,)),
            pltpu.SemaphoreType.DMA,
        ],
        compiler_params=pltpu.CompilerParams(vmem_limit_bytes=VMEM_LIMIT),
        cost_estimate=pl.CostEstimate(
            flops=5_000_000_000, bytes_accessed=12_000_000, transcendentals=0
        ),
        name="gradient_early" if so_far else "gradient_late",
    )(core, mixed_all, hidden_all, mine, other, *so_far)


def run_settle(got, scale, to_natural):
    wide, width = to_natural.shape
    devices = got.shape[0]
    return pl.pallas_call(
        settle_kernel,
        out_shape=(
            jax.ShapeDtypeStruct((OWN * 8, width), bf16),
            jax.ShapeDtypeStruct((devices, 128), f32),
        ),
        in_specs=[in_vmem()] * 3,
        out_specs=(in_vmem(),) * 2,
        scratch_shapes=[pltpu.VMEM((wide // 128, OWN * 8, 128), f32)],
        compiler_params=pltpu.CompilerParams(vmem_limit_bytes=VMEM_SMALL),
        name="settle",
    )(got, scale, to_natural)


def run_own(wall, ninth_in, late, early, in_rows, output_rows, gather, unpack, to_natural):
    width, natural = to_natural.shape
    rows = unpack.shape[0]
    return pl.pallas_call(
        own_kernel,
        out_shape=(jax.ShapeDtypeStruct((rows, natural), bf16),) * 2,
        in_specs=[in_place()] * 2 + [in_vmem()] * 7,
        out_specs=(in_vmem(),) * 2,
        scratch_shapes=[
            pltpu.VMEM((4, width, width), bf16),
            pltpu.SemaphoreType.DMA((8,)),
        ],
        compiler_params=pltpu.CompilerParams(vmem_limit_bytes=VMEM_LIMIT),
        cost_estimate=pl.CostEstimate(
            flops=8_000_000_000, bytes_accessed=15_000_000, transcendentals=0
        ),
        name="own",
    )(wall, ninth_in, late, early, in_rows, output_rows, gather, unpack, to_natural)


def split_exact(values):
    parts = []
    rest = values
    for _ in range(3):
        part = lax.reduce_precision(rest, 8, 7)
        parts.append(part.astype(bf16))
        rest = rest - part
    return parts


def body(
    inputs,
    d_out,
    h_start,
    c_start,
    pieces,
    in_mask,
    out_mask,
    w_mask,
    master,
    moment_one,
    moment_two,
):
    streams, steps, width = inputs.shape
    gates_n = 4 * width
    count_w = 2 * width * gates_n
    total = count_w + gates_n
    shard = master.shape[0]
    devices = lax.axis_size("batch")
    me = lax.axis_index("batch")
    wide = OWN * devices
    block = OWN * 2 * gates_n
    gap = block - shard
    most = gap * devices
    tokens = streams * steps
    rows_n = LATE + EARLY
    slot = -(-rows_n // 128) * 128
    line = 8
    lines = devices // line

    line_groups = [[line * q + m for m in range(line)] for q in range(lines)]
    column_groups = [
        [line * q + 2 * y + c for y in range(line // 2)] for q in range(lines) for c in range(2)
    ]
    twins = [(i, i ^ 1) for i in range(devices)]

    to_kept = one_hot(width, wide, lambda k, p: place_of(k, devices) == p)
    to_natural = one_hot(wide, width, lambda p, k: place_of(k, devices) == p)

    places = me * shard + lax.iota(jnp.int32, shard)
    recurrent = (places < count_w) & (places % (2 * gates_n) >= gates_n)
    scale_low = jnp.where(recurrent, w_mask.astype(bf16) * KEEP_RECURRENT, jnp.ones((), bf16))
    local_low = master.astype(bf16) * scale_low
    local_low = jnp.where(places < total, local_low, jnp.zeros((), bf16))

    def realigned(flat, following):
        joined = jnp.concatenate([flat, following])
        rows = lax.dynamic_slice(joined, (gap * me,), (block,)).reshape(OWN * 8, width)
        return dot(rows, to_kept).astype(bf16)

    before = [(i + 1, i) for i in range(devices - 1)]
    order = one_hot(
        OWN * 8,
        OWN * 8,
        lambda a, b: jnp.where(a < 64, (a % 8) * 8 + a // 8, 64 + a % 8) == b,
    )
    own = realigned(local_low, lax.ppermute(local_low[:most], "batch", before))
    own = dot(order, own).astype(bf16)
    own = jnp.concatenate([own[TILE * j : TILE * (j + 1)] for j in range(OWN)], axis=1)
    wall = lax.all_gather(own, "batch", axis=0, tiled=True)
    scales = realigned(scale_low, lax.ppermute(scale_low[:most], "batch", before))

    in_scale = in_mask.astype(f32) * KEEP_INPUT
    mixed = (inputs.astype(f32) * in_scale[:, None, :]).astype(bf16).reshape(tokens, width)
    spare = ((0, rows_n - tokens), (0, 0))
    mixed = dot(jnp.pad(mixed, spare), to_kept).astype(bf16)
    bias_place = place_of(jnp.int32(width), devices)
    column = lax.broadcasted_iota(jnp.int32, mixed.shape, 1)
    mixed = jnp.where(column == bias_place, jnp.ones((), bf16), mixed)
    coming = dot(jnp.pad(d_out.reshape(tokens, width), spare), to_kept).astype(bf16)
    small = jnp.concatenate(
        [h_start.astype(bf16)]
        + split_exact(c_start)
        + [in_mask.astype(bf16), out_mask.astype(bf16)],
        axis=0,
    )
    small = dot(small, to_kept)
    part = [small[streams * j : streams * (j + 1)] for j in range(6)]
    empty = jnp.zeros((LANES - streams, wide), f32)
    h_first = jnp.concatenate([part[0], empty], axis=0)
    c_first = jnp.concatenate([part[1] + part[2] + part[3], empty], axis=0)
    out_scale_kept = part[5] * KEEP_OUTPUT
    out_scale = jnp.concatenate(
        [out_scale_kept, out_scale_kept, jnp.zeros((LANES - 2 * streams, wide), f32)], axis=0
    )
    base = jnp.arange(streams, dtype=jnp.int32) * steps
    none = jnp.zeros((LANES - 2 * streams,), jnp.int32)
    begins = jnp.concatenate([base, base + pieces[:, 0], none])
    lengths = jnp.concatenate([pieces[:, 0], pieces[:, 1], none])
    ticks = lax.broadcasted_iota(jnp.int32, (LONGEST, LANES), 0)
    active = ticks < lengths[None, :]
    where = jnp.where(active, begins[None, :] + ticks, -1).reshape(-1)
    spread = (where[:, None] == lax.iota(jnp.int32, rows_n)[None, :]).astype(bf16)
    late_first = jnp.maximum(pieces[:, 0] - SPLIT, 0)
    late_base = jnp.arange(streams, dtype=jnp.int32) * LATE_BLOCK
    late_base = jnp.concatenate([late_base, late_base + late_first, none])
    early_base = LATE + SPLIT * jnp.arange(LANES, dtype=jnp.int32)
    packed = jnp.where(ticks < SPLIT, early_base[None] + ticks, late_base[None] + ticks - SPLIT)
    packed = jnp.where(active, packed, -1).reshape(-1)
    collect = (lax.iota(jnp.int32, slot)[:, None] == packed[None, :]).astype(bf16)
    pack = dot(collect, spread).astype(bf16)
    unpack = (
        lax.dot_general(spread, collect[:rows_n], (((0,), (1,)), ((), ())), preferred_element_type=f32)
    ).astype(bf16)
    mixed_turned = lax.dot_general(
        mixed, pack, (((0,), (1,)), ((), ())), preferred_element_type=f32
    ).astype(bf16)
    row_stream = lax.iota(jnp.int32, rows_n) // steps
    row_stream = (row_stream[:, None] == lax.iota(jnp.int32, streams)[None]).astype(bf16)
    in_rows = dot(pack[:rows_n], dot(row_stream, part[4].astype(bf16)).astype(bf16)).astype(bf16)

    begin = SPLIT * LANES
    ready = (wall, mixed, mixed_turned, coming, spread, collect, h_first, c_first, out_scale)
    ready += (in_rows, unpack, to_natural, scales, spread[:begin], spread[begin:])
    ready += (collect[LATE:rows_n, :begin], collect[:LATE, begin:], spread.T)
    ready = lax.optimization_barrier(ready)
    wall, mixed, mixed_turned, coming, spread, collect, h_first, c_first, out_scale = ready[:9]
    in_rows, unpack, to_natural, scales, spread_early, spread_late = ready[9:15]
    collect_early, collect_late, gather = ready[15:]
    mixed_all = lax.all_gather(
        mixed_turned, "batch", axis=0, tiled=True, axis_index_groups=line_groups
    )
    hidden_turned, output_rows, ninth_in, kept, turned = run_forward(
        wall, mixed, spread, collect, h_first, c_first, out_scale
    )
    hidden_turned, mixed_all = lax.optimization_barrier((hidden_turned, mixed_all))
    hidden_all = lax.all_gather(
        hidden_turned, "batch", axis=0, tiled=True, axis_index_groups=line_groups
    )
    late, carry = run_backward(
        turned, kept, coming, spread_late, collect_late, out_scale, out_scale, SPLIT
    )

    def exchange(rows):
        return lax.all_to_all(
            rows, "batch", 0, 0, tiled=True, axis_index_groups=column_groups
        )

    late_mine = exchange(late)
    (early,) = run_backward(
        turned, kept, coming, spread_early, collect_early, out_scale, carry, 0
    )
    late_mine, early = lax.optimization_barrier((late_mine, early))
    early_mine = exchange(early)
    core = (me % 2).reshape(1)
    so_far = run_gradient(
        core, mixed_all, hidden_all, late_mine, lax.ppermute(late_mine, "batch", twins), 0, devices
    )
    early_mine, so_far = lax.optimization_barrier((early_mine, so_far))
    message = run_gradient(
        core,
        mixed_all,
        hidden_all,
        early_mine,
        lax.ppermute(early_mine, "batch", twins),
        LATE,
        devices,
        (so_far,),
    )
    got = lax.all_to_all(message, "batch", 0, 0, tiled=True)

    d_rows, out_rows = run_own(
        wall, ninth_in, late, early, in_rows, output_rows, gather, unpack, to_natural
    )
    output = out_rows[:tokens].reshape(streams, steps, width)
    d_inputs = d_rows[:tokens].reshape(streams, steps, width)
    got, output, d_inputs = lax.optimization_barrier((got, output, d_inputs))

    home, squares = run_settle(got, scales, to_natural)
    squares = lax.all_to_all(squares, "batch", 0, 0, tiled=True)
    home = home.reshape(block)
    tail = lax.ppermute(home[block - most :], "batch", [(i, i + 1) for i in range(devices - 1)])
    grad_shard = lax.dynamic_slice(
        jnp.concatenate([tail, home]), (most - gap * me,), (shard,)
    ).astype(f32)
    grad_norm = jnp.sqrt(jnp.sum(squares[:, 0]))

    factor = jnp.minimum(1.0, CLIP_NORM / (grad_norm + 1e-06))
    clipped = grad_shard * factor
    moment_new = BETA_ONE * moment_one + (1.0 - BETA_ONE) * clipped
    second_new = BETA_TWO * moment_two + (1.0 - BETA_TWO) * clipped * clipped
    first_hat = moment_new / (1.0 - BETA_ONE**STEP)
    second_hat = second_new / (1.0 - BETA_TWO**STEP)
    master_new = master - LEARN_RATE * (
        first_hat / (jnp.sqrt(second_hat) + EPSILON) + WEIGHT_DECAY * master
    )
    return (output, d_inputs, moment_new, second_new, master_new, grad_norm)


def solution(mesh):
    placed = (
        P("batch", None, None),
        P("batch", None, None),
        P("batch", None),
        P("batch", None),
        P("batch", None),
        P("batch", None),
        P("batch", None),
        P("batch"),
        P("batch"),
        P("batch"),
        P("batch"),
    )
    return jax.shard_map(
        body,
        mesh=mesh,
        in_specs=placed,
        out_specs=(
            P("batch", None, None),
            P("batch", None, None),
            P("batch"),
            P("batch"),
            P("batch"),
            P(),
        ),
        check_vma=False,
    )
```

```python
import functools

import jax
import jax.numpy as jnp
from jax import lax
from jax.experimental import pallas as pl
from jax.experimental.pallas import tpu as pltpu
from jax.sharding import PartitionSpec as P

STEP = 10


LEARN_RATE = 0.03
BETA_ONE = 0.9
BETA_TWO = 0.999
WEIGHT_DECAY = 0.01
EPSILON = 1e-08
CLIP_NORM = 1.0
KEEP_INPUT = 4.0 / 3.0
KEEP_OUTPUT = 4.0 / 3.0
KEEP_RECURRENT = 2.0

LONGEST = 40
LANES = 8
TILE = 8
OWN = TILE + 1
KINDS = 6
SOON = 5
SPLIT = 10
LATE = 160
LATE_BLOCK = LATE // 3
EARLY = 64
EARLY_PLACE = 256
UNROLL_FORWARD = 3
UNROLL_BACKWARD = 4
MESSAGE = 88
VMEM_LIMIT = 60 * 2**20
VMEM_SMALL = 16 * 2**20

f32 = jnp.float32
bf16 = jnp.bfloat16


def dot(left, right):
    return lax.dot_general(left, right, (((1,), (0,)), ((), ())), preferred_element_type=f32)


def one_hot(rows, columns, wanted):
    row = lax.broadcasted_iota(jnp.int32, (rows, columns), 0)
    column = lax.broadcasted_iota(jnp.int32, (rows, columns), 1)
    return wanted(row, column).astype(bf16)


def place_of(natural, devices):
    owner, rest = natural // OWN, natural % OWN
    return jnp.where(rest < TILE, owner * TILE + rest, devices * TILE + owner)


def step_rows(step):
    return pl.ds(pl.multiple_of(step * LANES, LANES), LANES)


def kept_rows(step, kind):
    return pl.ds(pl.multiple_of((step * KINDS + kind) * LANES, LANES), LANES)


def fetch(sources, into, sems):
    copies = [
        pltpu.make_async_copy(source, place, sems.at[index])
        for index, (source, place) in enumerate(zip(sources, into))
    ]
    for copy in copies:
        copy.start()
    return copies


def forward_kernel(
    wall,
    mixed,
    spread,
    collect,
    h_first,
    c_first,
    out_scale,
    hidden_turned,
    output_rows,
    ninth_in,
    kept,
    turned,
    *refs,
):
    fetched, (square, w_rec, ninth, apart, pre, kept_here, hiddens, outs) = refs[:6], refs[6:14]
    sems_small, sems_in, sem_ninth, sem_rec, sems_kept, sems_turned = refs[14:]
    fetches = fetch((mixed, spread, collect, h_first, c_first, out_scale), fetched, sems_small)
    mixed, spread, collect, h_first, c_first, out_scale = fetched
    width = mixed.shape[1]
    main = wall.shape[0]
    devices = main // TILE
    gates_n = 4 * width

    copy_ninth = pltpu.make_async_copy(wall.at[:, pl.ds(2 * gates_n, width)], ninth, sem_ninth)
    copies_in = [
        pltpu.make_async_copy(
            wall.at[:, pl.ds(gate * width, width)],
            square.at[gate, pl.ds(0, main), :],
            sems_in.at[gate],
        )
        for gate in range(4)
    ]
    copy_rec = pltpu.make_async_copy(
        wall.at[:, pl.ds(gates_n, gates_n)], w_rec.at[pl.ds(0, main), :], sem_rec
    )
    copy_ninth.start()
    for copy in copies_in:
        copy.start()
    for copy in fetches:
        copy.wait()
    rows = dot(spread[...], mixed[...]).astype(bf16)
    copy_ninth.wait()
    for tile in range(width // 128):
        columns = pl.ds(tile * 128, 128)
        apart[tile] = ninth[:, columns].astype(f32)
        for gate in range(8):
            rest = apart[tile, pl.ds(gate, devices, stride=8), :].astype(bf16)
            if gate < 4:
                square[gate, pl.ds(main, devices), columns] = rest
                ninth_in[gate, :, columns] = rest
            else:
                there = pl.ds((gate - 4) * width + tile * 128, 128)
                w_rec[pl.ds(main, devices), there] = rest
    copy_rec.start()
    for gate in range(4):
        copies_in[gate].wait()
        pre[:, pl.ds(gate * width, width)] = dot(rows, square[gate])
    copy_rec.wait()
    scale = out_scale[...]
    soon = width - 128
    sizes = (256,) * (width // 256) + ((128,) if width % 256 else ())

    def step(index, carry):
        hidden, cell = carry
        at = step_rows(index)
        hiddens[at, :] = hidden
        low = hidden.astype(bf16)
        early = pre[at, :]
        for begin in range(0, soon, 512):
            here = slice(begin, min(begin + 512, soon))
            early = early + dot(low[:, here], w_rec[here, :])
        states = ([], [])
        begin = 0
        for size in sizes:
            lanes = pl.ds(begin, size)
            gates = []
            for gate in range(4):
                first = gate * width + begin
                late = dot(low[:, soon:], w_rec[pl.ds(soon, width - soon), pl.ds(first, size)])
                gates.append(early[:, first : first + size] + late)
            in_gate = jax.nn.sigmoid(gates[0])
            forget = jax.nn.sigmoid(gates[1])
            candid = jnp.tanh(gates[2])
            out_gate = jax.nn.sigmoid(gates[3])
            before = cell[:, begin : begin + size]
            cell_new = forget * before + in_gate * candid
            squash = jnp.tanh(cell_new)
            hidden_new = out_gate * squash
            outs[at, lanes] = hidden_new * scale[:, begin : begin + size]
            kept_here[kept_rows(index, 0), lanes] = out_gate * (1.0 - squash * squash)
            kept_here[kept_rows(index, 1), lanes] = candid * in_gate * (1.0 - in_gate)
            kept_here[kept_rows(index, 2), lanes] = before * forget * (1.0 - forget)
            kept_here[kept_rows(index, 3), lanes] = in_gate * (1.0 - candid * candid)
            kept_here[kept_rows(index, 4), lanes] = squash * out_gate * (1.0 - out_gate)
            kept_here[kept_rows(index, 5), lanes] = forget
            states[0].append(hidden_new)
            states[1].append(cell_new)
            begin += size
        return tuple(jnp.concatenate(state, axis=1) for state in states)

    turns = width // 128

    def copy_kept(part):
        size = turns * KINDS * LANES
        at = pl.ds(pl.multiple_of(part * size, LANES), size)
        return pltpu.make_async_copy(kept_here.at[at, :], kept.at[at, :], sems_kept.at[part])

    def copy_turned(gate):
        return pltpu.make_async_copy(square.at[gate], turned.at[gate], sems_turned.at[gate])

    def part(gate, carry):
        def turning(count, carry):
            columns = pl.ds(pl.multiple_of(gate * width + count * 128, 128), 128)
            into = pl.ds(pl.multiple_of(count * 128, 128), 128)
            square[gate, into, :] = w_rec[:, columns].T
            return step(gate * turns + count, carry)

        carry = lax.fori_loop(0, turns, turning, carry, unroll=UNROLL_FORWARD)
        copy_kept(gate).start()
        copy_turned(gate).start()
        return carry

    carry = lax.fori_loop(0, 4, part, (h_first[...], c_first[...]))
    lax.fori_loop(4 * turns, LONGEST, step, carry, unroll=UNROLL_FORWARD)
    begin = 4 * turns * KINDS * LANES
    rest = pl.ds(begin, kept_here.shape[0] - begin)
    last = pltpu.make_async_copy(kept_here.at[rest, :], kept.at[rest, :], sems_kept.at[4])
    last.start()
    hidden_turned[...] = lax.dot_general(
        hiddens[...].astype(bf16),
        collect[...],
        (((0,), (1,)), ((), ())),
        preferred_element_type=f32,
    ).astype(bf16)
    output_rows[...] = outs[...].astype(bf16)
    for gate in range(4):
        copy_kept(gate).wait()
        copy_turned(gate).wait()
    last.wait()


def backward_kernel(
    turned,
    kept,
    coming,
    spread,
    collect,
    out_scale,
    carry_in,
    gate_rows,
    *refs,
    first_step,
):
    carry_out = refs[0]
    *fetched, w_turned, kept_here, come, dgates, sems_small, sems_turned, sems_kept = refs[-12:]
    fetches = fetch((coming, spread, collect, out_scale, carry_in), fetched, sems_small)
    coming, spread, collect, out_scale, carry_in = fetched
    width = coming.shape[1]
    steps = spread.shape[0] // LANES
    size = KINDS * LANES

    def copy_kept(part):
        begin, count = ((steps - SOON) * size, SOON * size) if part == 0 else (
            0,
            (steps - SOON) * size,
        )
        return pltpu.make_async_copy(
            kept.at[pl.ds(first_step * size + begin, count), :],
            kept_here.at[pl.ds(begin, count), :],
            sems_kept.at[part],
        )

    copies = [
        pltpu.make_async_copy(
            turned.at[gate], w_turned.at[pl.ds(gate * width, width), :], sems_turned.at[gate]
        )
        for gate in range(4)
    ]
    copy_kept(0).start()
    for copy in copies:
        copy.start()
    for copy in fetches:
        copy.wait()
    come[...] = dot(spread[...], coming[...])
    scale = out_scale[...]

    def gradients(index, carry):
        dh_next, dc_next = carry
        at = step_rows(index)
        grad_h = come[at, :] * scale + dh_next
        grad_c = dc_next + grad_h * kept_here[kept_rows(index, 0), :]
        grads = jnp.concatenate(
            [
                grad_c * kept_here[kept_rows(index, 1), :],
                grad_c * kept_here[kept_rows(index, 2), :],
                grad_c * kept_here[kept_rows(index, 3), :],
                grad_h * kept_here[kept_rows(index, 4), :],
            ],
            axis=1,
        )
        dgates[at, :] = grads
        return (grads, grad_c * kept_here[kept_rows(index, 5), :])

    def step(index, carry):
        grads, dc_next = gradients(index, carry)
        return (dot(grads.astype(bf16), w_turned[...]), dc_next)

    def run(last, count, carry):
        return lax.fori_loop(
            0, count, lambda back, c: step(last - back, c), carry, unroll=UNROLL_BACKWARD
        )

    copy_kept(0).wait()
    if first_step > 0:
        carry = (jnp.zeros((LANES, width), f32),) * 2
    else:
        carry = (carry_in[pl.ds(0, LANES), :], carry_in[pl.ds(LANES, LANES), :])
    grads, dc_next = gradients(steps - 1, carry)
    grads = grads.astype(bf16)
    dh_next = jnp.zeros((LANES, width), f32)
    for gate in range(4):
        copies[gate].wait()
        here = slice(gate * width, (gate + 1) * width)
        dh_next = dh_next + dot(grads[:, here], w_turned[here, :])
    copy_kept(1).start()
    carry = run(steps - 2, SOON - 1, (dh_next, dc_next))
    copy_kept(1).wait()
    if first_step > 0:
        carry = run(steps - SOON - 1, steps - SOON, carry)
        carry_out[pl.ds(0, LANES), :] = carry[0]
        carry_out[pl.ds(LANES, LANES), :] = carry[1]
    else:
        carry = run(steps - SOON - 1, steps - SOON - 1, carry)
        gradients(0, carry)
    for gate in range(4):
        columns = pl.ds(gate * width, width)
        gate_rows[gate] = dot(collect[...], dgates[:, columns].astype(bf16)).astype(bf16)


def gradient_kernel(
    core,
    mixed_all,
    hidden_all,
    mine,
    other,
    *refs,
    begin,
):
    result, left, right, ninth, before, sems_left, sems_right, sem_before = refs[-8:]
    so_far = refs[:-8]
    half, rows, columns = mine.shape
    line = 2 * half
    width, size = left.shape[0], left.shape[1] // line
    which = core[0]

    def copies_left(source):
        found = []
        for place in range(line):
            chip, twin = place % half, place // half
            block = 2 * chip + (which if twin == 0 else 1 - which)
            found.append(
                pltpu.make_async_copy(
                    source.at[pl.ds(block * width, width), pl.ds(begin, size)],
                    left.at[:, pl.ds(place * size, size)],
                    sems_left.at[place],
                )
            )
        return found

    @pl.when(which == 0)
    def _():
        for copy in copies_left(mixed_all):
            copy.start()

    @pl.when(which != 0)
    def _():
        for copy in copies_left(hidden_all):
            copy.start()

    copies_right = [
        pltpu.make_async_copy(
            (mine if place < half else other).at[place % half],
            right.at[pl.ds(place * size, rows), :],
            sems_right.at[place],
        )
        for place in range(line)
    ]
    for copy in copies_right:
        copy.start()
    if so_far:
        copy_before = pltpu.make_async_copy(so_far[0], before, sem_before)
        copy_before.start()
    if rows < size:
        for place in range(line):
            right[pl.ds(place * size + rows, size - rows), :] = jnp.zeros(
                (size - rows, columns), bf16
            )
    for copy in copies_left(mixed_all) + copies_right:
        copy.wait()
    grad = dot(left[...], right[...])
    if not so_far:
        result[...] = grad
        return
    copy_before.wait()
    devices = result.shape[0]
    main = devices * TILE
    tiles = columns // 128
    ninth[...] = jnp.zeros(ninth.shape, f32)
    for tile in range(0, tiles, 2):
        parts = []
        for place in range(tile, min(tile + 2, tiles)):
            here = grad[:, place * 128 : (place + 1) * 128] + before[:, pl.ds(place * 128, 128)]
            parts.append(here[:main].reshape(devices, TILE, 128))
            ninth[:, place, :] = here[main:]
        if tile + 2 > tiles:
            parts.append(ninth[...])
        rows = jnp.concatenate(parts, axis=1)
        result[:, pl.ds(tile * TILE, rows.shape[1]), :] = rows.astype(bf16)


def settle_kernel(got, scale, to_natural, home, squares, placed):
    devices = got.shape[0]
    tiles = placed.shape[0]
    line = 8
    half = line // 2
    for source in range(line):
        gate = (source % 2) * half + source // 2
        found = got[source].astype(f32)
        for index in range(source + line, devices, line):
            found = found + got[index].astype(f32)
        for tile in range(tiles):
            placed[tile, pl.ds(gate, TILE, stride=8), :] = found[tile * TILE : (tile + 1) * TILE]
            ninth = OWN * TILE + tile
            placed[tile, pl.ds(TILE * 8 + gate, 1), :] = found[ninth : ninth + 1]
    values = jnp.concatenate([placed[tile] for tile in range(tiles)], axis=1)
    values = values * scale[...].astype(f32)
    total = jnp.sum(jnp.sum(values * values, axis=0, keepdims=True), axis=1, keepdims=True)
    squares[...] = jnp.broadcast_to(total, squares.shape)
    home[...] = dot(values.astype(bf16), to_natural[...]).astype(bf16)


def own_kernel(
    wall,
    ninth_in,
    late,
    early,
    in_rows,
    output_rows,
    gather,
    unpack,
    to_natural,
    d_out,
    out,
    square,
    sems,
):
    width = in_rows.shape[1]
    rows = in_rows.shape[0]
    main = wall.shape[0]
    rest = width - main
    copies = []
    for gate in range(4):
        copies.append(
            pltpu.make_async_copy(
                wall.at[:, pl.ds(gate * width, width)],
                square.at[gate, pl.ds(0, main), :],
                sems.at[2 * gate],
            )
        )
        copies.append(
            pltpu.make_async_copy(
                ninth_in.at[gate], square.at[gate, pl.ds(main, rest), :], sems.at[2 * gate + 1]
            )
        )
    for copy in copies:
        copy.start()

    def natural(places, values):
        return dot(dot(places[...], values).astype(bf16), to_natural[...]).astype(bf16)

    out[...] = natural(gather, output_rows[...])

    def right_product(left, matrix):
        return lax.dot_general(
            left, matrix, (((1,), (1,)), ((), ())), preferred_element_type=f32
        )

    found = jnp.zeros((rows, width), f32)
    for gate in range(4):
        copies[2 * gate].wait()
        copies[2 * gate + 1].wait()
        both = jnp.concatenate([late[gate], early[gate]], axis=0)
        found = found + right_product(both, square[gate])
    found = found * (in_rows[...].astype(f32) * KEEP_INPUT)
    d_out[...] = natural(unpack, found.astype(bf16))


def in_vmem():
    return pl.BlockSpec(memory_space=pltpu.VMEM)


def in_place():
    return pl.BlockSpec(memory_space=pl.ANY)


def places_for(*arrays):
    return [pltpu.VMEM(array.shape, array.dtype) for array in arrays]


def run_forward(wall, mixed, spread, collect, h_first, c_first, out_scale):
    steps_rows = spread.shape[0]
    rows, width = mixed.shape
    devices = wall.shape[0] // TILE
    all_kept = LONGEST * KINDS * LANES
    return pl.pallas_call(
        forward_kernel,
        out_shape=(
            jax.ShapeDtypeStruct((width, collect.shape[0]), bf16),
            jax.ShapeDtypeStruct((steps_rows, width), bf16),
            jax.ShapeDtypeStruct((4, devices, width), bf16),
            jax.ShapeDtypeStruct((all_kept, width), f32),
            jax.ShapeDtypeStruct((4, width, width), bf16),
        ),
        in_specs=[in_place()] * 7,
        out_specs=(in_vmem(),) * 3 + (in_place(),) * 2,
        scratch_shapes=places_for(mixed, spread, collect, h_first, c_first, out_scale)
        + [
            pltpu.VMEM((4, width, width), bf16),
            pltpu.VMEM((width, 4 * width), bf16),
            pltpu.VMEM((devices * TILE, width), bf16),
            pltpu.VMEM((width // 128, devices * TILE, 128), f32),
            pltpu.VMEM((steps_rows, 4 * width), f32),
            pltpu.VMEM((all_kept, width), f32),
            pltpu.VMEM((steps_rows, width), f32),
            pltpu.VMEM((steps_rows, width), f32),
            pltpu.SemaphoreType.DMA((6,)),
            pltpu.SemaphoreType.DMA((4,)),
            pltpu.SemaphoreType.DMA,
            pltpu.SemaphoreType.DMA,
            pltpu.SemaphoreType.DMA((5,)),
            pltpu.SemaphoreType.DMA((4,)),
        ],
        compiler_params=pltpu.CompilerParams(vmem_limit_bytes=VMEM_LIMIT),
        cost_estimate=pl.CostEstimate(
            flops=60_000_000_000, bytes_accessed=30_000_000, transcendentals=2_000_000
        ),
        name="forward",
    )(wall, mixed, spread, collect, h_first, c_first, out_scale)


def run_backward(turned, kept, coming, spread, collect, out_scale, carry, first_step):
    steps_rows = spread.shape[0]
    rows, width = collect.shape[0], coming.shape[1]
    results = [jax.ShapeDtypeStruct((4, rows, width), bf16)]
    if first_step > 0:
        results.append(jax.ShapeDtypeStruct((2 * LANES, width), f32))
    return pl.pallas_call(
        functools.partial(backward_kernel, first_step=first_step),
        out_shape=results,
        in_specs=[in_place()] * 7,
        out_specs=[in_vmem()] * len(results),
        scratch_shapes=places_for(coming, spread, collect, out_scale, carry)
        + [
            pltpu.VMEM((4 * width, width), bf16),
            pltpu.VMEM((steps_rows * KINDS, width), f32),
            pltpu.VMEM((steps_rows, width), f32),
            pltpu.VMEM((steps_rows, 4 * width), f32),
            pltpu.SemaphoreType.DMA((5,)),
            pltpu.SemaphoreType.DMA((4,)),
            pltpu.SemaphoreType.DMA((2,)),
        ],
        compiler_params=pltpu.CompilerParams(vmem_limit_bytes=VMEM_LIMIT),
        cost_estimate=pl.CostEstimate(
            flops=steps_rows // LANES * 1_500_000_000, bytes_accessed=20_000_000, transcendentals=0
        ),
        name="backward_late" if first_step else "backward_early",
    )(turned, kept, coming, spread, collect, out_scale, carry)


def run_gradient(core, mixed_all, hidden_all, mine, other, begin, devices, so_far=()):
    half, rows, columns = mine.shape
    line = 2 * half
    width = mixed_all.shape[0] // line
    size = -(-rows // 128) * 128
    if so_far:
        result = jax.ShapeDtypeStruct((devices, MESSAGE, 128), bf16)
    else:
        result = jax.ShapeDtypeStruct((width, columns), f32)
    return pl.pallas_call(
        functools.partial(gradient_kernel, begin=begin),
        out_shape=result,
        in_specs=[pl.BlockSpec(memory_space=pltpu.SMEM)]
        + [in_place()] * (4 + len(so_far)),
        out_specs=in_vmem(),
        scratch_shapes=[
            pltpu.VMEM((width, line * size), bf16),
            pltpu.VMEM((line * size, columns), bf16),
            pltpu.VMEM((devices, 2 * TILE, 128), f32),
            pltpu.VMEM((width, columns), f32),
            pltpu.SemaphoreType.DMA((line,)),
            pltpu.SemaphoreType.DMA((line,)),
            pltpu.SemaphoreType.DMA,
        ],
        compiler_params=pltpu.CompilerParams(vmem_limit_bytes=VMEM_LIMIT),
        cost_estimate=pl.CostEstimate(
            flops=5_000_000_000, bytes_accessed=12_000_000, transcendentals=0
        ),
        name="gradient_early" if so_far else "gradient_late",
    )(core, mixed_all, hidden_all, mine, other, *so_far)


def run_settle(got, scale, to_natural):
    wide, width = to_natural.shape
    devices = got.shape[0]
    return pl.pallas_call(
        settle_kernel,
        out_shape=(
            jax.ShapeDtypeStruct((OWN * 8, width), bf16),
            jax.ShapeDtypeStruct((devices, 128), f32),
        ),
        in_specs=[in_vmem()] * 3,
        out_specs=(in_vmem(),) * 2,
        scratch_shapes=[pltpu.VMEM((wide // 128, OWN * 8, 128), f32)],
        compiler_params=pltpu.CompilerParams(vmem_limit_bytes=VMEM_SMALL),
        name="settle",
    )(got, scale, to_natural)


def run_own(wall, ninth_in, late, early, in_rows, output_rows, gather, unpack, to_natural):
    width, natural = to_natural.shape
    rows = unpack.shape[0]
    return pl.pallas_call(
        own_kernel,
        out_shape=(jax.ShapeDtypeStruct((rows, natural), bf16),) * 2,
        in_specs=[in_place()] * 2 + [in_vmem()] * 7,
        out_specs=(in_vmem(),) * 2,
        scratch_shapes=[
            pltpu.VMEM((4, width, width), bf16),
            pltpu.SemaphoreType.DMA((8,)),
        ],
        compiler_params=pltpu.CompilerParams(vmem_limit_bytes=VMEM_LIMIT),
        cost_estimate=pl.CostEstimate(
            flops=8_000_000_000, bytes_accessed=15_000_000, transcendentals=0
        ),
        name="own",
    )(wall, ninth_in, late, early, in_rows, output_rows, gather, unpack, to_natural)


def split_exact(values):
    parts = []
    rest = values
    for _ in range(3):
        part = lax.reduce_precision(rest, 8, 7)
        parts.append(part.astype(bf16))
        rest = rest - part
    return parts


def body(
    inputs,
    d_out,
    h_start,
    c_start,
    pieces,
    in_mask,
    out_mask,
    w_mask,
    master,
    moment_one,
    moment_two,
):
    streams, steps, width = inputs.shape
    gates_n = 4 * width
    count_w = 2 * width * gates_n
    total = count_w + gates_n
    shard = master.shape[0]
    devices = lax.axis_size("batch")
    me = lax.axis_index("batch")
    wide = OWN * devices
    block = OWN * 2 * gates_n
    gap = block - shard
    most = gap * devices
    tokens = streams * steps
    rows_n = LATE + EARLY
    slot = EARLY_PLACE + -(-EARLY // 128) * 128
    line = 8
    lines = devices // line

    line_groups = [[line * q + m for m in range(line)] for q in range(lines)]
    column_groups = [
        [line * q + 2 * y + c for y in range(line // 2)] for q in range(lines) for c in range(2)
    ]
    twins = [(i, i ^ 1) for i in range(devices)]

    to_kept = one_hot(width, wide, lambda k, p: place_of(k, devices) == p)
    to_natural = one_hot(wide, width, lambda p, k: place_of(k, devices) == p)

    places = me * shard + lax.iota(jnp.int32, shard)
    recurrent = (places < count_w) & (places % (2 * gates_n) >= gates_n)
    scale_low = jnp.where(recurrent, w_mask.astype(bf16) * KEEP_RECURRENT, jnp.ones((), bf16))
    local_low = master.astype(bf16) * scale_low
    local_low = jnp.where(places < total, local_low, jnp.zeros((), bf16))

    def realigned(flat, following):
        joined = jnp.concatenate([flat, following])
        rows = lax.dynamic_slice(joined, (gap * me,), (block,)).reshape(OWN * 8, width)
        return dot(rows, to_kept).astype(bf16)

    before = [(i + 1, i) for i in range(devices - 1)]
    order = one_hot(
        OWN * 8,
        OWN * 8,
        lambda a, b: jnp.where(a < 64, (a % 8) * 8 + a // 8, 64 + a % 8) == b,
    )
    own = realigned(local_low, lax.ppermute(local_low[:most], "batch", before))
    own = dot(order, own).astype(bf16)
    own = jnp.concatenate([own[TILE * j : TILE * (j + 1)] for j in range(OWN)], axis=1)
    wall = lax.all_gather(own, "batch", axis=0, tiled=True)
    scales = realigned(scale_low, lax.ppermute(scale_low[:most], "batch", before))

    in_scale = in_mask.astype(f32) * KEEP_INPUT
    mixed = (inputs.astype(f32) * in_scale[:, None, :]).astype(bf16).reshape(tokens, width)
    spare = ((0, rows_n - tokens), (0, 0))
    mixed = dot(jnp.pad(mixed, spare), to_kept).astype(bf16)
    bias_place = place_of(jnp.int32(width), devices)
    column = lax.broadcasted_iota(jnp.int32, mixed.shape, 1)
    mixed = jnp.where(column == bias_place, jnp.ones((), bf16), mixed)
    coming = dot(jnp.pad(d_out.reshape(tokens, width), spare), to_kept).astype(bf16)
    small = jnp.concatenate(
        [h_start.astype(bf16)]
        + split_exact(c_start)
        + [in_mask.astype(bf16), out_mask.astype(bf16)],
        axis=0,
    )
    small = dot(small, to_kept)
    part = [small[streams * j : streams * (j + 1)] for j in range(6)]
    empty = jnp.zeros((LANES - streams, wide), f32)
    h_first = jnp.concatenate([part[0], empty], axis=0)
    c_first = jnp.concatenate([part[1] + part[2] + part[3], empty], axis=0)
    out_scale_kept = part[5] * KEEP_OUTPUT
    out_scale = jnp.concatenate(
        [out_scale_kept, out_scale_kept, jnp.zeros((LANES - 2 * streams, wide), f32)], axis=0
    )
    base = jnp.arange(streams, dtype=jnp.int32) * steps
    none = jnp.zeros((LANES - 2 * streams,), jnp.int32)
    begins = jnp.concatenate([base, base + pieces[:, 0], none])
    lengths = jnp.concatenate([pieces[:, 0], pieces[:, 1], none])
    ticks = lax.broadcasted_iota(jnp.int32, (LONGEST, LANES), 0)
    active = ticks < lengths[None, :]
    where = jnp.where(active, begins[None, :] + ticks, -1).reshape(-1)
    spread = (where[:, None] == lax.iota(jnp.int32, rows_n)[None, :]).astype(bf16)
    late_first = jnp.maximum(pieces[:, 0] - SPLIT, 0)
    late_base = jnp.arange(streams, dtype=jnp.int32) * LATE_BLOCK
    late_base = jnp.concatenate([late_base, late_base + late_first, none])
    early_base = EARLY_PLACE + SPLIT * jnp.arange(LANES, dtype=jnp.int32)
    packed = jnp.where(ticks < SPLIT, early_base[None] + ticks, late_base[None] + ticks - SPLIT)
    packed = jnp.where(active, packed, -1).reshape(-1)
    collect = (lax.iota(jnp.int32, slot)[:, None] == packed[None, :]).astype(bf16)
    collect_late, collect_early = collect[:LATE], collect[EARLY_PLACE : EARLY_PLACE + EARLY]
    together = jnp.concatenate([collect_late, collect_early], axis=0)
    pack = dot(collect, spread).astype(bf16)
    unpack = (
        lax.dot_general(spread, together, (((0,), (1,)), ((), ())), preferred_element_type=f32)
    ).astype(bf16)
    mixed_turned = lax.dot_general(
        mixed, pack, (((0,), (1,)), ((), ())), preferred_element_type=f32
    ).astype(bf16)
    row_stream = lax.iota(jnp.int32, rows_n) // steps
    row_stream = (row_stream[:, None] == lax.iota(jnp.int32, streams)[None]).astype(bf16)
    in_rows = dot(unpack.T, dot(row_stream, part[4].astype(bf16)).astype(bf16)).astype(bf16)

    begin = SPLIT * LANES
    ready = (wall, mixed, mixed_turned, coming, spread, collect, h_first, c_first, out_scale)
    ready += (in_rows, unpack, to_natural, scales, spread[:begin], spread[begin:])
    ready += (collect_early[:, :begin], collect_late[:, begin:], spread.T)
    ready = lax.optimization_barrier(ready)
    wall, mixed, mixed_turned, coming, spread, collect, h_first, c_first, out_scale = ready[:9]
    in_rows, unpack, to_natural, scales, spread_early, spread_late = ready[9:15]
    collect_early, collect_late, gather = ready[15:]
    mixed_all = lax.all_gather(
        mixed_turned, "batch", axis=0, tiled=True, axis_index_groups=line_groups
    )
    hidden_turned, output_rows, ninth_in, kept, turned = run_forward(
        wall, mixed, spread, collect, h_first, c_first, out_scale
    )
    hidden_turned, mixed_all = lax.optimization_barrier((hidden_turned, mixed_all))
    hidden_all = lax.all_gather(
        hidden_turned, "batch", axis=0, tiled=True, axis_index_groups=line_groups
    )
    late, carry = run_backward(
        turned, kept, coming, spread_late, collect_late, out_scale, out_scale, SPLIT
    )

    def exchange(rows):
        return lax.all_to_all(
            rows, "batch", 0, 0, tiled=True, axis_index_groups=column_groups
        )

    late_mine = exchange(late)
    (early,) = run_backward(
        turned, kept, coming, spread_early, collect_early, out_scale, carry, 0
    )
    late_mine, early = lax.optimization_barrier((late_mine, early))
    early_mine = exchange(early)
    core = (me % 2).reshape(1)
    so_far = run_gradient(
        core, mixed_all, hidden_all, late_mine, lax.ppermute(late_mine, "batch", twins), 0, devices
    )
    early_mine, so_far = lax.optimization_barrier((early_mine, so_far))
    message = run_gradient(
        core,
        mixed_all,
        hidden_all,
        early_mine,
        lax.ppermute(early_mine, "batch", twins),
        EARLY_PLACE,
        devices,
        (so_far,),
    )
    got = lax.all_to_all(message, "batch", 0, 0, tiled=True)

    d_rows, out_rows = run_own(
        wall, ninth_in, late, early, in_rows, output_rows, gather, unpack, to_natural
    )
    output = out_rows[:tokens].reshape(streams, steps, width)
    d_inputs = d_rows[:tokens].reshape(streams, steps, width)
    got, output, d_inputs = lax.optimization_barrier((got, output, d_inputs))

    home, squares = run_settle(got, scales, to_natural)
    squares = lax.all_to_all(squares, "batch", 0, 0, tiled=True)
    home = home.reshape(block)
    tail = lax.ppermute(home[block - most :], "batch", [(i, i + 1) for i in range(devices - 1)])
    grad_shard = lax.dynamic_slice(
        jnp.concatenate([tail, home]), (most - gap * me,), (shard,)
    ).astype(f32)
    grad_norm = jnp.sqrt(jnp.sum(squares[:, 0]))

    factor = jnp.minimum(1.0, CLIP_NORM / (grad_norm + 1e-06))
    clipped = grad_shard * factor
    moment_new = BETA_ONE * moment_one + (1.0 - BETA_ONE) * clipped
    second_new = BETA_TWO * moment_two + (1.0 - BETA_TWO) * clipped * clipped
    first_hat = moment_new / (1.0 - BETA_ONE**STEP)
    second_hat = second_new / (1.0 - BETA_TWO**STEP)
    master_new = master - LEARN_RATE * (
        first_hat / (jnp.sqrt(second_hat) + EPSILON) + WEIGHT_DECAY * master
    )
    return (output, d_inputs, moment_new, second_new, master_new, grad_norm)


def solution(mesh):
    placed = (
        P("batch", None, None),
        P("batch", None, None),
        P("batch", None),
        P("batch", None),
        P("batch", None),
        P("batch", None),
        P("batch", None),
        P("batch"),
        P("batch"),
        P("batch"),
        P("batch"),
    )
    return jax.shard_map(
        body,
        mesh=mesh,
        in_specs=placed,
        out_specs=(
            P("batch", None, None),
            P("batch", None, None),
            P("batch"),
            P("batch"),
            P("batch"),
            P(),
        ),
        check_vma=False,
    )
```

```python
import functools

import jax
import jax.numpy as jnp
from jax import lax
from jax.experimental import pallas as pl
from jax.experimental.pallas import tpu as pltpu
from jax.sharding import PartitionSpec as P

STEP = 10


LEARN_RATE = 0.03
BETA_ONE = 0.9
BETA_TWO = 0.999
WEIGHT_DECAY = 0.01
EPSILON = 1e-08
CLIP_NORM = 1.0
KEEP_INPUT = 4.0 / 3.0
KEEP_OUTPUT = 4.0 / 3.0
KEEP_RECURRENT = 2.0

LONGEST = 40
LANES = 8
TILE = 8
OWN = TILE + 1
KINDS = 6
SOON = 5
SPLIT = 10
LATE = 160
LATE_BLOCK = LATE // 3
EARLY = 64
UNROLL_FORWARD = 3
UNROLL_BACKWARD = 4
MESSAGE = 88
VMEM_LIMIT = 60 * 2**20
VMEM_SMALL = 16 * 2**20

f32 = jnp.float32
bf16 = jnp.bfloat16


def dot(left, right):
    return lax.dot_general(left, right, (((1,), (0,)), ((), ())), preferred_element_type=f32)


def one_hot(rows, columns, wanted):
    row = lax.broadcasted_iota(jnp.int32, (rows, columns), 0)
    column = lax.broadcasted_iota(jnp.int32, (rows, columns), 1)
    return wanted(row, column).astype(bf16)


def place_of(natural, devices):
    owner, rest = natural // OWN, natural % OWN
    return jnp.where(rest < TILE, owner * TILE + rest, devices * TILE + owner)


def step_rows(step):
    return pl.ds(pl.multiple_of(step * LANES, LANES), LANES)


def kept_rows(step, kind):
    return pl.ds(pl.multiple_of((step * KINDS + kind) * LANES, LANES), LANES)


def fetch(sources, into, sems):
    copies = [
        pltpu.make_async_copy(source, place, sems.at[index])
        for index, (source, place) in enumerate(zip(sources, into))
    ]
    for copy in copies:
        copy.start()
    return copies


def forward_kernel(
    wall,
    mixed,
    spread,
    collect,
    h_first,
    c_first,
    out_scale,
    hidden_rows,
    output_rows,
    ninth_in,
    kept,
    turned,
    *refs,
):
    fetched, (square, w_rec, ninth, apart, pre, kept_here, hiddens, outs) = refs[:6], refs[6:14]
    sems_small, sems_in, sem_ninth, sem_rec, sems_kept, sems_turned = refs[14:]
    fetches = fetch((mixed, spread, collect, h_first, c_first, out_scale), fetched, sems_small)
    mixed, spread, collect, h_first, c_first, out_scale = fetched
    width = mixed.shape[1]
    main = wall.shape[0]
    devices = main // TILE
    gates_n = 4 * width

    copy_ninth = pltpu.make_async_copy(wall.at[:, pl.ds(2 * gates_n, width)], ninth, sem_ninth)
    copies_in = [
        pltpu.make_async_copy(
            wall.at[:, pl.ds(gate * width, width)],
            square.at[gate, pl.ds(0, main), :],
            sems_in.at[gate],
        )
        for gate in range(4)
    ]
    copy_rec = pltpu.make_async_copy(
        wall.at[:, pl.ds(gates_n, gates_n)], w_rec.at[pl.ds(0, main), :], sem_rec
    )
    copy_ninth.start()
    for copy in copies_in:
        copy.start()
    for copy in fetches:
        copy.wait()
    rows = dot(spread[...], mixed[...]).astype(bf16)
    copy_ninth.wait()
    for tile in range(width // 128):
        columns = pl.ds(tile * 128, 128)
        apart[tile] = ninth[:, columns].astype(f32)
        for gate in range(8):
            rest = apart[tile, pl.ds(gate, devices, stride=8), :].astype(bf16)
            if gate < 4:
                square[gate, pl.ds(main, devices), columns] = rest
                ninth_in[gate, :, columns] = rest
            else:
                there = pl.ds((gate - 4) * width + tile * 128, 128)
                w_rec[pl.ds(main, devices), there] = rest
    copy_rec.start()
    for gate in range(4):
        copies_in[gate].wait()
        pre[:, pl.ds(gate * width, width)] = dot(rows, square[gate])
    copy_rec.wait()
    scale = out_scale[...]
    soon = width - 128
    sizes = (256,) * (width // 256) + ((128,) if width % 256 else ())

    def step(index, carry):
        hidden, cell = carry
        at = step_rows(index)
        hiddens[at, :] = hidden
        low = hidden.astype(bf16)
        early = pre[at, :]
        for begin in range(0, soon, 512):
            here = slice(begin, min(begin + 512, soon))
            early = early + dot(low[:, here], w_rec[here, :])
        states = ([], [])
        begin = 0
        for size in sizes:
            lanes = pl.ds(begin, size)
            gates = []
            for gate in range(4):
                first = gate * width + begin
                late = dot(low[:, soon:], w_rec[pl.ds(soon, width - soon), pl.ds(first, size)])
                gates.append(early[:, first : first + size] + late)
            in_gate = jax.nn.sigmoid(gates[0])
            forget = jax.nn.sigmoid(gates[1])
            candid = jnp.tanh(gates[2])
            out_gate = jax.nn.sigmoid(gates[3])
            before = cell[:, begin : begin + size]
            cell_new = forget * before + in_gate * candid
            squash = jnp.tanh(cell_new)
            hidden_new = out_gate * squash
            outs[at, lanes] = hidden_new * scale[:, begin : begin + size]
            kept_here[kept_rows(index, 0), lanes] = out_gate * (1.0 - squash * squash)
            kept_here[kept_rows(index, 1), lanes] = candid * in_gate * (1.0 - in_gate)
            kept_here[kept_rows(index, 2), lanes] = before * forget * (1.0 - forget)
            kept_here[kept_rows(index, 3), lanes] = in_gate * (1.0 - candid * candid)
            kept_here[kept_rows(index, 4), lanes] = squash * out_gate * (1.0 - out_gate)
            kept_here[kept_rows(index, 5), lanes] = forget
            states[0].append(hidden_new)
            states[1].append(cell_new)
            begin += size
        return tuple(jnp.concatenate(state, axis=1) for state in states)

    turns = width // 128

    def copy_kept(part):
        size = turns * KINDS * LANES
        at = pl.ds(pl.multiple_of(part * size, LANES), size)
        return pltpu.make_async_copy(kept_here.at[at, :], kept.at[at, :], sems_kept.at[part])

    def copy_turned(gate):
        return pltpu.make_async_copy(square.at[gate], turned.at[gate], sems_turned.at[gate])

    def part(gate, carry):
        def turning(count, carry):
            columns = pl.ds(pl.multiple_of(gate * width + count * 128, 128), 128)
            into = pl.ds(pl.multiple_of(count * 128, 128), 128)
            square[gate, into, :] = w_rec[:, columns].T
            return step(gate * turns + count, carry)

        carry = lax.fori_loop(0, turns, turning, carry, unroll=UNROLL_FORWARD)
        copy_kept(gate).start()
        copy_turned(gate).start()
        return carry

    carry = lax.fori_loop(0, 4, part, (h_first[...], c_first[...]))
    lax.fori_loop(4 * turns, LONGEST, step, carry, unroll=UNROLL_FORWARD)
    begin = 4 * turns * KINDS * LANES
    rest = pl.ds(begin, kept_here.shape[0] - begin)
    last = pltpu.make_async_copy(kept_here.at[rest, :], kept.at[rest, :], sems_kept.at[4])
    last.start()
    hidden_rows[...] = dot(collect[...], hiddens[...].astype(bf16)).astype(bf16)
    output_rows[...] = outs[...].astype(bf16)
    for gate in range(4):
        copy_kept(gate).wait()
        copy_turned(gate).wait()
    last.wait()


def backward_kernel(
    turned,
    kept,
    coming,
    spread,
    collect,
    out_scale,
    carry_in,
    gate_rows,
    *refs,
    first_step,
):
    carry_out = refs[0]
    *fetched, w_turned, kept_here, come, dgates, sems_small, sems_turned, sems_kept = refs[-12:]
    fetches = fetch((coming, spread, collect, out_scale, carry_in), fetched, sems_small)
    coming, spread, collect, out_scale, carry_in = fetched
    width = coming.shape[1]
    steps = spread.shape[0] // LANES
    size = KINDS * LANES

    def copy_kept(part):
        begin, count = ((steps - SOON) * size, SOON * size) if part == 0 else (
            0,
            (steps - SOON) * size,
        )
        return pltpu.make_async_copy(
            kept.at[pl.ds(first_step * size + begin, count), :],
            kept_here.at[pl.ds(begin, count), :],
            sems_kept.at[part],
        )

    copies = [
        pltpu.make_async_copy(
            turned.at[gate], w_turned.at[pl.ds(gate * width, width), :], sems_turned.at[gate]
        )
        for gate in range(4)
    ]
    copy_kept(0).start()
    for copy in copies:
        copy.start()
    for copy in fetches:
        copy.wait()
    come[...] = dot(spread[...], coming[...])
    scale = out_scale[...]

    def gradients(index, carry):
        dh_next, dc_next = carry
        at = step_rows(index)
        grad_h = come[at, :] * scale + dh_next
        grad_c = dc_next + grad_h * kept_here[kept_rows(index, 0), :]
        grads = jnp.concatenate(
            [
                grad_c * kept_here[kept_rows(index, 1), :],
                grad_c * kept_here[kept_rows(index, 2), :],
                grad_c * kept_here[kept_rows(index, 3), :],
                grad_h * kept_here[kept_rows(index, 4), :],
            ],
            axis=1,
        )
        dgates[at, :] = grads
        return (grads, grad_c * kept_here[kept_rows(index, 5), :])

    def step(index, carry):
        grads, dc_next = gradients(index, carry)
        return (dot(grads.astype(bf16), w_turned[...]), dc_next)

    def run(last, count, carry):
        return lax.fori_loop(
            0, count, lambda back, c: step(last - back, c), carry, unroll=UNROLL_BACKWARD
        )

    copy_kept(0).wait()
    if first_step > 0:
        carry = (jnp.zeros((LANES, width), f32),) * 2
    else:
        carry = (carry_in[pl.ds(0, LANES), :], carry_in[pl.ds(LANES, LANES), :])
    grads, dc_next = gradients(steps - 1, carry)
    grads = grads.astype(bf16)
    dh_next = jnp.zeros((LANES, width), f32)
    for gate in range(4):
        copies[gate].wait()
        here = slice(gate * width, (gate + 1) * width)
        dh_next = dh_next + dot(grads[:, here], w_turned[here, :])
    copy_kept(1).start()
    carry = run(steps - 2, SOON - 1, (dh_next, dc_next))
    copy_kept(1).wait()
    if first_step > 0:
        carry = run(steps - SOON - 1, steps - SOON, carry)
        carry_out[pl.ds(0, LANES), :] = carry[0]
        carry_out[pl.ds(LANES, LANES), :] = carry[1]
    else:
        carry = run(steps - SOON - 1, steps - SOON - 1, carry)
        gradients(0, carry)
    for gate in range(4):
        columns = pl.ds(gate * width, width)
        gate_rows[gate] = dot(collect[...], dgates[:, columns].astype(bf16)).astype(bf16)


def gradient_kernel(
    core,
    mixed_all,
    hidden_all,
    mine,
    other,
    *refs,
    begin,
):
    result, left, right, ninth, before, sems_left, sems_right, sem_before = refs[-8:]
    so_far = refs[:-8]
    half, rows, columns = mine.shape
    line = 2 * half
    each = mixed_all.shape[0] // line
    which = core[0]

    def copies_left(source):
        found = []
        for place in range(line):
            chip, twin = place % half, place // half
            block = 2 * chip + (which if twin == 0 else 1 - which)
            found.append(
                pltpu.make_async_copy(
                    source.at[pl.ds(pl.multiple_of(block * each + begin, 16), rows), :],
                    left.at[pl.ds(place * rows, rows), :],
                    sems_left.at[place],
                )
            )
        return found

    @pl.when(which == 0)
    def _():
        for copy in copies_left(mixed_all):
            copy.start()

    @pl.when(which != 0)
    def _():
        for copy in copies_left(hidden_all):
            copy.start()

    copies_right = [
        pltpu.make_async_copy(
            (mine if place < half else other).at[place % half],
            right.at[pl.ds(place * rows, rows), :],
            sems_right.at[place],
        )
        for place in range(line)
    ]
    for copy in copies_right:
        copy.start()
    if so_far:
        copy_before = pltpu.make_async_copy(so_far[0], before, sem_before)
        copy_before.start()
    for copy in copies_left(mixed_all) + copies_right:
        copy.wait()
    grad = lax.dot_general(
        left[...], right[...], (((0,), (0,)), ((), ())), preferred_element_type=f32
    )
    if not so_far:
        result[...] = grad
        return
    copy_before.wait()
    devices = result.shape[0]
    main = devices * TILE
    tiles = columns // 128
    ninth[...] = jnp.zeros(ninth.shape, f32)
    for tile in range(0, tiles, 2):
        parts = []
        for place in range(tile, min(tile + 2, tiles)):
            here = grad[:, place * 128 : (place + 1) * 128] + before[:, pl.ds(place * 128, 128)]
            parts.append(here[:main].reshape(devices, TILE, 128))
            ninth[:, place, :] = here[main:]
        if tile + 2 > tiles:
            parts.append(ninth[...])
        rows = jnp.concatenate(parts, axis=1)
        result[:, pl.ds(tile * TILE, rows.shape[1]), :] = rows.astype(bf16)


def settle_kernel(got, scale, to_natural, home, squares, placed):
    devices = got.shape[0]
    tiles = placed.shape[0]
    line = 8
    half = line // 2
    for source in range(line):
        gate = (source % 2) * half + source // 2
        found = got[source].astype(f32)
        for index in range(source + line, devices, line):
            found = found + got[index].astype(f32)
        for tile in range(tiles):
            placed[tile, pl.ds(gate, TILE, stride=8), :] = found[tile * TILE : (tile + 1) * TILE]
            ninth = OWN * TILE + tile
            placed[tile, pl.ds(TILE * 8 + gate, 1), :] = found[ninth : ninth + 1]
    values = jnp.concatenate([placed[tile] for tile in range(tiles)], axis=1)
    values = values * scale[...].astype(f32)
    total = jnp.sum(jnp.sum(values * values, axis=0, keepdims=True), axis=1, keepdims=True)
    squares[...] = jnp.broadcast_to(total, squares.shape)
    home[...] = dot(values.astype(bf16), to_natural[...]).astype(bf16)


def own_kernel(
    wall,
    ninth_in,
    late,
    early,
    in_rows,
    output_rows,
    gather,
    unpack,
    to_natural,
    d_out,
    out,
    square,
    sems,
):
    width = in_rows.shape[1]
    rows = in_rows.shape[0]
    main = wall.shape[0]
    rest = width - main
    copies = []
    for gate in range(4):
        copies.append(
            pltpu.make_async_copy(
                wall.at[:, pl.ds(gate * width, width)],
                square.at[gate, pl.ds(0, main), :],
                sems.at[2 * gate],
            )
        )
        copies.append(
            pltpu.make_async_copy(
                ninth_in.at[gate], square.at[gate, pl.ds(main, rest), :], sems.at[2 * gate + 1]
            )
        )
    for copy in copies:
        copy.start()

    def natural(places, values):
        return dot(dot(places[...], values).astype(bf16), to_natural[...]).astype(bf16)

    out[...] = natural(gather, output_rows[...])

    def right_product(left, matrix):
        return lax.dot_general(
            left, matrix, (((1,), (1,)), ((), ())), preferred_element_type=f32
        )

    found = jnp.zeros((rows, width), f32)
    for gate in range(4):
        copies[2 * gate].wait()
        copies[2 * gate + 1].wait()
        both = jnp.concatenate([late[gate], early[gate]], axis=0)
        found = found + right_product(both, square[gate])
    found = found * (in_rows[...].astype(f32) * KEEP_INPUT)
    d_out[...] = natural(unpack, found.astype(bf16))


def in_vmem():
    return pl.BlockSpec(memory_space=pltpu.VMEM)


def in_place():
    return pl.BlockSpec(memory_space=pl.ANY)


def places_for(*arrays):
    return [pltpu.VMEM(array.shape, array.dtype) for array in arrays]


def run_forward(wall, mixed, spread, collect, h_first, c_first, out_scale):
    steps_rows = spread.shape[0]
    rows, width = mixed.shape
    devices = wall.shape[0] // TILE
    all_kept = LONGEST * KINDS * LANES
    return pl.pallas_call(
        forward_kernel,
        out_shape=(
            jax.ShapeDtypeStruct((collect.shape[0], width), bf16),
            jax.ShapeDtypeStruct((steps_rows, width), bf16),
            jax.ShapeDtypeStruct((4, devices, width), bf16),
            jax.ShapeDtypeStruct((all_kept, width), f32),
            jax.ShapeDtypeStruct((4, width, width), bf16),
        ),
        in_specs=[in_place()] * 7,
        out_specs=(in_vmem(),) * 3 + (in_place(),) * 2,
        scratch_shapes=places_for(mixed, spread, collect, h_first, c_first, out_scale)
        + [
            pltpu.VMEM((4, width, width), bf16),
            pltpu.VMEM((width, 4 * width), bf16),
            pltpu.VMEM((devices * TILE, width), bf16),
            pltpu.VMEM((width // 128, devices * TILE, 128), f32),
            pltpu.VMEM((steps_rows, 4 * width), f32),
            pltpu.VMEM((all_kept, width), f32),
            pltpu.VMEM((steps_rows, width), f32),
            pltpu.VMEM((steps_rows, width), f32),
            pltpu.SemaphoreType.DMA((6,)),
            pltpu.SemaphoreType.DMA((4,)),
            pltpu.SemaphoreType.DMA,
            pltpu.SemaphoreType.DMA,
            pltpu.SemaphoreType.DMA((5,)),
            pltpu.SemaphoreType.DMA((4,)),
        ],
        compiler_params=pltpu.CompilerParams(vmem_limit_bytes=VMEM_LIMIT),
        cost_estimate=pl.CostEstimate(
            flops=60_000_000_000, bytes_accessed=30_000_000, transcendentals=2_000_000
        ),
        name="forward",
    )(wall, mixed, spread, collect, h_first, c_first, out_scale)


def run_backward(turned, kept, coming, spread, collect, out_scale, carry, first_step):
    steps_rows = spread.shape[0]
    rows, width = collect.shape[0], coming.shape[1]
    results = [jax.ShapeDtypeStruct((4, rows, width), bf16)]
    if first_step > 0:
        results.append(jax.ShapeDtypeStruct((2 * LANES, width), f32))
    return pl.pallas_call(
        functools.partial(backward_kernel, first_step=first_step),
        out_shape=results,
        in_specs=[in_place()] * 7,
        out_specs=[in_vmem()] * len(results),
        scratch_shapes=places_for(coming, spread, collect, out_scale, carry)
        + [
            pltpu.VMEM((4 * width, width), bf16),
            pltpu.VMEM((steps_rows * KINDS, width), f32),
            pltpu.VMEM((steps_rows, width), f32),
            pltpu.VMEM((steps_rows, 4 * width), f32),
            pltpu.SemaphoreType.DMA((5,)),
            pltpu.SemaphoreType.DMA((4,)),
            pltpu.SemaphoreType.DMA((2,)),
        ],
        compiler_params=pltpu.CompilerParams(vmem_limit_bytes=VMEM_LIMIT),
        cost_estimate=pl.CostEstimate(
            flops=steps_rows // LANES * 1_500_000_000, bytes_accessed=20_000_000, transcendentals=0
        ),
        name="backward_late" if first_step else "backward_early",
    )(turned, kept, coming, spread, collect, out_scale, carry)


def run_gradient(core, mixed_all, hidden_all, mine, other, begin, devices, so_far=()):
    half, rows, columns = mine.shape
    line = 2 * half
    width = mixed_all.shape[1]
    if so_far:
        result = jax.ShapeDtypeStruct((devices, MESSAGE, 128), bf16)
    else:
        result = jax.ShapeDtypeStruct((width, columns), f32)
    return pl.pallas_call(
        functools.partial(gradient_kernel, begin=begin),
        out_shape=result,
        in_specs=[pl.BlockSpec(memory_space=pltpu.SMEM)]
        + [in_place()] * (4 + len(so_far)),
        out_specs=in_vmem(),
        scratch_shapes=[
            pltpu.VMEM((line * rows, width), bf16),
            pltpu.VMEM((line * rows, columns), bf16),
            pltpu.VMEM((devices, 2 * TILE, 128), f32),
            pltpu.VMEM((width, columns), f32),
            pltpu.SemaphoreType.DMA((line,)),
            pltpu.SemaphoreType.DMA((line,)),
            pltpu.SemaphoreType.DMA,
        ],
        compiler_params=pltpu.CompilerParams(vmem_limit_bytes=VMEM_LIMIT),
        cost_estimate=pl.CostEstimate(
            flops=5_000_000_000, bytes_accessed=12_000_000, transcendentals=0
        ),
        name="gradient_early" if so_far else "gradient_late",
    )(core, mixed_all, hidden_all, mine, other, *so_far)


def run_settle(got, scale, to_natural):
    wide, width = to_natural.shape
    devices = got.shape[0]
    return pl.pallas_call(
        settle_kernel,
        out_shape=(
            jax.ShapeDtypeStruct((OWN * 8, width), bf16),
            jax.ShapeDtypeStruct((devices, 128), f32),
        ),
        in_specs=[in_vmem()] * 3,
        out_specs=(in_vmem(),) * 2,
        scratch_shapes=[pltpu.VMEM((wide // 128, OWN * 8, 128), f32)],
        compiler_params=pltpu.CompilerParams(vmem_limit_bytes=VMEM_SMALL),
        name="settle",
    )(got, scale, to_natural)


def run_own(wall, ninth_in, late, early, in_rows, output_rows, gather, unpack, to_natural):
    width, natural = to_natural.shape
    rows = unpack.shape[0]
    return pl.pallas_call(
        own_kernel,
        out_shape=(jax.ShapeDtypeStruct((rows, natural), bf16),) * 2,
        in_specs=[in_place()] * 2 + [in_vmem()] * 7,
        out_specs=(in_vmem(),) * 2,
        scratch_shapes=[
            pltpu.VMEM((4, width, width), bf16),
            pltpu.SemaphoreType.DMA((8,)),
        ],
        compiler_params=pltpu.CompilerParams(vmem_limit_bytes=VMEM_LIMIT),
        cost_estimate=pl.CostEstimate(
            flops=8_000_000_000, bytes_accessed=15_000_000, transcendentals=0
        ),
        name="own",
    )(wall, ninth_in, late, early, in_rows, output_rows, gather, unpack, to_natural)


def split_exact(values):
    parts = []
    rest = values
    for _ in range(3):
        part = lax.reduce_precision(rest, 8, 7)
        parts.append(part.astype(bf16))
        rest = rest - part
    return parts


def body(
    inputs,
    d_out,
    h_start,
    c_start,
    pieces,
    in_mask,
    out_mask,
    w_mask,
    master,
    moment_one,
    moment_two,
):
    streams, steps, width = inputs.shape
    gates_n = 4 * width
    count_w = 2 * width * gates_n
    total = count_w + gates_n
    shard = master.shape[0]
    devices = lax.axis_size("batch")
    me = lax.axis_index("batch")
    wide = OWN * devices
    block = OWN * 2 * gates_n
    gap = block - shard
    most = gap * devices
    tokens = streams * steps
    rows_n = LATE + EARLY
    line = 8
    lines = devices // line

    line_groups = [[line * q + m for m in range(line)] for q in range(lines)]
    column_groups = [
        [line * q + 2 * y + c for y in range(line // 2)] for q in range(lines) for c in range(2)
    ]
    twins = [(i, i ^ 1) for i in range(devices)]

    to_kept = one_hot(width, wide, lambda k, p: place_of(k, devices) == p)
    to_natural = one_hot(wide, width, lambda p, k: place_of(k, devices) == p)

    places = me * shard + lax.iota(jnp.int32, shard)
    recurrent = (places < count_w) & (places % (2 * gates_n) >= gates_n)
    scale_low = jnp.where(recurrent, w_mask.astype(bf16) * KEEP_RECURRENT, jnp.ones((), bf16))
    local_low = master.astype(bf16) * scale_low
    local_low = jnp.where(places < total, local_low, jnp.zeros((), bf16))

    def realigned(flat, following):
        joined = jnp.concatenate([flat, following])
        rows = lax.dynamic_slice(joined, (gap * me,), (block,)).reshape(OWN * 8, width)
        return dot(rows, to_kept).astype(bf16)

    before = [(i + 1, i) for i in range(devices - 1)]
    order = one_hot(
        OWN * 8,
        OWN * 8,
        lambda a, b: jnp.where(a < 64, (a % 8) * 8 + a // 8, 64 + a % 8) == b,
    )
    own = realigned(local_low, lax.ppermute(local_low[:most], "batch", before))
    own = dot(order, own).astype(bf16)
    own = jnp.concatenate([own[TILE * j : TILE * (j + 1)] for j in range(OWN)], axis=1)
    wall = lax.all_gather(own, "batch", axis=0, tiled=True)
    scales = realigned(scale_low, lax.ppermute(scale_low[:most], "batch", before))

    in_scale = in_mask.astype(f32) * KEEP_INPUT
    mixed = (inputs.astype(f32) * in_scale[:, None, :]).astype(bf16).reshape(tokens, width)
    spare = ((0, rows_n - tokens), (0, 0))
    mixed = dot(jnp.pad(mixed, spare), to_kept).astype(bf16)
    bias_place = place_of(jnp.int32(width), devices)
    column = lax.broadcasted_iota(jnp.int32, mixed.shape, 1)
    mixed = jnp.where(column == bias_place, jnp.ones((), bf16), mixed)
    coming = dot(jnp.pad(d_out.reshape(tokens, width), spare), to_kept).astype(bf16)
    small = jnp.concatenate(
        [h_start.astype(bf16)]
        + split_exact(c_start)
        + [in_mask.astype(bf16), out_mask.astype(bf16)],
        axis=0,
    )
    small = dot(small, to_kept)
    part = [small[streams * j : streams * (j + 1)] for j in range(6)]
    empty = jnp.zeros((LANES - streams, wide), f32)
    h_first = jnp.concatenate([part[0], empty], axis=0)
    c_first = jnp.concatenate([part[1] + part[2] + part[3], empty], axis=0)
    out_scale_kept = part[5] * KEEP_OUTPUT
    out_scale = jnp.concatenate(
        [out_scale_kept, out_scale_kept, jnp.zeros((LANES - 2 * streams, wide), f32)], axis=0
    )
    base = jnp.arange(streams, dtype=jnp.int32) * steps
    none = jnp.zeros((LANES - 2 * streams,), jnp.int32)
    begins = jnp.concatenate([base, base + pieces[:, 0], none])
    lengths = jnp.concatenate([pieces[:, 0], pieces[:, 1], none])
    ticks = lax.broadcasted_iota(jnp.int32, (LONGEST, LANES), 0)
    active = ticks < lengths[None, :]
    where = jnp.where(active, begins[None, :] + ticks, -1).reshape(-1)
    spread = (where[:, None] == lax.iota(jnp.int32, rows_n)[None, :]).astype(bf16)
    late_first = jnp.maximum(pieces[:, 0] - SPLIT, 0)
    late_base = jnp.arange(streams, dtype=jnp.int32) * LATE_BLOCK
    late_base = jnp.concatenate([late_base, late_base + late_first, none])
    early_base = LATE + SPLIT * jnp.arange(LANES, dtype=jnp.int32)
    packed = jnp.where(ticks < SPLIT, early_base[None] + ticks, late_base[None] + ticks - SPLIT)
    packed = jnp.where(active, packed, -1).reshape(-1)
    collect = (lax.iota(jnp.int32, rows_n)[:, None] == packed[None, :]).astype(bf16)
    pack = dot(collect, spread).astype(bf16)
    unpack = (
        lax.dot_general(spread, collect, (((0,), (1,)), ((), ())), preferred_element_type=f32)
    ).astype(bf16)
    mixed_rows = dot(pack, mixed).astype(bf16)
    row_stream = lax.iota(jnp.int32, rows_n) // steps
    row_stream = (row_stream[:, None] == lax.iota(jnp.int32, streams)[None]).astype(bf16)
    in_rows = dot(pack, dot(row_stream, part[4].astype(bf16)).astype(bf16)).astype(bf16)

    begin = SPLIT * LANES
    ready = (wall, mixed, mixed_rows, coming, spread, collect, h_first, c_first, out_scale)
    ready += (in_rows, unpack, to_natural, scales, spread[:begin], spread[begin:])
    ready += (collect[LATE:, :begin], collect[:LATE, begin:], spread.T)
    ready = lax.optimization_barrier(ready)
    wall, mixed, mixed_rows, coming, spread, collect, h_first, c_first, out_scale = ready[:9]
    in_rows, unpack, to_natural, scales, spread_early, spread_late = ready[9:15]
    collect_early, collect_late, gather = ready[15:]
    mixed_all = lax.all_gather(
        mixed_rows, "batch", axis=0, tiled=True, axis_index_groups=line_groups
    )
    hidden_rows, output_rows, ninth_in, kept, turned = run_forward(
        wall, mixed, spread, collect, h_first, c_first, out_scale
    )
    hidden_rows, mixed_all = lax.optimization_barrier((hidden_rows, mixed_all))
    hidden_all = lax.all_gather(
        hidden_rows, "batch", axis=0, tiled=True, axis_index_groups=line_groups
    )
    late, carry = run_backward(
        turned, kept, coming, spread_late, collect_late, out_scale, out_scale, SPLIT
    )

    def exchange(rows):
        return lax.all_to_all(
            rows, "batch", 0, 0, tiled=True, axis_index_groups=column_groups
        )

    late_mine = exchange(late)
    (early,) = run_backward(
        turned, kept, coming, spread_early, collect_early, out_scale, carry, 0
    )
    late_mine, early = lax.optimization_barrier((late_mine, early))
    early_mine = exchange(early)
    core = (me % 2).reshape(1)
    so_far = run_gradient(
        core, mixed_all, hidden_all, late_mine, lax.ppermute(late_mine, "batch", twins), 0, devices
    )
    early_mine, so_far = lax.optimization_barrier((early_mine, so_far))
    message = run_gradient(
        core,
        mixed_all,
        hidden_all,
        early_mine,
        lax.ppermute(early_mine, "batch", twins),
        LATE,
        devices,
        (so_far,),
    )
    got = lax.all_to_all(message, "batch", 0, 0, tiled=True)

    d_rows, out_rows = run_own(
        wall, ninth_in, late, early, in_rows, output_rows, gather, unpack, to_natural
    )
    output = out_rows[:tokens].reshape(streams, steps, width)
    d_inputs = d_rows[:tokens].reshape(streams, steps, width)
    got, output, d_inputs = lax.optimization_barrier((got, output, d_inputs))

    home, squares = run_settle(got, scales, to_natural)
    squares = lax.all_to_all(squares, "batch", 0, 0, tiled=True)
    home = home.reshape(block)
    tail = lax.ppermute(home[block - most :], "batch", [(i, i + 1) for i in range(devices - 1)])
    grad_shard = lax.dynamic_slice(
        jnp.concatenate([tail, home]), (most - gap * me,), (shard,)
    ).astype(f32)
    grad_norm = jnp.sqrt(jnp.sum(squares[:, 0]))

    factor = jnp.minimum(1.0, CLIP_NORM / (grad_norm + 1e-06))
    clipped = grad_shard * factor
    moment_new = BETA_ONE * moment_one + (1.0 - BETA_ONE) * clipped
    second_new = BETA_TWO * moment_two + (1.0 - BETA_TWO) * clipped * clipped
    first_hat = moment_new / (1.0 - BETA_ONE**STEP)
    second_hat = second_new / (1.0 - BETA_TWO**STEP)
    master_new = master - LEARN_RATE * (
        first_hat / (jnp.sqrt(second_hat) + EPSILON) + WEIGHT_DECAY * master
    )
    return (output, d_inputs, moment_new, second_new, master_new, grad_norm)


def solution(mesh):
    placed = (
        P("batch", None, None),
        P("batch", None, None),
        P("batch", None),
        P("batch", None),
        P("batch", None),
        P("batch", None),
        P("batch", None),
        P("batch"),
        P("batch"),
        P("batch"),
        P("batch"),
    )
    return jax.shard_map(
        body,
        mesh=mesh,
        in_specs=placed,
        out_specs=(
            P("batch", None, None),
            P("batch", None, None),
            P("batch"),
            P("batch"),
            P("batch"),
            P(),
        ),
        check_vma=False,
    )
```

```python
import functools

import jax
import jax.numpy as jnp
from jax import lax
from jax.experimental import pallas as pl
from jax.experimental.pallas import tpu as pltpu
from jax.sharding import PartitionSpec as P

STEP = 10


LEARN_RATE = 0.03
BETA_ONE = 0.9
BETA_TWO = 0.999
WEIGHT_DECAY = 0.01
EPSILON = 1e-08
CLIP_NORM = 1.0
KEEP_INPUT = 4.0 / 3.0
KEEP_OUTPUT = 4.0 / 3.0
KEEP_RECURRENT = 2.0

LONGEST = 40
LANES = 8
TILE = 8
OWN = TILE + 1
KINDS = 6
SOON = 5
SPLIT = 10
LATE = 160
LATE_BLOCK = LATE // 3
EARLY = 64
UNROLL_FORWARD = 3
UNROLL_BACKWARD = 4
MESSAGE = 88
VMEM_LIMIT = 60 * 2**20
VMEM_SMALL = 16 * 2**20

f32 = jnp.float32
bf16 = jnp.bfloat16


def dot(left, right):
    return lax.dot_general(left, right, (((1,), (0,)), ((), ())), preferred_element_type=f32)


def one_hot(rows, columns, wanted):
    row = lax.broadcasted_iota(jnp.int32, (rows, columns), 0)
    column = lax.broadcasted_iota(jnp.int32, (rows, columns), 1)
    return wanted(row, column).astype(bf16)


def place_of(natural, devices):
    owner, rest = natural // OWN, natural % OWN
    return jnp.where(rest < TILE, owner * TILE + rest, devices * TILE + owner)


def step_rows(step):
    return pl.ds(pl.multiple_of(step * LANES, LANES), LANES)


def kept_rows(step, kind):
    return pl.ds(pl.multiple_of((step * KINDS + kind) * LANES, LANES), LANES)


def fetch(sources, into, sems):
    copies = [
        pltpu.make_async_copy(source, place, sems.at[index])
        for index, (source, place) in enumerate(zip(sources, into))
    ]
    for copy in copies:
        copy.start()
    return copies


def forward_kernel(
    wall,
    mixed,
    spread,
    collect,
    h_first,
    c_first,
    out_scale,
    hidden_rows,
    output_rows,
    ninth_in,
    kept,
    turned,
    *refs,
):
    fetched, (square, w_rec, ninth, apart, pre, kept_here, hiddens, outs) = refs[:6], refs[6:14]
    sems_small, sems_in, sem_ninth, sem_rec, sems_kept, sems_turned = refs[14:]
    fetches = fetch((mixed, spread, collect, h_first, c_first, out_scale), fetched, sems_small)
    mixed, spread, collect, h_first, c_first, out_scale = fetched
    width = mixed.shape[1]
    main = wall.shape[0]
    devices = main // TILE
    gates_n = 4 * width

    copy_ninth = pltpu.make_async_copy(wall.at[:, pl.ds(2 * gates_n, width)], ninth, sem_ninth)
    copies_in = [
        pltpu.make_async_copy(
            wall.at[:, pl.ds(gate * width, width)],
            square.at[pl.ds(0, main), pl.ds(gate * width, width)],
            sems_in.at[gate],
        )
        for gate in range(4)
    ]
    copy_rec = pltpu.make_async_copy(
        wall.at[:, pl.ds(gates_n, gates_n)], w_rec.at[pl.ds(0, main), :], sem_rec
    )
    for copy in copies_in + [copy_ninth, copy_rec]:
        copy.start()
    for copy in fetches:
        copy.wait()
    rows = dot(spread[...], mixed[...]).astype(bf16)
    chunk = gates_n // 3
    arrived = 0
    for begin in range(0, gates_n, chunk):
        while arrived * width < begin + chunk:
            copies_in[arrived].wait()
            arrived += 1
        here = pl.ds(begin, chunk)
        pre[:, here] = dot(rows[:, :main], square[pl.ds(0, main), here])
    copy_ninth.wait()
    for tile in range(width // 128):
        columns = pl.ds(tile * 128, 128)
        apart[tile] = ninth[:, columns].astype(f32)
        for gate in range(8):
            rest = apart[tile, pl.ds(gate, devices, stride=8), :].astype(bf16)
            there = pl.ds(gate % 4 * width + tile * 128, 128)
            if gate < 4:
                square[pl.ds(main, devices), there] = rest
                ninth_in[gate, :, columns] = rest
            else:
                w_rec[pl.ds(main, devices), there] = rest
    for begin in range(0, gates_n, chunk):
        here = pl.ds(begin, chunk)
        pre[:, here] = pre[:, here] + dot(rows[:, main:], square[pl.ds(main, devices), here])
    copy_rec.wait()
    scale = out_scale[...]
    soon = width - 128
    sizes = (256,) * (width // 256) + ((128,) if width % 256 else ())

    def step(index, carry):
        hidden, cell = carry
        at = step_rows(index)
        hiddens[at, :] = hidden
        low = hidden.astype(bf16)
        early = pre[at, :]
        for begin in range(0, soon, 512):
            here = slice(begin, min(begin + 512, soon))
            early = early + dot(low[:, here], w_rec[here, :])
        states = ([], [])
        begin = 0
        for size in sizes:
            lanes = pl.ds(begin, size)
            gates = []
            for gate in range(4):
                first = gate * width + begin
                late = dot(low[:, soon:], w_rec[pl.ds(soon, width - soon), pl.ds(first, size)])
                gates.append(early[:, first : first + size] + late)
            in_gate = jax.nn.sigmoid(gates[0])
            forget = jax.nn.sigmoid(gates[1])
            candid = jnp.tanh(gates[2])
            out_gate = jax.nn.sigmoid(gates[3])
            before = cell[:, begin : begin + size]
            cell_new = forget * before + in_gate * candid
            squash = jnp.tanh(cell_new)
            hidden_new = out_gate * squash
            outs[at, lanes] = hidden_new * scale[:, begin : begin + size]
            kept_here[kept_rows(index, 0), lanes] = out_gate * (1.0 - squash * squash)
            kept_here[kept_rows(index, 1), lanes] = candid * in_gate * (1.0 - in_gate)
            kept_here[kept_rows(index, 2), lanes] = before * forget * (1.0 - forget)
            kept_here[kept_rows(index, 3), lanes] = in_gate * (1.0 - candid * candid)
            kept_here[kept_rows(index, 4), lanes] = squash * out_gate * (1.0 - out_gate)
            kept_here[kept_rows(index, 5), lanes] = forget
            states[0].append(hidden_new)
            states[1].append(cell_new)
            begin += size
        return tuple(jnp.concatenate(state, axis=1) for state in states)

    turns = width // 128

    def copy_kept(part):
        size = turns * KINDS * LANES
        at = pl.ds(pl.multiple_of(part * size, LANES), size)
        return pltpu.make_async_copy(kept_here.at[at, :], kept.at[at, :], sems_kept.at[part])

    def copy_turned(gate):
        here = pl.ds(pl.multiple_of(gate * width, 128), width)
        return pltpu.make_async_copy(square.at[:, here], turned.at[gate], sems_turned.at[gate])

    def part(gate, carry):
        def turning(count, carry):
            columns = pl.ds(pl.multiple_of(gate * width + count * 128, 128), 128)
            into = pl.ds(pl.multiple_of(count * 128, 128), 128)
            square[into, pl.ds(pl.multiple_of(gate * width, 128), width)] = w_rec[:, columns].T
            return step(gate * turns + count, carry)

        carry = lax.fori_loop(0, turns, turning, carry, unroll=UNROLL_FORWARD)
        copy_kept(gate).start()
        copy_turned(gate).start()
        return carry

    carry = lax.fori_loop(0, 4, part, (h_first[...], c_first[...]))
    lax.fori_loop(4 * turns, LONGEST, step, carry, unroll=UNROLL_FORWARD)
    begin = 4 * turns * KINDS * LANES
    rest = pl.ds(begin, kept_here.shape[0] - begin)
    last = pltpu.make_async_copy(kept_here.at[rest, :], kept.at[rest, :], sems_kept.at[4])
    last.start()
    hidden_rows[...] = dot(collect[...], hiddens[...].astype(bf16)).astype(bf16)
    output_rows[...] = outs[...].astype(bf16)
    for gate in range(4):
        copy_kept(gate).wait()
        copy_turned(gate).wait()
    last.wait()


def backward_kernel(
    turned,
    kept,
    coming,
    spread,
    collect,
    out_scale,
    carry_in,
    gate_rows,
    *refs,
    first_step,
):
    carry_out = refs[0]
    *fetched, w_turned, kept_here, come, dgates, sems_small, sems_turned, sems_kept = refs[-12:]
    fetches = fetch((coming, spread, collect, out_scale, carry_in), fetched, sems_small)
    coming, spread, collect, out_scale, carry_in = fetched
    width = coming.shape[1]
    steps = spread.shape[0] // LANES
    size = KINDS * LANES

    def copy_kept(part):
        begin, count = ((steps - SOON) * size, SOON * size) if part == 0 else (
            0,
            (steps - SOON) * size,
        )
        return pltpu.make_async_copy(
            kept.at[pl.ds(first_step * size + begin, count), :],
            kept_here.at[pl.ds(begin, count), :],
            sems_kept.at[part],
        )

    copies = [
        pltpu.make_async_copy(
            turned.at[gate], w_turned.at[pl.ds(gate * width, width), :], sems_turned.at[gate]
        )
        for gate in range(4)
    ]
    copy_kept(0).start()
    for copy in copies:
        copy.start()
    for copy in fetches:
        copy.wait()
    come[...] = dot(spread[...], coming[...])
    scale = out_scale[...]

    def gradients(index, carry):
        dh_next, dc_next = carry
        at = step_rows(index)
        grad_h = come[at, :] * scale + dh_next
        grad_c = dc_next + grad_h * kept_here[kept_rows(index, 0), :]
        grads = jnp.concatenate(
            [
                grad_c * kept_here[kept_rows(index, 1), :],
                grad_c * kept_here[kept_rows(index, 2), :],
                grad_c * kept_here[kept_rows(index, 3), :],
                grad_h * kept_here[kept_rows(index, 4), :],
            ],
            axis=1,
        )
        dgates[at, :] = grads
        return (grads, grad_c * kept_here[kept_rows(index, 5), :])

    def step(index, carry):
        grads, dc_next = gradients(index, carry)
        return (dot(grads.astype(bf16), w_turned[...]), dc_next)

    def run(last, count, carry):
        return lax.fori_loop(
            0, count, lambda back, c: step(last - back, c), carry, unroll=UNROLL_BACKWARD
        )

    copy_kept(0).wait()
    if first_step > 0:
        carry = (jnp.zeros((LANES, width), f32),) * 2
    else:
        carry = (carry_in[pl.ds(0, LANES), :], carry_in[pl.ds(LANES, LANES), :])
    grads, dc_next = gradients(steps - 1, carry)
    grads = grads.astype(bf16)
    dh_next = jnp.zeros((LANES, width), f32)
    for gate in range(4):
        copies[gate].wait()
        here = slice(gate * width, (gate + 1) * width)
        dh_next = dh_next + dot(grads[:, here], w_turned[here, :])
    copy_kept(1).start()
    carry = run(steps - 2, SOON - 1, (dh_next, dc_next))
    copy_kept(1).wait()
    if first_step > 0:
        carry = run(steps - SOON - 1, steps - SOON, carry)
        carry_out[pl.ds(0, LANES), :] = carry[0]
        carry_out[pl.ds(LANES, LANES), :] = carry[1]
    else:
        carry = run(steps - SOON - 1, steps - SOON - 1, carry)
        gradients(0, carry)
    for gate in range(4):
        columns = pl.ds(gate * width, width)
        gate_rows[gate] = dot(collect[...], dgates[:, columns].astype(bf16)).astype(bf16)


def gradient_kernel(
    core,
    mixed_all,
    hidden_all,
    mine,
    other,
    *refs,
    begin,
):
    result, left, right, ninth, before, sems_left, sems_right, sem_before = refs[-8:]
    so_far = refs[:-8]
    half, rows, columns = mine.shape
    line = 2 * half
    each = mixed_all.shape[0] // line
    which = core[0]

    def copies_left(source):
        found = []
        for place in range(line):
            chip, twin = place % half, place // half
            block = 2 * chip + (which if twin == 0 else 1 - which)
            found.append(
                pltpu.make_async_copy(
                    source.at[pl.ds(pl.multiple_of(block * each + begin, 16), rows), :],
                    left.at[pl.ds(place * rows, rows), :],
                    sems_left.at[place],
                )
            )
        return found

    @pl.when(which == 0)
    def _():
        for copy in copies_left(mixed_all):
            copy.start()

    @pl.when(which != 0)
    def _():
        for copy in copies_left(hidden_all):
            copy.start()

    copies_right = [
        pltpu.make_async_copy(
            (mine if place < half else other).at[place % half],
            right.at[pl.ds(place * rows, rows), :],
            sems_right.at[place],
        )
        for place in range(line)
    ]
    for copy in copies_right:
        copy.start()
    if so_far:
        copy_before = pltpu.make_async_copy(so_far[0], before, sem_before)
        copy_before.start()
    for copy in copies_left(mixed_all) + copies_right:
        copy.wait()
    grad = lax.dot_general(
        left[...], right[...], (((0,), (0,)), ((), ())), preferred_element_type=f32
    )
    if not so_far:
        result[...] = grad
        return
    copy_before.wait()
    devices = result.shape[0]
    main = devices * TILE
    tiles = columns // 128
    ninth[...] = jnp.zeros(ninth.shape, f32)
    for tile in range(0, tiles, 2):
        parts = []
        for place in range(tile, min(tile + 2, tiles)):
            here = grad[:, place * 128 : (place + 1) * 128] + before[:, pl.ds(place * 128, 128)]
            parts.append(here[:main].reshape(devices, TILE, 128))
            ninth[:, place, :] = here[main:]
        if tile + 2 > tiles:
            parts.append(ninth[...])
        rows = jnp.concatenate(parts, axis=1)
        result[:, pl.ds(tile * TILE, rows.shape[1]), :] = rows.astype(bf16)


def settle_kernel(got, scale, to_natural, home, squares, placed):
    devices = got.shape[0]
    tiles = placed.shape[0]
    line = 8
    half = line // 2
    for source in range(line):
        gate = (source % 2) * half + source // 2
        found = got[source].astype(f32)
        for index in range(source + line, devices, line):
            found = found + got[index].astype(f32)
        for tile in range(tiles):
            placed[tile, pl.ds(gate, TILE, stride=8), :] = found[tile * TILE : (tile + 1) * TILE]
            ninth = OWN * TILE + tile
            placed[tile, pl.ds(TILE * 8 + gate, 1), :] = found[ninth : ninth + 1]
    values = jnp.concatenate([placed[tile] for tile in range(tiles)], axis=1)
    values = values * scale[...].astype(f32)
    total = jnp.sum(jnp.sum(values * values, axis=0, keepdims=True), axis=1, keepdims=True)
    squares[...] = jnp.broadcast_to(total, squares.shape)
    home[...] = dot(values.astype(bf16), to_natural[...]).astype(bf16)


def own_kernel(
    wall,
    ninth_in,
    late,
    early,
    in_rows,
    output_rows,
    gather,
    unpack,
    to_natural,
    d_out,
    out,
    square,
    sems,
):
    width = in_rows.shape[1]
    rows = in_rows.shape[0]
    main = wall.shape[0]
    rest = width - main
    copies = []
    for gate in range(4):
        copies.append(
            pltpu.make_async_copy(
                wall.at[:, pl.ds(gate * width, width)],
                square.at[gate, pl.ds(0, main), :],
                sems.at[2 * gate],
            )
        )
        copies.append(
            pltpu.make_async_copy(
                ninth_in.at[gate], square.at[gate, pl.ds(main, rest), :], sems.at[2 * gate + 1]
            )
        )
    for copy in copies:
        copy.start()

    def natural(places, values):
        return dot(dot(places[...], values).astype(bf16), to_natural[...]).astype(bf16)

    out[...] = natural(gather, output_rows[...])

    def right_product(left, matrix):
        return lax.dot_general(
            left, matrix, (((1,), (1,)), ((), ())), preferred_element_type=f32
        )

    found = jnp.zeros((rows, width), f32)
    for gate in range(4):
        copies[2 * gate].wait()
        copies[2 * gate + 1].wait()
        both = jnp.concatenate([late[gate], early[gate]], axis=0)
        found = found + right_product(both, square[gate])
    found = found * (in_rows[...].astype(f32) * KEEP_INPUT)
    d_out[...] = natural(unpack, found.astype(bf16))


def in_vmem():
    return pl.BlockSpec(memory_space=pltpu.VMEM)


def in_place():
    return pl.BlockSpec(memory_space=pl.ANY)


def places_for(*arrays):
    return [pltpu.VMEM(array.shape, array.dtype) for array in arrays]


def run_forward(wall, mixed, spread, collect, h_first, c_first, out_scale):
    steps_rows = spread.shape[0]
    rows, width = mixed.shape
    devices = wall.shape[0] // TILE
    all_kept = LONGEST * KINDS * LANES
    return pl.pallas_call(
        forward_kernel,
        out_shape=(
            jax.ShapeDtypeStruct((collect.shape[0], width), bf16),
            jax.ShapeDtypeStruct((steps_rows, width), bf16),
            jax.ShapeDtypeStruct((4, devices, width), bf16),
            jax.ShapeDtypeStruct((all_kept, width), f32),
            jax.ShapeDtypeStruct((4, width, width), bf16),
        ),
        in_specs=[in_place()] * 7,
        out_specs=(in_vmem(),) * 3 + (in_place(),) * 2,
        scratch_shapes=places_for(mixed, spread, collect, h_first, c_first, out_scale)
        + [
            pltpu.VMEM((width, 4 * width), bf16),
            pltpu.VMEM((width, 4 * width), bf16),
            pltpu.VMEM((devices * TILE, width), bf16),
            pltpu.VMEM((width // 128, devices * TILE, 128), f32),
            pltpu.VMEM((steps_rows, 4 * width), f32),
            pltpu.VMEM((all_kept, width), f32),
            pltpu.VMEM((steps_rows, width), f32),
            pltpu.VMEM((steps_rows, width), f32),
            pltpu.SemaphoreType.DMA((6,)),
            pltpu.SemaphoreType.DMA((4,)),
            pltpu.SemaphoreType.DMA,
            pltpu.SemaphoreType.DMA,
            pltpu.SemaphoreType.DMA((5,)),
            pltpu.SemaphoreType.DMA((4,)),
        ],
        compiler_params=pltpu.CompilerParams(vmem_limit_bytes=VMEM_LIMIT),
        cost_estimate=pl.CostEstimate(
            flops=60_000_000_000, bytes_accessed=30_000_000, transcendentals=2_000_000
        ),
        name="forward",
    )(wall, mixed, spread, collect, h_first, c_first, out_scale)


def run_backward(turned, kept, coming, spread, collect, out_scale, carry, first_step):
    steps_rows = spread.shape[0]
    rows, width = collect.shape[0], coming.shape[1]
    results = [jax.ShapeDtypeStruct((4, rows, width), bf16)]
    if first_step > 0:
        results.append(jax.ShapeDtypeStruct((2 * LANES, width), f32))
    return pl.pallas_call(
        functools.partial(backward_kernel, first_step=first_step),
        out_shape=results,
        in_specs=[in_place()] * 7,
        out_specs=[in_vmem()] * len(results),
        scratch_shapes=places_for(coming, spread, collect, out_scale, carry)
        + [
            pltpu.VMEM((4 * width, width), bf16),
            pltpu.VMEM((steps_rows * KINDS, width), f32),
            pltpu.VMEM((steps_rows, width), f32),
            pltpu.VMEM((steps_rows, 4 * width), f32),
            pltpu.SemaphoreType.DMA((5,)),
            pltpu.SemaphoreType.DMA((4,)),
            pltpu.SemaphoreType.DMA((2,)),
        ],
        compiler_params=pltpu.CompilerParams(vmem_limit_bytes=VMEM_LIMIT),
        cost_estimate=pl.CostEstimate(
            flops=steps_rows // LANES * 1_500_000_000, bytes_accessed=20_000_000, transcendentals=0
        ),
        name="backward_late" if first_step else "backward_early",
    )(turned, kept, coming, spread, collect, out_scale, carry)


def run_gradient(core, mixed_all, hidden_all, mine, other, begin, devices, so_far=()):
    half, rows, columns = mine.shape
    line = 2 * half
    width = mixed_all.shape[1]
    if so_far:
        result = jax.ShapeDtypeStruct((devices, MESSAGE, 128), bf16)
    else:
        result = jax.ShapeDtypeStruct((width, columns), f32)
    return pl.pallas_call(
        functools.partial(gradient_kernel, begin=begin),
        out_shape=result,
        in_specs=[pl.BlockSpec(memory_space=pltpu.SMEM)]
        + [in_place()] * (4 + len(so_far)),
        out_specs=in_vmem(),
        scratch_shapes=[
            pltpu.VMEM((line * rows, width), bf16),
            pltpu.VMEM((line * rows, columns), bf16),
            pltpu.VMEM((devices, 2 * TILE, 128), f32),
            pltpu.VMEM((width, columns), f32),
            pltpu.SemaphoreType.DMA((line,)),
            pltpu.SemaphoreType.DMA((line,)),
            pltpu.SemaphoreType.DMA,
        ],
        compiler_params=pltpu.CompilerParams(vmem_limit_bytes=VMEM_LIMIT),
        cost_estimate=pl.CostEstimate(
            flops=5_000_000_000, bytes_accessed=12_000_000, transcendentals=0
        ),
        name="gradient_early" if so_far else "gradient_late",
    )(core, mixed_all, hidden_all, mine, other, *so_far)


def run_settle(got, scale, to_natural):
    wide, width = to_natural.shape
    devices = got.shape[0]
    return pl.pallas_call(
        settle_kernel,
        out_shape=(
            jax.ShapeDtypeStruct((OWN * 8, width), bf16),
            jax.ShapeDtypeStruct((devices, 128), f32),
        ),
        in_specs=[in_vmem()] * 3,
        out_specs=(in_vmem(),) * 2,
        scratch_shapes=[pltpu.VMEM((wide // 128, OWN * 8, 128), f32)],
        compiler_params=pltpu.CompilerParams(vmem_limit_bytes=VMEM_SMALL),
        name="settle",
    )(got, scale, to_natural)


def run_own(wall, ninth_in, late, early, in_rows, output_rows, gather, unpack, to_natural):
    width, natural = to_natural.shape
    rows = unpack.shape[0]
    return pl.pallas_call(
        own_kernel,
        out_shape=(jax.ShapeDtypeStruct((rows, natural), bf16),) * 2,
        in_specs=[in_place()] * 2 + [in_vmem()] * 7,
        out_specs=(in_vmem(),) * 2,
        scratch_shapes=[
            pltpu.VMEM((4, width, width), bf16),
            pltpu.SemaphoreType.DMA((8,)),
        ],
        compiler_params=pltpu.CompilerParams(vmem_limit_bytes=VMEM_LIMIT),
        cost_estimate=pl.CostEstimate(
            flops=8_000_000_000, bytes_accessed=15_000_000, transcendentals=0
        ),
        name="own",
    )(wall, ninth_in, late, early, in_rows, output_rows, gather, unpack, to_natural)


def split_exact(values):
    parts = []
    rest = values
    for _ in range(3):
        part = lax.reduce_precision(rest, 8, 7)
        parts.append(part.astype(bf16))
        rest = rest - part
    return parts


def body(
    inputs,
    d_out,
    h_start,
    c_start,
    pieces,
    in_mask,
    out_mask,
    w_mask,
    master,
    moment_one,
    moment_two,
):
    streams, steps, width = inputs.shape
    gates_n = 4 * width
    count_w = 2 * width * gates_n
    total = count_w + gates_n
    shard = master.shape[0]
    devices = lax.axis_size("batch")
    me = lax.axis_index("batch")
    wide = OWN * devices
    block = OWN * 2 * gates_n
    gap = block - shard
    most = gap * devices
    tokens = streams * steps
    rows_n = LATE + EARLY
    line = 8
    lines = devices // line

    line_groups = [[line * q + m for m in range(line)] for q in range(lines)]
    column_groups = [
        [line * q + 2 * y + c for y in range(line // 2)] for q in range(lines) for c in range(2)
    ]
    twins = [(i, i ^ 1) for i in range(devices)]

    to_kept = one_hot(width, wide, lambda k, p: place_of(k, devices) == p)
    to_natural = one_hot(wide, width, lambda p, k: place_of(k, devices) == p)

    places = me * shard + lax.iota(jnp.int32, shard)
    recurrent = (places < count_w) & (places % (2 * gates_n) >= gates_n)
    scale_low = jnp.where(recurrent, w_mask.astype(bf16) * KEEP_RECURRENT, jnp.ones((), bf16))
    local_low = master.astype(bf16) * scale_low
    local_low = jnp.where(places < total, local_low, jnp.zeros((), bf16))

    def realigned(flat, following):
        joined = jnp.concatenate([flat, following])
        rows = lax.dynamic_slice(joined, (gap * me,), (block,)).reshape(OWN * 8, width)
        return dot(rows, to_kept).astype(bf16)

    before = [(i + 1, i) for i in range(devices - 1)]
    order = one_hot(
        OWN * 8,
        OWN * 8,
        lambda a, b: jnp.where(a < 64, (a % 8) * 8 + a // 8, 64 + a % 8) == b,
    )
    own = realigned(local_low, lax.ppermute(local_low[:most], "batch", before))
    own = dot(order, own).astype(bf16)
    own = jnp.concatenate([own[TILE * j : TILE * (j + 1)] for j in range(OWN)], axis=1)
    wall = lax.all_gather(own, "batch", axis=0, tiled=True)
    scales = realigned(scale_low, lax.ppermute(scale_low[:most], "batch", before))

    in_scale = in_mask.astype(f32) * KEEP_INPUT
    mixed = (inputs.astype(f32) * in_scale[:, None, :]).astype(bf16).reshape(tokens, width)
    spare = ((0, rows_n - tokens), (0, 0))
    mixed = dot(jnp.pad(mixed, spare), to_kept).astype(bf16)
    bias_place = place_of(jnp.int32(width), devices)
    column = lax.broadcasted_iota(jnp.int32, mixed.shape, 1)
    mixed = jnp.where(column == bias_place, jnp.ones((), bf16), mixed)
    coming = dot(jnp.pad(d_out.reshape(tokens, width), spare), to_kept).astype(bf16)
    small = jnp.concatenate(
        [h_start.astype(bf16)]
        + split_exact(c_start)
        + [in_mask.astype(bf16), out_mask.astype(bf16)],
        axis=0,
    )
    small = dot(small, to_kept)
    part = [small[streams * j : streams * (j + 1)] for j in range(6)]
    empty = jnp.zeros((LANES - streams, wide), f32)
    h_first = jnp.concatenate([part[0], empty], axis=0)
    c_first = jnp.concatenate([part[1] + part[2] + part[3], empty], axis=0)
    out_scale_kept = part[5] * KEEP_OUTPUT
    out_scale = jnp.concatenate(
        [out_scale_kept, out_scale_kept, jnp.zeros((LANES - 2 * streams, wide), f32)], axis=0
    )
    base = jnp.arange(streams, dtype=jnp.int32) * steps
    none = jnp.zeros((LANES - 2 * streams,), jnp.int32)
    begins = jnp.concatenate([base, base + pieces[:, 0], none])
    lengths = jnp.concatenate([pieces[:, 0], pieces[:, 1], none])
    ticks = lax.broadcasted_iota(jnp.int32, (LONGEST, LANES), 0)
    active = ticks < lengths[None, :]
    where = jnp.where(active, begins[None, :] + ticks, -1).reshape(-1)
    spread = (where[:, None] == lax.iota(jnp.int32, rows_n)[None, :]).astype(bf16)
    late_first = jnp.maximum(pieces[:, 0] - SPLIT, 0)
    late_base = jnp.arange(streams, dtype=jnp.int32) * LATE_BLOCK
    late_base = jnp.concatenate([late_base, late_base + late_first, none])
    early_base = LATE + SPLIT * jnp.arange(LANES, dtype=jnp.int32)
    packed = jnp.where(ticks < SPLIT, early_base[None] + ticks, late_base[None] + ticks - SPLIT)
    packed = jnp.where(active, packed, -1).reshape(-1)
    collect = (lax.iota(jnp.int32, rows_n)[:, None] == packed[None, :]).astype(bf16)
    pack = dot(collect, spread).astype(bf16)
    unpack = (
        lax.dot_general(spread, collect, (((0,), (1,)), ((), ())), preferred_element_type=f32)
    ).astype(bf16)
    mixed_rows = dot(pack, mixed).astype(bf16)
    row_stream = lax.iota(jnp.int32, rows_n) // steps
    row_stream = (row_stream[:, None] == lax.iota(jnp.int32, streams)[None]).astype(bf16)
    in_rows = dot(pack, dot(row_stream, part[4].astype(bf16)).astype(bf16)).astype(bf16)

    begin = SPLIT * LANES
    ready = (wall, mixed, mixed_rows, coming, spread, collect, h_first, c_first, out_scale)
    ready += (in_rows, unpack, to_natural, scales, spread[:begin], spread[begin:])
    ready += (collect[LATE:, :begin], collect[:LATE, begin:], spread.T)
    ready = lax.optimization_barrier(ready)
    wall, mixed, mixed_rows, coming, spread, collect, h_first, c_first, out_scale = ready[:9]
    in_rows, unpack, to_natural, scales, spread_early, spread_late = ready[9:15]
    collect_early, collect_late, gather = ready[15:]
    mixed_all = lax.all_gather(
        mixed_rows, "batch", axis=0, tiled=True, axis_index_groups=line_groups
    )
    hidden_rows, output_rows, ninth_in, kept, turned = run_forward(
        wall, mixed, spread, collect, h_first, c_first, out_scale
    )
    hidden_rows, mixed_all = lax.optimization_barrier((hidden_rows, mixed_all))
    hidden_all = lax.all_gather(
        hidden_rows, "batch", axis=0, tiled=True, axis_index_groups=line_groups
    )
    late, carry = run_backward(
        turned, kept, coming, spread_late, collect_late, out_scale, out_scale, SPLIT
    )

    def exchange(rows):
        return lax.all_to_all(
            rows, "batch", 0, 0, tiled=True, axis_index_groups=column_groups
        )

    late_mine = exchange(late)
    (early,) = run_backward(
        turned, kept, coming, spread_early, collect_early, out_scale, carry, 0
    )
    late_mine, early = lax.optimization_barrier((late_mine, early))
    early_mine = exchange(early)
    core = (me % 2).reshape(1)
    so_far = run_gradient(
        core, mixed_all, hidden_all, late_mine, lax.ppermute(late_mine, "batch", twins), 0, devices
    )
    early_mine, so_far = lax.optimization_barrier((early_mine, so_far))
    message = run_gradient(
        core,
        mixed_all,
        hidden_all,
        early_mine,
        lax.ppermute(early_mine, "batch", twins),
        LATE,
        devices,
        (so_far,),
    )
    got = lax.all_to_all(message, "batch", 0, 0, tiled=True)

    d_rows, out_rows = run_own(
        wall, ninth_in, late, early, in_rows, output_rows, gather, unpack, to_natural
    )
    output = out_rows[:tokens].reshape(streams, steps, width)
    d_inputs = d_rows[:tokens].reshape(streams, steps, width)
    got, output, d_inputs = lax.optimization_barrier((got, output, d_inputs))

    home, squares = run_settle(got, scales, to_natural)
    squares = lax.all_to_all(squares, "batch", 0, 0, tiled=True)
    home = home.reshape(block)
    tail = lax.ppermute(home[block - most :], "batch", [(i, i + 1) for i in range(devices - 1)])
    grad_shard = lax.dynamic_slice(
        jnp.concatenate([tail, home]), (most - gap * me,), (shard,)
    ).astype(f32)
    grad_norm = jnp.sqrt(jnp.sum(squares[:, 0]))

    grad_shard, grad_norm = lax.optimization_barrier((grad_shard, grad_norm))
    factor = jnp.minimum(1.0, CLIP_NORM / (grad_norm + 1e-06))
    clipped = grad_shard * factor
    moment_new = BETA_ONE * moment_one + (1.0 - BETA_ONE) * clipped
    second_new = BETA_TWO * moment_two + (1.0 - BETA_TWO) * clipped * clipped
    first_hat = moment_new / (1.0 - BETA_ONE**STEP)
    second_hat = second_new / (1.0 - BETA_TWO**STEP)
    master_new = master - LEARN_RATE * (
        first_hat / (jnp.sqrt(second_hat) + EPSILON) + WEIGHT_DECAY * master
    )
    return (output, d_inputs, moment_new, second_new, master_new, grad_norm)


def solution(mesh):
    placed = (
        P("batch", None, None),
        P("batch", None, None),
        P("batch", None),
        P("batch", None),
        P("batch", None),
        P("batch", None),
        P("batch", None),
        P("batch"),
        P("batch"),
        P("batch"),
        P("batch"),
    )
    return jax.shard_map(
        body,
        mesh=mesh,
        in_specs=placed,
        out_specs=(
            P("batch", None, None),
            P("batch", None, None),
            P("batch"),
            P("batch"),
            P("batch"),
            P(),
        ),
        check_vma=False,
    )
```

```python
import functools

import jax
import jax.numpy as jnp
from jax import lax
from jax.experimental import pallas as pl
from jax.experimental.pallas import tpu as pltpu
from jax.sharding import PartitionSpec as P

STEP = 10


LEARN_RATE = 0.03
BETA_ONE = 0.9
BETA_TWO = 0.999
WEIGHT_DECAY = 0.01
EPSILON = 1e-08
CLIP_NORM = 1.0
KEEP_INPUT = 4.0 / 3.0
KEEP_OUTPUT = 4.0 / 3.0
KEEP_RECURRENT = 2.0

LONGEST = 40
LANES = 8
TILE = 8
OWN = TILE + 1
KINDS = 6
SOON = 5
SPLIT = 10
LATE = 160
LATE_BLOCK = LATE // 3
EARLY = 64
UNROLL_FORWARD = 3
UNROLL_BACKWARD = 4
MESSAGE = 88
VMEM_LIMIT = 60 * 2**20
VMEM_SMALL = 16 * 2**20

f32 = jnp.float32
bf16 = jnp.bfloat16


def dot(left, right):
    return lax.dot_general(left, right, (((1,), (0,)), ((), ())), preferred_element_type=f32)


def one_hot(rows, columns, wanted):
    row = lax.broadcasted_iota(jnp.int32, (rows, columns), 0)
    column = lax.broadcasted_iota(jnp.int32, (rows, columns), 1)
    return wanted(row, column).astype(bf16)


def place_of(natural, devices):
    owner, rest = natural // OWN, natural % OWN
    return jnp.where(rest < TILE, owner * TILE + rest, devices * TILE + owner)


def step_rows(step):
    return pl.ds(pl.multiple_of(step * LANES, LANES), LANES)


def kept_rows(step, kind):
    return pl.ds(pl.multiple_of((step * KINDS + kind) * LANES, LANES), LANES)


def fetch(sources, into, sems):
    copies = [
        pltpu.make_async_copy(source, place, sems.at[index])
        for index, (source, place) in enumerate(zip(sources, into))
    ]
    for copy in copies:
        copy.start()
    return copies


def forward_kernel(
    wall,
    mixed,
    spread,
    collect,
    h_first,
    c_first,
    out_scale,
    hidden_rows,
    output_rows,
    ninth_in,
    kept,
    turned,
    *refs,
):
    fetched, (square, w_rec, ninth, apart, pre, kept_here, hiddens, outs) = refs[:6], refs[6:14]
    sems_small, sems_in, sem_ninth, sem_rec, sems_kept, sems_turned = refs[14:]
    fetches = fetch((mixed, spread, collect, h_first, c_first, out_scale), fetched, sems_small)
    mixed, spread, collect, h_first, c_first, out_scale = fetched
    width = mixed.shape[1]
    main = wall.shape[0]
    devices = main // TILE
    gates_n = 4 * width

    copy_ninth = pltpu.make_async_copy(wall.at[:, pl.ds(2 * gates_n, width)], ninth, sem_ninth)
    copies_in = [
        pltpu.make_async_copy(
            wall.at[:, pl.ds(gate * width, width)],
            square.at[pl.ds(0, main), pl.ds(gate * width, width)],
            sems_in.at[gate],
        )
        for gate in range(4)
    ]
    copy_rec = pltpu.make_async_copy(
        wall.at[:, pl.ds(gates_n, gates_n)], w_rec.at[pl.ds(0, main), :], sem_rec
    )
    for copy in copies_in + [copy_ninth, copy_rec]:
        copy.start()
    for copy in fetches:
        copy.wait()
    rows = dot(spread[...], mixed[...]).astype(bf16)
    chunk = gates_n // 3
    arrived = 0
    for begin in range(0, gates_n, chunk):
        while arrived * width < begin + chunk:
            copies_in[arrived].wait()
            arrived += 1
        here = pl.ds(begin, chunk)
        pre[:, here] = dot(rows[:, :main], square[pl.ds(0, main), here])
    copy_ninth.wait()
    for tile in range(width // 128):
        columns = pl.ds(tile * 128, 128)
        apart[tile] = ninth[:, columns].astype(f32)
        for gate in range(8):
            rest = apart[tile, pl.ds(gate, devices, stride=8), :].astype(bf16)
            there = pl.ds(gate % 4 * width + tile * 128, 128)
            if gate < 4:
                square[pl.ds(main, devices), there] = rest
                ninth_in[gate, :, columns] = rest
            else:
                w_rec[pl.ds(main, devices), there] = rest
    for begin in range(0, gates_n, chunk):
        here = pl.ds(begin, chunk)
        pre[:, here] = pre[:, here] + dot(rows[:, main:], square[pl.ds(main, devices), here])
    copy_rec.wait()
    scale = out_scale[...]
    soon = width - 128
    sizes = (256,) * (width // 256) + ((128,) if width % 256 else ())

    def step(index, carry):
        hidden, cell = carry
        at = step_rows(index)
        hiddens[at, :] = hidden
        low = hidden.astype(bf16)
        early = pre[at, :]
        for begin in range(0, soon, 512):
            here = slice(begin, min(begin + 512, soon))
            early = early + dot(low[:, here], w_rec[here, :])
        states = ([], [])
        begin = 0
        for size in sizes:
            lanes = pl.ds(begin, size)
            gates = []
            for gate in range(4):
                first = gate * width + begin
                late = dot(low[:, soon:], w_rec[pl.ds(soon, width - soon), pl.ds(first, size)])
                gates.append(early[:, first : first + size] + late)
            in_gate = jax.nn.sigmoid(gates[0])
            forget = jax.nn.sigmoid(gates[1])
            candid = jnp.tanh(gates[2])
            out_gate = jax.nn.sigmoid(gates[3])
            before = cell[:, begin : begin + size]
            cell_new = forget * before + in_gate * candid
            squash = jnp.tanh(cell_new)
            hidden_new = out_gate * squash
            outs[at, lanes] = hidden_new * scale[:, begin : begin + size]
            kept_here[kept_rows(index, 0), lanes] = out_gate * (1.0 - squash * squash)
            kept_here[kept_rows(index, 1), lanes] = candid * in_gate * (1.0 - in_gate)
            kept_here[kept_rows(index, 2), lanes] = before * forget * (1.0 - forget)
            kept_here[kept_rows(index, 3), lanes] = in_gate * (1.0 - candid * candid)
            kept_here[kept_rows(index, 4), lanes] = squash * out_gate * (1.0 - out_gate)
            kept_here[kept_rows(index, 5), lanes] = forget
            states[0].append(hidden_new)
            states[1].append(cell_new)
            begin += size
        return tuple(jnp.concatenate(state, axis=1) for state in states)

    turns = width // 128

    def copy_kept(part):
        size = turns * KINDS * LANES
        at = pl.ds(pl.multiple_of(part * size, LANES), size)
        return pltpu.make_async_copy(kept_here.at[at, :], kept.at[at, :], sems_kept.at[part])

    def copy_turned(gate):
        here = pl.ds(pl.multiple_of(gate * width, 128), width)
        return pltpu.make_async_copy(square.at[:, here], turned.at[gate], sems_turned.at[gate])

    def part(gate, carry):
        def turning(count, carry):
            columns = pl.ds(pl.multiple_of(gate * width + count * 128, 128), 128)
            into = pl.ds(pl.multiple_of(count * 128, 128), 128)
            square[into, pl.ds(pl.multiple_of(gate * width, 128), width)] = w_rec[:, columns].T
            return step(gate * turns + count, carry)

        carry = lax.fori_loop(0, turns, turning, carry, unroll=UNROLL_FORWARD)
        copy_kept(gate).start()
        copy_turned(gate).start()
        return carry

    carry = lax.fori_loop(0, 4, part, (h_first[...], c_first[...]))
    lax.fori_loop(4 * turns, LONGEST, step, carry, unroll=UNROLL_FORWARD)
    begin = 4 * turns * KINDS * LANES
    rest = pl.ds(begin, kept_here.shape[0] - begin)
    last = pltpu.make_async_copy(kept_here.at[rest, :], kept.at[rest, :], sems_kept.at[4])
    last.start()
    hidden_rows[...] = dot(collect[...], hiddens[...].astype(bf16)).astype(bf16)
    output_rows[...] = outs[...].astype(bf16)
    for gate in range(4):
        copy_kept(gate).wait()
        copy_turned(gate).wait()
    last.wait()


def backward_kernel(
    turned,
    kept,
    coming,
    spread,
    collect,
    out_scale,
    carry_in,
    gate_rows,
    *refs,
    first_step,
):
    carry_out = refs[0]
    *fetched, w_turned, kept_here, come, dgates, sems_small, sems_turned, sems_kept = refs[-12:]
    fetches = fetch((coming, spread, collect, out_scale, carry_in), fetched, sems_small)
    coming, spread, collect, out_scale, carry_in = fetched
    width = coming.shape[1]
    steps = spread.shape[0] // LANES
    size = KINDS * LANES

    def copy_kept(part):
        begin, count = ((steps - SOON) * size, SOON * size) if part == 0 else (
            0,
            (steps - SOON) * size,
        )
        return pltpu.make_async_copy(
            kept.at[pl.ds(first_step * size + begin, count), :],
            kept_here.at[pl.ds(begin, count), :],
            sems_kept.at[part],
        )

    copies = [
        pltpu.make_async_copy(
            turned.at[gate], w_turned.at[pl.ds(gate * width, width), :], sems_turned.at[gate]
        )
        for gate in range(4)
    ]
    copy_kept(0).start()
    for copy in copies:
        copy.start()
    for copy in fetches:
        copy.wait()
    come[...] = dot(spread[...], coming[...])
    scale = out_scale[...]

    def gradients(index, carry):
        dh_next, dc_next = carry
        at = step_rows(index)
        grad_h = come[at, :] * scale + dh_next
        grad_c = dc_next + grad_h * kept_here[kept_rows(index, 0), :]
        grads = jnp.concatenate(
            [
                grad_c * kept_here[kept_rows(index, 1), :],
                grad_c * kept_here[kept_rows(index, 2), :],
                grad_c * kept_here[kept_rows(index, 3), :],
                grad_h * kept_here[kept_rows(index, 4), :],
            ],
            axis=1,
        )
        dgates[at, :] = grads
        return (grads, grad_c * kept_here[kept_rows(index, 5), :])

    def step(index, carry):
        grads, dc_next = gradients(index, carry)
        return (dot(grads.astype(bf16), w_turned[...]), dc_next)

    def run(last, count, carry):
        return lax.fori_loop(
            0, count, lambda back, c: step(last - back, c), carry, unroll=UNROLL_BACKWARD
        )

    copy_kept(0).wait()
    if first_step > 0:
        carry = (jnp.zeros((LANES, width), f32),) * 2
    else:
        carry = (carry_in[pl.ds(0, LANES), :], carry_in[pl.ds(LANES, LANES), :])
    grads, dc_next = gradients(steps - 1, carry)
    grads = grads.astype(bf16)
    dh_next = jnp.zeros((LANES, width), f32)
    for gate in range(4):
        copies[gate].wait()
        here = slice(gate * width, (gate + 1) * width)
        dh_next = dh_next + dot(grads[:, here], w_turned[here, :])
    copy_kept(1).start()
    carry = run(steps - 2, SOON - 1, (dh_next, dc_next))
    copy_kept(1).wait()
    if first_step > 0:
        carry = run(steps - SOON - 1, steps - SOON, carry)
        carry_out[pl.ds(0, LANES), :] = carry[0]
        carry_out[pl.ds(LANES, LANES), :] = carry[1]
    else:
        carry = run(steps - SOON - 1, steps - SOON - 1, carry)
        gradients(0, carry)
    for gate in range(4):
        columns = pl.ds(gate * width, width)
        gate_rows[gate] = dot(collect[...], dgates[:, columns].astype(bf16)).astype(bf16)


def gradient_kernel(
    core,
    mixed_all,
    hidden_all,
    mine,
    other,
    *refs,
    begin,
):
    result, left, right, ninth, before, sems_left, sems_right, sem_before = refs[-8:]
    so_far = refs[:-8]
    half, rows, columns = mine.shape
    line = 2 * half
    each = mixed_all.shape[0] // line
    which = core[0]

    def copies_left(source):
        found = []
        for place in range(line):
            chip, twin = place % half, place // half
            block = 2 * chip + (which if twin == 0 else 1 - which)
            found.append(
                pltpu.make_async_copy(
                    source.at[pl.ds(pl.multiple_of(block * each + begin, 16), rows), :],
                    left.at[pl.ds(place * rows, rows), :],
                    sems_left.at[place],
                )
            )
        return found

    @pl.when(which == 0)
    def _():
        for copy in copies_left(mixed_all):
            copy.start()

    @pl.when(which != 0)
    def _():
        for copy in copies_left(hidden_all):
            copy.start()

    copies_right = [
        pltpu.make_async_copy(
            (mine if place < half else other).at[place % half],
            right.at[pl.ds(place * rows, rows), :],
            sems_right.at[place],
        )
        for place in range(line)
    ]
    for copy in copies_right:
        copy.start()
    if so_far:
        copy_before = pltpu.make_async_copy(so_far[0], before, sem_before)
        copy_before.start()
    for copy in copies_left(mixed_all) + copies_right:
        copy.wait()
    grad = lax.dot_general(
        left[...], right[...], (((0,), (0,)), ((), ())), preferred_element_type=f32
    )
    if not so_far:
        result[...] = grad
        return
    copy_before.wait()
    devices = result.shape[0]
    main = devices * TILE
    tiles = columns // 128
    ninth[...] = jnp.zeros(ninth.shape, f32)
    for tile in range(0, tiles, 2):
        parts = []
        for place in range(tile, min(tile + 2, tiles)):
            here = grad[:, place * 128 : (place + 1) * 128] + before[:, pl.ds(place * 128, 128)]
            parts.append(here[:main].reshape(devices, TILE, 128))
            ninth[:, place, :] = here[main:]
        if tile + 2 > tiles:
            parts.append(ninth[...])
        rows = jnp.concatenate(parts, axis=1)
        result[:, pl.ds(tile * TILE, rows.shape[1]), :] = rows.astype(bf16)


def settle_kernel(got, scale, to_natural, home, squares, placed):
    devices = got.shape[0]
    tiles = placed.shape[0]
    line = 8
    half = line // 2
    for source in range(line):
        gate = (source % 2) * half + source // 2
        found = got[source].astype(f32)
        for index in range(source + line, devices, line):
            found = found + got[index].astype(f32)
        for tile in range(tiles):
            placed[tile, pl.ds(gate, TILE, stride=8), :] = found[tile * TILE : (tile + 1) * TILE]
            ninth = OWN * TILE + tile
            placed[tile, pl.ds(TILE * 8 + gate, 1), :] = found[ninth : ninth + 1]
    values = jnp.concatenate([placed[tile] for tile in range(tiles)], axis=1)
    values = values * scale[...].astype(f32)
    total = jnp.sum(jnp.sum(values * values, axis=0, keepdims=True), axis=1, keepdims=True)
    squares[...] = jnp.broadcast_to(total, squares.shape)
    home[...] = dot(values.astype(bf16), to_natural[...]).astype(bf16)


def own_kernel(
    wall,
    ninth_in,
    late,
    early,
    in_rows,
    output_rows,
    gather,
    unpack,
    to_natural,
    d_out,
    out,
    square,
    sems,
):
    width = in_rows.shape[1]
    rows = in_rows.shape[0]
    main = wall.shape[0]
    rest = width - main
    copies = []
    for gate in range(4):
        copies.append(
            pltpu.make_async_copy(
                wall.at[:, pl.ds(gate * width, width)],
                square.at[gate, pl.ds(0, main), :],
                sems.at[2 * gate],
            )
        )
        copies.append(
            pltpu.make_async_copy(
                ninth_in.at[gate], square.at[gate, pl.ds(main, rest), :], sems.at[2 * gate + 1]
            )
        )
    for copy in copies:
        copy.start()

    def natural(places, values):
        return dot(dot(places[...], values).astype(bf16), to_natural[...]).astype(bf16)

    out[...] = natural(gather, output_rows[...])

    def right_product(left, matrix):
        return lax.dot_general(
            left, matrix, (((1,), (1,)), ((), ())), preferred_element_type=f32
        )

    found = jnp.zeros((rows, width), f32)
    for gate in range(4):
        copies[2 * gate].wait()
        copies[2 * gate + 1].wait()
        both = jnp.concatenate([late[gate], early[gate]], axis=0)
        found = found + right_product(both, square[gate])
    found = found * (in_rows[...].astype(f32) * KEEP_INPUT)
    d_out[...] = natural(unpack, found.astype(bf16))


def in_vmem():
    return pl.BlockSpec(memory_space=pltpu.VMEM)


def in_place():
    return pl.BlockSpec(memory_space=pl.ANY)


def places_for(*arrays):
    return [pltpu.VMEM(array.shape, array.dtype) for array in arrays]


def run_forward(wall, mixed, spread, collect, h_first, c_first, out_scale):
    steps_rows = spread.shape[0]
    rows, width = mixed.shape
    devices = wall.shape[0] // TILE
    all_kept = LONGEST * KINDS * LANES
    return pl.pallas_call(
        forward_kernel,
        out_shape=(
            jax.ShapeDtypeStruct((collect.shape[0], width), bf16),
            jax.ShapeDtypeStruct((steps_rows, width), bf16),
            jax.ShapeDtypeStruct((4, devices, width), bf16),
            jax.ShapeDtypeStruct((all_kept, width), f32),
            jax.ShapeDtypeStruct((4, width, width), bf16),
        ),
        in_specs=[in_place()] * 7,
        out_specs=(in_vmem(),) * 3 + (in_place(),) * 2,
        scratch_shapes=places_for(mixed, spread, collect, h_first, c_first, out_scale)
        + [
            pltpu.VMEM((width, 4 * width), bf16),
            pltpu.VMEM((width, 4 * width), bf16),
            pltpu.VMEM((devices * TILE, width), bf16),
            pltpu.VMEM((width // 128, devices * TILE, 128), f32),
            pltpu.VMEM((steps_rows, 4 * width), f32),
            pltpu.VMEM((all_kept, width), f32),
            pltpu.VMEM((steps_rows, width), f32),
            pltpu.VMEM((steps_rows, width), f32),
            pltpu.SemaphoreType.DMA((6,)),
            pltpu.SemaphoreType.DMA((4,)),
            pltpu.SemaphoreType.DMA,
            pltpu.SemaphoreType.DMA,
            pltpu.SemaphoreType.DMA((5,)),
            pltpu.SemaphoreType.DMA((4,)),
        ],
        compiler_params=pltpu.CompilerParams(vmem_limit_bytes=VMEM_LIMIT),
        cost_estimate=pl.CostEstimate(
            flops=60_000_000_000, bytes_accessed=30_000_000, transcendentals=2_000_000
        ),
        name="forward",
    )(wall, mixed, spread, collect, h_first, c_first, out_scale)


def run_backward(turned, kept, coming, spread, collect, out_scale, carry, first_step):
    steps_rows = spread.shape[0]
    rows, width = collect.shape[0], coming.shape[1]
    results = [jax.ShapeDtypeStruct((4, rows, width), bf16)]
    if first_step > 0:
        results.append(jax.ShapeDtypeStruct((2 * LANES, width), f32))
    return pl.pallas_call(
        functools.partial(backward_kernel, first_step=first_step),
        out_shape=results,
        in_specs=[in_place()] * 7,
        out_specs=[in_vmem()] * len(results),
        scratch_shapes=places_for(coming, spread, collect, out_scale, carry)
        + [
            pltpu.VMEM((4 * width, width), bf16),
            pltpu.VMEM((steps_rows * KINDS, width), f32),
            pltpu.VMEM((steps_rows, width), f32),
            pltpu.VMEM((steps_rows, 4 * width), f32),
            pltpu.SemaphoreType.DMA((5,)),
            pltpu.SemaphoreType.DMA((4,)),
            pltpu.SemaphoreType.DMA((2,)),
        ],
        compiler_params=pltpu.CompilerParams(vmem_limit_bytes=VMEM_LIMIT),
        cost_estimate=pl.CostEstimate(
            flops=steps_rows // LANES * 1_500_000_000, bytes_accessed=20_000_000, transcendentals=0
        ),
        name="backward_late" if first_step else "backward_early",
    )(turned, kept, coming, spread, collect, out_scale, carry)


def run_gradient(core, mixed_all, hidden_all, mine, other, begin, devices, so_far=()):
    half, rows, columns = mine.shape
    line = 2 * half
    width = mixed_all.shape[1]
    if so_far:
        result = jax.ShapeDtypeStruct((devices, MESSAGE, 128), bf16)
    else:
        result = jax.ShapeDtypeStruct((width, columns), f32)
    return pl.pallas_call(
        functools.partial(gradient_kernel, begin=begin),
        out_shape=result,
        in_specs=[pl.BlockSpec(memory_space=pltpu.SMEM)]
        + [in_place()] * (4 + len(so_far)),
        out_specs=in_vmem(),
        scratch_shapes=[
            pltpu.VMEM((line * rows, width), bf16),
            pltpu.VMEM((line * rows, columns), bf16),
            pltpu.VMEM((devices, 2 * TILE, 128), f32),
            pltpu.VMEM((width, columns), f32),
            pltpu.SemaphoreType.DMA((line,)),
            pltpu.SemaphoreType.DMA((line,)),
            pltpu.SemaphoreType.DMA,
        ],
        compiler_params=pltpu.CompilerParams(vmem_limit_bytes=VMEM_LIMIT),
        cost_estimate=pl.CostEstimate(
            flops=5_000_000_000, bytes_accessed=12_000_000, transcendentals=0
        ),
        name="gradient_early" if so_far else "gradient_late",
    )(core, mixed_all, hidden_all, mine, other, *so_far)


def run_settle(got, scale, to_natural):
    wide, width = to_natural.shape
    devices = got.shape[0]
    return pl.pallas_call(
        settle_kernel,
        out_shape=(
            jax.ShapeDtypeStruct((OWN * 8, width), bf16),
            jax.ShapeDtypeStruct((devices, 128), f32),
        ),
        in_specs=[in_vmem()] * 3,
        out_specs=(in_vmem(),) * 2,
        scratch_shapes=[pltpu.VMEM((wide // 128, OWN * 8, 128), f32)],
        compiler_params=pltpu.CompilerParams(vmem_limit_bytes=VMEM_SMALL),
        name="settle",
    )(got, scale, to_natural)


def run_own(wall, ninth_in, late, early, in_rows, output_rows, gather, unpack, to_natural):
    width, natural = to_natural.shape
    rows = unpack.shape[0]
    return pl.pallas_call(
        own_kernel,
        out_shape=(jax.ShapeDtypeStruct((rows, natural), bf16),) * 2,
        in_specs=[in_place()] * 2 + [in_vmem()] * 7,
        out_specs=(in_vmem(),) * 2,
        scratch_shapes=[
            pltpu.VMEM((4, width, width), bf16),
            pltpu.SemaphoreType.DMA((8,)),
        ],
        compiler_params=pltpu.CompilerParams(vmem_limit_bytes=VMEM_LIMIT),
        cost_estimate=pl.CostEstimate(
            flops=8_000_000_000, bytes_accessed=15_000_000, transcendentals=0
        ),
        name="own",
    )(wall, ninth_in, late, early, in_rows, output_rows, gather, unpack, to_natural)


def split_exact(values):
    parts = []
    rest = values
    for _ in range(3):
        part = lax.reduce_precision(rest, 8, 7)
        parts.append(part.astype(bf16))
        rest = rest - part
    return parts


def body(
    inputs,
    d_out,
    h_start,
    c_start,
    pieces,
    in_mask,
    out_mask,
    w_mask,
    master,
    moment_one,
    moment_two,
):
    streams, steps, width = inputs.shape
    gates_n = 4 * width
    count_w = 2 * width * gates_n
    total = count_w + gates_n
    shard = master.shape[0]
    devices = lax.axis_size("batch")
    me = lax.axis_index("batch")
    wide = OWN * devices
    block = OWN * 2 * gates_n
    gap = block - shard
    most = gap * devices
    tokens = streams * steps
    rows_n = LATE + EARLY
    line = 8
    lines = devices // line

    line_groups = [[line * q + m for m in range(line)] for q in range(lines)]
    column_groups = [
        [line * q + 2 * y + c for y in range(line // 2)] for q in range(lines) for c in range(2)
    ]
    twins = [(i, i ^ 1) for i in range(devices)]

    to_kept = one_hot(width, wide, lambda k, p: place_of(k, devices) == p)
    to_natural = one_hot(wide, width, lambda p, k: place_of(k, devices) == p)

    places = me * shard + lax.iota(jnp.int32, shard)
    recurrent = (places < count_w) & (places % (2 * gates_n) >= gates_n)
    scale_low = jnp.where(recurrent, w_mask.astype(bf16) * KEEP_RECURRENT, jnp.ones((), bf16))
    local_low = master.astype(bf16) * scale_low
    local_low = jnp.where(places < total, local_low, jnp.zeros((), bf16))

    def realigned(flat, following):
        joined = jnp.concatenate([flat, following])
        rows = lax.dynamic_slice(joined, (gap * me,), (block,)).reshape(OWN * 8, width)
        return dot(rows, to_kept).astype(bf16)

    before = [(i + 1, i) for i in range(devices - 1)]
    order = one_hot(
        OWN * 8,
        OWN * 8,
        lambda a, b: jnp.where(a < 64, (a % 8) * 8 + a // 8, 64 + a % 8) == b,
    )
    own = realigned(local_low, lax.ppermute(local_low[:most], "batch", before))
    own = dot(order, own).astype(bf16)
    own = jnp.concatenate([own[TILE * j : TILE * (j + 1)] for j in range(OWN)], axis=1)
    wall = lax.all_gather(own, "batch", axis=0, tiled=True)
    scales = realigned(scale_low, lax.ppermute(scale_low[:most], "batch", before))

    in_scale = in_mask.astype(f32) * KEEP_INPUT
    mixed = (inputs.astype(f32) * in_scale[:, None, :]).astype(bf16).reshape(tokens, width)
    spare = ((0, rows_n - tokens), (0, 0))
    mixed = dot(jnp.pad(mixed, spare), to_kept).astype(bf16)
    bias_place = place_of(jnp.int32(width), devices)
    column = lax.broadcasted_iota(jnp.int32, mixed.shape, 1)
    mixed = jnp.where(column == bias_place, jnp.ones((), bf16), mixed)
    coming = dot(jnp.pad(d_out.reshape(tokens, width), spare), to_kept).astype(bf16)
    small = jnp.concatenate(
        [h_start.astype(bf16)]
        + split_exact(c_start)
        + [in_mask.astype(bf16), out_mask.astype(bf16)],
        axis=0,
    )
    small = dot(small, to_kept)
    part = [small[streams * j : streams * (j + 1)] for j in range(6)]
    empty = jnp.zeros((LANES - streams, wide), f32)
    h_first = jnp.concatenate([part[0], empty], axis=0)
    c_first = jnp.concatenate([part[1] + part[2] + part[3], empty], axis=0)
    out_scale_kept = part[5] * KEEP_OUTPUT
    out_scale = jnp.concatenate(
        [out_scale_kept, out_scale_kept, jnp.zeros((LANES - 2 * streams, wide), f32)], axis=0
    )
    base = jnp.arange(streams, dtype=jnp.int32) * steps
    none = jnp.zeros((LANES - 2 * streams,), jnp.int32)
    begins = jnp.concatenate([base, base + pieces[:, 0], none])
    lengths = jnp.concatenate([pieces[:, 0], pieces[:, 1], none])
    ticks = lax.broadcasted_iota(jnp.int32, (LONGEST, LANES), 0)
    active = ticks < lengths[None, :]
    where = jnp.where(active, begins[None, :] + ticks, -1).reshape(-1)
    spread = (where[:, None] == lax.iota(jnp.int32, rows_n)[None, :]).astype(bf16)
    late_first = jnp.maximum(pieces[:, 0] - SPLIT, 0)
    late_base = jnp.arange(streams, dtype=jnp.int32) * LATE_BLOCK
    late_base = jnp.concatenate([late_base, late_base + late_first, none])
    early_base = LATE + SPLIT * jnp.arange(LANES, dtype=jnp.int32)
    packed = jnp.where(ticks < SPLIT, early_base[None] + ticks, late_base[None] + ticks - SPLIT)
    packed = jnp.where(active, packed, -1).reshape(-1)
    collect = (lax.iota(jnp.int32, rows_n)[:, None] == packed[None, :]).astype(bf16)
    pack = dot(collect, spread).astype(bf16)
    unpack = (
        lax.dot_general(spread, collect, (((0,), (1,)), ((), ())), preferred_element_type=f32)
    ).astype(bf16)
    mixed_rows = dot(pack, mixed).astype(bf16)
    row_stream = lax.iota(jnp.int32, rows_n) // steps
    row_stream = (row_stream[:, None] == lax.iota(jnp.int32, streams)[None]).astype(bf16)
    in_rows = dot(pack, dot(row_stream, part[4].astype(bf16)).astype(bf16)).astype(bf16)

    begin = SPLIT * LANES
    ready = (wall, mixed, mixed_rows, coming, spread, collect, h_first, c_first, out_scale)
    ready += (in_rows, unpack, to_natural, scales, spread[:begin], spread[begin:])
    ready += (collect[LATE:, :begin], collect[:LATE, begin:], spread.T)
    ready = lax.optimization_barrier(ready)
    wall, mixed, mixed_rows, coming, spread, collect, h_first, c_first, out_scale = ready[:9]
    in_rows, unpack, to_natural, scales, spread_early, spread_late = ready[9:15]
    collect_early, collect_late, gather = ready[15:]
    mixed_all = lax.all_gather(
        mixed_rows, "batch", axis=0, tiled=True, axis_index_groups=line_groups
    )
    hidden_rows, output_rows, ninth_in, kept, turned = run_forward(
        wall, mixed, spread, collect, h_first, c_first, out_scale
    )
    hidden_rows, mixed_all = lax.optimization_barrier((hidden_rows, mixed_all))
    hidden_all = lax.all_gather(
        hidden_rows, "batch", axis=0, tiled=True, axis_index_groups=line_groups
    )
    late, carry = run_backward(
        turned, kept, coming, spread_late, collect_late, out_scale, out_scale, SPLIT
    )

    def exchange(rows):
        return lax.all_to_all(
            rows, "batch", 0, 0, tiled=True, axis_index_groups=column_groups
        )

    late_mine = exchange(late)
    (early,) = run_backward(
        turned, kept, coming, spread_early, collect_early, out_scale, carry, 0
    )
    late_mine, early = lax.optimization_barrier((late_mine, early))
    early_mine = exchange(early)
    core = (me % 2).reshape(1)
    so_far = run_gradient(
        core, mixed_all, hidden_all, late_mine, lax.ppermute(late_mine, "batch", twins), 0, devices
    )
    early_mine, so_far = lax.optimization_barrier((early_mine, so_far))
    message = run_gradient(
        core,
        mixed_all,
        hidden_all,
        early_mine,
        lax.ppermute(early_mine, "batch", twins),
        LATE,
        devices,
        (so_far,),
    )
    got = lax.all_to_all(message, "batch", 0, 0, tiled=True)

    d_rows, out_rows = run_own(
        wall, ninth_in, late, early, in_rows, output_rows, gather, unpack, to_natural
    )
    output = out_rows[:tokens].reshape(streams, steps, width)
    d_inputs = d_rows[:tokens].reshape(streams, steps, width)
    got, output, d_inputs = lax.optimization_barrier((got, output, d_inputs))

    home, squares = run_settle(got, scales, to_natural)
    squares = lax.all_to_all(squares, "batch", 0, 0, tiled=True)
    home = home.reshape(block)
    tail = lax.ppermute(home[block - most :], "batch", [(i, i + 1) for i in range(devices - 1)])
    grad_shard = lax.dynamic_slice(
        jnp.concatenate([tail, home]), (most - gap * me,), (shard,)
    ).astype(f32)
    grad_norm = jnp.sqrt(jnp.sum(squares[:, 0]))

    factor = jnp.minimum(1.0, CLIP_NORM / (grad_norm + 1e-06))
    clipped = grad_shard * factor
    moment_new = BETA_ONE * moment_one + (1.0 - BETA_ONE) * clipped
    second_new = BETA_TWO * moment_two + (1.0 - BETA_TWO) * clipped * clipped
    first_hat = moment_new / (1.0 - BETA_ONE**STEP)
    second_hat = second_new / (1.0 - BETA_TWO**STEP)
    master_new = master - LEARN_RATE * (
        first_hat / (jnp.sqrt(second_hat) + EPSILON) + WEIGHT_DECAY * master
    )
    return (output, d_inputs, moment_new, second_new, master_new, grad_norm)


def solution(mesh):
    placed = (
        P("batch", None, None),
        P("batch", None, None),
        P("batch", None),
        P("batch", None),
        P("batch", None),
        P("batch", None),
        P("batch", None),
        P("batch"),
        P("batch"),
        P("batch"),
        P("batch"),
    )
    return jax.shard_map(
        body,
        mesh=mesh,
        in_specs=placed,
        out_specs=(
            P("batch", None, None),
            P("batch", None, None),
            P("batch"),
            P("batch"),
            P("batch"),
            P(),
        ),
        check_vma=False,
    )
```

```python
import functools

import jax
import jax.numpy as jnp
from jax import lax
from jax.experimental import pallas as pl
from jax.experimental.pallas import tpu as pltpu
from jax.sharding import PartitionSpec as P

STEP = 10


LEARN_RATE = 0.03
BETA_ONE = 0.9
BETA_TWO = 0.999
WEIGHT_DECAY = 0.01
EPSILON = 1e-08
CLIP_NORM = 1.0
KEEP_INPUT = 4.0 / 3.0
KEEP_OUTPUT = 4.0 / 3.0
KEEP_RECURRENT = 2.0

LONGEST = 40
LANES = 8
TILE = 8
OWN = TILE + 1
KINDS = 6
SOON = 5
SPLIT = 10
LATE = 160
LATE_BLOCK = LATE // 3
EARLY = 64
UNROLL_FORWARD = 3
UNROLL_BACKWARD = 4
MESSAGE = 88
VMEM_LIMIT = 60 * 2**20
VMEM_SMALL = 16 * 2**20

f32 = jnp.float32
bf16 = jnp.bfloat16


def dot(left, right):
    return lax.dot_general(left, right, (((1,), (0,)), ((), ())), preferred_element_type=f32)


def one_hot(rows, columns, wanted):
    row = lax.broadcasted_iota(jnp.int32, (rows, columns), 0)
    column = lax.broadcasted_iota(jnp.int32, (rows, columns), 1)
    return wanted(row, column).astype(bf16)


def place_of(natural, devices):
    owner, rest = natural // OWN, natural % OWN
    return jnp.where(rest < TILE, owner * TILE + rest, devices * TILE + owner)


def step_rows(step):
    return pl.ds(pl.multiple_of(step * LANES, LANES), LANES)


def kept_rows(step, kind):
    return pl.ds(pl.multiple_of((step * KINDS + kind) * LANES, LANES), LANES)


def fetch(sources, into, sems):
    copies = [
        pltpu.make_async_copy(source, place, sems.at[index])
        for index, (source, place) in enumerate(zip(sources, into))
    ]
    for copy in copies:
        copy.start()
    return copies


def forward_kernel(
    wall,
    mixed,
    spread,
    collect,
    h_first,
    c_first,
    out_scale,
    hidden_rows,
    output_rows,
    ninth_in,
    kept,
    turned,
    *refs,
):
    fetched, (square, w_rec, ninth, apart, pre, kept_here, hiddens, outs) = refs[:6], refs[6:14]
    sems_small, sems_in, sem_ninth, sem_rec, sems_kept, sems_turned = refs[14:]
    fetches = fetch((mixed, spread, collect, h_first, c_first, out_scale), fetched, sems_small)
    mixed, spread, collect, h_first, c_first, out_scale = fetched
    width = mixed.shape[1]
    main = wall.shape[0]
    devices = main // TILE
    gates_n = 4 * width

    copy_ninth = pltpu.make_async_copy(wall.at[:, pl.ds(2 * gates_n, width)], ninth, sem_ninth)
    copies_in = [
        pltpu.make_async_copy(
            wall.at[:, pl.ds(gate * width, width)],
            square.at[pl.ds(0, main), pl.ds(gate * width, width)],
            sems_in.at[gate],
        )
        for gate in range(4)
    ]
    copy_rec = pltpu.make_async_copy(
        wall.at[:, pl.ds(gates_n, gates_n)], w_rec.at[pl.ds(0, main), :], sem_rec
    )
    for copy in copies_in + [copy_ninth, copy_rec]:
        copy.start()
    for copy in fetches:
        copy.wait()
    rows = dot(spread[...], mixed[...]).astype(bf16)
    chunk = gates_n // 3
    arrived = 0
    for begin in range(0, gates_n, chunk):
        while arrived * width < begin + chunk:
            copies_in[arrived].wait()
            arrived += 1
        here = pl.ds(begin, chunk)
        pre[:, here] = dot(rows[:, :main], square[pl.ds(0, main), here])
    copy_ninth.wait()
    for tile in range(width // 128):
        columns = pl.ds(tile * 128, 128)
        apart[tile] = ninth[:, columns].astype(f32)
        for gate in range(8):
            rest = apart[tile, pl.ds(gate, devices, stride=8), :].astype(bf16)
            there = pl.ds(gate % 4 * width + tile * 128, 128)
            if gate < 4:
                square[pl.ds(main, devices), there] = rest
                ninth_in[gate, :, columns] = rest
            else:
                w_rec[pl.ds(main, devices), there] = rest
    for begin in range(0, gates_n, chunk):
        here = pl.ds(begin, chunk)
        pre[:, here] = pre[:, here] + dot(rows[:, main:], square[pl.ds(main, devices), here])
    copy_rec.wait()
    scale = out_scale[...]
    soon = width - 128
    sizes = (256,) * (width // 256) + ((128,) if width % 256 else ())

    def step(index, carry):
        hidden, cell = carry
        at = step_rows(index)
        hiddens[at, :] = hidden
        low = hidden.astype(bf16)
        early = pre[at, :]
        for begin in range(0, soon, 512):
            here = slice(begin, min(begin + 512, soon))
            early = early + dot(low[:, here], w_rec[here, :])
        states = ([], [])
        begin = 0
        for size in sizes:
            lanes = pl.ds(begin, size)
            gates = []
            for gate in range(4):
                first = gate * width + begin
                late = dot(low[:, soon:], w_rec[pl.ds(soon, width - soon), pl.ds(first, size)])
                gates.append(early[:, first : first + size] + late)
            in_gate = jax.nn.sigmoid(gates[0])
            forget = jax.nn.sigmoid(gates[1])
            candid = jnp.tanh(gates[2])
            out_gate = jax.nn.sigmoid(gates[3])
            before = cell[:, begin : begin + size]
            cell_new = forget * before + in_gate * candid
            squash = jnp.tanh(cell_new)
            hidden_new = out_gate * squash
            outs[at, lanes] = hidden_new * scale[:, begin : begin + size]
            kept_here[kept_rows(index, 0), lanes] = out_gate * (1.0 - squash * squash)
            kept_here[kept_rows(index, 1), lanes] = candid * in_gate * (1.0 - in_gate)
            kept_here[kept_rows(index, 2), lanes] = before * forget * (1.0 - forget)
            kept_here[kept_rows(index, 3), lanes] = in_gate * (1.0 - candid * candid)
            kept_here[kept_rows(index, 4), lanes] = squash * out_gate * (1.0 - out_gate)
            kept_here[kept_rows(index, 5), lanes] = forget
            states[0].append(hidden_new)
            states[1].append(cell_new)
            begin += size
        return tuple(jnp.concatenate(state, axis=1) for state in states)

    turns = width // 128

    def copy_kept(part):
        size = turns * KINDS * LANES
        at = pl.ds(pl.multiple_of(part * size, LANES), size)
        return pltpu.make_async_copy(kept_here.at[at, :], kept.at[at, :], sems_kept.at[part])

    def copy_turned(gate):
        here = pl.ds(pl.multiple_of(gate * width, 128), width)
        return pltpu.make_async_copy(square.at[:, here], turned.at[gate], sems_turned.at[gate])

    def part(gate, carry):
        def turning(count, carry):
            columns = pl.ds(pl.multiple_of(gate * width + count * 128, 128), 128)
            into = pl.ds(pl.multiple_of(count * 128, 128), 128)
            square[into, pl.ds(pl.multiple_of(gate * width, 128), width)] = w_rec[:, columns].T
            return step(gate * turns + count, carry)

        carry = lax.fori_loop(0, turns, turning, carry, unroll=UNROLL_FORWARD)
        copy_kept(gate).start()
        copy_turned(gate).start()
        return carry

    carry = lax.fori_loop(0, 4, part, (h_first[...], c_first[...]))
    lax.fori_loop(4 * turns, LONGEST, step, carry, unroll=UNROLL_FORWARD)
    begin = 4 * turns * KINDS * LANES
    rest = pl.ds(begin, kept_here.shape[0] - begin)
    last = pltpu.make_async_copy(kept_here.at[rest, :], kept.at[rest, :], sems_kept.at[4])
    last.start()
    hidden_rows[...] = dot(collect[...], hiddens[...].astype(bf16)).astype(bf16)
    output_rows[...] = outs[...].astype(bf16)
    for gate in range(4):
        copy_kept(gate).wait()
        copy_turned(gate).wait()
    last.wait()


def backward_kernel(
    turned,
    kept,
    coming,
    spread,
    collect,
    out_scale,
    carry_in,
    gate_rows,
    *refs,
    first_step,
):
    carry_out = refs[0]
    *fetched, w_turned, kept_here, come, dgates, sems_small, sems_turned, sems_kept = refs[-12:]
    fetches = fetch((coming, spread, collect, out_scale, carry_in), fetched, sems_small)
    coming, spread, collect, out_scale, carry_in = fetched
    width = coming.shape[1]
    steps = spread.shape[0] // LANES
    size = KINDS * LANES

    def copy_kept(part):
        begin, count = ((steps - SOON) * size, SOON * size) if part == 0 else (
            0,
            (steps - SOON) * size,
        )
        return pltpu.make_async_copy(
            kept.at[pl.ds(first_step * size + begin, count), :],
            kept_here.at[pl.ds(begin, count), :],
            sems_kept.at[part],
        )

    copies = [
        pltpu.make_async_copy(
            turned.at[gate], w_turned.at[pl.ds(gate * width, width), :], sems_turned.at[gate]
        )
        for gate in range(4)
    ]
    copy_kept(0).start()
    for copy in copies:
        copy.start()
    for copy in fetches:
        copy.wait()
    come[...] = dot(spread[...], coming[...])
    scale = out_scale[...]

    def gradients(index, carry):
        dh_next, dc_next = carry
        at = step_rows(index)
        grad_h = come[at, :] * scale + dh_next
        grad_c = dc_next + grad_h * kept_here[kept_rows(index, 0), :]
        grads = jnp.concatenate(
            [
                grad_c * kept_here[kept_rows(index, 1), :],
                grad_c * kept_here[kept_rows(index, 2), :],
                grad_c * kept_here[kept_rows(index, 3), :],
                grad_h * kept_here[kept_rows(index, 4), :],
            ],
            axis=1,
        )
        dgates[at, :] = grads
        return (grads, grad_c * kept_here[kept_rows(index, 5), :])

    def step(index, carry):
        grads, dc_next = gradients(index, carry)
        return (dot(grads.astype(bf16), w_turned[...]), dc_next)

    def run(last, count, carry):
        return lax.fori_loop(
            0, count, lambda back, c: step(last - back, c), carry, unroll=UNROLL_BACKWARD
        )

    copy_kept(0).wait()
    if first_step > 0:
        carry = (jnp.zeros((LANES, width), f32),) * 2
    else:
        carry = (carry_in[pl.ds(0, LANES), :], carry_in[pl.ds(LANES, LANES), :])
    grads, dc_next = gradients(steps - 1, carry)
    grads = grads.astype(bf16)
    dh_next = jnp.zeros((LANES, width), f32)
    for gate in range(4):
        copies[gate].wait()
        here = slice(gate * width, (gate + 1) * width)
        dh_next = dh_next + dot(grads[:, here], w_turned[here, :])
    copy_kept(1).start()
    carry = run(steps - 2, SOON - 1, (dh_next, dc_next))
    copy_kept(1).wait()
    if first_step > 0:
        carry = run(steps - SOON - 1, steps - SOON, carry)
        carry_out[pl.ds(0, LANES), :] = carry[0]
        carry_out[pl.ds(LANES, LANES), :] = carry[1]
    else:
        carry = run(steps - SOON - 1, steps - SOON - 1, carry)
        gradients(0, carry)
    for gate in range(4):
        columns = pl.ds(gate * width, width)
        gate_rows[gate] = dot(collect[...], dgates[:, columns].astype(bf16)).astype(bf16)


def gradient_kernel(
    core,
    mixed_all,
    hidden_all,
    mine,
    other,
    *refs,
    begin,
):
    result, left, right, ninth, before, sems_left, sems_right, sem_before = refs[-8:]
    so_far = refs[:-8]
    half, rows, columns = mine.shape
    line = 2 * half
    each = mixed_all.shape[0] // line
    which = core[0]

    def copies_left(source):
        found = []
        for place in range(line):
            chip, twin = place % half, place // half
            block = 2 * chip + (which if twin == 0 else 1 - which)
            found.append(
                pltpu.make_async_copy(
                    source.at[pl.ds(pl.multiple_of(block * each + begin, 16), rows), :],
                    left.at[pl.ds(place * rows, rows), :],
                    sems_left.at[place],
                )
            )
        return found

    @pl.when(which == 0)
    def _():
        for copy in copies_left(mixed_all):
            copy.start()

    @pl.when(which != 0)
    def _():
        for copy in copies_left(hidden_all):
            copy.start()

    copies_right = [
        pltpu.make_async_copy(
            (mine if place < half else other).at[place % half],
            right.at[pl.ds(place * rows, rows), :],
            sems_right.at[place],
        )
        for place in range(line)
    ]
    for copy in copies_right:
        copy.start()
    if so_far:
        copy_before = pltpu.make_async_copy(so_far[0], before, sem_before)
        copy_before.start()
    for copy in copies_left(mixed_all) + copies_right:
        copy.wait()
    grad = lax.dot_general(
        left[...], right[...], (((0,), (0,)), ((), ())), preferred_element_type=f32
    )
    if not so_far:
        result[...] = grad
        return
    copy_before.wait()
    devices = result.shape[0]
    main = devices * TILE
    tiles = columns // 128
    ninth[...] = jnp.zeros(ninth.shape, f32)
    for tile in range(0, tiles, 2):
        parts = []
        for place in range(tile, min(tile + 2, tiles)):
            here = grad[:, place * 128 : (place + 1) * 128] + before[:, pl.ds(place * 128, 128)]
            parts.append(here[:main].reshape(devices, TILE, 128))
            ninth[:, place, :] = here[main:]
        if tile + 2 > tiles:
            parts.append(ninth[...])
        rows = jnp.concatenate(parts, axis=1)
        result[:, pl.ds(tile * TILE, rows.shape[1]), :] = rows.astype(bf16)


def settle_kernel(got, scale, home, squares, placed):
    devices = got.shape[0]
    tiles = placed.shape[0]
    line = 8
    half = line // 2
    for source in range(line):
        gate = (source % 2) * half + source // 2
        found = got[source].astype(f32)
        for index in range(source + line, devices, line):
            found = found + got[index].astype(f32)
        for tile in range(tiles):
            placed[tile, pl.ds(gate, TILE, stride=8), :] = found[tile * TILE : (tile + 1) * TILE]
            ninth = OWN * TILE + tile
            placed[tile, pl.ds(TILE * 8 + gate, 1), :] = found[ninth : ninth + 1]
    values = jnp.concatenate([placed[tile] for tile in range(tiles)], axis=1)
    values = values * scale[...].astype(f32)
    total = jnp.sum(jnp.sum(values * values, axis=0, keepdims=True), axis=1, keepdims=True)
    squares[...] = jnp.broadcast_to(total, squares.shape)
    low = values.astype(bf16)
    width = home.shape[1]
    main = devices * TILE
    for begin in range(0, width, 128):
        first = min(begin // (16 * OWN) * 128, main - 256)
        natural = begin + lax.broadcasted_iota(jnp.int32, (1, 128), 1)
        owner = lax.shift_right_logical(natural * 7282, 16)
        rest = natural - OWN * owner
        source = jnp.where(rest < TILE, owner * TILE + rest - first, 256 + owner)
        row = lax.broadcasted_iota(jnp.int32, (384, 128), 0)
        order = jnp.where(row == source, 1.0, 0.0).astype(bf16)
        near = jnp.concatenate([low[:, first : first + 256], low[:, main:]], axis=1)
        size = min(128, width - begin)
        home[:, pl.ds(begin, size)] = dot(near, order).astype(bf16)[:, :size]


def own_kernel(
    wall,
    ninth_in,
    late,
    early,
    in_rows,
    output_rows,
    gather,
    unpack,
    to_natural,
    d_out,
    out,
    square,
    sems,
):
    width = in_rows.shape[1]
    rows = in_rows.shape[0]
    main = wall.shape[0]
    rest = width - main
    copies = []
    for gate in range(4):
        copies.append(
            pltpu.make_async_copy(
                wall.at[:, pl.ds(gate * width, width)],
                square.at[gate, pl.ds(0, main), :],
                sems.at[2 * gate],
            )
        )
        copies.append(
            pltpu.make_async_copy(
                ninth_in.at[gate], square.at[gate, pl.ds(main, rest), :], sems.at[2 * gate + 1]
            )
        )
    for copy in copies:
        copy.start()

    def natural(places, values):
        return dot(dot(places[...], values).astype(bf16), to_natural[...]).astype(bf16)

    out[...] = natural(gather, output_rows[...])

    def right_product(left, matrix):
        return lax.dot_general(
            left, matrix, (((1,), (1,)), ((), ())), preferred_element_type=f32
        )

    found = jnp.zeros((rows, width), f32)
    for gate in range(4):
        copies[2 * gate].wait()
        copies[2 * gate + 1].wait()
        both = jnp.concatenate([late[gate], early[gate]], axis=0)
        found = found + right_product(both, square[gate])
    found = found * (in_rows[...].astype(f32) * KEEP_INPUT)
    d_out[...] = natural(unpack, found.astype(bf16))


def in_vmem():
    return pl.BlockSpec(memory_space=pltpu.VMEM)


def in_place():
    return pl.BlockSpec(memory_space=pl.ANY)


def places_for(*arrays):
    return [pltpu.VMEM(array.shape, array.dtype) for array in arrays]


def run_forward(wall, mixed, spread, collect, h_first, c_first, out_scale):
    steps_rows = spread.shape[0]
    rows, width = mixed.shape
    devices = wall.shape[0] // TILE
    all_kept = LONGEST * KINDS * LANES
    return pl.pallas_call(
        forward_kernel,
        out_shape=(
            jax.ShapeDtypeStruct((collect.shape[0], width), bf16),
            jax.ShapeDtypeStruct((steps_rows, width), bf16),
            jax.ShapeDtypeStruct((4, devices, width), bf16),
            jax.ShapeDtypeStruct((all_kept, width), f32),
            jax.ShapeDtypeStruct((4, width, width), bf16),
        ),
        in_specs=[in_place()] * 7,
        out_specs=(in_vmem(),) * 3 + (in_place(),) * 2,
        scratch_shapes=places_for(mixed, spread, collect, h_first, c_first, out_scale)
        + [
            pltpu.VMEM((width, 4 * width), bf16),
            pltpu.VMEM((width, 4 * width), bf16),
            pltpu.VMEM((devices * TILE, width), bf16),
            pltpu.VMEM((width // 128, devices * TILE, 128), f32),
            pltpu.VMEM((steps_rows, 4 * width), f32),
            pltpu.VMEM((all_kept, width), f32),
            pltpu.VMEM((steps_rows, width), f32),
            pltpu.VMEM((steps_rows, width), f32),
            pltpu.SemaphoreType.DMA((6,)),
            pltpu.SemaphoreType.DMA((4,)),
            pltpu.SemaphoreType.DMA,
            pltpu.SemaphoreType.DMA,
            pltpu.SemaphoreType.DMA((5,)),
            pltpu.SemaphoreType.DMA((4,)),
        ],
        compiler_params=pltpu.CompilerParams(vmem_limit_bytes=VMEM_LIMIT),
        cost_estimate=pl.CostEstimate(
            flops=60_000_000_000, bytes_accessed=30_000_000, transcendentals=2_000_000
        ),
        name="forward",
    )(wall, mixed, spread, collect, h_first, c_first, out_scale)


def run_backward(turned, kept, coming, spread, collect, out_scale, carry, first_step):
    steps_rows = spread.shape[0]
    rows, width = collect.shape[0], coming.shape[1]
    results = [jax.ShapeDtypeStruct((4, rows, width), bf16)]
    if first_step > 0:
        results.append(jax.ShapeDtypeStruct((2 * LANES, width), f32))
    return pl.pallas_call(
        functools.partial(backward_kernel, first_step=first_step),
        out_shape=results,
        in_specs=[in_place()] * 7,
        out_specs=[in_vmem()] * len(results),
        scratch_shapes=places_for(coming, spread, collect, out_scale, carry)
        + [
            pltpu.VMEM((4 * width, width), bf16),
            pltpu.VMEM((steps_rows * KINDS, width), f32),
            pltpu.VMEM((steps_rows, width), f32),
            pltpu.VMEM((steps_rows, 4 * width), f32),
            pltpu.SemaphoreType.DMA((5,)),
            pltpu.SemaphoreType.DMA((4,)),
            pltpu.SemaphoreType.DMA((2,)),
        ],
        compiler_params=pltpu.CompilerParams(vmem_limit_bytes=VMEM_LIMIT),
        cost_estimate=pl.CostEstimate(
            flops=steps_rows // LANES * 1_500_000_000, bytes_accessed=20_000_000, transcendentals=0
        ),
        name="backward_late" if first_step else "backward_early",
    )(turned, kept, coming, spread, collect, out_scale, carry)


def run_gradient(core, mixed_all, hidden_all, mine, other, begin, devices, so_far=()):
    half, rows, columns = mine.shape
    line = 2 * half
    width = mixed_all.shape[1]
    if so_far:
        result = jax.ShapeDtypeStruct((devices, MESSAGE, 128), bf16)
    else:
        result = jax.ShapeDtypeStruct((width, columns), f32)
    return pl.pallas_call(
        functools.partial(gradient_kernel, begin=begin),
        out_shape=result,
        in_specs=[pl.BlockSpec(memory_space=pltpu.SMEM)]
        + [in_place()] * (4 + len(so_far)),
        out_specs=in_vmem(),
        scratch_shapes=[
            pltpu.VMEM((line * rows, width), bf16),
            pltpu.VMEM((line * rows, columns), bf16),
            pltpu.VMEM((devices, 2 * TILE, 128), f32),
            pltpu.VMEM((width, columns), f32),
            pltpu.SemaphoreType.DMA((line,)),
            pltpu.SemaphoreType.DMA((line,)),
            pltpu.SemaphoreType.DMA,
        ],
        compiler_params=pltpu.CompilerParams(vmem_limit_bytes=VMEM_LIMIT),
        cost_estimate=pl.CostEstimate(
            flops=5_000_000_000, bytes_accessed=12_000_000, transcendentals=0
        ),
        name="gradient_early" if so_far else "gradient_late",
    )(core, mixed_all, hidden_all, mine, other, *so_far)


def run_settle(got, scale, width):
    devices = got.shape[0]
    wide = scale.shape[1]
    return pl.pallas_call(
        settle_kernel,
        out_shape=(
            jax.ShapeDtypeStruct((OWN * 8, width), bf16),
            jax.ShapeDtypeStruct((devices, 128), f32),
        ),
        in_specs=[in_vmem()] * 2,
        out_specs=(in_vmem(),) * 2,
        scratch_shapes=[pltpu.VMEM((wide // 128, OWN * 8, 128), f32)],
        compiler_params=pltpu.CompilerParams(vmem_limit_bytes=VMEM_SMALL),
        name="settle",
    )(got, scale)


def run_own(wall, ninth_in, late, early, in_rows, output_rows, gather, unpack, to_natural):
    width, natural = to_natural.shape
    rows = unpack.shape[0]
    return pl.pallas_call(
        own_kernel,
        out_shape=(jax.ShapeDtypeStruct((rows, natural), bf16),) * 2,
        in_specs=[in_place()] * 2 + [in_vmem()] * 7,
        out_specs=(in_vmem(),) * 2,
        scratch_shapes=[
            pltpu.VMEM((4, width, width), bf16),
            pltpu.SemaphoreType.DMA((8,)),
        ],
        compiler_params=pltpu.CompilerParams(vmem_limit_bytes=VMEM_LIMIT),
        cost_estimate=pl.CostEstimate(
            flops=8_000_000_000, bytes_accessed=15_000_000, transcendentals=0
        ),
        name="own",
    )(wall, ninth_in, late, early, in_rows, output_rows, gather, unpack, to_natural)


def split_exact(values):
    parts = []
    rest = values
    for _ in range(3):
        part = lax.reduce_precision(rest, 8, 7)
        parts.append(part.astype(bf16))
        rest = rest - part
    return parts


def body(
    inputs,
    d_out,
    h_start,
    c_start,
    pieces,
    in_mask,
    out_mask,
    w_mask,
    master,
    moment_one,
    moment_two,
):
    streams, steps, width = inputs.shape
    gates_n = 4 * width
    count_w = 2 * width * gates_n
    total = count_w + gates_n
    shard = master.shape[0]
    devices = lax.axis_size("batch")
    me = lax.axis_index("batch")
    wide = OWN * devices
    block = OWN * 2 * gates_n
    gap = block - shard
    most = gap * devices
    tokens = streams * steps
    rows_n = LATE + EARLY
    line = 8
    lines = devices // line

    line_groups = [[line * q + m for m in range(line)] for q in range(lines)]
    column_groups = [
        [line * q + 2 * y + c for y in range(line // 2)] for q in range(lines) for c in range(2)
    ]
    twins = [(i, i ^ 1) for i in range(devices)]

    to_kept = one_hot(width, wide, lambda k, p: place_of(k, devices) == p)
    to_natural = one_hot(wide, width, lambda p, k: place_of(k, devices) == p)

    places = me * shard + lax.iota(jnp.int32, shard)
    recurrent = (places < count_w) & (places % (2 * gates_n) >= gates_n)
    scale_low = jnp.where(recurrent, w_mask.astype(bf16) * KEEP_RECURRENT, jnp.ones((), bf16))
    local_low = master.astype(bf16) * scale_low
    local_low = jnp.where(places < total, local_low, jnp.zeros((), bf16))

    def realigned(flat, following):
        joined = jnp.concatenate([flat, following])
        rows = lax.dynamic_slice(joined, (gap * me,), (block,)).reshape(OWN * 8, width)
        return dot(rows, to_kept).astype(bf16)

    before = [(i + 1, i) for i in range(devices - 1)]
    order = one_hot(
        OWN * 8,
        OWN * 8,
        lambda a, b: jnp.where(a < 64, (a % 8) * 8 + a // 8, 64 + a % 8) == b,
    )
    own = realigned(local_low, lax.ppermute(local_low[:most], "batch", before))
    own = dot(order, own).astype(bf16)
    own = jnp.concatenate([own[TILE * j : TILE * (j + 1)] for j in range(OWN)], axis=1)
    wall = lax.all_gather(own, "batch", axis=0, tiled=True)
    scales = realigned(scale_low, lax.ppermute(scale_low[:most], "batch", before))

    in_scale = in_mask.astype(f32) * KEEP_INPUT
    mixed = (inputs.astype(f32) * in_scale[:, None, :]).astype(bf16).reshape(tokens, width)
    spare = ((0, rows_n - tokens), (0, 0))
    mixed = dot(jnp.pad(mixed, spare), to_kept).astype(bf16)
    bias_place = place_of(jnp.int32(width), devices)
    column = lax.broadcasted_iota(jnp.int32, mixed.shape, 1)
    mixed = jnp.where(column == bias_place, jnp.ones((), bf16), mixed)
    coming = dot(jnp.pad(d_out.reshape(tokens, width), spare), to_kept).astype(bf16)
    small = jnp.concatenate(
        [h_start.astype(bf16)]
        + split_exact(c_start)
        + [in_mask.astype(bf16), out_mask.astype(bf16)],
        axis=0,
    )
    small = dot(small, to_kept)
    part = [small[streams * j : streams * (j + 1)] for j in range(6)]
    empty = jnp.zeros((LANES - streams, wide), f32)
    h_first = jnp.concatenate([part[0], empty], axis=0)
    c_first = jnp.concatenate([part[1] + part[2] + part[3], empty], axis=0)
    out_scale_kept = part[5] * KEEP_OUTPUT
    out_scale = jnp.concatenate(
        [out_scale_kept, out_scale_kept, jnp.zeros((LANES - 2 * streams, wide), f32)], axis=0
    )
    base = jnp.arange(streams, dtype=jnp.int32) * steps
    none = jnp.zeros((LANES - 2 * streams,), jnp.int32)
    begins = jnp.concatenate([base, base + pieces[:, 0], none])
    lengths = jnp.concatenate([pieces[:, 0], pieces[:, 1], none])
    ticks = lax.broadcasted_iota(jnp.int32, (LONGEST, LANES), 0)
    active = ticks < lengths[None, :]
    where = jnp.where(active, begins[None, :] + ticks, -1).reshape(-1)
    spread = (where[:, None] == lax.iota(jnp.int32, rows_n)[None, :]).astype(bf16)
    late_first = jnp.maximum(pieces[:, 0] - SPLIT, 0)
    late_base = jnp.arange(streams, dtype=jnp.int32) * LATE_BLOCK
    late_base = jnp.concatenate([late_base, late_base + late_first, none])
    early_base = LATE + SPLIT * jnp.arange(LANES, dtype=jnp.int32)
    packed = jnp.where(ticks < SPLIT, early_base[None] + ticks, late_base[None] + ticks - SPLIT)
    packed = jnp.where(active, packed, -1).reshape(-1)
    collect = (lax.iota(jnp.int32, rows_n)[:, None] == packed[None, :]).astype(bf16)
    pack = dot(collect, spread).astype(bf16)
    unpack = (
        lax.dot_general(spread, collect, (((0,), (1,)), ((), ())), preferred_element_type=f32)
    ).astype(bf16)
    mixed_rows = dot(pack, mixed).astype(bf16)
    row_stream = lax.iota(jnp.int32, rows_n) // steps
    row_stream = (row_stream[:, None] == lax.iota(jnp.int32, streams)[None]).astype(bf16)
    in_rows = dot(pack, dot(row_stream, part[4].astype(bf16)).astype(bf16)).astype(bf16)

    begin = SPLIT * LANES
    ready = (wall, mixed, mixed_rows, coming, spread, collect, h_first, c_first, out_scale)
    ready += (in_rows, unpack, to_natural, scales, spread[:begin], spread[begin:])
    ready += (collect[LATE:, :begin], collect[:LATE, begin:], spread.T)
    ready = lax.optimization_barrier(ready)
    wall, mixed, mixed_rows, coming, spread, collect, h_first, c_first, out_scale = ready[:9]
    in_rows, unpack, to_natural, scales, spread_early, spread_late = ready[9:15]
    collect_early, collect_late, gather = ready[15:]
    mixed_all = lax.all_gather(
        mixed_rows, "batch", axis=0, tiled=True, axis_index_groups=line_groups
    )
    hidden_rows, output_rows, ninth_in, kept, turned = run_forward(
        wall, mixed, spread, collect, h_first, c_first, out_scale
    )
    hidden_rows, mixed_all = lax.optimization_barrier((hidden_rows, mixed_all))
    hidden_all = lax.all_gather(
        hidden_rows, "batch", axis=0, tiled=True, axis_index_groups=line_groups
    )
    late, carry = run_backward(
        turned, kept, coming, spread_late, collect_late, out_scale, out_scale, SPLIT
    )

    def exchange(rows):
        return lax.all_to_all(
            rows, "batch", 0, 0, tiled=True, axis_index_groups=column_groups
        )

    late_mine = exchange(late)
    (early,) = run_backward(
        turned, kept, coming, spread_early, collect_early, out_scale, carry, 0
    )
    late_mine, early = lax.optimization_barrier((late_mine, early))
    early_mine = exchange(early)
    core = (me % 2).reshape(1)
    so_far = run_gradient(
        core, mixed_all, hidden_all, late_mine, lax.ppermute(late_mine, "batch", twins), 0, devices
    )
    early_mine, so_far = lax.optimization_barrier((early_mine, so_far))
    message = run_gradient(
        core,
        mixed_all,
        hidden_all,
        early_mine,
        lax.ppermute(early_mine, "batch", twins),
        LATE,
        devices,
        (so_far,),
    )
    got = lax.all_to_all(message, "batch", 0, 0, tiled=True)

    d_rows, out_rows = run_own(
        wall, ninth_in, late, early, in_rows, output_rows, gather, unpack, to_natural
    )
    output = out_rows[:tokens].reshape(streams, steps, width)
    d_inputs = d_rows[:tokens].reshape(streams, steps, width)
    got, output, d_inputs = lax.optimization_barrier((got, output, d_inputs))

    home, squares = run_settle(got, scales, width)
    squares = lax.all_to_all(squares, "batch", 0, 0, tiled=True)
    home = home.reshape(block)
    tail = lax.ppermute(home[block - most :], "batch", [(i, i + 1) for i in range(devices - 1)])
    grad_shard = lax.dynamic_slice(
        jnp.concatenate([tail, home]), (most - gap * me,), (shard,)
    ).astype(f32)
    grad_norm = jnp.sqrt(jnp.sum(squares[:, 0]))

    factor = jnp.minimum(1.0, CLIP_NORM / (grad_norm + 1e-06))
    clipped = grad_shard * factor
    moment_new = BETA_ONE * moment_one + (1.0 - BETA_ONE) * clipped
    second_new = BETA_TWO * moment_two + (1.0 - BETA_TWO) * clipped * clipped
    first_hat = moment_new / (1.0 - BETA_ONE**STEP)
    second_hat = second_new / (1.0 - BETA_TWO**STEP)
    master_new = master - LEARN_RATE * (
        first_hat / (jnp.sqrt(second_hat) + EPSILON) + WEIGHT_DECAY * master
    )
    return (output, d_inputs, moment_new, second_new, master_new, grad_norm)


def solution(mesh):
    placed = (
        P("batch", None, None),
        P("batch", None, None),
        P("batch", None),
        P("batch", None),
        P("batch", None),
        P("batch", None),
        P("batch", None),
        P("batch"),
        P("batch"),
        P("batch"),
        P("batch"),
    )
    return jax.shard_map(
        body,
        mesh=mesh,
        in_specs=placed,
        out_specs=(
            P("batch", None, None),
            P("batch", None, None),
            P("batch"),
            P("batch"),
            P("batch"),
            P(),
        ),
        check_vma=False,
    )
```

```python
import functools

import jax
import jax.numpy as jnp
from jax import lax
from jax.experimental import pallas as pl
from jax.experimental.pallas import tpu as pltpu
from jax.sharding import PartitionSpec as P

STEP = 10


LEARN_RATE = 0.03
BETA_ONE = 0.9
BETA_TWO = 0.999
WEIGHT_DECAY = 0.01
EPSILON = 1e-08
CLIP_NORM = 1.0
KEEP_INPUT = 4.0 / 3.0
KEEP_OUTPUT = 4.0 / 3.0
KEEP_RECURRENT = 2.0

LONGEST = 40
LANES = 8
TILE = 8
OWN = TILE + 1
KINDS = 6
SOON = 5
SPLIT = 11
LATE = 144
LATE_BLOCK = LATE // 3
EARLY = 80
UNROLL_FORWARD = 3
UNROLL_BACKWARD = 4
MESSAGE = 88
VMEM_LIMIT = 60 * 2**20
VMEM_SMALL = 16 * 2**20

f32 = jnp.float32
bf16 = jnp.bfloat16


def dot(left, right):
    return lax.dot_general(left, right, (((1,), (0,)), ((), ())), preferred_element_type=f32)


def one_hot(rows, columns, wanted):
    row = lax.broadcasted_iota(jnp.int32, (rows, columns), 0)
    column = lax.broadcasted_iota(jnp.int32, (rows, columns), 1)
    return wanted(row, column).astype(bf16)


def place_of(natural, devices):
    owner, rest = natural // OWN, natural % OWN
    return jnp.where(rest < TILE, owner * TILE + rest, devices * TILE + owner)


def step_rows(step):
    return pl.ds(pl.multiple_of(step * LANES, LANES), LANES)


def kept_rows(step, kind):
    return pl.ds(pl.multiple_of((step * KINDS + kind) * LANES, LANES), LANES)


def fetch(sources, into, sems):
    copies = [
        pltpu.make_async_copy(source, place, sems.at[index])
        for index, (source, place) in enumerate(zip(sources, into))
    ]
    for copy in copies:
        copy.start()
    return copies


def forward_kernel(
    wall,
    mixed,
    spread,
    collect,
    h_first,
    c_first,
    out_scale,
    hidden_rows,
    output_rows,
    ninth_in,
    kept,
    turned,
    *refs,
):
    fetched, (square, w_rec, ninth, apart, pre, kept_here, hiddens, outs) = refs[:6], refs[6:14]
    sems_small, sems_in, sem_ninth, sem_rec, sems_kept, sems_turned = refs[14:]
    fetches = fetch((mixed, spread, collect, h_first, c_first, out_scale), fetched, sems_small)
    mixed, spread, collect, h_first, c_first, out_scale = fetched
    width = mixed.shape[1]
    main = wall.shape[0]
    devices = main // TILE
    gates_n = 4 * width

    copy_ninth = pltpu.make_async_copy(wall.at[:, pl.ds(2 * gates_n, width)], ninth, sem_ninth)
    copies_in = [
        pltpu.make_async_copy(
            wall.at[:, pl.ds(gate * width, width)],
            square.at[pl.ds(0, main), pl.ds(gate * width, width)],
            sems_in.at[gate],
        )
        for gate in range(4)
    ]
    copy_rec = pltpu.make_async_copy(
        wall.at[:, pl.ds(gates_n, gates_n)], w_rec.at[pl.ds(0, main), :], sem_rec
    )
    for copy in copies_in + [copy_ninth, copy_rec]:
        copy.start()
    for copy in fetches:
        copy.wait()
    rows = dot(spread[...], mixed[...]).astype(bf16)
    chunk = gates_n // 3
    arrived = 0
    for begin in range(0, gates_n, chunk):
        while arrived * width < begin + chunk:
            copies_in[arrived].wait()
            arrived += 1
        here = pl.ds(begin, chunk)
        pre[:, here] = dot(rows[:, :main], square[pl.ds(0, main), here])
    copy_ninth.wait()
    for tile in range(width // 128):
        columns = pl.ds(tile * 128, 128)
        apart[tile] = ninth[:, columns].astype(f32)
        for gate in range(8):
            rest = apart[tile, pl.ds(gate, devices, stride=8), :].astype(bf16)
            there = pl.ds(gate % 4 * width + tile * 128, 128)
            if gate < 4:
                square[pl.ds(main, devices), there] = rest
                ninth_in[gate, :, columns] = rest
            else:
                w_rec[pl.ds(main, devices), there] = rest
    for begin in range(0, gates_n, chunk):
        here = pl.ds(begin, chunk)
        pre[:, here] = pre[:, here] + dot(rows[:, main:], square[pl.ds(main, devices), here])
    copy_rec.wait()
    scale = out_scale[...]
    soon = width - 128
    sizes = (256,) * (width // 256) + ((128,) if width % 256 else ())

    def step(index, carry):
        hidden, cell = carry
        at = step_rows(index)
        hiddens[at, :] = hidden
        low = hidden.astype(bf16)
        early = pre[at, :]
        for begin in range(0, soon, 512):
            here = slice(begin, min(begin + 512, soon))
            early = early + dot(low[:, here], w_rec[here, :])
        states = ([], [])
        begin = 0
        for size in sizes:
            lanes = pl.ds(begin, size)
            gates = []
            for gate in range(4):
                first = gate * width + begin
                late = dot(low[:, soon:], w_rec[pl.ds(soon, width - soon), pl.ds(first, size)])
                gates.append(early[:, first : first + size] + late)
            in_gate = jax.nn.sigmoid(gates[0])
            forget = jax.nn.sigmoid(gates[1])
            candid = jnp.tanh(gates[2])
            out_gate = jax.nn.sigmoid(gates[3])
            before = cell[:, begin : begin + size]
            cell_new = forget * before + in_gate * candid
            squash = jnp.tanh(cell_new)
            hidden_new = out_gate * squash
            outs[at, lanes] = hidden_new * scale[:, begin : begin + size]
            kept_here[kept_rows(index, 0), lanes] = out_gate * (1.0 - squash * squash)
            kept_here[kept_rows(index, 1), lanes] = candid * in_gate * (1.0 - in_gate)
            kept_here[kept_rows(index, 2), lanes] = before * forget * (1.0 - forget)
            kept_here[kept_rows(index, 3), lanes] = in_gate * (1.0 - candid * candid)
            kept_here[kept_rows(index, 4), lanes] = squash * out_gate * (1.0 - out_gate)
            kept_here[kept_rows(index, 5), lanes] = forget
            states[0].append(hidden_new)
            states[1].append(cell_new)
            begin += size
        return tuple(jnp.concatenate(state, axis=1) for state in states)

    turns = width // 128

    def copy_kept(part):
        size = turns * KINDS * LANES
        at = pl.ds(pl.multiple_of(part * size, LANES), size)
        return pltpu.make_async_copy(kept_here.at[at, :], kept.at[at, :], sems_kept.at[part])

    def copy_turned(gate):
        here = pl.ds(pl.multiple_of(gate * width, 128), width)
        return pltpu.make_async_copy(square.at[:, here], turned.at[gate], sems_turned.at[gate])

    def part(gate, carry):
        def turning(count, carry):
            columns = pl.ds(pl.multiple_of(gate * width + count * 128, 128), 128)
            into = pl.ds(pl.multiple_of(count * 128, 128), 128)
            square[into, pl.ds(pl.multiple_of(gate * width, 128), width)] = w_rec[:, columns].T
            return step(gate * turns + count, carry)

        carry = lax.fori_loop(0, turns, turning, carry, unroll=UNROLL_FORWARD)
        copy_kept(gate).start()
        copy_turned(gate).start()
        return carry

    carry = lax.fori_loop(0, 4, part, (h_first[...], c_first[...]))
    lax.fori_loop(4 * turns, LONGEST, step, carry, unroll=UNROLL_FORWARD)
    begin = 4 * turns * KINDS * LANES
    rest = pl.ds(begin, kept_here.shape[0] - begin)
    last = pltpu.make_async_copy(kept_here.at[rest, :], kept.at[rest, :], sems_kept.at[4])
    last.start()
    hidden_rows[...] = dot(collect[...], hiddens[...].astype(bf16)).astype(bf16)
    output_rows[...] = outs[...].astype(bf16)
    for gate in range(4):
        copy_kept(gate).wait()
        copy_turned(gate).wait()
    last.wait()


def backward_kernel(
    turned,
    kept,
    coming,
    spread,
    collect,
    out_scale,
    carry_in,
    gate_rows,
    *refs,
    first_step,
):
    carry_out = refs[0]
    *fetched, w_turned, kept_here, come, dgates, sems_small, sems_turned, sems_kept = refs[-12:]
    fetches = fetch((coming, spread, collect, out_scale, carry_in), fetched, sems_small)
    coming, spread, collect, out_scale, carry_in = fetched
    width = coming.shape[1]
    steps = spread.shape[0] // LANES
    size = KINDS * LANES

    def copy_kept(part):
        begin, count = ((steps - SOON) * size, SOON * size) if part == 0 else (
            0,
            (steps - SOON) * size,
        )
        return pltpu.make_async_copy(
            kept.at[pl.ds(first_step * size + begin, count), :],
            kept_here.at[pl.ds(begin, count), :],
            sems_kept.at[part],
        )

    copies = [
        pltpu.make_async_copy(
            turned.at[gate], w_turned.at[pl.ds(gate * width, width), :], sems_turned.at[gate]
        )
        for gate in range(4)
    ]
    copy_kept(0).start()
    for copy in copies:
        copy.start()
    for copy in fetches:
        copy.wait()
    come[...] = dot(spread[...], coming[...])
    scale = out_scale[...]

    def gradients(index, carry):
        dh_next, dc_next = carry
        at = step_rows(index)
        grad_h = come[at, :] * scale + dh_next
        grad_c = dc_next + grad_h * kept_here[kept_rows(index, 0), :]
        grads = jnp.concatenate(
            [
                grad_c * kept_here[kept_rows(index, 1), :],
                grad_c * kept_here[kept_rows(index, 2), :],
                grad_c * kept_here[kept_rows(index, 3), :],
                grad_h * kept_here[kept_rows(index, 4), :],
            ],
            axis=1,
        )
        dgates[at, :] = grads
        return (grads, grad_c * kept_here[kept_rows(index, 5), :])

    def step(index, carry):
        grads, dc_next = gradients(index, carry)
        return (dot(grads.astype(bf16), w_turned[...]), dc_next)

    def run(last, count, carry):
        return lax.fori_loop(
            0, count, lambda back, c: step(last - back, c), carry, unroll=UNROLL_BACKWARD
        )

    copy_kept(0).wait()
    if first_step > 0:
        carry = (jnp.zeros((LANES, width), f32),) * 2
    else:
        carry = (carry_in[pl.ds(0, LANES), :], carry_in[pl.ds(LANES, LANES), :])
    grads, dc_next = gradients(steps - 1, carry)
    grads = grads.astype(bf16)
    dh_next = jnp.zeros((LANES, width), f32)
    for gate in range(4):
        copies[gate].wait()
        here = slice(gate * width, (gate + 1) * width)
        dh_next = dh_next + dot(grads[:, here], w_turned[here, :])
    copy_kept(1).start()
    carry = run(steps - 2, SOON - 1, (dh_next, dc_next))
    copy_kept(1).wait()
    if first_step > 0:
        carry = run(steps - SOON - 1, steps - SOON, carry)
        carry_out[pl.ds(0, LANES), :] = carry[0]
        carry_out[pl.ds(LANES, LANES), :] = carry[1]
    else:
        carry = run(steps - SOON - 1, steps - SOON - 1, carry)
        gradients(0, carry)
    for gate in range(4):
        columns = pl.ds(gate * width, width)
        gate_rows[gate] = dot(collect[...], dgates[:, columns].astype(bf16)).astype(bf16)


def gradient_kernel(
    core,
    mixed_all,
    hidden_all,
    mine,
    other,
    *refs,
    begin,
):
    result, left, right, ninth, before, sems_left, sems_right, sem_before = refs[-8:]
    so_far = refs[:-8]
    half, rows, columns = mine.shape
    line = 2 * half
    each = mixed_all.shape[0] // line
    which = core[0]

    def copies_left(source):
        found = []
        for place in range(line):
            chip, twin = place % half, place // half
            block = 2 * chip + (which if twin == 0 else 1 - which)
            found.append(
                pltpu.make_async_copy(
                    source.at[pl.ds(pl.multiple_of(block * each + begin, 16), rows), :],
                    left.at[pl.ds(place * rows, rows), :],
                    sems_left.at[place],
                )
            )
        return found

    @pl.when(which == 0)
    def _():
        for copy in copies_left(mixed_all):
            copy.start()

    @pl.when(which != 0)
    def _():
        for copy in copies_left(hidden_all):
            copy.start()

    copies_right = [
        pltpu.make_async_copy(
            (mine if place < half else other).at[place % half],
            right.at[pl.ds(place * rows, rows), :],
            sems_right.at[place],
        )
        for place in range(line)
    ]
    for copy in copies_right:
        copy.start()
    if so_far:
        copy_before = pltpu.make_async_copy(so_far[0], before, sem_before)
        copy_before.start()
    for copy in copies_left(mixed_all) + copies_right:
        copy.wait()
    grad = lax.dot_general(
        left[...], right[...], (((0,), (0,)), ((), ())), preferred_element_type=f32
    )
    if not so_far:
        result[...] = grad
        return
    copy_before.wait()
    devices = result.shape[0]
    main = devices * TILE
    tiles = columns // 128
    ninth[...] = jnp.zeros(ninth.shape, f32)
    for tile in range(0, tiles, 2):
        parts = []
        for place in range(tile, min(tile + 2, tiles)):
            here = grad[:, place * 128 : (place + 1) * 128] + before[:, pl.ds(place * 128, 128)]
            parts.append(here[:main].reshape(devices, TILE, 128))
            ninth[:, place, :] = here[main:]
        if tile + 2 > tiles:
            parts.append(ninth[...])
        rows = jnp.concatenate(parts, axis=1)
        result[:, pl.ds(tile * TILE, rows.shape[1]), :] = rows.astype(bf16)


def settle_kernel(got, scale, home, squares, placed):
    devices = got.shape[0]
    tiles = placed.shape[0]
    line = 8
    half = line // 2
    for source in range(line):
        gate = (source % 2) * half + source // 2
        found = got[source].astype(f32)
        for index in range(source + line, devices, line):
            found = found + got[index].astype(f32)
        for tile in range(tiles):
            placed[tile, pl.ds(gate, TILE, stride=8), :] = found[tile * TILE : (tile + 1) * TILE]
            ninth = OWN * TILE + tile
            placed[tile, pl.ds(TILE * 8 + gate, 1), :] = found[ninth : ninth + 1]
    values = jnp.concatenate([placed[tile] for tile in range(tiles)], axis=1)
    values = values * scale[...].astype(f32)
    total = jnp.sum(jnp.sum(values * values, axis=0, keepdims=True), axis=1, keepdims=True)
    squares[...] = jnp.broadcast_to(total, squares.shape)
    low = values.astype(bf16)
    width = home.shape[1]
    main = devices * TILE
    for begin in range(0, width, 128):
        first = min(begin // (16 * OWN) * 128, main - 256)
        natural = begin + lax.broadcasted_iota(jnp.int32, (1, 128), 1)
        owner = lax.shift_right_logical(natural * 7282, 16)
        rest = natural - OWN * owner
        source = jnp.where(rest < TILE, owner * TILE + rest - first, 256 + owner)
        row = lax.broadcasted_iota(jnp.int32, (384, 128), 0)
        order = jnp.where(row == source, 1.0, 0.0).astype(bf16)
        near = jnp.concatenate([low[:, first : first + 256], low[:, main:]], axis=1)
        size = min(128, width - begin)
        home[:, pl.ds(begin, size)] = dot(near, order).astype(bf16)[:, :size]


def own_kernel(
    wall,
    ninth_in,
    late,
    early,
    in_rows,
    output_rows,
    gather,
    unpack,
    to_natural,
    d_out,
    out,
    square,
    sems,
):
    width = in_rows.shape[1]
    rows = in_rows.shape[0]
    main = wall.shape[0]
    rest = width - main
    copies = []
    for gate in range(4):
        copies.append(
            pltpu.make_async_copy(
                wall.at[:, pl.ds(gate * width, width)],
                square.at[gate, pl.ds(0, main), :],
                sems.at[2 * gate],
            )
        )
        copies.append(
            pltpu.make_async_copy(
                ninth_in.at[gate], square.at[gate, pl.ds(main, rest), :], sems.at[2 * gate + 1]
            )
        )
    for copy in copies:
        copy.start()

    def natural(places, values):
        return dot(dot(places[...], values).astype(bf16), to_natural[...]).astype(bf16)

    out[...] = natural(gather, output_rows[...])

    def right_product(left, matrix):
        return lax.dot_general(
            left, matrix, (((1,), (1,)), ((), ())), preferred_element_type=f32
        )

    found = jnp.zeros((rows, width), f32)
    for gate in range(4):
        copies[2 * gate].wait()
        copies[2 * gate + 1].wait()
        both = jnp.concatenate([late[gate], early[gate]], axis=0)
        found = found + right_product(both, square[gate])
    found = found * (in_rows[...].astype(f32) * KEEP_INPUT)
    d_out[...] = natural(unpack, found.astype(bf16))


def in_vmem():
    return pl.BlockSpec(memory_space=pltpu.VMEM)


def in_place():
    return pl.BlockSpec(memory_space=pl.ANY)


def places_for(*arrays):
    return [pltpu.VMEM(array.shape, array.dtype) for array in arrays]


def run_forward(wall, mixed, spread, collect, h_first, c_first, out_scale):
    steps_rows = spread.shape[0]
    rows, width = mixed.shape
    devices = wall.shape[0] // TILE
    all_kept = LONGEST * KINDS * LANES
    return pl.pallas_call(
        forward_kernel,
        out_shape=(
            jax.ShapeDtypeStruct((collect.shape[0], width), bf16),
            jax.ShapeDtypeStruct((steps_rows, width), bf16),
            jax.ShapeDtypeStruct((4, devices, width), bf16),
            jax.ShapeDtypeStruct((all_kept, width), f32),
            jax.ShapeDtypeStruct((4, width, width), bf16),
        ),
        in_specs=[in_place()] * 7,
        out_specs=(in_vmem(),) * 3 + (in_place(),) * 2,
        scratch_shapes=places_for(mixed, spread, collect, h_first, c_first, out_scale)
        + [
            pltpu.VMEM((width, 4 * width), bf16),
            pltpu.VMEM((width, 4 * width), bf16),
            pltpu.VMEM((devices * TILE, width), bf16),
            pltpu.VMEM((width // 128, devices * TILE, 128), f32),
            pltpu.VMEM((steps_rows, 4 * width), f32),
            pltpu.VMEM((all_kept, width), f32),
            pltpu.VMEM((steps_rows, width), f32),
            pltpu.VMEM((steps_rows, width), f32),
            pltpu.SemaphoreType.DMA((6,)),
            pltpu.SemaphoreType.DMA((4,)),
            pltpu.SemaphoreType.DMA,
            pltpu.SemaphoreType.DMA,
            pltpu.SemaphoreType.DMA((5,)),
            pltpu.SemaphoreType.DMA((4,)),
        ],
        compiler_params=pltpu.CompilerParams(vmem_limit_bytes=VMEM_LIMIT),
        cost_estimate=pl.CostEstimate(
            flops=60_000_000_000, bytes_accessed=30_000_000, transcendentals=2_000_000
        ),
        name="forward",
    )(wall, mixed, spread, collect, h_first, c_first, out_scale)


def run_backward(turned, kept, coming, spread, collect, out_scale, carry, first_step):
    steps_rows = spread.shape[0]
    rows, width = collect.shape[0], coming.shape[1]
    results = [jax.ShapeDtypeStruct((4, rows, width), bf16)]
    if first_step > 0:
        results.append(jax.ShapeDtypeStruct((2 * LANES, width), f32))
    return pl.pallas_call(
        functools.partial(backward_kernel, first_step=first_step),
        out_shape=results,
        in_specs=[in_place()] * 7,
        out_specs=[in_vmem()] * len(results),
        scratch_shapes=places_for(coming, spread, collect, out_scale, carry)
        + [
            pltpu.VMEM((4 * width, width), bf16),
            pltpu.VMEM((steps_rows * KINDS, width), f32),
            pltpu.VMEM((steps_rows, width), f32),
            pltpu.VMEM((steps_rows, 4 * width), f32),
            pltpu.SemaphoreType.DMA((5,)),
            pltpu.SemaphoreType.DMA((4,)),
            pltpu.SemaphoreType.DMA((2,)),
        ],
        compiler_params=pltpu.CompilerParams(vmem_limit_bytes=VMEM_LIMIT),
        cost_estimate=pl.CostEstimate(
            flops=steps_rows // LANES * 1_500_000_000, bytes_accessed=20_000_000, transcendentals=0
        ),
        name="backward_late" if first_step else "backward_early",
    )(turned, kept, coming, spread, collect, out_scale, carry)


def run_gradient(core, mixed_all, hidden_all, mine, other, begin, devices, so_far=()):
    half, rows, columns = mine.shape
    line = 2 * half
    width = mixed_all.shape[1]
    if so_far:
        result = jax.ShapeDtypeStruct((devices, MESSAGE, 128), bf16)
    else:
        result = jax.ShapeDtypeStruct((width, columns), f32)
    return pl.pallas_call(
        functools.partial(gradient_kernel, begin=begin),
        out_shape=result,
        in_specs=[pl.BlockSpec(memory_space=pltpu.SMEM)]
        + [in_place()] * (4 + len(so_far)),
        out_specs=in_vmem(),
        scratch_shapes=[
            pltpu.VMEM((line * rows, width), bf16),
            pltpu.VMEM((line * rows, columns), bf16),
            pltpu.VMEM((devices, 2 * TILE, 128), f32),
            pltpu.VMEM((width, columns), f32),
            pltpu.SemaphoreType.DMA((line,)),
            pltpu.SemaphoreType.DMA((line,)),
            pltpu.SemaphoreType.DMA,
        ],
        compiler_params=pltpu.CompilerParams(vmem_limit_bytes=VMEM_LIMIT),
        cost_estimate=pl.CostEstimate(
            flops=5_000_000_000, bytes_accessed=12_000_000, transcendentals=0
        ),
        name="gradient_early" if so_far else "gradient_late",
    )(core, mixed_all, hidden_all, mine, other, *so_far)


def run_settle(got, scale, width):
    devices = got.shape[0]
    wide = scale.shape[1]
    return pl.pallas_call(
        settle_kernel,
        out_shape=(
            jax.ShapeDtypeStruct((OWN * 8, width), bf16),
            jax.ShapeDtypeStruct((devices, 128), f32),
        ),
        in_specs=[in_vmem()] * 2,
        out_specs=(in_vmem(),) * 2,
        scratch_shapes=[pltpu.VMEM((wide // 128, OWN * 8, 128), f32)],
        compiler_params=pltpu.CompilerParams(vmem_limit_bytes=VMEM_SMALL),
        name="settle",
    )(got, scale)


def run_own(wall, ninth_in, late, early, in_rows, output_rows, gather, unpack, to_natural):
    width, natural = to_natural.shape
    rows = unpack.shape[0]
    return pl.pallas_call(
        own_kernel,
        out_shape=(jax.ShapeDtypeStruct((rows, natural), bf16),) * 2,
        in_specs=[in_place()] * 2 + [in_vmem()] * 7,
        out_specs=(in_vmem(),) * 2,
        scratch_shapes=[
            pltpu.VMEM((4, width, width), bf16),
            pltpu.SemaphoreType.DMA((8,)),
        ],
        compiler_params=pltpu.CompilerParams(vmem_limit_bytes=VMEM_LIMIT),
        cost_estimate=pl.CostEstimate(
            flops=8_000_000_000, bytes_accessed=15_000_000, transcendentals=0
        ),
        name="own",
    )(wall, ninth_in, late, early, in_rows, output_rows, gather, unpack, to_natural)


def split_exact(values):
    parts = []
    rest = values
    for _ in range(3):
        part = lax.reduce_precision(rest, 8, 7)
        parts.append(part.astype(bf16))
        rest = rest - part
    return parts


def body(
    inputs,
    d_out,
    h_start,
    c_start,
    pieces,
    in_mask,
    out_mask,
    w_mask,
    master,
    moment_one,
    moment_two,
):
    streams, steps, width = inputs.shape
    gates_n = 4 * width
    count_w = 2 * width * gates_n
    total = count_w + gates_n
    shard = master.shape[0]
    devices = lax.axis_size("batch")
    me = lax.axis_index("batch")
    wide = OWN * devices
    block = OWN * 2 * gates_n
    gap = block - shard
    most = gap * devices
    tokens = streams * steps
    rows_n = LATE + EARLY
    line = 8
    lines = devices // line

    line_groups = [[line * q + m for m in range(line)] for q in range(lines)]
    column_groups = [
        [line * q + 2 * y + c for y in range(line // 2)] for q in range(lines) for c in range(2)
    ]
    twins = [(i, i ^ 1) for i in range(devices)]

    to_kept = one_hot(width, wide, lambda k, p: place_of(k, devices) == p)
    to_natural = one_hot(wide, width, lambda p, k: place_of(k, devices) == p)

    places = me * shard + lax.iota(jnp.int32, shard)
    recurrent = (places < count_w) & (places % (2 * gates_n) >= gates_n)
    scale_low = jnp.where(recurrent, w_mask.astype(bf16) * KEEP_RECURRENT, jnp.ones((), bf16))
    local_low = master.astype(bf16) * scale_low
    local_low = jnp.where(places < total, local_low, jnp.zeros((), bf16))

    def realigned(flat, following):
        joined = jnp.concatenate([flat, following])
        rows = lax.dynamic_slice(joined, (gap * me,), (block,)).reshape(OWN * 8, width)
        return dot(rows, to_kept).astype(bf16)

    before = [(i + 1, i) for i in range(devices - 1)]
    order = one_hot(
        OWN * 8,
        OWN * 8,
        lambda a, b: jnp.where(a < 64, (a % 8) * 8 + a // 8, 64 + a % 8) == b,
    )
    own = realigned(local_low, lax.ppermute(local_low[:most], "batch", before))
    own = dot(order, own).astype(bf16)
    own = jnp.concatenate([own[TILE * j : TILE * (j + 1)] for j in range(OWN)], axis=1)
    wall = lax.all_gather(own, "batch", axis=0, tiled=True)
    scales = realigned(scale_low, lax.ppermute(scale_low[:most], "batch", before))

    in_scale = in_mask.astype(f32) * KEEP_INPUT
    mixed = (inputs.astype(f32) * in_scale[:, None, :]).astype(bf16).reshape(tokens, width)
    spare = ((0, rows_n - tokens), (0, 0))
    mixed = dot(jnp.pad(mixed, spare), to_kept).astype(bf16)
    bias_place = place_of(jnp.int32(width), devices)
    column = lax.broadcasted_iota(jnp.int32, mixed.shape, 1)
    mixed = jnp.where(column == bias_place, jnp.ones((), bf16), mixed)
    coming = dot(jnp.pad(d_out.reshape(tokens, width), spare), to_kept).astype(bf16)
    small = jnp.concatenate(
        [h_start.astype(bf16)]
        + split_exact(c_start)
        + [in_mask.astype(bf16), out_mask.astype(bf16)],
        axis=0,
    )
    small = dot(small, to_kept)
    part = [small[streams * j : streams * (j + 1)] for j in range(6)]
    empty = jnp.zeros((LANES - streams, wide), f32)
    h_first = jnp.concatenate([part[0], empty], axis=0)
    c_first = jnp.concatenate([part[1] + part[2] + part[3], empty], axis=0)
    out_scale_kept = part[5] * KEEP_OUTPUT
    out_scale = jnp.concatenate(
        [out_scale_kept, out_scale_kept, jnp.zeros((LANES - 2 * streams, wide), f32)], axis=0
    )
    base = jnp.arange(streams, dtype=jnp.int32) * steps
    none = jnp.zeros((LANES - 2 * streams,), jnp.int32)
    begins = jnp.concatenate([base, base + pieces[:, 0], none])
    lengths = jnp.concatenate([pieces[:, 0], pieces[:, 1], none])
    ticks = lax.broadcasted_iota(jnp.int32, (LONGEST, LANES), 0)
    active = ticks < lengths[None, :]
    where = jnp.where(active, begins[None, :] + ticks, -1).reshape(-1)
    spread = (where[:, None] == lax.iota(jnp.int32, rows_n)[None, :]).astype(bf16)
    late_first = jnp.maximum(pieces[:, 0] - SPLIT, 0)
    late_base = jnp.arange(streams, dtype=jnp.int32) * LATE_BLOCK
    late_base = jnp.concatenate([late_base, late_base + late_first, none])
    early_base = LATE + SPLIT * jnp.arange(LANES, dtype=jnp.int32)
    packed = jnp.where(ticks < SPLIT, early_base[None] + ticks, late_base[None] + ticks - SPLIT)
    packed = jnp.where(active, packed, -1).reshape(-1)
    collect = (lax.iota(jnp.int32, rows_n)[:, None] == packed[None, :]).astype(bf16)
    pack = dot(collect, spread).astype(bf16)
    unpack = (
        lax.dot_general(spread, collect, (((0,), (1,)), ((), ())), preferred_element_type=f32)
    ).astype(bf16)
    mixed_rows = dot(pack, mixed).astype(bf16)
    row_stream = lax.iota(jnp.int32, rows_n) // steps
    row_stream = (row_stream[:, None] == lax.iota(jnp.int32, streams)[None]).astype(bf16)
    in_rows = dot(pack, dot(row_stream, part[4].astype(bf16)).astype(bf16)).astype(bf16)

    begin = SPLIT * LANES
    ready = (wall, mixed, mixed_rows, coming, spread, collect, h_first, c_first, out_scale)
    ready += (in_rows, unpack, to_natural, scales, spread[:begin], spread[begin:])
    ready += (collect[LATE:, :begin], collect[:LATE, begin:], spread.T)
    ready = lax.optimization_barrier(ready)
    wall, mixed, mixed_rows, coming, spread, collect, h_first, c_first, out_scale = ready[:9]
    in_rows, unpack, to_natural, scales, spread_early, spread_late = ready[9:15]
    collect_early, collect_late, gather = ready[15:]
    mixed_all = lax.all_gather(
        mixed_rows, "batch", axis=0, tiled=True, axis_index_groups=line_groups
    )
    hidden_rows, output_rows, ninth_in, kept, turned = run_forward(
        wall, mixed, spread, collect, h_first, c_first, out_scale
    )
    hidden_rows, mixed_all = lax.optimization_barrier((hidden_rows, mixed_all))
    hidden_all = lax.all_gather(
        hidden_rows, "batch", axis=0, tiled=True, axis_index_groups=line_groups
    )
    late, carry = run_backward(
        turned, kept, coming, spread_late, collect_late, out_scale, out_scale, SPLIT
    )

    def exchange(rows):
        return lax.all_to_all(
            rows, "batch", 0, 0, tiled=True, axis_index_groups=column_groups
        )

    late_mine = exchange(late)
    (early,) = run_backward(
        turned, kept, coming, spread_early, collect_early, out_scale, carry, 0
    )
    late_mine, early = lax.optimization_barrier((late_mine, early))
    early_mine = exchange(early)
    core = (me % 2).reshape(1)
    so_far = run_gradient(
        core, mixed_all, hidden_all, late_mine, lax.ppermute(late_mine, "batch", twins), 0, devices
    )
    early_mine, so_far = lax.optimization_barrier((early_mine, so_far))
    message = run_gradient(
        core,
        mixed_all,
        hidden_all,
        early_mine,
        lax.ppermute(early_mine, "batch", twins),
        LATE,
        devices,
        (so_far,),
    )
    got = lax.all_to_all(message, "batch", 0, 0, tiled=True)

    d_rows, out_rows = run_own(
        wall, ninth_in, late, early, in_rows, output_rows, gather, unpack, to_natural
    )
    output = out_rows[:tokens].reshape(streams, steps, width)
    d_inputs = d_rows[:tokens].reshape(streams, steps, width)
    got, output, d_inputs = lax.optimization_barrier((got, output, d_inputs))

    home, squares = run_settle(got, scales, width)
    squares = lax.all_to_all(squares, "batch", 0, 0, tiled=True)
    home = home.reshape(block)
    tail = lax.ppermute(home[block - most :], "batch", [(i, i + 1) for i in range(devices - 1)])
    grad_shard = lax.dynamic_slice(
        jnp.concatenate([tail, home]), (most - gap * me,), (shard,)
    ).astype(f32)
    grad_norm = jnp.sqrt(jnp.sum(squares[:, 0]))

    factor = jnp.minimum(1.0, CLIP_NORM / (grad_norm + 1e-06))
    clipped = grad_shard * factor
    moment_new = BETA_ONE * moment_one + (1.0 - BETA_ONE) * clipped
    second_new = BETA_TWO * moment_two + (1.0 - BETA_TWO) * clipped * clipped
    first_hat = moment_new / (1.0 - BETA_ONE**STEP)
    second_hat = second_new / (1.0 - BETA_TWO**STEP)
    master_new = master - LEARN_RATE * (
        first_hat / (jnp.sqrt(second_hat) + EPSILON) + WEIGHT_DECAY * master
    )
    return (output, d_inputs, moment_new, second_new, master_new, grad_norm)


def solution(mesh):
    placed = (
        P("batch", None, None),
        P("batch", None, None),
        P("batch", None),
        P("batch", None),
        P("batch", None),
        P("batch", None),
        P("batch", None),
        P("batch"),
        P("batch"),
        P("batch"),
        P("batch"),
    )
    return jax.shard_map(
        body,
        mesh=mesh,
        in_specs=placed,
        out_specs=(
            P("batch", None, None),
            P("batch", None, None),
            P("batch"),
            P("batch"),
            P("batch"),
            P(),
        ),
        check_vma=False,
    )
```
